32 devices in a mesh: row: 8 (over z, x), col: 2 (over core), vec: 2 (over y).
Axes of the slice: x: 2, y: 2, z: 4, core: 2. Of those that a mesh axis runs over, the one named last changes fastest.
Arguments:
- vectors: bfloat16 [131072, 256], P(('row', 'col'), 'vec'), parts along dimension 1, may hold values from -6 to 6
- tile_blocks: bfloat16 [8, 2, 32, 256, 256], P('row', 'col'), may hold values from -0.375 to 0.375
- block_rows: int32 [8, 2, 32], P('row', 'col'), may hold values from 0 to 63, as said below
- block_cols: int32 [8, 2, 32], P('row', 'col'), may hold values from 0 to 255, as said below
- counts: int32 [8, 2], P('row', 'col'), may hold values from 1 to 32, as said below
Outputs:
- filtered: bfloat16 [131072, 256], P(('row', 'col'), 'vec'), parts along dimension 1
The draws below stay inside these ranges and needn't reach their ends.
There are 2 independent parts, one for each index of `vec`. The reference program is written for one: setup_inputs(seed, part) draws one part's arguments, and reference() takes and returns one part's arrays. A program takes and returns all parts, laid end to end along the dimension named above; an argument that names none is the same for every part. Nothing has to cross between parts.
Inputs may be any that keep to these rules, and one draw needn't show every extreme that they name: The pairs (block_rows, block_cols // 32) of the 32 slots of one tile are all distinct. Within one tile, all slots whose block columns lie in the same group of 32 (same block_cols // 32) name the same block column. `counts`: some tile uses all 32 slots.
All inputs are finite; a program needn't handle non-finite values.
Results may differ from the reference program's by a relative error of at most 0.015.
Values may be sent and summed in bfloat16 or wider, within the bound.
No kernel may reach another device: no remote copies, remote signals or barrier semaphores. Data moves between devices by JAX's collectives and lax.ppermute only.
A program may use at most 64 MiB of HBM per device.

```python
import jax
import jax.numpy as jnp
from jax import lax

B = 256
NB = 512
K = 128
MAXB = 32
DEGREE = 3
ORDER = 131072
RB = 64
PB = 32
N_ROW = 8
N_COL = 2


def pattern(key):
    base = jax.random.fold_in(key, 7)
    first_key, second_key, third_key, fourth_key = jax.random.split(base, 4)
    tile_keys = jax.random.split(first_key, N_ROW * N_COL)
    picks = jax.vmap(lambda k: jax.random.permutation(k, NB))(tile_keys)[:, :MAXB]
    picks = picks.reshape(N_ROW, N_COL, MAXB).astype(jnp.int32)
    slot_rows = (picks // N_ROW).astype(jnp.int32)
    piece_num = (picks % N_ROW).astype(jnp.int32)
    which = jax.random.randint(second_key, (N_ROW, N_COL, N_ROW), 0, PB).astype(jnp.int32)
    offset = jnp.take_along_axis(which, piece_num, axis=2)
    slot_cols = (piece_num * PB + offset).astype(jnp.int32)
    shifts = jax.random.randint(third_key, (N_ROW, N_COL), 0, 4).astype(jnp.int32)
    used = jnp.maximum(jnp.right_shift(jnp.full((N_ROW, N_COL), MAXB, jnp.int32), shifts), 1)
    busiest = jax.random.randint(fourth_key, (), 0, N_ROW * N_COL).astype(jnp.int32)
    flat_index = jnp.arange(N_ROW * N_COL, dtype=jnp.int32).reshape(N_ROW, N_COL)
    used = jnp.where(flat_index == busiest, MAXB, used).astype(jnp.int32)
    return (slot_rows, slot_cols, used)


def draw_block_rows(key, part):
    return pattern(key)[0]


def draw_block_cols(key, part):
    return pattern(key)[1]


def draw_counts(key, part):
    return pattern(key)[2]


def shard_levels(own_key, dims, pieces, low, high):
    level, own = 1.0, jax.random.fold_in(own_key, 6)
    for axis_at, blocks in pieces:
        steps = jnp.exp(jax.random.uniform(jax.random.fold_in(own, axis_at), (blocks,), jnp.float32, low / len(pieces), high / len(pieces)))
        level = level * jnp.repeat(steps, dims[axis_at] // blocks).reshape([-1 if axis == axis_at else 1 for axis in range(len(dims))])
    return level


def noise(stream_key, extent, width, reach, cuts=(), kind=jnp.bfloat16):
    gain = shard_levels(stream_key, extent, cuts, -0.22, 0.18) if cuts else 1.0
    entries = jax.random.normal(stream_key, extent, jnp.float32) * width * gain
    return jnp.minimum(jnp.maximum(entries, -reach), reach).astype(kind)


def setup_inputs(seed: int = 0, part: int = 0) -> dict:
    key_of = jax.random.split(jax.random.key(seed), 6)
    part_splits = jax.random.split(jax.random.fold_in(key_of[5], part), 6)
    vectors = noise(part_splits[0], (ORDER, K), 1.0, 6.0, ((0, 16),))
    tile_blocks = noise(key_of[1], (N_ROW, N_COL, MAXB, B, B), (B * max(1, N_COL * MAXB // (2 * RB))) ** -0.5, 0.375, ((0, 8), (1, 2)))
    block_rows = draw_block_rows(jax.random.fold_in(key_of[5], 71), part)
    block_cols = draw_block_cols(jax.random.fold_in(key_of[5], 71), part)
    counts = draw_counts(jax.random.fold_in(key_of[5], 71), part)
    return {"vectors": vectors, "tile_blocks": tile_blocks, "block_rows": block_rows, "block_cols": block_cols, "counts": counts}


center_value = 0.5
half_width = 2.0


def tile_term(tile_data, slot_rows, slot_cols, used, vec_all, tile_col):
    piece_num = slot_cols // PB
    offset = slot_cols % PB
    global_col = ((piece_num * N_COL + tile_col) * PB + offset).astype(jnp.int32)
    vec_blocks = jnp.take(vec_all, global_col, axis=0).astype(jnp.float32)
    products = jnp.einsum('sij,sjk->sik', tile_data.astype(jnp.float32), vec_blocks, precision=lax.Precision.HIGHEST)
    live = (jnp.arange(MAXB) < used).astype(jnp.float32)
    onehot = (slot_rows[None, :] == jnp.arange(RB)[:, None]).astype(jnp.float32) * live[None, :]
    term = jnp.einsum('ls,sik->lik', onehot, products, precision=lax.Precision.HIGHEST)
    return term.astype(jnp.bfloat16)


def apply_tiles(current, tile_blocks, block_rows, block_cols, counts):
    vec_all = current.reshape(NB, B, K)

    def one_row(tile_row):
        def one_col(tile_col):
            term = tile_term(tile_blocks[tile_row, tile_col], block_rows[tile_row, tile_col],
                             block_cols[tile_row, tile_col], counts[tile_row, tile_col], vec_all, tile_col)
            return term.astype(jnp.float32)
        terms = lax.map(one_col, jnp.arange(N_COL))
        return jnp.sum(terms, axis=0)

    summed = lax.map(one_row, jnp.arange(N_ROW))
    return summed.reshape(ORDER, K)


def reference(vectors, tile_blocks, block_rows, block_cols, counts):
    previous = vectors
    applied = apply_tiles(vectors, tile_blocks, block_rows, block_cols, counts)
    current = ((applied - center_value * previous.astype(jnp.float32)) / half_width).astype(jnp.bfloat16)
    for repeat in range(DEGREE - 1):
        applied = apply_tiles(current, tile_blocks, block_rows, block_cols, counts)
        following = (2.0 * (applied - center_value * current.astype(jnp.float32)) / half_width
                     - previous.astype(jnp.float32)).astype(jnp.bfloat16)
        previous, current = current, following
    return current
```

```python
import functools

import jax
import jax.numpy as jnp
from jax import lax
from jax.experimental import pallas as pl
from jax.experimental.pallas import tpu as pltpu
from jax.sharding import PartitionSpec as P

DEGREE = 3

center_value = 0.5
half_width = 2.0

VMEM = pltpu.VMEM
SMEM = pltpu.SMEM
VMEM_LIMIT = 48 * 1024 * 1024


def spec(space):
    return pl.BlockSpec(memory_space=space)


def plan_kernel(n_row, piece_blocks, place, rows_a, cols_a, used_a, rows_b, cols_b, used_b, out):
    me = place[0]
    half = place[1]
    first_row = half * piece_blocks

    def scan(rows, cols, used, side, at):
        def step(s, at):
            row = rows[s] - first_row
            mine = (row >= 0) & (row < piece_blocks)

            @pl.when(mine)
            def _():
                out[8 + 3 * at] = s
                out[9 + 3 * at] = row
                out[10 + 3 * at] = side * n_row + lax.bitwise_xor(cols[s] // piece_blocks, me)

            return at + mine.astype(jnp.int32)

        return lax.fori_loop(0, used[0], step, at)

    own = scan(rows_a, cols_a, used_a, 0, jnp.int32(0))
    both = scan(rows_b, cols_b, used_b, 1, own)
    out[8 + 3 * both] = 0
    out[9 + 3 * both] = piece_blocks
    out[10 + 3 * both] = 0
    out[0] = own
    out[1] = both


def pick_kernel(n_row, block_size, place, wanted, vectors, *rest):
    outs, sems = rest[:-1], rest[-1]
    me = place[0]
    copies = []
    for k in range(n_row):
        at = wanted[lax.bitwise_xor(me, k)] * block_size
        copies.append(
            pltpu.make_async_copy(vectors.at[pl.ds(at, block_size)], outs[k], sems.at[k])
        )
    for copy in copies:
        copy.start()
    for copy in copies:
        copy.wait()


def apply_kernel(n_row, first, last, place, wanted, plan, tile_a, tile_b, *rest):
    pieces = rest[: 2 * n_row]
    rest = rest[2 * n_row :]
    if first:
        current, rest = rest[0], rest[1:]
        previous = None
    else:
        current, previous, rest = rest[0], rest[1], rest[2:]
    following, rest = rest[0], rest[1:]
    outs, rest = (rest[:0], rest) if last else (rest[:n_row], rest[n_row:])
    blocks, vec, total, sems = rest
    block_size = blocks.shape[-1]
    piece_blocks = total.shape[0] - 1
    own, both = plan[0], plan[1]

    def fetch(tile, i):
        return pltpu.make_async_copy(tile.at[plan[8 + 3 * i]], blocks.at[i], sems.at[i])

    @pl.loop(0, own)
    def _(i):
        fetch(tile_a, i).start()

    @pl.loop(own, both)
    def _(i):
        fetch(tile_b, i).start()

    for q in range(2 * n_row):
        vec[q] = pieces[q][...]

    @pl.loop(0, piece_blocks)
    def _(b):
        at = pl.ds(pl.multiple_of(b * block_size, block_size), block_size)
        value = -center_value * current[at, :].astype(jnp.float32)
        if previous is not None:
            value = value - previous[at, :].astype(jnp.float32)
        total[b] = value

    def product(i):
        return jnp.dot(
            blocks[i], vec[plan[10 + 3 * i]], preferred_element_type=jnp.float32
        )

    @pl.loop(0, (both + 1) // 2)
    def _(j):
        i = 2 * j
        fetch(tile_a, i).wait()

        @pl.when(i + 1 < both)
        def _():
            fetch(tile_a, i + 1).wait()

        one = product(i)
        two = product(i + 1)
        total[plan[9 + 3 * i]] += one
        total[plan[12 + 3 * i]] += two

    scale = 1.0 / half_width if first else 2.0 / half_width

    @pl.loop(0, piece_blocks)
    def _(b):
        at = pl.ds(pl.multiple_of(b * block_size, block_size), block_size)
        value = total[b]
        if scale != 1.0:
            value = value * scale
        following[at, :] = value.astype(jnp.bfloat16)

    if not last:
        me = place[0]
        for k in range(n_row):
            at = pl.multiple_of(wanted[lax.bitwise_xor(me, k)] * block_size, block_size)
            outs[k][...] = following[pl.ds(at, block_size), :]


def on_pair(vectors, tile_blocks, block_rows, block_cols, counts):
    n_row = lax.axis_size("row")
    tile = tile_blocks[0, 0]
    slot_rows = block_rows[0, 0]
    slot_cols = block_cols[0, 0]
    used = counts[0]
    slot_count, block_size, _ = tile.shape
    width = vectors.shape[1]
    piece_blocks = vectors.shape[0] // block_size
    me = lax.axis_index("row")
    place = jnp.stack([me, lax.axis_index("col")]).astype(jnp.int32)

    source_piece = slot_cols // piece_blocks
    offset = slot_cols % piece_blocks
    live = jnp.arange(slot_count) < used[0]
    needed = jnp.max(
        jnp.where(
            (source_piece[None, :] == jnp.arange(n_row)[:, None]) & live[None, :],
            offset[None, :],
            0,
        ),
        axis=1,
    )
    wanted = lax.all_to_all(
        needed.reshape(n_row, 1), "row", split_axis=0, concat_axis=0, tiled=True
    ).reshape(n_row)

    swap = [(0, 1), (1, 0)]
    across = functools.partial(lax.ppermute, axis_name="col", perm=swap)
    meta = across(jnp.concatenate([slot_rows, slot_cols, used]))
    tile_other = across(tile)
    plan = pl.pallas_call(
        functools.partial(plan_kernel, n_row, piece_blocks),
        out_shape=jax.ShapeDtypeStruct((8 + 3 * (2 * slot_count + 1),), jnp.int32),
        in_specs=[spec(SMEM)] * 7,
        out_specs=spec(SMEM),
    )(
        place,
        slot_rows,
        slot_cols,
        used,
        meta[:slot_count],
        meta[slot_count : 2 * slot_count],
        meta[2 * slot_count :],
    )

    block_shape = jax.ShapeDtypeStruct((block_size, width), jnp.bfloat16)
    order = sorted(range(1, n_row), reverse=True)

    def exchange(outgoing):
        received = [None] * n_row
        received[0] = outgoing[0]
        for k in order:
            received[k] = lax.ppermute(
                outgoing[k], "row", [(i, i ^ k) for i in range(n_row)]
            )
        return received + [across(block) for block in received]

    def apply(first, last, pieces, current, previous):
        args = (current,) if first else (current, previous)
        whole = jax.ShapeDtypeStruct(vectors.shape, jnp.bfloat16)
        outs = pl.pallas_call(
            functools.partial(apply_kernel, n_row, first, last),
            out_shape=[whole] + ([] if last else [block_shape] * n_row),
            in_specs=[spec(SMEM)] * 3
            + [spec(pl.ANY)] * 2
            + [spec(VMEM)] * (2 * n_row + len(args)),
            out_specs=[spec(VMEM)] * (1 if last else 1 + n_row),
            scratch_shapes=[
                VMEM((2 * slot_count + 1, block_size, block_size), jnp.bfloat16),
                VMEM((2 * n_row, block_size, width), jnp.bfloat16),
                VMEM((piece_blocks + 1, block_size, width), jnp.float32),
                pltpu.SemaphoreType.DMA((2 * slot_count + 1,)),
            ],
            compiler_params=pltpu.CompilerParams(vmem_limit_bytes=VMEM_LIMIT),
        )(place, wanted, plan, tile, tile_other, *pieces, *args)
        return outs[0], outs[1:]

    outgoing = pl.pallas_call(
        functools.partial(pick_kernel, n_row, block_size),
        out_shape=[block_shape] * n_row,
        in_specs=[spec(SMEM)] * 2 + [spec(pl.ANY)],
        out_specs=[spec(pl.ANY)] * n_row,
        scratch_shapes=[pltpu.SemaphoreType.DMA((n_row,))],
    )(place, wanted, vectors)

    previous, current = None, vectors
    for repeat in range(DEGREE):
        following, outgoing = apply(
            repeat == 0, repeat == DEGREE - 1, exchange(outgoing), current, previous
        )
        previous, current = current, following
    return current


def on_any(vectors, tile_blocks, block_rows, block_cols, counts):
    n_row = lax.axis_size("row")
    n_col = lax.axis_size("col")
    tile_data = tile_blocks[0, 0]
    slot_rows = block_rows[0, 0]
    slot_cols = block_cols[0, 0]
    used = counts[0, 0]
    block_size = tile_data.shape[-1]
    width = vectors.shape[1]
    piece_blocks = vectors.shape[0] // block_size
    row_blocks = piece_blocks * n_col
    slot_count = tile_data.shape[0]
    live = (jnp.arange(slot_count) < used).astype(jnp.float32)
    onehot = (slot_rows[None, :] == jnp.arange(row_blocks)[:, None]).astype(jnp.float32) * live[
        None, :
    ]
    source_piece = slot_cols // piece_blocks
    offset = slot_cols % piece_blocks
    needed = jnp.max(
        jnp.where(source_piece[None, :] == jnp.arange(n_row)[:, None], offset[None, :], 0), axis=1
    )
    wanted = lax.all_to_all(
        needed.reshape(n_row, 1), "row", split_axis=0, concat_axis=0, tiled=True
    ).reshape(n_row)

    def apply_tiles(current):
        own_blocks = current.reshape(piece_blocks, block_size, width)
        outgoing = jnp.take(own_blocks, wanted, axis=0)
        received = lax.all_to_all(outgoing, "row", split_axis=0, concat_axis=0, tiled=True)
        vec_blocks = jnp.take(received, source_piece, axis=0)
        products = jnp.einsum(
            "sij,sjk->sik", tile_data, vec_blocks, preferred_element_type=jnp.float32
        )
        term = jnp.einsum("ls,sik->lik", onehot, products, precision=lax.Precision.HIGHEST)
        term = term.reshape(row_blocks * block_size, width)
        return lax.psum_scatter(
            term.astype(jnp.bfloat16), "col", scatter_dimension=0, tiled=True
        ).astype(jnp.float32)

    previous = vectors
    applied = apply_tiles(vectors)
    current = ((applied - center_value * previous.astype(jnp.float32)) / half_width).astype(
        jnp.bfloat16
    )
    for repeat in range(DEGREE - 1):
        applied = apply_tiles(current)
        following = (
            2.0 * (applied - center_value * current.astype(jnp.float32)) / half_width
            - previous.astype(jnp.float32)
        ).astype(jnp.bfloat16)
        previous, current = (current, following)
    return current


def solution(mesh):
    n_row, n_col = mesh.shape["row"], mesh.shape["col"]
    paired = n_col == 2 and n_row & (n_row - 1) == 0
    return jax.shard_map(
        on_pair if paired else on_any,
        mesh=mesh,
        in_specs=(
            P(("row", "col"), "vec"),
            P("row", "col", None, None, None),
            P("row", "col", None),
            P("row", "col", None),
            P("row", "col"),
        ),
        out_specs=P(("row", "col"), "vec"),
        check_vma=False,
    )
```

```python
import functools

import jax
import jax.numpy as jnp
from jax import lax
from jax.experimental import pallas as pl
from jax.experimental.pallas import tpu as pltpu
from jax.sharding import PartitionSpec as P

DEGREE = 3

center_value = 0.5
half_width = 2.0

VMEM = pltpu.VMEM
SMEM = pltpu.SMEM
LANES = 128
UNROLL = 2
HEAD = 8


def spec(space):
    return pl.BlockSpec(memory_space=space)


def params(mib):
    return pltpu.CompilerParams(vmem_limit_bytes=mib * 1024 * 1024)


def round_up(n, step):
    return (n + step - 1) // step * step


def plan_kernel(n_row, piece_blocks, wanted_at, place, wanted, rows_a, cols_a, used_a, meta_b, out):
    slot_count = rows_a.shape[0]
    first_row = place[1] * piece_blocks

    def write(at, one, two, three):
        out[at] = one
        out[at + 1] = two
        out[at + 2] = three

    def scan(row_of, col_of, used, at, sent):
        def step(s, carry):
            at, sent = carry
            row = row_of(s) - first_row
            mine = ((row >= 0) & (row < piece_blocks)).astype(jnp.int32)
            piece = col_of(s) // piece_blocks
            write(HEAD + 3 * at, s, row, piece)
            for k in range(n_row):
                write(wanted_at + 3 * sent, at, k, piece)
                sent = sent + jnp.where(wanted[k, 0] == row, mine, 0)
            return at + mine, sent

        at, sent = lax.fori_loop(0, used, step, (at, sent))
        for _ in range(UNROLL):
            write(HEAD + 3 * at, 0, piece_blocks, 0)
            write(wanted_at + 3 * sent, 0, n_row, 0)
            at = at + jnp.where(at % UNROLL == 0, 0, 1)
            sent = sent + jnp.where(sent % UNROLL == 0, 0, 1)
        return at, sent

    zero = jnp.int32(0)
    at, sent = scan(lambda s: rows_a[s], lambda s: cols_a[s], used_a[0], zero, zero)
    out[0] = at
    out[2] = sent
    at, sent = scan(
        lambda s: meta_b[s], lambda s: meta_b[slot_count + s], meta_b[2 * slot_count], at, sent
    )
    out[1] = at
    out[3] = sent


def pick_kernel(n_row, block_size, wanted, vectors, out):
    for k in range(n_row):
        at = pl.multiple_of(wanted[k, 0] * block_size, block_size)
        out[k] = vectors[pl.ds(at, block_size), :]


def load_kernel(plan, tile_a, tile_b, blocks, sem):
    def copy(tile, i):
        return pltpu.make_async_copy(tile.at[plan[HEAD + 3 * i]], blocks.at[i], sem)

    @pl.loop(0, plan[0])
    def _(i):
        copy(tile_a, i).start()

    @pl.loop(plan[0], plan[1])
    def _(i):
        copy(tile_b, i).start()

    @pl.loop(0, plan[1])
    def _(i):
        copy(tile_a, i).wait()


def add_products(plan, base, begin, end, position, blocks, pieces, total):
    @pl.loop(begin // UNROLL, end // UNROLL)
    def _(j):
        values = []
        for u in range(UNROLL):
            at = base + 3 * (UNROLL * j + u)
            block = plan[at] if position else UNROLL * j + u
            values.append(
                jnp.dot(blocks[block], pieces[plan[at + 2]], preferred_element_type=jnp.float32)
            )
        for u in range(UNROLL):
            total[plan[base + 3 * (UNROLL * j + u) + 1]] += values[u]


def start_value(current, previous, at):
    value = -center_value * current[at, :].astype(jnp.float32)
    if previous is not None:
        value = value - previous[at, :].astype(jnp.float32)
    return value


def scaled(first, value):
    return (value / half_width if first else value).astype(jnp.bfloat16)


def split_refs(first, rest):
    if first:
        return rest[0], None, rest[1:]
    return rest[0], rest[1], rest[2:]


def sent_kernel(n_row, first, wanted_at, wanted, plan, blocks, pieces_a, pieces_b, *rest):
    current, previous, (out, total) = split_refs(first, rest)
    block_size = blocks.shape[-1]
    for k in range(n_row):
        at = pl.ds(pl.multiple_of(wanted[k, 0] * block_size, block_size), block_size)
        total[k] = start_value(current, previous, at)
    add_products(plan, wanted_at, 0, plan[2], True, blocks, pieces_a, total)
    add_products(plan, wanted_at, plan[2], plan[3], True, blocks, pieces_b, total)
    for k in range(n_row):
        out[k] = scaled(first, total[k])


def all_kernel(first, plan, blocks, pieces_a, pieces_b, *rest):
    current, previous, (out, total) = split_refs(first, rest)
    block_size = blocks.shape[-1]
    piece_blocks = total.shape[0] - 1

    def rows(b):
        return pl.ds(pl.multiple_of(b * block_size, block_size), block_size)

    @pl.loop(0, piece_blocks)
    def _(b):
        total[b] = start_value(current, previous, rows(b))

    add_products(plan, HEAD, 0, plan[0], False, blocks, pieces_a, total)
    add_products(plan, HEAD, plan[0], plan[1], False, blocks, pieces_b, total)

    @pl.loop(0, piece_blocks)
    def _(b):
        out[rows(b), :] = scaled(first, total[b])


def on_pair(vectors, tile_blocks, block_rows, block_cols, counts):
    n_row = lax.axis_size("row")
    tile = tile_blocks[0, 0]
    slot_rows = block_rows[0, 0]
    slot_cols = block_cols[0, 0]
    used = counts[0]
    slot_count, block_size, _ = tile.shape
    width = vectors.shape[1]
    piece_blocks = vectors.shape[0] // block_size
    place = jnp.stack([lax.axis_index("row"), lax.axis_index("col")]).astype(jnp.int32)

    source_piece = slot_cols // piece_blocks
    offset = slot_cols % piece_blocks
    live = jnp.arange(slot_count) < used[0]
    needed = jnp.max(
        jnp.where(
            (source_piece[None, :] == jnp.arange(n_row)[:, None]) & live[None, :],
            offset[None, :],
            0,
        ),
        axis=1,
        keepdims=True,
    )
    wanted = lax.all_to_all(
        jnp.broadcast_to(needed, (n_row, LANES)), "row", split_axis=0, concat_axis=0, tiled=True
    )
    outgoing = pl.pallas_call(
        functools.partial(pick_kernel, n_row, block_size),
        out_shape=jax.ShapeDtypeStruct((n_row, block_size, width), jnp.bfloat16),
        in_specs=[spec(SMEM), spec(VMEM)],
        out_specs=spec(VMEM),
        name="pick",
    )(wanted, vectors)

    across = functools.partial(lax.ppermute, axis_name="col", perm=[(0, 1), (1, 0)])
    meta = across(jnp.concatenate([slot_rows, slot_cols, used]))
    tile_other = across(tile)

    capacity = round_up(slot_count, UNROLL) * 2
    wanted_at = HEAD + 3 * (capacity + 1)
    plan_size = wanted_at + 3 * (2 * n_row * n_row + 2 * UNROLL + 1)
    plan = pl.pallas_call(
        functools.partial(plan_kernel, n_row, piece_blocks, wanted_at),
        out_shape=jax.ShapeDtypeStruct((plan_size,), jnp.int32),
        in_specs=[spec(SMEM)] * 6,
        out_specs=spec(SMEM),
        name="plan",
    )(place, wanted, slot_rows, slot_cols, used, meta)
    blocks = pl.pallas_call(
        load_kernel,
        out_shape=jax.ShapeDtypeStruct((capacity, block_size, block_size), jnp.bfloat16),
        in_specs=[spec(SMEM)] + [spec(pl.ANY)] * 2,
        out_specs=spec(VMEM),
        scratch_shapes=[pltpu.SemaphoreType.DMA],
        compiler_params=params(16),
        name="load",
    )(plan, tile, tile_other)

    def cost(products, rows):
        size = block_size * width
        return pl.CostEstimate(
            flops=2 * products * block_size * size,
            bytes_accessed=2 * (products * block_size * block_size + 3 * rows * size),
            transcendentals=0,
        )

    def sent_blocks(first, args):
        return pl.pallas_call(
            functools.partial(sent_kernel, n_row, first, wanted_at),
            out_shape=jax.ShapeDtypeStruct((n_row, block_size, width), jnp.bfloat16),
            in_specs=[spec(SMEM)] * 2 + [spec(VMEM)] * (len(args) + 1),
            out_specs=spec(VMEM),
            scratch_shapes=[VMEM((n_row + 1, block_size, width), jnp.float32)],
            cost_estimate=cost(n_row, n_row),
            name="sent",
        )(wanted, plan, blocks, *args)

    def all_blocks(first, args):
        return pl.pallas_call(
            functools.partial(all_kernel, first),
            out_shape=jax.ShapeDtypeStruct(vectors.shape, jnp.bfloat16),
            in_specs=[spec(SMEM)] + [spec(VMEM)] * (len(args) + 1),
            out_specs=spec(VMEM),
            scratch_shapes=[VMEM((piece_blocks + 1, block_size, width), jnp.float32)],
            cost_estimate=cost(slot_count, piece_blocks),
            name="all",
        )(plan, blocks, *args)

    previous, current = None, vectors
    for repeat in range(DEGREE):
        first = repeat == 0
        pieces = lax.all_to_all(outgoing, "row", split_axis=0, concat_axis=0, tiled=True)
        args = (pieces, across(pieces), current) + (() if first else (previous,))
        if repeat < DEGREE - 1:
            outgoing = sent_blocks(first, args)
        previous, current = current, all_blocks(first, args)
    return current


def on_any(vectors, tile_blocks, block_rows, block_cols, counts):
    n_row = lax.axis_size("row")
    n_col = lax.axis_size("col")
    tile_data = tile_blocks[0, 0]
    slot_rows = block_rows[0, 0]
    slot_cols = block_cols[0, 0]
    used = counts[0, 0]
    block_size = tile_data.shape[-1]
    width = vectors.shape[1]
    piece_blocks = vectors.shape[0] // block_size
    row_blocks = piece_blocks * n_col
    slot_count = tile_data.shape[0]
    live = (jnp.arange(slot_count) < used).astype(jnp.float32)
    onehot = (slot_rows[None, :] == jnp.arange(row_blocks)[:, None]).astype(jnp.float32) * live[
        None, :
    ]
    source_piece = slot_cols // piece_blocks
    offset = slot_cols % piece_blocks
    needed = jnp.max(
        jnp.where(source_piece[None, :] == jnp.arange(n_row)[:, None], offset[None, :], 0), axis=1
    )
    wanted = lax.all_to_all(
        needed.reshape(n_row, 1), "row", split_axis=0, concat_axis=0, tiled=True
    ).reshape(n_row)

    def apply_tiles(current):
        own_blocks = current.reshape(piece_blocks, block_size, width)
        outgoing = jnp.take(own_blocks, wanted, axis=0)
        received = lax.all_to_all(outgoing, "row", split_axis=0, concat_axis=0, tiled=True)
        vec_blocks = jnp.take(received, source_piece, axis=0)
        products = jnp.einsum(
            "sij,sjk->sik", tile_data, vec_blocks, preferred_element_type=jnp.float32
        )
        term = jnp.einsum("ls,sik->lik", onehot, products, precision=lax.Precision.HIGHEST)
        term = term.reshape(row_blocks * block_size, width)
        return lax.psum_scatter(
            term.astype(jnp.bfloat16), "col", scatter_dimension=0, tiled=True
        ).astype(jnp.float32)

    previous = vectors
    applied = apply_tiles(vectors)
    current = ((applied - center_value * previous.astype(jnp.float32)) / half_width).astype(
        jnp.bfloat16
    )
    for repeat in range(DEGREE - 1):
        applied = apply_tiles(current)
        following = (
            2.0 * (applied - center_value * current.astype(jnp.float32)) / half_width
            - previous.astype(jnp.float32)
        ).astype(jnp.bfloat16)
        previous, current = (current, following)
    return current


def solution(mesh):
    n_row, n_col = mesh.shape["row"], mesh.shape["col"]
    paired = n_col == 2 and n_row & (n_row - 1) == 0
    return jax.shard_map(
        on_pair if paired else on_any,
        mesh=mesh,
        in_specs=(
            P(("row", "col"), "vec"),
            P("row", "col", None, None, None),
            P("row", "col", None),
            P("row", "col", None),
            P("row", "col"),
        ),
        out_specs=P(("row", "col"), "vec"),
        check_vma=False,
    )
```

```python
import functools

import jax
import jax.numpy as jnp
from jax import lax
from jax.experimental import pallas as pl
from jax.experimental.pallas import tpu as pltpu
from jax.sharding import PartitionSpec as P

DEGREE = 3

center_value = 0.5
half_width = 2.0

VMEM = pltpu.VMEM
SMEM = pltpu.SMEM
DMA = pltpu.SemaphoreType.DMA
LANES = 128
UNROLL = 2
RING = 16
HEAD = 8


def spec(space):
    return pl.BlockSpec(memory_space=space)


def params(mib):
    return pltpu.CompilerParams(vmem_limit_bytes=mib * 1024 * 1024)


def round_up(n, step):
    return (n + step - 1) // step * step


def plan_kernel(n_row, piece_blocks, sent_at, place, wanted, rows_a, cols_a, used_a, meta_b, out):
    slot_count = rows_a.shape[0]
    first_row = place[1] * piece_blocks

    def write(at, one, two, three):
        out[at] = one
        out[at + 1] = two
        out[at + 2] = three

    def scan(row_of, col_of, used, at, sent):
        def step(s, carry):
            at, sent = carry
            row = row_of(s) - first_row
            mine = ((row >= 0) & (row < piece_blocks)).astype(jnp.int32)
            piece = col_of(s) // piece_blocks
            write(HEAD + 3 * at, s, row, piece)
            for k in range(n_row):
                write(sent_at + 3 * sent, s, k, piece)
                sent = sent + jnp.where(wanted[k, 0] == row, mine, 0)
            return at + mine, sent

        at, sent = lax.fori_loop(0, used, step, (at, sent))
        for _ in range(UNROLL):
            write(HEAD + 3 * at, 0, piece_blocks, 0)
            write(sent_at + 3 * sent, 0, n_row, 0)
            at = at + jnp.where(at % UNROLL == 0, 0, 1)
            sent = sent + jnp.where(sent % UNROLL == 0, 0, 1)
        return at, sent

    zero = jnp.int32(0)
    at, sent = scan(lambda s: rows_a[s], lambda s: cols_a[s], used_a[0], zero, zero)
    out[0] = at
    out[2] = sent
    at, sent = scan(
        lambda s: meta_b[s], lambda s: meta_b[slot_count + s], meta_b[2 * slot_count], at, sent
    )
    out[1] = at
    out[3] = sent


def pick_kernel(n_row, block_size, wanted, vectors, out, sem):
    def copy(k):
        at = pl.multiple_of(wanted[k, 0] * block_size, block_size)
        return pltpu.make_async_copy(vectors.at[pl.ds(at, block_size)], out.at[k], sem.at[k])

    for k in range(n_row):
        copy(k).start()
    for k in range(n_row):
        copy(k).wait()


def add_products(plan, base, ends, tiles, vec, total, ring, sems, ready):
    mid, end = plan[ends], plan[ends + 1]

    def copy(side, i):
        at = lax.rem(i, RING)
        return pltpu.make_async_copy(tiles[side].at[plan[base + 3 * i]], ring.at[at], sems.at[at])

    def start(i):
        @pl.when(i < mid)
        def _():
            copy(0, i).start()

        @pl.when((i >= mid) & (i < end))
        def _():
            copy(1, i).start()

    for i in range(RING):
        start(jnp.int32(i))
    ready()

    def run(side, begin, end):
        @pl.loop(begin // UNROLL, end // UNROLL)
        def _(j):
            i = UNROLL * j
            for u in range(UNROLL):
                copy(0, i + u).wait()
            values = []
            for u in range(UNROLL):
                block = ring[lax.rem(i + u, RING)]
                piece = vec[side, plan[base + 3 * (i + u) + 2]]
                values.append(jnp.dot(block, piece, preferred_element_type=jnp.float32))
            for u in range(UNROLL):
                total[plan[base + 3 * (i + u) + 1]] += values[u]
            for u in range(UNROLL):
                start(i + RING + u)

    run(0, 0, mid)
    run(1, mid, end)


def sent_kernel(first, sent_at, plan, tile_a, tile_b, pieces_a, pieces_b, *rest):
    if first:
        current, out, vec, total, ring, sems, vec_sems = rest
        previous = None
    else:
        current, previous, out, vec, total, ring, sems, vec_sems = rest
    n_row = out.shape[0]

    def ready():
        for side, pieces in enumerate((pieces_a, pieces_b)):
            pltpu.make_async_copy(pieces, vec.at[side], vec_sems.at[side]).start()
        for k in range(n_row):
            value = -center_value * current[k].astype(jnp.float32)
            if not first:
                value = value - previous[k].astype(jnp.float32)
            total[k] = value
        for side, pieces in enumerate((pieces_a, pieces_b)):
            pltpu.make_async_copy(pieces, vec.at[side], vec_sems.at[side]).wait()

    add_products(plan, sent_at, 2, (tile_a, tile_b), vec, total, ring, sems, ready)
    for k in range(n_row):
        value = total[k]
        out[k] = (value / half_width if first else value).astype(jnp.bfloat16)


def early_kernel(plan, tile_a, tile_b, pieces, others, vectors, base, vec, total, ring, sems, vec_sems):
    width = vectors.shape[1]
    block_size = ring.shape[-1]
    piece_blocks = base.shape[0]

    def ready():
        copies = [
            pltpu.make_async_copy(
                refs[step], vec.at[side, :, :, pl.ds(step * width, width)], vec_sems.at[step, side]
            )
            for side, refs in enumerate((pieces, others))
            for step in range(2)
        ]
        for copy in copies:
            copy.start()

        @pl.loop(0, piece_blocks)
        def _(b):
            at = pl.ds(pl.multiple_of(b * block_size, block_size), block_size)
            value = vectors[at, :].astype(jnp.float32)
            total[b, :, :width] = -center_value * value
            total[b, :, width:] = -value

        for copy in copies:
            copy.wait()

    add_products(plan, HEAD, 0, (tile_a, tile_b), vec, total, ring, sems, ready)

    @pl.loop(0, piece_blocks)
    def _(b):
        first = (total[b, :, :width] / half_width).astype(jnp.bfloat16).astype(jnp.float32)
        second = total[b, :, width:] - center_value * first
        second = second.astype(jnp.bfloat16).astype(jnp.float32)
        base[b] = -center_value * second - first


def last_kernel(plan, tile_a, tile_b, pieces_a, pieces_b, base, out, vec, total, ring, sems, vec_sems):
    piece_blocks, block_size, _ = base.shape

    def ready():
        copies = [
            pltpu.make_async_copy(pieces, vec.at[side], vec_sems.at[side])
            for side, pieces in enumerate((pieces_a, pieces_b))
        ]
        copies.append(
            pltpu.make_async_copy(base, total.at[pl.ds(0, piece_blocks)], vec_sems.at[2])
        )
        for copy in copies:
            copy.start()
        for copy in copies:
            copy.wait()

    add_products(plan, HEAD, 0, (tile_a, tile_b), vec, total, ring, sems, ready)

    @pl.loop(0, piece_blocks)
    def _(b):
        at = pl.ds(pl.multiple_of(b * block_size, block_size), block_size)
        out[at, :] = total[b].astype(jnp.bfloat16)


def after(value, *others):
    return lax.optimization_barrier((value, *others))[0]


def on_pair(vectors, tile_blocks, block_rows, block_cols, counts):
    n_row = lax.axis_size("row")
    tile = tile_blocks[0, 0]
    slot_rows = block_rows[0, 0]
    slot_cols = block_cols[0, 0]
    used = counts[0]
    slot_count, block_size, _ = tile.shape
    width = vectors.shape[1]
    piece_blocks = vectors.shape[0] // block_size
    place = jnp.stack([lax.axis_index("row"), lax.axis_index("col")]).astype(jnp.int32)

    across = functools.partial(lax.ppermute, axis_name="col", perm=[(0, 1), (1, 0)])
    meta = across(jnp.concatenate([slot_rows, slot_cols, used]))
    tile_other = across(tile)

    source_piece = slot_cols // piece_blocks
    offset = slot_cols % piece_blocks
    live = jnp.arange(slot_count) < used[0]
    needed = jnp.max(
        jnp.where(
            (source_piece[None, :] == jnp.arange(n_row)[:, None]) & live[None, :],
            offset[None, :],
            0,
        ),
        axis=1,
        keepdims=True,
    )
    exchange = functools.partial(
        lax.all_to_all, axis_name="row", split_axis=0, concat_axis=0, tiled=True
    )
    wanted = after(exchange(jnp.broadcast_to(needed, (n_row, LANES))), meta, place)
    sent_shape = jax.ShapeDtypeStruct((n_row, block_size, width), jnp.bfloat16)
    sent = pl.pallas_call(
        functools.partial(pick_kernel, n_row, block_size),
        out_shape=sent_shape,
        in_specs=[spec(SMEM), spec(pl.ANY)],
        out_specs=spec(VMEM),
        scratch_shapes=[DMA((n_row,))],
        name="pick",
    )(wanted, vectors)

    capacity = 2 * round_up(slot_count, UNROLL)
    sent_at = HEAD + 3 * (capacity + 1)
    plan_size = sent_at + 3 * (2 * n_row * n_row + 2 * UNROLL + 1)
    plan = pl.pallas_call(
        functools.partial(plan_kernel, n_row, piece_blocks, sent_at),
        out_shape=jax.ShapeDtypeStruct((plan_size,), jnp.int32),
        in_specs=[spec(SMEM)] * 6,
        out_specs=spec(SMEM),
        name="plan",
    )(place, wanted, slot_rows, slot_cols, used, meta)

    def cost(products, rows):
        size = block_size * width
        return pl.CostEstimate(
            flops=2 * products * block_size * size,
            bytes_accessed=2 * (products * block_size * block_size + 3 * rows * size),
            transcendentals=0,
        )

    def scratch(rows, wide, vec_sems):
        return [
            VMEM((2, n_row, block_size, wide), jnp.bfloat16),
            VMEM((rows + 1, block_size, wide), jnp.float32),
            VMEM((RING, block_size, block_size), jnp.bfloat16),
            DMA((RING,)),
            DMA(vec_sems),
        ]

    def sent_blocks(first, pieces, others, args):
        return pl.pallas_call(
            functools.partial(sent_kernel, first, sent_at),
            out_shape=sent_shape,
            in_specs=[spec(SMEM)] + [spec(pl.ANY)] * 4 + [spec(VMEM)] * len(args),
            out_specs=spec(VMEM),
            scratch_shapes=scratch(n_row, width, (2,)),
            compiler_params=params(16),
            cost_estimate=cost(n_row, n_row),
            name="sent",
        )(plan, tile, tile_other, pieces, others, *args)

    def early(pieces, others):
        return pl.pallas_call(
            lambda plan, a, b, p1, p2, o1, o2, *rest: early_kernel(
                plan, a, b, (p1, p2), (o1, o2), *rest
            ),
            out_shape=jax.ShapeDtypeStruct((piece_blocks, block_size, width), jnp.float32),
            in_specs=[spec(SMEM)] + [spec(pl.ANY)] * 6 + [spec(VMEM)],
            out_specs=spec(VMEM),
            scratch_shapes=scratch(piece_blocks, 2 * width, (2, 2)),
            compiler_params=params(32),
            cost_estimate=cost(2 * slot_count, 2 * piece_blocks),
            name="early",
        )(plan, tile, tile_other, *pieces, *others, vectors)

    def last(pieces, others, base):
        return pl.pallas_call(
            last_kernel,
            out_shape=jax.ShapeDtypeStruct(vectors.shape, jnp.bfloat16),
            in_specs=[spec(SMEM)] + [spec(pl.ANY)] * 5,
            out_specs=spec(VMEM),
            scratch_shapes=scratch(piece_blocks, width, (3,)),
            compiler_params=params(24),
            cost_estimate=cost(slot_count, piece_blocks),
            name="last",
        )(plan, tile, tile_other, pieces, others, base)

    pieces = after(exchange(sent), plan)
    others = across(pieces)
    previous, sent = sent, sent_blocks(True, pieces, others, (sent,))
    all_pieces, all_others = [pieces], [others]
    pieces = exchange(sent)
    others = across(pieces)
    sent = sent_blocks(False, pieces, others, (sent, previous))
    all_pieces.append(pieces)
    all_others.append(others)
    base = early(all_pieces, all_others)
    pieces = after(exchange(sent), base)
    others = across(pieces)
    return last(pieces, others, base)


def on_any(vectors, tile_blocks, block_rows, block_cols, counts):
    n_row = lax.axis_size("row")
    n_col = lax.axis_size("col")
    tile_data = tile_blocks[0, 0]
    slot_rows = block_rows[0, 0]
    slot_cols = block_cols[0, 0]
    used = counts[0, 0]
    block_size = tile_data.shape[-1]
    width = vectors.shape[1]
    piece_blocks = vectors.shape[0] // block_size
    row_blocks = piece_blocks * n_col
    slot_count = tile_data.shape[0]
    live = (jnp.arange(slot_count) < used).astype(jnp.float32)
    onehot = (slot_rows[None, :] == jnp.arange(row_blocks)[:, None]).astype(jnp.float32) * live[
        None, :
    ]
    source_piece = slot_cols // piece_blocks
    offset = slot_cols % piece_blocks
    needed = jnp.max(
        jnp.where(source_piece[None, :] == jnp.arange(n_row)[:, None], offset[None, :], 0), axis=1
    )
    wanted = lax.all_to_all(
        needed.reshape(n_row, 1), "row", split_axis=0, concat_axis=0, tiled=True
    ).reshape(n_row)

    def apply_tiles(current):
        own_blocks = current.reshape(piece_blocks, block_size, width)
        outgoing = jnp.take(own_blocks, wanted, axis=0)
        received = lax.all_to_all(outgoing, "row", split_axis=0, concat_axis=0, tiled=True)
        vec_blocks = jnp.take(received, source_piece, axis=0)
        products = jnp.einsum(
            "sij,sjk->sik", tile_data, vec_blocks, preferred_element_type=jnp.float32
        )
        term = jnp.einsum("ls,sik->lik", onehot, products, precision=lax.Precision.HIGHEST)
        term = term.reshape(row_blocks * block_size, width)
        return lax.psum_scatter(
            term.astype(jnp.bfloat16), "col", scatter_dimension=0, tiled=True
        ).astype(jnp.float32)

    previous = vectors
    applied = apply_tiles(vectors)
    current = ((applied - center_value * previous.astype(jnp.float32)) / half_width).astype(
        jnp.bfloat16
    )
    for repeat in range(DEGREE - 1):
        applied = apply_tiles(current)
        following = (
            2.0 * (applied - center_value * current.astype(jnp.float32)) / half_width
            - previous.astype(jnp.float32)
        ).astype(jnp.bfloat16)
        previous, current = (current, following)
    return current


def solution(mesh):
    n_row, n_col = mesh.shape["row"], mesh.shape["col"]
    paired = n_col == 2 and n_row & (n_row - 1) == 0
    return jax.shard_map(
        on_pair if paired else on_any,
        mesh=mesh,
        in_specs=(
            P(("row", "col"), "vec"),
            P("row", "col", None, None, None),
            P("row", "col", None),
            P("row", "col", None),
            P("row", "col"),
        ),
        out_specs=P(("row", "col"), "vec"),
        check_vma=False,
    )
```

```python
import functools

import jax
import jax.numpy as jnp
from jax import lax
from jax.experimental import pallas as pl
from jax.experimental.pallas import tpu as pltpu
from jax.sharding import PartitionSpec as P

DEGREE = 3

center_value = 0.5
half_width = 2.0

VMEM = pltpu.VMEM
SMEM = pltpu.SMEM
HBM = pltpu.HBM
DMA = pltpu.SemaphoreType.DMA
LANES = 128
UNROLL = 4
RING = 16
HEAD = 8
GRANT = 50


def spec(space):
    return pl.BlockSpec(memory_space=space)


def params(mib):
    return pltpu.CompilerParams(vmem_limit_bytes=mib * 1024 * 1024)


def round_up(n, step):
    return (n + step - 1) // step * step


def plan_kernel(n_row, piece_blocks, sent_at, place, wanted, rows_a, cols_a, used_a, meta_b, out):
    slot_count = rows_a.shape[0]
    first_row = place[1] * piece_blocks

    def write(at, one, two, three):
        out[at] = one
        out[at + 1] = two
        out[at + 2] = three

    def scan(row_of, col_of, used, at, sent):
        def step(s, carry):
            at, sent = carry
            row = row_of(s) - first_row
            mine = ((row >= 0) & (row < piece_blocks)).astype(jnp.int32)
            piece = col_of(s) // piece_blocks
            write(HEAD + 3 * at, s, row, piece)
            for k in range(n_row):
                write(sent_at + 3 * sent, s, k, piece)
                sent = sent + jnp.where(wanted[k, 0] == row, mine, 0)
            return at + mine, sent

        at, sent = lax.fori_loop(0, used, step, (at, sent))
        for _ in range(UNROLL):
            write(HEAD + 3 * at, 0, piece_blocks, 0)
            write(sent_at + 3 * sent, 0, n_row, 0)
            at = at + jnp.where(at % UNROLL == 0, 0, 1)
            sent = sent + jnp.where(sent % UNROLL == 0, 0, 1)
        return at, sent

    zero = jnp.int32(0)
    at, sent = scan(lambda s: rows_a[s], lambda s: cols_a[s], used_a[0], zero, zero)
    out[0] = at
    out[2] = sent
    at, sent = scan(
        lambda s: meta_b[s], lambda s: meta_b[slot_count + s], meta_b[2 * slot_count], at, sent
    )
    out[1] = at
    out[3] = sent


def pick_kernel(n_row, block_size, wanted, vectors, out, sem):
    def copy(k):
        at = pl.multiple_of(wanted[k, 0] * block_size, block_size)
        return pltpu.make_async_copy(vectors.at[pl.ds(at, block_size)], out.at[k], sem.at[k])

    for k in range(n_row):
        copy(k).start()
    for k in range(n_row):
        copy(k).wait()


def add_products(plan, base, ends, tiles, vec, total, ring, sems, ready):
    mid, end = plan[ends], plan[ends + 1]

    def copy(side, i):
        at = lax.rem(i, RING)
        return pltpu.make_async_copy(tiles[side].at[plan[base + 3 * i]], ring.at[at], sems.at[at])

    def start(i):
        @pl.when(i < mid)
        def _():
            copy(0, i).start()

        @pl.when((i >= mid) & (i < end))
        def _():
            copy(1, i).start()

    for i in range(RING):
        start(jnp.int32(i))
    ready()

    def run(side, begin, end):
        @pl.loop(begin // UNROLL, end // UNROLL)
        def _(j):
            i = UNROLL * j
            for u in range(UNROLL):
                copy(0, i + u).wait()
            values = []
            for u in range(UNROLL):
                block = ring[lax.rem(i + u, RING)]
                piece = vec[side][plan[base + 3 * (i + u) + 2]]
                values.append(jnp.dot(block, piece, preferred_element_type=jnp.float32))
            for u in range(UNROLL):
                total[plan[base + 3 * (i + u) + 1]] += values[u]
            for u in range(UNROLL):
                start(i + RING + u)

    run(0, 0, mid)
    run(1, mid, end)


def sent_kernel(first, sent_at, plan, tile_a, tile_b, pieces_a, pieces_b, *rest):
    if first:
        current, out, total, ring, sems = rest
        previous = None
    else:
        current, previous, out, total, ring, sems = rest
    n_row = out.shape[0]

    def ready():
        for k in range(n_row):
            value = -center_value * current[k].astype(jnp.float32)
            if not first:
                value = value - previous[k].astype(jnp.float32)
            total[k] = value

    add_products(plan, sent_at, 2, (tile_a, tile_b), (pieces_a, pieces_b), total, ring, sems, ready)
    for k in range(n_row):
        value = total[k]
        out[k] = (value / half_width if first else value).astype(jnp.bfloat16)


def early_kernel(
    plan, tile_a, tile_b, pieces, others, vectors, base, total, ring, sems, vec, own, row_sems
):
    width = vectors.shape[1]
    piece_blocks, block_size, _ = base.shape

    def ready():
        copy = pltpu.make_async_copy(vectors, own, row_sems.at[0])
        copy.start()
        for side, refs in enumerate((pieces, others)):
            for step in range(2):
                vec[side, :, :, step * width : (step + 1) * width] = refs[step][...]
        copy.wait()

        @pl.loop(0, piece_blocks)
        def _(b):
            at = pl.ds(pl.multiple_of(b * block_size, block_size), block_size)
            value = own[at, :].astype(jnp.float32)
            total[b, :, :width] = -center_value * value
            total[b, :, width:] = -value

    add_products(plan, HEAD, 0, (tile_a, tile_b), (vec.at[0], vec.at[1]), total, ring, sems, ready)

    def put(b):
        return pltpu.make_async_copy(total.at[b, :, pl.ds(0, width)], base.at[b], row_sems.at[b])

    @pl.loop(0, piece_blocks)
    def _(b):
        first = (total[b, :, :width] / half_width).astype(jnp.bfloat16).astype(jnp.float32)
        second = total[b, :, width:] - center_value * first
        second = second.astype(jnp.bfloat16).astype(jnp.float32)
        total[b, :, :width] = -center_value * second - first
        put(b).start()

    @pl.loop(0, piece_blocks)
    def _(b):
        put(b).wait()


def last_kernel(
    plan, tile_a, tile_b, pieces_a, pieces_b, base, out, total, ring, sems, own, row_sems
):
    piece_blocks, block_size, _ = base.shape

    def ready():
        copy = pltpu.make_async_copy(base, total.at[pl.ds(0, piece_blocks)], row_sems.at[0])
        copy.start()
        copy.wait()

    add_products(plan, HEAD, 0, (tile_a, tile_b), (pieces_a, pieces_b), total, ring, sems, ready)

    def put(b):
        at = pl.ds(pl.multiple_of(b * block_size, block_size), block_size)
        return pltpu.make_async_copy(own.at[at], out.at[at], row_sems.at[b])

    @pl.loop(0, piece_blocks)
    def _(b):
        at = pl.ds(pl.multiple_of(b * block_size, block_size), block_size)
        own[at, :] = total[b].astype(jnp.bfloat16)
        put(b).start()

    @pl.loop(0, piece_blocks)
    def _(b):
        put(b).wait()


def after(value, *others):
    return lax.optimization_barrier((value, *others))[0]


def on_pair(vectors, tile_blocks, block_rows, block_cols, counts):
    n_row = lax.axis_size("row")
    tile = tile_blocks[0, 0]
    slot_rows = block_rows[0, 0]
    slot_cols = block_cols[0, 0]
    used = counts[0]
    slot_count, block_size, _ = tile.shape
    width = vectors.shape[1]
    piece_blocks = vectors.shape[0] // block_size
    place = jnp.stack([lax.axis_index("row"), lax.axis_index("col")]).astype(jnp.int32)

    across = functools.partial(lax.ppermute, axis_name="col", perm=[(0, 1), (1, 0)])
    meta = across(jnp.concatenate([slot_rows, slot_cols, used]))
    tile_other = across(tile)

    source_piece = slot_cols // piece_blocks
    offset = slot_cols % piece_blocks
    live = jnp.arange(slot_count) < used[0]
    needed = jnp.max(
        jnp.where(
            (source_piece[None, :] == jnp.arange(n_row)[:, None]) & live[None, :],
            offset[None, :],
            0,
        ),
        axis=1,
        keepdims=True,
    )
    exchange = functools.partial(
        lax.all_to_all, axis_name="row", split_axis=0, concat_axis=0, tiled=True
    )
    wanted = after(exchange(jnp.broadcast_to(needed, (n_row, LANES))), meta, place)
    sent_shape = jax.ShapeDtypeStruct((n_row, block_size, width), jnp.bfloat16)
    sent = pl.pallas_call(
        functools.partial(pick_kernel, n_row, block_size),
        out_shape=sent_shape,
        in_specs=[spec(SMEM), spec(HBM)],
        out_specs=spec(VMEM),
        scratch_shapes=[DMA((n_row,))],
        compiler_params=params(GRANT),
        name="pick",
    )(wanted, vectors)

    capacity = 2 * round_up(slot_count, UNROLL)
    sent_at = HEAD + 3 * (capacity + 1)
    plan_size = sent_at + 3 * (2 * n_row * n_row + 2 * UNROLL + 1)
    plan = pl.pallas_call(
        functools.partial(plan_kernel, n_row, piece_blocks, sent_at),
        out_shape=jax.ShapeDtypeStruct((plan_size,), jnp.int32),
        in_specs=[spec(SMEM)] * 6,
        out_specs=spec(SMEM),
        name="plan",
    )(place, wanted, slot_rows, slot_cols, used, meta)

    def cost(products, rows):
        size = block_size * width
        return pl.CostEstimate(
            flops=2 * products * block_size * size,
            bytes_accessed=2 * (products * block_size * block_size + 3 * rows * size),
            transcendentals=0,
        )

    def scratch(rows, wide):
        return [
            VMEM((rows + 1, block_size, wide), jnp.float32),
            VMEM((RING, block_size, block_size), jnp.bfloat16),
            DMA((RING,)),
        ]

    own_rows = [VMEM(vectors.shape, jnp.bfloat16), DMA((piece_blocks,))]

    def sent_blocks(first, pieces, others, args):
        return pl.pallas_call(
            functools.partial(sent_kernel, first, sent_at),
            out_shape=sent_shape,
            in_specs=[spec(SMEM)] + [spec(HBM)] * 2 + [spec(VMEM)] * (2 + len(args)),
            out_specs=spec(VMEM),
            scratch_shapes=scratch(n_row, width),
            compiler_params=params(GRANT),
            cost_estimate=cost(n_row, n_row),
            name="sent",
        )(plan, tile, tile_other, pieces, others, *args)

    def early(pieces, others):
        return pl.pallas_call(
            lambda plan, a, b, p1, p2, o1, o2, *rest: early_kernel(
                plan, a, b, (p1, p2), (o1, o2), *rest
            ),
            out_shape=jax.ShapeDtypeStruct((piece_blocks, block_size, width), jnp.float32),
            in_specs=[spec(SMEM)] + [spec(HBM)] * 2 + [spec(VMEM)] * 4 + [spec(HBM)],
            out_specs=spec(HBM),
            scratch_shapes=scratch(piece_blocks, 2 * width)
            + [VMEM((2, n_row, block_size, 2 * width), jnp.bfloat16)]
            + own_rows,
            compiler_params=params(GRANT),
            cost_estimate=cost(2 * slot_count, 2 * piece_blocks),
            name="early",
        )(plan, tile, tile_other, *pieces, *others, vectors)

    def last(pieces, others, base):
        return pl.pallas_call(
            last_kernel,
            out_shape=jax.ShapeDtypeStruct(vectors.shape, jnp.bfloat16),
            in_specs=[spec(SMEM)] + [spec(HBM)] * 2 + [spec(VMEM)] * 2 + [spec(HBM)],
            out_specs=spec(HBM),
            scratch_shapes=scratch(piece_blocks, width) + own_rows,
            compiler_params=params(GRANT),
            cost_estimate=cost(slot_count, piece_blocks),
            name="last",
        )(plan, tile, tile_other, pieces, others, base)

    pieces = after(exchange(sent), plan, tile_other)
    others = across(pieces)
    previous, sent = sent, sent_blocks(True, pieces, others, (sent,))
    all_pieces, all_others = [pieces], [others]
    pieces = exchange(sent)
    others = across(pieces)
    sent = sent_blocks(False, pieces, others, (sent, previous))
    all_pieces.append(pieces)
    all_others.append(others)
    base = early(all_pieces, all_others)
    pieces = after(exchange(sent), base)
    others = across(pieces)
    return last(pieces, others, base)


def on_any(vectors, tile_blocks, block_rows, block_cols, counts):
    n_row = lax.axis_size("row")
    n_col = lax.axis_size("col")
    tile_data = tile_blocks[0, 0]
    slot_rows = block_rows[0, 0]
    slot_cols = block_cols[0, 0]
    used = counts[0, 0]
    block_size = tile_data.shape[-1]
    width = vectors.shape[1]
    piece_blocks = vectors.shape[0] // block_size
    row_blocks = piece_blocks * n_col
    slot_count = tile_data.shape[0]
    live = (jnp.arange(slot_count) < used).astype(jnp.float32)
    onehot = (slot_rows[None, :] == jnp.arange(row_blocks)[:, None]).astype(jnp.float32) * live[
        None, :
    ]
    source_piece = slot_cols // piece_blocks
    offset = slot_cols % piece_blocks
    needed = jnp.max(
        jnp.where(source_piece[None, :] == jnp.arange(n_row)[:, None], offset[None, :], 0), axis=1
    )
    wanted = lax.all_to_all(
        needed.reshape(n_row, 1), "row", split_axis=0, concat_axis=0, tiled=True
    ).reshape(n_row)

    def apply_tiles(current):
        own_blocks = current.reshape(piece_blocks, block_size, width)
        outgoing = jnp.take(own_blocks, wanted, axis=0)
        received = lax.all_to_all(outgoing, "row", split_axis=0, concat_axis=0, tiled=True)
        vec_blocks = jnp.take(received, source_piece, axis=0)
        products = jnp.einsum(
            "sij,sjk->sik", tile_data, vec_blocks, preferred_element_type=jnp.float32
        )
        term = jnp.einsum("ls,sik->lik", onehot, products, precision=lax.Precision.HIGHEST)
        term = term.reshape(row_blocks * block_size, width)
        return lax.psum_scatter(
            term.astype(jnp.bfloat16), "col", scatter_dimension=0, tiled=True
        ).astype(jnp.float32)

    previous = vectors
    applied = apply_tiles(vectors)
    current = ((applied - center_value * previous.astype(jnp.float32)) / half_width).astype(
        jnp.bfloat16
    )
    for repeat in range(DEGREE - 1):
        applied = apply_tiles(current)
        following = (
            2.0 * (applied - center_value * current.astype(jnp.float32)) / half_width
            - previous.astype(jnp.float32)
        ).astype(jnp.bfloat16)
        previous, current = (current, following)
    return current


def solution(mesh):
    n_row, n_col = mesh.shape["row"], mesh.shape["col"]
    paired = n_col == 2 and n_row & (n_row - 1) == 0
    return jax.shard_map(
        on_pair if paired else on_any,
        mesh=mesh,
        in_specs=(
            P(("row", "col"), "vec"),
            P("row", "col", None, None, None),
            P("row", "col", None),
            P("row", "col", None),
            P("row", "col"),
        ),
        out_specs=P(("row", "col"), "vec"),
        check_vma=False,
    )
```

```python
import functools

import jax
import jax.numpy as jnp
from jax import lax
from jax.experimental import pallas as pl
from jax.experimental.pallas import tpu as pltpu
from jax.sharding import PartitionSpec as P

DEGREE = 3

center_value = 0.5
half_width = 2.0

VMEM = pltpu.VMEM
SMEM = pltpu.SMEM
HBM = pltpu.HBM
DMA = pltpu.SemaphoreType.DMA
LANES = 128
UNROLL = 2
RING = 16
HEAD = 8
GRANT = 50
PARTS = 2


def spec(space):
    return pl.BlockSpec(memory_space=space)


def params(mib):
    return pltpu.CompilerParams(vmem_limit_bytes=mib * 1024 * 1024)


def round_up(n, step):
    return (n + step - 1) // step * step


def plan_kernel(n_row, piece_blocks, sent_at, place, wanted, rows_a, cols_a, used_a, meta_b, out):
    slot_count = rows_a.shape[0]
    first_row = place[1] * piece_blocks

    def write(at, one, two, three):
        out[at] = one
        out[at + 1] = two
        out[at + 2] = three

    def scan(row_of, col_of, used, at, sent):
        def step(s, carry):
            at, sent = carry
            row = row_of(s) - first_row
            mine = ((row >= 0) & (row < piece_blocks)).astype(jnp.int32)
            piece = col_of(s) // piece_blocks
            write(HEAD + 3 * at, s, row, piece)
            for k in range(n_row):
                write(sent_at + 3 * sent, s, k, piece)
                sent = sent + jnp.where(wanted[k, 0] == row, mine, 0)
            return at + mine, sent

        at, sent = lax.fori_loop(0, used, step, (at, sent))
        for _ in range(UNROLL):
            write(HEAD + 3 * at, 0, piece_blocks, 0)
            write(sent_at + 3 * sent, 0, n_row, 0)
            at = at + jnp.where(at % UNROLL == 0, 0, 1)
            sent = sent + jnp.where(sent % UNROLL == 0, 0, 1)
        return at, sent

    zero = jnp.int32(0)
    at, sent = scan(lambda s: rows_a[s], lambda s: cols_a[s], used_a[0], zero, zero)
    out[0] = at
    out[2] = sent
    at, sent = scan(
        lambda s: meta_b[s], lambda s: meta_b[slot_count + s], meta_b[2 * slot_count], at, sent
    )
    out[1] = at
    out[3] = sent


def packed(value):
    half = value.shape[0] // 2
    return jnp.concatenate([value[:half], value[half:]], axis=1)


def unpack_into(ref, at, value):
    index, column = at
    rows, width = value.shape[0], value.shape[1] // 2
    for h in range(2):
        ref[index, h * rows : (h + 1) * rows, column : column + width] = value[
            :, h * width : (h + 1) * width
        ]


def pick_kernel(n_row, block_size, wanted, vectors, *rest):
    outs, blocks, sem = rest[:PARTS], rest[PARTS], rest[PARTS + 1]
    width = vectors.shape[1] // PARTS

    def copy(k):
        at = pl.multiple_of(wanted[k, 0] * block_size, block_size)
        return pltpu.make_async_copy(vectors.at[pl.ds(at, block_size)], blocks.at[k], sem.at[k])

    for k in range(n_row):
        copy(k).start()
    for k in range(n_row):
        copy(k).wait()
        for part in range(PARTS):
            outs[part][k] = packed(blocks[k, :, part * width : (part + 1) * width])


def add_products(plan, base, ends, tiles, vec, total, ring, sems, ready):
    mid, end = plan[ends], plan[ends + 1]

    def copy(side, i):
        at = lax.rem(i, RING)
        return pltpu.make_async_copy(tiles[side].at[plan[base + 3 * i]], ring.at[at], sems.at[at])

    def start(i):
        @pl.when(i < mid)
        def _():
            copy(0, i).start()

        @pl.when((i >= mid) & (i < end))
        def _():
            copy(1, i).start()

    for i in range(RING):
        start(jnp.int32(i))
    ready()

    def run(side, begin, end):
        @pl.loop(begin // UNROLL, end // UNROLL)
        def _(j):
            i = UNROLL * j
            for u in range(UNROLL):
                copy(0, i + u).wait()
            for u in range(UNROLL):
                block = ring[lax.rem(i + u, RING)]
                piece = vec[side, plan[base + 3 * (i + u) + 2]]
                total[plan[base + 3 * (i + u) + 1]] += jnp.dot(
                    block, piece, preferred_element_type=jnp.float32
                )
            for u in range(UNROLL):
                start(i + RING + u)

    run(0, 0, mid)
    run(1, mid, end)


def sent_kernel(first, sent_at, plan, tile_a, tile_b, pieces_a, pieces_b, *rest):
    if first:
        current, out, moved, vec, total, ring, sems, moved_sem = rest
        sources = (pieces_a, pieces_b, current)
    else:
        current, previous, out, moved, vec, total, ring, sems, moved_sem = rest
        sources = (pieces_a, pieces_b, current, previous)
    n_row = out.shape[0]
    copies = [
        pltpu.make_async_copy(source, moved.at[i], moved_sem.at[i])
        for i, source in enumerate(sources)
    ]

    def ready():
        for copy in copies:
            copy.start()
        total[...] = jnp.zeros_like(total)
        for copy in copies:
            copy.wait()
        for side in range(2):
            for p in range(n_row):
                unpack_into(vec.at[side], (p, 0), moved[side, p])

    add_products(plan, sent_at, 2, (tile_a, tile_b), vec, total, ring, sems, ready)
    for k in range(n_row):
        value = packed(total[k]) - center_value * moved[2, k].astype(jnp.float32)
        if first:
            value = value / half_width
        else:
            value = value - moved[3, k].astype(jnp.float32)
        out[k] = value.astype(jnp.bfloat16)


def move_pieces(groups, moved, moved_sems, vec):
    copies = [
        pltpu.make_async_copy(source, moved.at[side, i], moved_sems.at[side, i])
        for side, group in enumerate(groups)
        for i, source in enumerate(group)
    ]

    def start():
        for copy in copies:
            copy.start()

    def finish():
        for copy in copies:
            copy.wait()
        for side, group in enumerate(groups):
            for i in range(len(group)):
                for p in range(vec.shape[1]):
                    value = moved[side, i, p]
                    unpack_into(vec.at[side], (p, i * (value.shape[1] // 2)), value)

    return start, finish


def early_kernel(plan, tile_a, tile_b, *rest):
    pieces, others = rest[: 2 * PARTS], rest[2 * PARTS : 4 * PARTS]
    vectors, base, moved, vec, total, ring, sems, moved_sems, own, row_sems = rest[4 * PARTS :]
    width = vectors.shape[1]
    piece_blocks, block_size, _ = base.shape
    start, finish = move_pieces((pieces, others), moved, moved_sems, vec)

    def ready():
        copy = pltpu.make_async_copy(vectors, own, row_sems.at[0])
        copy.start()
        start()
        copy.wait()

        @pl.loop(0, piece_blocks)
        def _(b):
            at = pl.ds(pl.multiple_of(b * block_size, block_size), block_size)
            value = own[at, :].astype(jnp.float32)
            total[b, :, :width] = -center_value * value
            total[b, :, width:] = -value

        finish()

    add_products(plan, HEAD, 0, (tile_a, tile_b), vec, total, ring, sems, ready)

    def put(b):
        return pltpu.make_async_copy(total.at[b, :, pl.ds(0, width)], base.at[b], row_sems.at[b])

    @pl.loop(0, piece_blocks)
    def _(b):
        first = (total[b, :, :width] / half_width).astype(jnp.bfloat16).astype(jnp.float32)
        second = total[b, :, width:] - center_value * first
        second = second.astype(jnp.bfloat16).astype(jnp.float32)
        total[b, :, :width] = -center_value * second - first
        put(b).start()

    @pl.loop(0, piece_blocks)
    def _(b):
        put(b).wait()


def last_kernel(plan, tile_a, tile_b, *rest):
    pieces, others = rest[:PARTS], rest[PARTS : 2 * PARTS]
    base, out, moved, vec, total, ring, sems, moved_sems, own, row_sems = rest[2 * PARTS :]
    piece_blocks, block_size, _ = base.shape
    start, finish = move_pieces((pieces, others), moved, moved_sems, vec)

    def ready():
        copy = pltpu.make_async_copy(base, total.at[pl.ds(0, piece_blocks)], row_sems.at[0])
        start()
        copy.start()
        finish()
        copy.wait()

    add_products(plan, HEAD, 0, (tile_a, tile_b), vec, total, ring, sems, ready)

    def put(b):
        at = pl.ds(pl.multiple_of(b * block_size, block_size), block_size)
        return pltpu.make_async_copy(own.at[at], out.at[at], row_sems.at[b])

    @pl.loop(0, piece_blocks)
    def _(b):
        at = pl.ds(pl.multiple_of(b * block_size, block_size), block_size)
        own[at, :] = total[b].astype(jnp.bfloat16)
        put(b).start()

    @pl.loop(0, piece_blocks)
    def _(b):
        put(b).wait()


def after(value, *others):
    return lax.optimization_barrier((value, *others))[0]


def on_pair(vectors, tile_blocks, block_rows, block_cols, counts):
    n_row = lax.axis_size("row")
    tile = tile_blocks[0, 0]
    slot_rows = block_rows[0, 0]
    slot_cols = block_cols[0, 0]
    used = counts[0]
    slot_count, block_size, _ = tile.shape
    width = vectors.shape[1]
    piece_blocks = vectors.shape[0] // block_size
    place = jnp.stack([lax.axis_index("row"), lax.axis_index("col")]).astype(jnp.int32)

    across = functools.partial(lax.ppermute, axis_name="col", perm=[(0, 1), (1, 0)])
    meta = across(jnp.concatenate([slot_rows, slot_cols, used]))
    tile_other = across(tile)

    source_piece = slot_cols // piece_blocks
    offset = slot_cols % piece_blocks
    live = jnp.arange(slot_count) < used[0]
    needed = jnp.max(
        jnp.where(
            (source_piece[None, :] == jnp.arange(n_row)[:, None]) & live[None, :],
            offset[None, :],
            0,
        ),
        axis=1,
        keepdims=True,
    )
    exchange = functools.partial(
        lax.all_to_all, axis_name="row", split_axis=0, concat_axis=0, tiled=True
    )
    wanted = after(exchange(jnp.broadcast_to(needed, (n_row, LANES))), meta, place)
    part_width = width // PARTS
    part_shape = (n_row, block_size // 2, 2 * part_width)
    sent_shape = jax.ShapeDtypeStruct(part_shape, jnp.bfloat16)
    sent = pl.pallas_call(
        functools.partial(pick_kernel, n_row, block_size),
        out_shape=[sent_shape] * PARTS,
        in_specs=[spec(SMEM), spec(HBM)],
        out_specs=[spec(VMEM)] * PARTS,
        scratch_shapes=[VMEM((n_row, block_size, width), jnp.bfloat16), DMA((n_row,))],
        compiler_params=params(62),
        name="pick",
    )(wanted, vectors)

    capacity = 2 * round_up(slot_count, UNROLL)
    sent_at = HEAD + 3 * (capacity + 1)
    plan_size = sent_at + 3 * (2 * n_row * n_row + 2 * UNROLL + 1)
    plan = pl.pallas_call(
        functools.partial(plan_kernel, n_row, piece_blocks, sent_at),
        out_shape=jax.ShapeDtypeStruct((plan_size,), jnp.int32),
        in_specs=[spec(SMEM)] * 6,
        out_specs=spec(SMEM),
        name="plan",
    )(place, wanted, slot_rows, slot_cols, used, meta)

    def cost(products, rows):
        size = block_size * width
        return pl.CostEstimate(
            flops=2 * products * block_size * size,
            bytes_accessed=2 * (products * block_size * block_size + 3 * rows * size),
            transcendentals=0,
        )

    def scratch(rows, wide, sources):
        return [
            VMEM((*sources, *part_shape), jnp.bfloat16),
            VMEM((2, n_row, block_size, wide), jnp.bfloat16),
            VMEM((rows + 1, block_size, wide), jnp.float32),
            VMEM((RING, block_size, block_size), jnp.bfloat16),
            DMA((RING,)),
            DMA(sources),
        ]

    own_rows = [VMEM(vectors.shape, jnp.bfloat16), DMA((piece_blocks,))]

    def sent_blocks(pieces, others, *args):
        first = len(args) == 1
        return pl.pallas_call(
            functools.partial(sent_kernel, first, sent_at),
            out_shape=sent_shape,
            in_specs=[spec(SMEM)] + [spec(HBM)] * 2 + [spec(pl.ANY)] * (2 + len(args)),
            out_specs=spec(VMEM),
            scratch_shapes=scratch(n_row, part_width, (2 + len(args),)),
            compiler_params=params(GRANT),
            cost_estimate=cost(n_row, n_row),
            name="sent",
        )(plan, tile, tile_other, pieces, others, *args)

    def early(pieces, others):
        return pl.pallas_call(
            early_kernel,
            out_shape=jax.ShapeDtypeStruct((piece_blocks, block_size, width), jnp.float32),
            in_specs=[spec(SMEM)] + [spec(HBM)] * 2 + [spec(pl.ANY)] * (4 * PARTS) + [spec(HBM)],
            out_specs=spec(HBM),
            scratch_shapes=scratch(piece_blocks, 2 * width, (2, 2 * PARTS)) + own_rows,
            compiler_params=params(GRANT),
            cost_estimate=cost(2 * slot_count, 2 * piece_blocks),
            name="early",
        )(plan, tile, tile_other, *pieces, *others, vectors)

    def last(pieces, others, base):
        return pl.pallas_call(
            last_kernel,
            out_shape=jax.ShapeDtypeStruct(vectors.shape, jnp.bfloat16),
            in_specs=[spec(SMEM)] + [spec(HBM)] * 2 + [spec(pl.ANY)] * (2 * PARTS) + [spec(HBM)],
            out_specs=spec(HBM),
            scratch_shapes=scratch(piece_blocks, width, (2, PARTS)) + own_rows,
            compiler_params=params(GRANT),
            cost_estimate=cost(slot_count, piece_blocks),
            name="last",
        )(plan, tile, tile_other, *pieces, *others, base)

    pieces, others, older = [], [], [()] * PARTS
    for step in range(DEGREE):
        received = [exchange(block) for block in sent]
        if step == 0:
            received[0] = after(received[0], plan, tile_other)
        if step == DEGREE - 1:
            base = early(pieces, others)
            received[0] = after(received[0], base)
        swapped = [across(piece) for piece in received]
        if step < DEGREE - 1:
            pieces += received
            others += swapped
            following = [
                sent_blocks(received[i], swapped[i], sent[i], *older[i]) for i in range(PARTS)
            ]
            older = [(block,) for block in sent]
            sent = following
    return last(received, swapped, base)


def on_any(vectors, tile_blocks, block_rows, block_cols, counts):
    n_row = lax.axis_size("row")
    n_col = lax.axis_size("col")
    tile_data = tile_blocks[0, 0]
    slot_rows = block_rows[0, 0]
    slot_cols = block_cols[0, 0]
    used = counts[0, 0]
    block_size = tile_data.shape[-1]
    width = vectors.shape[1]
    piece_blocks = vectors.shape[0] // block_size
    row_blocks = piece_blocks * n_col
    slot_count = tile_data.shape[0]
    live = (jnp.arange(slot_count) < used).astype(jnp.float32)
    onehot = (slot_rows[None, :] == jnp.arange(row_blocks)[:, None]).astype(jnp.float32) * live[
        None, :
    ]
    source_piece = slot_cols // piece_blocks
    offset = slot_cols % piece_blocks
    needed = jnp.max(
        jnp.where(source_piece[None, :] == jnp.arange(n_row)[:, None], offset[None, :], 0), axis=1
    )
    wanted = lax.all_to_all(
        needed.reshape(n_row, 1), "row", split_axis=0, concat_axis=0, tiled=True
    ).reshape(n_row)

    def apply_tiles(current):
        own_blocks = current.reshape(piece_blocks, block_size, width)
        outgoing = jnp.take(own_blocks, wanted, axis=0)
        received = lax.all_to_all(outgoing, "row", split_axis=0, concat_axis=0, tiled=True)
        vec_blocks = jnp.take(received, source_piece, axis=0)
        products = jnp.einsum(
            "sij,sjk->sik", tile_data, vec_blocks, preferred_element_type=jnp.float32
        )
        term = jnp.einsum("ls,sik->lik", onehot, products, precision=lax.Precision.HIGHEST)
        term = term.reshape(row_blocks * block_size, width)
        return lax.psum_scatter(
            term.astype(jnp.bfloat16), "col", scatter_dimension=0, tiled=True
        ).astype(jnp.float32)

    previous = vectors
    applied = apply_tiles(vectors)
    current = ((applied - center_value * previous.astype(jnp.float32)) / half_width).astype(
        jnp.bfloat16
    )
    for repeat in range(DEGREE - 1):
        applied = apply_tiles(current)
        following = (
            2.0 * (applied - center_value * current.astype(jnp.float32)) / half_width
            - previous.astype(jnp.float32)
        ).astype(jnp.bfloat16)
        previous, current = (current, following)
    return current


def solution(mesh):
    n_row, n_col = mesh.shape["row"], mesh.shape["col"]
    paired = n_col == 2 and n_row & (n_row - 1) == 0
    return jax.shard_map(
        on_pair if paired else on_any,
        mesh=mesh,
        in_specs=(
            P(("row", "col"), "vec"),
            P("row", "col", None, None, None),
            P("row", "col", None),
            P("row", "col", None),
            P("row", "col"),
        ),
        out_specs=P(("row", "col"), "vec"),
        check_vma=False,
    )
```

```python
import functools

import jax
import jax.numpy as jnp
from jax import lax
from jax.experimental import pallas as pl
from jax.experimental.pallas import tpu as pltpu
from jax.sharding import PartitionSpec as P

DEGREE = 3

center_value = 0.5
half_width = 2.0

VMEM = pltpu.VMEM
SMEM = pltpu.SMEM
HBM = pltpu.HBM
DMA = pltpu.SemaphoreType.DMA
LANES = 128
UNROLL = 2
RING = 16
HEAD = 8
GRANT = 50


def spec(space):
    return pl.BlockSpec(memory_space=space)


def params(mib):
    return pltpu.CompilerParams(vmem_limit_bytes=mib * 1024 * 1024)


def round_up(n, step):
    return (n + step - 1) // step * step


def plan_kernel(n_row, piece_blocks, sent_at, place, wanted, rows_a, cols_a, used_a, meta_b, out):
    slot_count = rows_a.shape[0]
    first_row = place[1] * piece_blocks

    def write(at, one, two, three):
        out[at] = one
        out[at + 1] = two
        out[at + 2] = three

    def scan(row_of, col_of, used, at, sent):
        def step(s, carry):
            at, sent = carry
            row = row_of(s) - first_row
            mine = ((row >= 0) & (row < piece_blocks)).astype(jnp.int32)
            piece = col_of(s) // piece_blocks
            write(HEAD + 3 * at, s, row, piece)
            for k in range(n_row):
                write(sent_at + 3 * sent, s, k, piece)
                sent = sent + jnp.where(wanted[k, 0] == row, mine, 0)
            return at + mine, sent

        at, sent = lax.fori_loop(0, used, step, (at, sent))
        for _ in range(UNROLL):
            write(HEAD + 3 * at, 0, piece_blocks, 0)
            write(sent_at + 3 * sent, 0, n_row, 0)
            at = at + jnp.where(at % UNROLL == 0, 0, 1)
            sent = sent + jnp.where(sent % UNROLL == 0, 0, 1)
        return at, sent

    zero = jnp.int32(0)
    at, sent = scan(lambda s: rows_a[s], lambda s: cols_a[s], used_a[0], zero, zero)
    out[0] = at
    out[2] = sent
    at, sent = scan(
        lambda s: meta_b[s], lambda s: meta_b[slot_count + s], meta_b[2 * slot_count], at, sent
    )
    out[1] = at
    out[3] = sent


def pick_kernel(n_row, block_size, wanted, vectors, out, sem):
    def copy(k):
        at = pl.multiple_of(wanted[k, 0] * block_size, block_size)
        return pltpu.make_async_copy(vectors.at[pl.ds(at, block_size)], out.at[k], sem.at[k])

    for k in range(n_row):
        copy(k).start()
    for k in range(n_row):
        copy(k).wait()


def add_products(plan, base, ends, tiles, vec, total, ring, sems, ready):
    mid, end = plan[ends], plan[ends + 1]

    def copy(side, i):
        at = lax.rem(i, RING)
        return pltpu.make_async_copy(tiles[side].at[plan[base + 3 * i]], ring.at[at], sems.at[at])

    def start(i):
        @pl.when(i < mid)
        def _():
            copy(0, i).start()

        @pl.when((i >= mid) & (i < end))
        def _():
            copy(1, i).start()

    for i in range(RING):
        start(jnp.int32(i))
    ready()

    def run(side, begin, end):
        @pl.loop(begin // UNROLL, end // UNROLL)
        def _(j):
            i = UNROLL * j
            for u in range(UNROLL):
                copy(0, i + u).wait()
            for u in range(UNROLL):
                block = ring[lax.rem(i + u, RING)]
                piece = vec[side, plan[base + 3 * (i + u) + 2]]
                total[plan[base + 3 * (i + u) + 1]] += jnp.dot(
                    block, piece, preferred_element_type=jnp.float32
                )
            for u in range(UNROLL):
                start(i + RING + u)

    run(0, 0, mid)
    run(1, mid, end)


def sent_kernel(first, sent_at, plan, tile_a, tile_b, pieces, others, current, *rest):
    if first:
        out, vec, total, ring, sems, vec_sems = rest
    else:
        previous, out, vec, total, ring, sems, vec_sems = rest
    n_row = out.shape[0]
    copies = [
        pltpu.make_async_copy(source, vec.at[side], vec_sems.at[side])
        for side, source in enumerate((pieces, others))
    ]
    for copy in copies:
        copy.start()

    def ready():
        for k in range(n_row):
            value = -center_value * current[k].astype(jnp.float32)
            if not first:
                value = value - previous[k].astype(jnp.float32)
            total[k] = value
        for copy in copies:
            copy.wait()

    add_products(plan, sent_at, 2, (tile_a, tile_b), vec, total, ring, sems, ready)
    for k in range(n_row):
        value = total[k]
        out[k] = (value / half_width if first else value).astype(jnp.bfloat16)


def early_kernel(
    plan, tile_a, tile_b, p1, p2, o1, o2, vectors, base, vec, total, ring, sems, vec_sems, own, row_sems
):
    width = vectors.shape[1]
    piece_blocks, block_size, _ = base.shape
    copies = [
        pltpu.make_async_copy(
            source, vec.at[side, :, :, pl.ds(step * width, width)], vec_sems.at[side, step]
        )
        for side, step, source in ((0, 0, p1), (0, 1, p2), (1, 0, o1), (1, 1, o2))
    ]
    copies.append(pltpu.make_async_copy(vectors, own, row_sems.at[0]))

    def ready():
        for copy in reversed(copies):
            copy.start()
        copies[-1].wait()

        @pl.loop(0, piece_blocks)
        def _(b):
            at = pl.ds(pl.multiple_of(b * block_size, block_size), block_size)
            value = own[at, :].astype(jnp.float32)
            total[b, :, :width] = -center_value * value
            total[b, :, width:] = -value

        for copy in copies[:-1]:
            copy.wait()

    add_products(plan, HEAD, 0, (tile_a, tile_b), vec, total, ring, sems, ready)

    def put(b):
        return pltpu.make_async_copy(total.at[b, :, pl.ds(0, width)], base.at[b], row_sems.at[b])

    @pl.loop(0, piece_blocks)
    def _(b):
        first = (total[b, :, :width] / half_width).astype(jnp.bfloat16).astype(jnp.float32)
        second = total[b, :, width:] - center_value * first
        second = second.astype(jnp.bfloat16).astype(jnp.float32)
        total[b, :, :width] = -center_value * second - first
        put(b).start()

    @pl.loop(0, piece_blocks)
    def _(b):
        put(b).wait()


def last_kernel(
    plan, tile_a, tile_b, pieces, others, base, out, vec, total, ring, sems, vec_sems, start, own, row_sems
):
    piece_blocks, block_size, _ = base.shape
    copies = [
        pltpu.make_async_copy(pieces, vec.at[0], vec_sems.at[0]),
        pltpu.make_async_copy(others, vec.at[1], vec_sems.at[1]),
    ]
    base_copy = pltpu.make_async_copy(base, start, vec_sems.at[2])
    for copy in copies:
        copy.start()

    def ready():
        base_copy.start()

        @pl.loop(0, piece_blocks)
        def _(b):
            total[b] = jnp.zeros(total.shape[1:], jnp.float32)

        for copy in copies:
            copy.wait()

    add_products(plan, HEAD, 0, (tile_a, tile_b), vec, total, ring, sems, ready)
    base_copy.wait()

    def put(b):
        at = pl.ds(pl.multiple_of(b * block_size, block_size), block_size)
        return pltpu.make_async_copy(own.at[at], out.at[at], row_sems.at[b])

    @pl.loop(0, piece_blocks)
    def _(b):
        at = pl.ds(pl.multiple_of(b * block_size, block_size), block_size)
        own[at, :] = (total[b] + start[b]).astype(jnp.bfloat16)
        put(b).start()

    @pl.loop(0, piece_blocks)
    def _(b):
        put(b).wait()


def after(value, *others):
    return lax.optimization_barrier((value, *others))[0]


def on_pair(vectors, tile_blocks, block_rows, block_cols, counts):
    n_row = lax.axis_size("row")
    tile = tile_blocks[0, 0]
    slot_rows = block_rows[0, 0]
    slot_cols = block_cols[0, 0]
    used = counts[0]
    slot_count, block_size, _ = tile.shape
    width = vectors.shape[1]
    piece_blocks = vectors.shape[0] // block_size
    place = jnp.stack([lax.axis_index("row"), lax.axis_index("col")]).astype(jnp.int32)

    across = functools.partial(lax.ppermute, axis_name="col", perm=[(0, 1), (1, 0)])
    meta = across(jnp.concatenate([slot_rows, slot_cols, used]))
    tile_other = across(after(tile, meta))

    needed = jnp.max(
        jnp.where(
            slot_cols[None, :] // piece_blocks == jnp.arange(n_row)[:, None],
            slot_cols[None, :] % piece_blocks,
            0,
        ),
        axis=1,
        keepdims=True,
    )
    exchange = functools.partial(
        lax.all_to_all, axis_name="row", split_axis=0, concat_axis=0, tiled=True
    )
    wanted = after(exchange(jnp.broadcast_to(needed, (n_row, LANES))), meta, place)
    sent_shape = jax.ShapeDtypeStruct((n_row, block_size, width), jnp.bfloat16)
    sent = pl.pallas_call(
        functools.partial(pick_kernel, n_row, block_size),
        out_shape=sent_shape,
        in_specs=[spec(SMEM), spec(HBM)],
        out_specs=spec(VMEM),
        scratch_shapes=[DMA((n_row,))],
        compiler_params=params(62),
        name="pick",
    )(wanted, vectors)

    capacity = 2 * round_up(slot_count, UNROLL)
    sent_at = HEAD + 3 * (capacity + 1)
    plan_size = sent_at + 3 * (2 * n_row * n_row + 2 * UNROLL + 1)
    plan = pl.pallas_call(
        functools.partial(plan_kernel, n_row, piece_blocks, sent_at),
        out_shape=jax.ShapeDtypeStruct((plan_size,), jnp.int32),
        in_specs=[spec(SMEM)] * 6,
        out_specs=spec(SMEM),
        name="plan",
    )(place, wanted, slot_rows, slot_cols, used, meta)

    def cost(products, rows):
        size = block_size * width
        return pl.CostEstimate(
            flops=2 * products * block_size * size,
            bytes_accessed=2 * (products * block_size * block_size + 3 * rows * size),
            transcendentals=0,
        )

    def scratch(rows, wide, sources, sems):
        return [
            VMEM((sources, n_row, block_size, wide), jnp.bfloat16),
            VMEM((rows + 1, block_size, wide), jnp.float32),
            VMEM((RING, block_size, block_size), jnp.bfloat16),
            DMA((RING,)),
            DMA(sems),
        ]

    own_rows = [VMEM(vectors.shape, jnp.bfloat16), DMA((piece_blocks,))]
    base_shape = (piece_blocks, block_size, width)

    def call(kernel, out_shape, out_space, args, scratch_shapes, estimate, name, started=0):
        return pl.pallas_call(
            kernel,
            out_shape=out_shape,
            in_specs=[spec(SMEM)]
            + [spec(pl.ANY)] * (2 + len(args) - started)
            + [spec(VMEM)] * started,
            out_specs=spec(out_space),
            scratch_shapes=scratch_shapes,
            compiler_params=params(GRANT),
            cost_estimate=estimate,
            name=name,
        )(plan, tile, tile_other, *args)

    def sent_blocks(*args):
        return call(
            functools.partial(sent_kernel, len(args) == 3, sent_at),
            sent_shape,
            VMEM,
            args,
            scratch(n_row, width, 2, (2,)),
            cost(n_row, n_row),
            "sent",
            len(args) - 2,
        )

    def early(*pieces):
        return call(
            early_kernel,
            jax.ShapeDtypeStruct(base_shape, jnp.float32),
            HBM,
            (*pieces, vectors),
            scratch(piece_blocks, 2 * width, 2, (2, 2)) + own_rows,
            cost(2 * slot_count, 2 * piece_blocks),
            "early",
        )

    def last(*args):
        return call(
            last_kernel,
            jax.ShapeDtypeStruct(vectors.shape, jnp.bfloat16),
            HBM,
            args,
            scratch(piece_blocks, width, 2, (3,)) + [VMEM(base_shape, jnp.float32)] + own_rows,
            cost(slot_count, piece_blocks),
            "last",
        )

    p1 = after(exchange(sent), plan, tile_other)
    o1 = across(p1)
    first_sent = sent_blocks(p1, o1, sent)
    p2 = exchange(first_sent)
    o2 = across(p2)
    second_sent = sent_blocks(p2, o2, first_sent, sent)
    base = early(p1, p2, o1, o2)
    p3 = after(exchange(second_sent), base)
    return last(p3, across(p3), base)


def on_any(vectors, tile_blocks, block_rows, block_cols, counts):
    n_row = lax.axis_size("row")
    n_col = lax.axis_size("col")
    tile_data = tile_blocks[0, 0]
    slot_rows = block_rows[0, 0]
    slot_cols = block_cols[0, 0]
    used = counts[0, 0]
    block_size = tile_data.shape[-1]
    width = vectors.shape[1]
    piece_blocks = vectors.shape[0] // block_size
    row_blocks = piece_blocks * n_col
    slot_count = tile_data.shape[0]
    live = (jnp.arange(slot_count) < used).astype(jnp.float32)
    onehot = (slot_rows[None, :] == jnp.arange(row_blocks)[:, None]).astype(jnp.float32) * live[
        None, :
    ]
    source_piece = slot_cols // piece_blocks
    offset = slot_cols % piece_blocks
    needed = jnp.max(
        jnp.where(source_piece[None, :] == jnp.arange(n_row)[:, None], offset[None, :], 0), axis=1
    )
    wanted = lax.all_to_all(
        needed.reshape(n_row, 1), "row", split_axis=0, concat_axis=0, tiled=True
    ).reshape(n_row)

    def apply_tiles(current):
        own_blocks = current.reshape(piece_blocks, block_size, width)
        outgoing = jnp.take(own_blocks, wanted, axis=0)
        received = lax.all_to_all(outgoing, "row", split_axis=0, concat_axis=0, tiled=True)
        vec_blocks = jnp.take(received, source_piece, axis=0)
        products = jnp.einsum(
            "sij,sjk->sik", tile_data, vec_blocks, preferred_element_type=jnp.float32
        )
        term = jnp.einsum("ls,sik->lik", onehot, products, precision=lax.Precision.HIGHEST)
        term = term.reshape(row_blocks * block_size, width)
        return lax.psum_scatter(
            term.astype(jnp.bfloat16), "col", scatter_dimension=0, tiled=True
        ).astype(jnp.float32)

    previous = vectors
    applied = apply_tiles(vectors)
    current = ((applied - center_value * previous.astype(jnp.float32)) / half_width).astype(
        jnp.bfloat16
    )
    for repeat in range(DEGREE - 1):
        applied = apply_tiles(current)
        following = (
            2.0 * (applied - center_value * current.astype(jnp.float32)) / half_width
            - previous.astype(jnp.float32)
        ).astype(jnp.bfloat16)
        previous, current = (current, following)
    return current


def solution(mesh):
    n_row, n_col = mesh.shape["row"], mesh.shape["col"]
    paired = n_col == 2 and n_row & (n_row - 1) == 0
    return jax.shard_map(
        on_pair if paired else on_any,
        mesh=mesh,
        in_specs=(
            P(("row", "col"), "vec"),
            P("row", "col", None, None, None),
            P("row", "col", None),
            P("row", "col", None),
            P("row", "col"),
        ),
        out_specs=P(("row", "col"), "vec"),
        check_vma=False,
    )
```

```python
import functools

import jax
import jax.numpy as jnp
from jax import lax
from jax.experimental import pallas as pl
from jax.experimental.pallas import tpu as pltpu
from jax.sharding import PartitionSpec as P

DEGREE = 3

center_value = 0.5
half_width = 2.0

VMEM = pltpu.VMEM
SMEM = pltpu.SMEM
HBM = pltpu.HBM
DMA = pltpu.SemaphoreType.DMA
LANES = 128
UNROLL = 2
RING = 16
HEAD = 8
GRANT = 50
PICK = 53


def spec(space):
    return pl.BlockSpec(memory_space=space)


def params(mib):
    return pltpu.CompilerParams(vmem_limit_bytes=mib * 1024 * 1024)


def round_up(n, step):
    return (n + step - 1) // step * step


def plan_kernel(n_row, piece_blocks, sent_at, place, wanted, rows_a, cols_a, used_a, meta_b, out):
    slot_count = rows_a.shape[0]
    first_row = place[1] * piece_blocks

    def write(at, one, two, three):
        out[at] = one
        out[at + 1] = two
        out[at + 2] = three

    def scan(row_of, col_of, used, at, sent):
        def step(s, carry):
            at, sent = carry
            row = row_of(s) - first_row
            mine = ((row >= 0) & (row < piece_blocks)).astype(jnp.int32)
            piece = col_of(s) // piece_blocks
            write(HEAD + 3 * at, s, row, piece)
            for k in range(n_row):
                write(sent_at + 3 * sent, s, k, piece)
                sent = sent + jnp.where(wanted[k, 0] == row, mine, 0)
            return at + mine, sent

        at, sent = lax.fori_loop(0, used, step, (at, sent))
        for _ in range(UNROLL):
            write(HEAD + 3 * at, 0, piece_blocks, 0)
            write(sent_at + 3 * sent, 0, n_row, 0)
            at = at + jnp.where(at % UNROLL == 0, 0, 1)
            sent = sent + jnp.where(sent % UNROLL == 0, 0, 1)
        return at, sent

    zero = jnp.int32(0)
    at, sent = scan(lambda s: rows_a[s], lambda s: cols_a[s], used_a[0], zero, zero)
    out[0] = at
    out[2] = sent
    at, sent = scan(
        lambda s: meta_b[s], lambda s: meta_b[slot_count + s], meta_b[2 * slot_count], at, sent
    )
    out[1] = at
    out[3] = sent


def pick_kernel(n_row, block_size, wanted, vectors, out, sem):
    def copy(k):
        at = pl.multiple_of(wanted[k, 0] * block_size, block_size)
        return pltpu.make_async_copy(vectors.at[pl.ds(at, block_size)], out.at[k], sem.at[k])

    for k in range(n_row):
        copy(k).start()
    for k in range(n_row):
        copy(k).wait()


def add_products(plan, base, ends, tiles, vec, total, ring, sems, ready):
    mid, end = plan[ends], plan[ends + 1]

    def copy(side, i):
        at = lax.rem(i, RING)
        return pltpu.make_async_copy(tiles[side].at[plan[base + 3 * i]], ring.at[at], sems.at[at])

    def start(i):
        @pl.when(i < mid)
        def _():
            copy(0, i).start()

        @pl.when((i >= mid) & (i < end))
        def _():
            copy(1, i).start()

    for i in range(RING):
        start(jnp.int32(i))
    ready()

    def run(side, begin, end):
        @pl.loop(begin // UNROLL, end // UNROLL)
        def _(j):
            i = UNROLL * j
            for u in range(UNROLL):
                copy(0, i + u).wait()
            for u in range(UNROLL):
                block = ring[lax.rem(i + u, RING)]
                piece = vec[side, plan[base + 3 * (i + u) + 2]]
                total[plan[base + 3 * (i + u) + 1]] += jnp.dot(
                    block, piece, preferred_element_type=jnp.float32
                )
            for u in range(UNROLL):
                start(i + RING + u)

    run(0, 0, mid)
    run(1, mid, end)


def sent_kernel(first, sent_at, plan, tile_a, tile_b, pieces, others, current, *rest):
    if first:
        out, vec, total, ring, sems, vec_sems = rest
    else:
        previous, out, vec, total, ring, sems, vec_sems = rest
    n_row = out.shape[0]
    copies = [
        pltpu.make_async_copy(source, vec.at[side], vec_sems.at[side])
        for side, source in enumerate((pieces, others))
    ]
    for copy in copies:
        copy.start()

    def ready():
        for k in range(n_row):
            value = -center_value * current[k].astype(jnp.float32)
            if not first:
                value = value - previous[k].astype(jnp.float32)
            total[k] = value
        for copy in copies:
            copy.wait()

    add_products(plan, sent_at, 2, (tile_a, tile_b), vec, total, ring, sems, ready)
    for k in range(n_row):
        value = total[k]
        out[k] = (value / half_width if first else value).astype(jnp.bfloat16)


def early_kernel(
    plan, tile_a, tile_b, p1, p2, o1, o2, vectors, base, vec, total, ring, sems, vec_sems, own, row_sems
):
    width = vectors.shape[1]
    piece_blocks, block_size, _ = base.shape
    copies = [
        pltpu.make_async_copy(
            source, vec.at[side, :, :, pl.ds(step * width, width)], vec_sems.at[side, step]
        )
        for side, step, source in ((0, 0, p1), (0, 1, p2), (1, 0, o1), (1, 1, o2))
    ]
    copies.append(pltpu.make_async_copy(vectors, own, row_sems.at[0]))

    def ready():
        for copy in reversed(copies):
            copy.start()
        copies[-1].wait()

        @pl.loop(0, piece_blocks)
        def _(b):
            at = pl.ds(pl.multiple_of(b * block_size, block_size), block_size)
            value = own[at, :].astype(jnp.float32)
            total[b, :, :width] = -center_value * value
            total[b, :, width:] = -value

        for copy in copies[:-1]:
            copy.wait()

    add_products(plan, HEAD, 0, (tile_a, tile_b), vec, total, ring, sems, ready)

    def put(b):
        return pltpu.make_async_copy(total.at[b, :, pl.ds(0, width)], base.at[b], row_sems.at[b])

    @pl.loop(0, piece_blocks)
    def _(b):
        first = (total[b, :, :width] / half_width).astype(jnp.bfloat16).astype(jnp.float32)
        second = total[b, :, width:] - center_value * first
        second = second.astype(jnp.bfloat16).astype(jnp.float32)
        total[b, :, :width] = -center_value * second - first
        put(b).start()

    @pl.loop(0, piece_blocks)
    def _(b):
        put(b).wait()


def last_kernel(
    plan, tile_a, tile_b, pieces, others, base, out, vec, total, ring, sems, vec_sems, start, own, row_sems
):
    piece_blocks, block_size, _ = base.shape
    copies = [
        pltpu.make_async_copy(pieces, vec.at[0], vec_sems.at[0]),
        pltpu.make_async_copy(others, vec.at[1], vec_sems.at[1]),
    ]
    base_copy = pltpu.make_async_copy(base, start, vec_sems.at[2])
    for copy in copies:
        copy.start()

    def ready():
        base_copy.start()

        @pl.loop(0, piece_blocks)
        def _(b):
            total[b] = jnp.zeros(total.shape[1:], jnp.float32)

        for copy in copies:
            copy.wait()

    add_products(plan, HEAD, 0, (tile_a, tile_b), vec, total, ring, sems, ready)
    base_copy.wait()

    def put(b):
        at = pl.ds(pl.multiple_of(b * block_size, block_size), block_size)
        return pltpu.make_async_copy(own.at[at], out.at[at], row_sems.at[b])

    @pl.loop(0, piece_blocks)
    def _(b):
        at = pl.ds(pl.multiple_of(b * block_size, block_size), block_size)
        own[at, :] = (total[b] + start[b]).astype(jnp.bfloat16)
        put(b).start()

    @pl.loop(0, piece_blocks)
    def _(b):
        put(b).wait()


def after(value, *others):
    return lax.optimization_barrier((value, *others))[0]


def on_pair(vectors, tile_blocks, block_rows, block_cols, counts):
    n_row = lax.axis_size("row")
    tile = tile_blocks[0, 0]
    slot_rows = block_rows[0, 0]
    slot_cols = block_cols[0, 0]
    used = counts[0]
    slot_count, block_size, _ = tile.shape
    width = vectors.shape[1]
    piece_blocks = vectors.shape[0] // block_size
    place = jnp.stack([lax.axis_index("row"), lax.axis_index("col")]).astype(jnp.int32)

    across = functools.partial(lax.ppermute, axis_name="col", perm=[(0, 1), (1, 0)])
    meta = across(jnp.concatenate([slot_rows, slot_cols, used]))

    needed = jnp.max(
        jnp.where(
            slot_cols[None, :] // piece_blocks == jnp.arange(n_row)[:, None],
            slot_cols[None, :] % piece_blocks,
            0,
        ),
        axis=1,
        keepdims=True,
    )
    exchange = functools.partial(
        lax.all_to_all, axis_name="row", split_axis=0, concat_axis=0, tiled=True
    )
    wanted = after(exchange(jnp.broadcast_to(needed, (n_row, LANES))), meta, place)
    sent_shape = jax.ShapeDtypeStruct((n_row, block_size, width), jnp.bfloat16)
    sent = pl.pallas_call(
        functools.partial(pick_kernel, n_row, block_size),
        out_shape=sent_shape,
        in_specs=[spec(SMEM), spec(HBM)],
        out_specs=spec(VMEM),
        scratch_shapes=[DMA((n_row,))],
        compiler_params=params(PICK),
        name="pick",
    )(wanted, vectors)

    tile_other = across(after(tile, sent))

    capacity = 2 * round_up(slot_count, UNROLL)
    sent_at = HEAD + 3 * (capacity + 1)
    plan_size = sent_at + 3 * (2 * n_row * n_row + 2 * UNROLL + 1)
    plan = pl.pallas_call(
        functools.partial(plan_kernel, n_row, piece_blocks, sent_at),
        out_shape=jax.ShapeDtypeStruct((plan_size,), jnp.int32),
        in_specs=[spec(SMEM)] * 6,
        out_specs=spec(SMEM),
        compiler_params=params(PICK),
        name="plan",
    )(place, wanted, slot_rows, slot_cols, used, meta)

    def cost(products, rows):
        size = block_size * width
        return pl.CostEstimate(
            flops=2 * products * block_size * size,
            bytes_accessed=2 * (products * block_size * block_size + 3 * rows * size),
            transcendentals=0,
        )

    def scratch(rows, wide, sources, sems):
        return [
            VMEM((sources, n_row, block_size, wide), jnp.bfloat16),
            VMEM((rows + 1, block_size, wide), jnp.float32),
            VMEM((RING, block_size, block_size), jnp.bfloat16),
            DMA((RING,)),
            DMA(sems),
        ]

    own_rows = [VMEM(vectors.shape, jnp.bfloat16), DMA((piece_blocks,))]
    base_shape = (piece_blocks, block_size, width)

    def call(kernel, out_shape, out_space, args, scratch_shapes, estimate, name, started=0):
        return pl.pallas_call(
            kernel,
            out_shape=out_shape,
            in_specs=[spec(SMEM)]
            + [spec(pl.ANY)] * (2 + len(args) - started)
            + [spec(VMEM)] * started,
            out_specs=spec(out_space),
            scratch_shapes=scratch_shapes,
            compiler_params=params(GRANT),
            cost_estimate=estimate,
            name=name,
        )(plan, tile, tile_other, *args)

    def sent_blocks(*args):
        return call(
            functools.partial(sent_kernel, len(args) == 3, sent_at),
            sent_shape,
            VMEM,
            args,
            scratch(n_row, width, 2, (2,)),
            cost(n_row, n_row),
            "sent",
            len(args) - 2,
        )

    def early(*pieces):
        return call(
            early_kernel,
            jax.ShapeDtypeStruct(base_shape, jnp.float32),
            HBM,
            (*pieces, vectors),
            scratch(piece_blocks, 2 * width, 2, (2, 2)) + own_rows,
            cost(2 * slot_count, 2 * piece_blocks),
            "early",
        )

    def last(*args):
        return call(
            last_kernel,
            jax.ShapeDtypeStruct(vectors.shape, jnp.bfloat16),
            HBM,
            args,
            scratch(piece_blocks, width, 2, (3,)) + [VMEM(base_shape, jnp.float32)] + own_rows,
            cost(slot_count, piece_blocks),
            "last",
        )

    p1 = after(exchange(sent), plan)
    o1 = across(p1)
    first_sent = sent_blocks(p1, o1, sent)
    p2 = exchange(first_sent)
    o2 = across(p2)
    second_sent = sent_blocks(p2, o2, first_sent, sent)
    base = early(p1, p2, o1, o2)
    p3 = after(exchange(second_sent), base)
    return last(p3, across(p3), base)


def on_any(vectors, tile_blocks, block_rows, block_cols, counts):
    n_row = lax.axis_size("row")
    n_col = lax.axis_size("col")
    tile_data = tile_blocks[0, 0]
    slot_rows = block_rows[0, 0]
    slot_cols = block_cols[0, 0]
    used = counts[0, 0]
    block_size = tile_data.shape[-1]
    width = vectors.shape[1]
    piece_blocks = vectors.shape[0] // block_size
    row_blocks = piece_blocks * n_col
    slot_count = tile_data.shape[0]
    live = (jnp.arange(slot_count) < used).astype(jnp.float32)
    onehot = (slot_rows[None, :] == jnp.arange(row_blocks)[:, None]).astype(jnp.float32) * live[
        None, :
    ]
    source_piece = slot_cols // piece_blocks
    offset = slot_cols % piece_blocks
    needed = jnp.max(
        jnp.where(source_piece[None, :] == jnp.arange(n_row)[:, None], offset[None, :], 0), axis=1
    )
    wanted = lax.all_to_all(
        needed.reshape(n_row, 1), "row", split_axis=0, concat_axis=0, tiled=True
    ).reshape(n_row)

    def apply_tiles(current):
        own_blocks = current.reshape(piece_blocks, block_size, width)
        outgoing = jnp.take(own_blocks, wanted, axis=0)
        received = lax.all_to_all(outgoing, "row", split_axis=0, concat_axis=0, tiled=True)
        vec_blocks = jnp.take(received, source_piece, axis=0)
        products = jnp.einsum(
            "sij,sjk->sik", tile_data, vec_blocks, preferred_element_type=jnp.float32
        )
        term = jnp.einsum("ls,sik->lik", onehot, products, precision=lax.Precision.HIGHEST)
        term = term.reshape(row_blocks * block_size, width)
        return lax.psum_scatter(
            term.astype(jnp.bfloat16), "col", scatter_dimension=0, tiled=True
        ).astype(jnp.float32)

    previous = vectors
    applied = apply_tiles(vectors)
    current = ((applied - center_value * previous.astype(jnp.float32)) / half_width).astype(
        jnp.bfloat16
    )
    for repeat in range(DEGREE - 1):
        applied = apply_tiles(current)
        following = (
            2.0 * (applied - center_value * current.astype(jnp.float32)) / half_width
            - previous.astype(jnp.float32)
        ).astype(jnp.bfloat16)
        previous, current = (current, following)
    return current


def solution(mesh):
    n_row, n_col = mesh.shape["row"], mesh.shape["col"]
    paired = n_col == 2 and n_row & (n_row - 1) == 0
    return jax.shard_map(
        on_pair if paired else on_any,
        mesh=mesh,
        in_specs=(
            P(("row", "col"), "vec"),
            P("row", "col", None, None, None),
            P("row", "col", None),
            P("row", "col", None),
            P("row", "col"),
        ),
        out_specs=P(("row", "col"), "vec"),
        check_vma=False,
    )
```

```python
import functools

import jax
import jax.numpy as jnp
from jax import lax
from jax.experimental import pallas as pl
from jax.experimental.pallas import tpu as pltpu
from jax.sharding import PartitionSpec as P

DEGREE = 3

center_value = 0.5
half_width = 2.0

VMEM = pltpu.VMEM
SMEM = pltpu.SMEM
HBM = pltpu.HBM
DMA = pltpu.SemaphoreType.DMA
LANES = 128
UNROLL = 2
HEAD = 8


def spec(space):
    return pl.BlockSpec(memory_space=space)


def params(mib):
    return pltpu.CompilerParams(vmem_limit_bytes=mib * 1024 * 1024)


def round_up(n, step):
    return (n + step - 1) // step * step


def plan_kernel(n_row, piece_blocks, sent_at, place, wanted, rows_a, cols_a, used_a, meta_b, out):
    slot_count = rows_a.shape[0]
    first_row = place[1] * piece_blocks

    def write(at, one, two, three):
        out[at] = one
        out[at + 1] = two
        out[at + 2] = three

    def scan(row_of, col_of, used, at, sent):
        def step(s, carry):
            at, sent = carry
            row = row_of(s) - first_row
            mine = ((row >= 0) & (row < piece_blocks)).astype(jnp.int32)
            piece = col_of(s) // piece_blocks
            write(HEAD + 3 * at, s, row, piece)
            for k in range(n_row):
                write(sent_at + 3 * sent, at, k, piece)
                sent = sent + jnp.where(wanted[k, 0] == row, mine, 0)
            return at + mine, sent

        at, sent = lax.fori_loop(0, used, step, (at, sent))
        for _ in range(UNROLL):
            write(HEAD + 3 * at, 0, piece_blocks, 0)
            write(sent_at + 3 * sent, 0, n_row, 0)
            at = at + jnp.where(at % UNROLL == 0, 0, 1)
            sent = sent + jnp.where(sent % UNROLL == 0, 0, 1)
        return at, sent

    zero = jnp.int32(0)
    at, sent = scan(lambda s: rows_a[s], lambda s: cols_a[s], used_a[0], zero, zero)
    out[0] = at
    out[2] = sent
    at, sent = scan(
        lambda s: meta_b[s], lambda s: meta_b[slot_count + s], meta_b[2 * slot_count], at, sent
    )
    out[1] = at
    out[3] = sent


def pick_kernel(n_row, block_size, wanted, vectors, out, sem):
    def copy(k):
        at = pl.multiple_of(wanted[k, 0] * block_size, block_size)
        return pltpu.make_async_copy(vectors.at[pl.ds(at, block_size)], out.at[k], sem.at[k])

    for k in range(n_row):
        copy(k).start()
    for k in range(n_row):
        copy(k).wait()


def load_kernel(plan, tile_a, tile_b, blocks, sems):
    def copy(tile, i):
        return pltpu.make_async_copy(tile.at[plan[HEAD + 3 * i]], blocks.at[i], sems.at[i])

    @pl.loop(0, plan[0])
    def _(i):
        copy(tile_a, i).start()

    @pl.loop(plan[0], plan[1])
    def _(i):
        copy(tile_b, i).start()

    @pl.loop(0, plan[1])
    def _(i):
        copy(tile_a, i).wait()


def add_products(plan, base, ends, blocks, pieces, total):
    mid, end = plan[ends], plan[ends + 1]

    def run(piece_ref, begin, end):
        @pl.loop(begin // UNROLL, end // UNROLL)
        def _(j):
            for u in range(UNROLL):
                i = UNROLL * j + u
                at = base + 3 * i
                block = blocks[i if base == HEAD else plan[at]]
                total[plan[at + 1]] += jnp.dot(
                    block, piece_ref[plan[at + 2]], preferred_element_type=jnp.float32
                )

    run(pieces[0], 0, mid)
    run(pieces[1], mid, end)


def sent_kernel(first, sent_at, plan, blocks, pieces, others, current, *rest):
    if first:
        out, total = rest
    else:
        previous, out, total = rest
    n_row = out.shape[0]
    for k in range(n_row):
        value = -center_value * current[k].astype(jnp.float32)
        if not first:
            value = value - previous[k].astype(jnp.float32)
        total[k] = value
    add_products(plan, sent_at, 2, blocks, (pieces, others), total)
    for k in range(n_row):
        value = total[k]
        out[k] = (value / half_width if first else value).astype(jnp.bfloat16)


def early_kernel(plan, blocks, p1, p2, o1, o2, vectors, base, vec, total, own, sems):
    width = vectors.shape[1]
    piece_blocks, block_size, _ = base.shape
    copies = [
        pltpu.make_async_copy(
            source, vec.at[side, :, :, pl.ds(step * width, width)], sems.at[2 * side + step]
        )
        for side, step, source in ((0, 0, p1), (0, 1, p2), (1, 0, o1), (1, 1, o2))
    ]
    copies.append(pltpu.make_async_copy(vectors, own, sems.at[4]))
    for copy in copies:
        copy.start()
    copies[-1].wait()

    @pl.loop(0, piece_blocks)
    def _(b):
        at = pl.ds(pl.multiple_of(b * block_size, block_size), block_size)
        value = own[at, :].astype(jnp.float32)
        total[b, :, :width] = -center_value * value
        total[b, :, width:] = -value

    for copy in copies[:-1]:
        copy.wait()
    add_products(plan, HEAD, 0, blocks, (vec.at[0], vec.at[1]), total)

    @pl.loop(0, piece_blocks)
    def _(b):
        first = (total[b, :, :width] / half_width).astype(jnp.bfloat16).astype(jnp.float32)
        second = total[b, :, width:] - center_value * first
        second = second.astype(jnp.bfloat16).astype(jnp.float32)
        base[b] = -center_value * second - first


def last_kernel(plan, blocks, pieces, others, base, out, total, own, row_sems):
    piece_blocks, block_size, _ = base.shape

    @pl.loop(0, piece_blocks)
    def _(b):
        total[b] = jnp.zeros(total.shape[1:], jnp.float32)

    add_products(plan, HEAD, 0, blocks, (pieces, others), total)

    def put(b):
        at = pl.ds(pl.multiple_of(b * block_size, block_size), block_size)
        return pltpu.make_async_copy(own.at[at], out.at[at], row_sems.at[b])

    @pl.loop(0, piece_blocks)
    def _(b):
        at = pl.ds(pl.multiple_of(b * block_size, block_size), block_size)
        own[at, :] = (total[b] + base[b]).astype(jnp.bfloat16)
        put(b).start()

    @pl.loop(0, piece_blocks)
    def _(b):
        put(b).wait()


def after(value, *others):
    return lax.optimization_barrier((value, *others))[0]


def call(kernel, out, args, spaces, scratch, mib, name, estimate=None):
    args = [
        pltpu.with_memory_space_constraint(arg, space) if space in (VMEM, HBM) or tied else arg
        for arg, (space, tied) in zip(args, spaces)
    ]
    shape, dtype, out_space = out
    return pl.pallas_call(
        kernel,
        out_shape=out_space(shape, dtype),
        in_specs=[spec(space) for space, _ in spaces],
        out_specs=spec(out_space),
        scratch_shapes=scratch,
        compiler_params=params(mib),
        cost_estimate=estimate,
        name=name,
    )(*args)


HERE = (VMEM, True)
FAR = (HBM, True)
LIST = (SMEM, True)
SCALARS = (SMEM, False)
ANYWHERE = (pl.ANY, False)


def on_pair(vectors, tile_blocks, block_rows, block_cols, counts):
    n_row = lax.axis_size("row")
    tile = tile_blocks[0, 0]
    slot_rows = block_rows[0, 0]
    slot_cols = block_cols[0, 0]
    used = counts[0]
    slot_count, block_size, _ = tile.shape
    width = vectors.shape[1]
    piece_blocks = vectors.shape[0] // block_size
    place = jnp.stack([lax.axis_index("row"), lax.axis_index("col")]).astype(jnp.int32)

    across = functools.partial(lax.ppermute, axis_name="col", perm=[(0, 1), (1, 0)])
    meta = across(jnp.concatenate([slot_rows, slot_cols, used]))

    needed = jnp.max(
        jnp.where(
            slot_cols[None, :] // piece_blocks == jnp.arange(n_row)[:, None],
            slot_cols[None, :] % piece_blocks,
            0,
        ),
        axis=1,
        keepdims=True,
    )
    exchange = functools.partial(
        lax.all_to_all, axis_name="row", split_axis=0, concat_axis=0, tiled=True
    )
    wanted = after(exchange(jnp.broadcast_to(needed, (n_row, LANES))), meta, place)
    sent_shape = (n_row, block_size, width)
    sent = call(
        functools.partial(pick_kernel, n_row, block_size),
        (sent_shape, jnp.bfloat16, VMEM),
        (wanted, vectors),
        (SCALARS, FAR),
        [DMA((n_row,))],
        2,
        "pick",
    )
    tile_other = across(after(tile, sent))

    capacity = 2 * round_up(slot_count, UNROLL)
    sent_at = HEAD + 3 * (capacity + 1)
    plan_size = sent_at + 3 * (2 * n_row * n_row + 2 * UNROLL + 1)
    plan = call(
        functools.partial(plan_kernel, n_row, piece_blocks, sent_at),
        ((plan_size,), jnp.int32, SMEM),
        (place, wanted, slot_rows, slot_cols, used, meta),
        (SCALARS,) * 6,
        [],
        2,
        "plan",
    )
    blocks = call(
        load_kernel,
        ((capacity, block_size, block_size), jnp.bfloat16, VMEM),
        (plan, tile, tile_other),
        (LIST, FAR, ANYWHERE),
        [DMA((capacity,))],
        2,
        "load",
    )

    def cost(products, rows):
        size = block_size * width
        return pl.CostEstimate(
            flops=2 * products * block_size * size,
            bytes_accessed=2 * (products * block_size * block_size + 3 * rows * size),
            transcendentals=0,
        )

    def sent_blocks(*args):
        return call(
            functools.partial(sent_kernel, len(args) == 3, sent_at),
            (sent_shape, jnp.bfloat16, VMEM),
            (plan, blocks, *args),
            (LIST,) + (HERE,) * (1 + len(args)),
            [VMEM((n_row + 1, block_size, width), jnp.float32)],
            4,
            "sent",
            cost(n_row, n_row),
        )

    def early(*pieces):
        return call(
            early_kernel,
            ((piece_blocks, block_size, width), jnp.float32, VMEM),
            (plan, blocks, *pieces, vectors),
            (LIST,) + (HERE,) * 5 + (FAR,),
            [
                VMEM((2, n_row, block_size, 2 * width), jnp.bfloat16),
                VMEM((piece_blocks + 1, block_size, 2 * width), jnp.float32),
                VMEM(vectors.shape, jnp.bfloat16),
                DMA((5,)),
            ],
            18,
            "early",
            cost(2 * slot_count, 2 * piece_blocks),
        )

    def last(*args):
        return call(
            last_kernel,
            (vectors.shape, jnp.bfloat16, HBM),
            (plan, blocks, *args),
            (LIST,) + (HERE,) * 4,
            [
                VMEM((piece_blocks + 1, block_size, width), jnp.float32),
                VMEM(vectors.shape, jnp.bfloat16),
                DMA((piece_blocks,)),
            ],
            10,
            "last",
            cost(slot_count, piece_blocks),
        )

    p1 = after(exchange(sent), blocks)
    o1 = across(p1)
    first_sent = sent_blocks(p1, o1, sent)
    p2 = exchange(first_sent)
    o2 = across(p2)
    second_sent = sent_blocks(p2, o2, first_sent, sent)
    base = early(p1, p2, o1, o2)
    p3 = after(exchange(second_sent), base)
    return last(p3, across(p3), base)


def on_any(vectors, tile_blocks, block_rows, block_cols, counts):
    n_row = lax.axis_size("row")
    n_col = lax.axis_size("col")
    tile_data = tile_blocks[0, 0]
    slot_rows = block_rows[0, 0]
    slot_cols = block_cols[0, 0]
    used = counts[0, 0]
    block_size = tile_data.shape[-1]
    width = vectors.shape[1]
    piece_blocks = vectors.shape[0] // block_size
    row_blocks = piece_blocks * n_col
    slot_count = tile_data.shape[0]
    live = (jnp.arange(slot_count) < used).astype(jnp.float32)
    onehot = (slot_rows[None, :] == jnp.arange(row_blocks)[:, None]).astype(jnp.float32) * live[
        None, :
    ]
    source_piece = slot_cols // piece_blocks
    offset = slot_cols % piece_blocks
    needed = jnp.max(
        jnp.where(source_piece[None, :] == jnp.arange(n_row)[:, None], offset[None, :], 0), axis=1
    )
    wanted = lax.all_to_all(
        needed.reshape(n_row, 1), "row", split_axis=0, concat_axis=0, tiled=True
    ).reshape(n_row)

    def apply_tiles(current):
        own_blocks = current.reshape(piece_blocks, block_size, width)
        outgoing = jnp.take(own_blocks, wanted, axis=0)
        received = lax.all_to_all(outgoing, "row", split_axis=0, concat_axis=0, tiled=True)
        vec_blocks = jnp.take(received, source_piece, axis=0)
        products = jnp.einsum(
            "sij,sjk->sik", tile_data, vec_blocks, preferred_element_type=jnp.float32
        )
        term = jnp.einsum("ls,sik->lik", onehot, products, precision=lax.Precision.HIGHEST)
        term = term.reshape(row_blocks * block_size, width)
        return lax.psum_scatter(
            term.astype(jnp.bfloat16), "col", scatter_dimension=0, tiled=True
        ).astype(jnp.float32)

    previous = vectors
    applied = apply_tiles(vectors)
    current = ((applied - center_value * previous.astype(jnp.float32)) / half_width).astype(
        jnp.bfloat16
    )
    for repeat in range(DEGREE - 1):
        applied = apply_tiles(current)
        following = (
            2.0 * (applied - center_value * current.astype(jnp.float32)) / half_width
            - previous.astype(jnp.float32)
        ).astype(jnp.bfloat16)
        previous, current = (current, following)
    return current


def solution(mesh):
    n_row, n_col = mesh.shape["row"], mesh.shape["col"]
    paired = n_col == 2 and n_row & (n_row - 1) == 0
    return jax.shard_map(
        on_pair if paired else on_any,
        mesh=mesh,
        in_specs=(
            P(("row", "col"), "vec"),
            P("row", "col", None, None, None),
            P("row", "col", None),
            P("row", "col", None),
            P("row", "col"),
        ),
        out_specs=P(("row", "col"), "vec"),
        check_vma=False,
    )
```

```python
import functools

import jax
import jax.numpy as jnp
from jax import lax
from jax.experimental import pallas as pl
from jax.experimental.pallas import tpu as pltpu
from jax.sharding import PartitionSpec as P

DEGREE = 3

center_value = 0.5
half_width = 2.0

VMEM = pltpu.VMEM
SMEM = pltpu.SMEM
HBM = pltpu.HBM
DMA = pltpu.SemaphoreType.DMA
LANES = 128
UNROLL = 2
HEAD = 8


def spec(space):
    return pl.BlockSpec(memory_space=space)


def params(mib):
    return pltpu.CompilerParams(vmem_limit_bytes=mib * 1024 * 1024)


def round_up(n, step):
    return (n + step - 1) // step * step


def plan_kernel(n_row, piece_blocks, sent_at, load_at, place, wanted, rows_a, cols_a, used_a, meta_b, out):
    slot_count = rows_a.shape[0]
    first_row = place[1] * piece_blocks

    def write(at, one, two, three):
        out[at] = one
        out[at + 1] = two
        out[at + 2] = three

    def scan(row_of, col_of, used, at, sent, load):
        def step(s, carry):
            at, sent, load = carry
            row = row_of(s) - first_row
            mine = ((row >= 0) & (row < piece_blocks)).astype(jnp.int32)
            piece = col_of(s) // piece_blocks
            write(HEAD + 3 * at, s, row, piece)
            out[load_at + load] = s
            before = sent
            for k in range(n_row):
                write(sent_at + 3 * sent, load, k, piece)
                sent = sent + jnp.where(wanted[k, 0] == row, mine, 0)
            return at + mine, sent, load + (sent > before).astype(jnp.int32)

        at, sent, load = lax.fori_loop(0, used, step, (at, sent, load))
        for _ in range(UNROLL):
            write(HEAD + 3 * at, 0, piece_blocks, 0)
            write(sent_at + 3 * sent, 0, n_row, 0)
            at = at + jnp.where(at % UNROLL == 0, 0, 1)
            sent = sent + jnp.where(sent % UNROLL == 0, 0, 1)
        return at, sent, load

    zero = jnp.int32(0)
    at, sent, load = scan(
        lambda s: rows_a[s], lambda s: cols_a[s], used_a[0], zero, zero, zero
    )
    out[0] = at
    out[2] = sent
    out[4] = load
    at, sent, load = scan(
        lambda s: meta_b[s],
        lambda s: meta_b[slot_count + s],
        meta_b[2 * slot_count],
        at,
        sent,
        load,
    )
    out[1] = at
    out[3] = sent
    out[5] = load


def pick_kernel(n_row, block_size, wanted, vectors, out, sem):
    def copy(k):
        at = pl.multiple_of(wanted[k, 0] * block_size, block_size)
        return pltpu.make_async_copy(vectors.at[pl.ds(at, block_size)], out.at[k], sem.at[k])

    for k in range(n_row):
        copy(k).start()
    for k in range(n_row):
        copy(k).wait()


def load_kernel(base, stride, ends, plan, tile_a, tile_b, blocks, sems):
    mid, end = plan[ends], plan[ends + 1]

    def copy(tile, i):
        slot = plan[base + stride * i]
        return pltpu.make_async_copy(tile.at[slot], blocks.at[i], sems.at[i])

    @pl.loop(0, mid)
    def _(i):
        copy(tile_a, i).start()

    @pl.loop(mid, end)
    def _(i):
        copy(tile_b, i).start()

    @pl.loop(0, end)
    def _(i):
        copy(tile_a, i).wait()


def add_products(plan, base, ends, blocks, pieces, total):
    mid, end = plan[ends], plan[ends + 1]

    def run(piece_ref, begin, end):
        @pl.loop(begin // UNROLL, end // UNROLL)
        def _(j):
            for u in range(UNROLL):
                i = UNROLL * j + u
                at = base + 3 * i
                block = blocks[i if base == HEAD else plan[at]]
                total[plan[at + 1]] += jnp.dot(
                    block, piece_ref[plan[at + 2]], preferred_element_type=jnp.float32
                )

    run(pieces[0], 0, mid)
    run(pieces[1], mid, end)


def sent_kernel(first, sent_at, plan, blocks, pieces, others, current, *rest):
    if first:
        out, total = rest
    else:
        previous, out, total = rest
    n_row = out.shape[0]
    for k in range(n_row):
        value = -center_value * current[k].astype(jnp.float32)
        if not first:
            value = value - previous[k].astype(jnp.float32)
        total[k] = value
    add_products(plan, sent_at, 2, blocks, (pieces, others), total)
    for k in range(n_row):
        value = total[k]
        out[k] = (value / half_width if first else value).astype(jnp.bfloat16)


def early_kernel(plan, blocks, p1, p2, o1, o2, vectors, base, vec, total, own, sems, row_sems):
    width = vectors.shape[1]
    piece_blocks, block_size, _ = base.shape
    copies = [
        pltpu.make_async_copy(
            source, vec.at[side, :, :, pl.ds(step * width, width)], sems.at[2 * side + step]
        )
        for side, step, source in ((0, 0, p1), (0, 1, p2), (1, 0, o1), (1, 1, o2))
    ]
    copies.append(pltpu.make_async_copy(vectors, own, sems.at[4]))
    for copy in copies:
        copy.start()
    copies[-1].wait()

    @pl.loop(0, piece_blocks)
    def _(b):
        at = pl.ds(pl.multiple_of(b * block_size, block_size), block_size)
        value = own[at, :].astype(jnp.float32)
        total[b, :, :width] = -center_value * value
        total[b, :, width:] = -value

    for copy in copies[:-1]:
        copy.wait()
    add_products(plan, HEAD, 0, blocks, (vec.at[0], vec.at[1]), total)

    def put(b):
        return pltpu.make_async_copy(total.at[b, :, pl.ds(0, width)], base.at[b], row_sems.at[b])

    @pl.loop(0, piece_blocks)
    def _(b):
        first = (total[b, :, :width] / half_width).astype(jnp.bfloat16).astype(jnp.float32)
        second = total[b, :, width:] - center_value * first
        second = second.astype(jnp.bfloat16).astype(jnp.float32)
        total[b, :, :width] = -center_value * second - first
        put(b).start()

    @pl.loop(0, piece_blocks)
    def _(b):
        put(b).wait()


def last_kernel(plan, blocks, pieces, others, base, out, start, total, own, base_sem, row_sems):
    piece_blocks, block_size, _ = base.shape
    base_copy = pltpu.make_async_copy(base, start, base_sem)
    base_copy.start()

    @pl.loop(0, piece_blocks)
    def _(b):
        total[b] = jnp.zeros(total.shape[1:], jnp.float32)

    add_products(plan, HEAD, 0, blocks, (pieces, others), total)
    base_copy.wait()

    def put(b):
        at = pl.ds(pl.multiple_of(b * block_size, block_size), block_size)
        return pltpu.make_async_copy(own.at[at], out.at[at], row_sems.at[b])

    @pl.loop(0, piece_blocks)
    def _(b):
        at = pl.ds(pl.multiple_of(b * block_size, block_size), block_size)
        own[at, :] = (total[b] + start[b]).astype(jnp.bfloat16)
        put(b).start()

    @pl.loop(0, piece_blocks)
    def _(b):
        put(b).wait()


def after(value, *others):
    return lax.optimization_barrier((value, *others))[0]


def call(kernel, out, args, spaces, scratch, mib, name, estimate=None):
    args = [
        pltpu.with_memory_space_constraint(arg, space) if space in (VMEM, HBM) or tied else arg
        for arg, (space, tied) in zip(args, spaces)
    ]
    shape, dtype, out_space = out
    return pl.pallas_call(
        kernel,
        out_shape=out_space(shape, dtype),
        in_specs=[spec(space) for space, _ in spaces],
        out_specs=spec(out_space),
        scratch_shapes=scratch,
        compiler_params=params(mib),
        cost_estimate=estimate,
        name=name,
    )(*args)


HERE = (VMEM, True)
FAR = (HBM, True)
LIST = (SMEM, True)
SCALARS = (SMEM, False)
ANYWHERE = (pl.ANY, False)


def on_pair(vectors, tile_blocks, block_rows, block_cols, counts):
    n_row = lax.axis_size("row")
    tile = tile_blocks[0, 0]
    slot_rows = block_rows[0, 0]
    slot_cols = block_cols[0, 0]
    used = counts[0]
    slot_count, block_size, _ = tile.shape
    width = vectors.shape[1]
    piece_blocks = vectors.shape[0] // block_size
    place = jnp.stack([lax.axis_index("row"), lax.axis_index("col")]).astype(jnp.int32)

    across = functools.partial(lax.ppermute, axis_name="col", perm=[(0, 1), (1, 0)])
    meta = across(jnp.concatenate([slot_rows, slot_cols, used]))

    needed = jnp.max(
        jnp.where(
            slot_cols[None, :] // piece_blocks == jnp.arange(n_row)[:, None],
            slot_cols[None, :] % piece_blocks,
            0,
        ),
        axis=1,
        keepdims=True,
    )
    exchange = functools.partial(
        lax.all_to_all, axis_name="row", split_axis=0, concat_axis=0, tiled=True
    )
    wanted = after(exchange(jnp.broadcast_to(needed, (n_row, LANES))), meta, place)
    sent_shape = (n_row, block_size, width)
    sent = call(
        functools.partial(pick_kernel, n_row, block_size),
        (sent_shape, jnp.bfloat16, VMEM),
        (wanted, vectors),
        (SCALARS, FAR),
        [DMA((n_row,))],
        2,
        "pick",
    )
    tile_other = across(after(tile, sent))

    capacity = 2 * round_up(slot_count, UNROLL)
    sent_at = HEAD + 3 * (capacity + 1)
    load_at = sent_at + 3 * (2 * n_row * n_row + 2 * UNROLL + 1)
    plan_size = load_at + 2 * slot_count + 1
    plan = call(
        functools.partial(plan_kernel, n_row, piece_blocks, sent_at, load_at),
        ((plan_size,), jnp.int32, SMEM),
        (place, wanted, slot_rows, slot_cols, used, meta),
        (SCALARS,) * 6,
        [],
        2,
        "plan",
    )
    def load(base, stride, ends, cue):
        return call(
            functools.partial(load_kernel, base, stride, ends),
            ((capacity, block_size, block_size), jnp.bfloat16, VMEM),
            (after(plan, cue), tile, tile_other),
            (LIST, FAR, ANYWHERE),
            [DMA((capacity,))],
            2,
            "load",
        )

    def cost(products, rows):
        size = block_size * width
        return pl.CostEstimate(
            flops=2 * products * block_size * size,
            bytes_accessed=2 * (products * block_size * block_size + 3 * rows * size),
            transcendentals=0,
        )

    def sent_blocks(blocks, *args):
        return call(
            functools.partial(sent_kernel, len(args) == 3, sent_at),
            (sent_shape, jnp.bfloat16, VMEM),
            (plan, blocks, *args),
            (LIST,) + (HERE,) * (1 + len(args)),
            [VMEM((n_row + 1, block_size, width), jnp.float32)],
            4,
            "sent",
            cost(n_row, n_row),
        )

    base_shape = (piece_blocks, block_size, width)

    def early(blocks, *pieces):
        return call(
            early_kernel,
            (base_shape, jnp.float32, HBM),
            (plan, blocks, *pieces, vectors),
            (LIST,) + (HERE,) * 5 + (FAR,),
            [
                VMEM((2, n_row, block_size, 2 * width), jnp.bfloat16),
                VMEM((piece_blocks + 1, block_size, 2 * width), jnp.float32),
                VMEM(vectors.shape, jnp.bfloat16),
                DMA((5,)),
                DMA((piece_blocks,)),
            ],
            18,
            "early",
            cost(2 * slot_count, 2 * piece_blocks),
        )

    def last(blocks, *args):
        return call(
            last_kernel,
            (vectors.shape, jnp.bfloat16, HBM),
            (plan, blocks, *args),
            (LIST,) + (HERE,) * 3 + (FAR,),
            [
                VMEM(base_shape, jnp.float32),
                VMEM((piece_blocks + 1, block_size, width), jnp.float32),
                VMEM(vectors.shape, jnp.bfloat16),
                DMA,
                DMA((piece_blocks,)),
            ],
            14,
            "last",
            cost(slot_count, piece_blocks),
        )

    p1 = after(exchange(sent), plan)
    o1 = across(p1)
    blocks = load(load_at, 1, 4, p1)
    first_sent = sent_blocks(blocks, p1, o1, sent)
    p2 = exchange(first_sent)
    o2 = across(p2)
    second_sent = sent_blocks(blocks, p2, o2, first_sent, sent)
    base = early(load(HEAD, 3, 0, second_sent), p1, p2, o1, o2)
    p3 = after(exchange(second_sent), base)
    return last(load(HEAD, 3, 0, p3), p3, across(p3), base)


def on_any(vectors, tile_blocks, block_rows, block_cols, counts):
    n_row = lax.axis_size("row")
    n_col = lax.axis_size("col")
    tile_data = tile_blocks[0, 0]
    slot_rows = block_rows[0, 0]
    slot_cols = block_cols[0, 0]
    used = counts[0, 0]
    block_size = tile_data.shape[-1]
    width = vectors.shape[1]
    piece_blocks = vectors.shape[0] // block_size
    row_blocks = piece_blocks * n_col
    slot_count = tile_data.shape[0]
    live = (jnp.arange(slot_count) < used).astype(jnp.float32)
    onehot = (slot_rows[None, :] == jnp.arange(row_blocks)[:, None]).astype(jnp.float32) * live[
        None, :
    ]
    source_piece = slot_cols // piece_blocks
    offset = slot_cols % piece_blocks
    needed = jnp.max(
        jnp.where(source_piece[None, :] == jnp.arange(n_row)[:, None], offset[None, :], 0), axis=1
    )
    wanted = lax.all_to_all(
        needed.reshape(n_row, 1), "row", split_axis=0, concat_axis=0, tiled=True
    ).reshape(n_row)

    def apply_tiles(current):
        own_blocks = current.reshape(piece_blocks, block_size, width)
        outgoing = jnp.take(own_blocks, wanted, axis=0)
        received = lax.all_to_all(outgoing, "row", split_axis=0, concat_axis=0, tiled=True)
        vec_blocks = jnp.take(received, source_piece, axis=0)
        products = jnp.einsum(
            "sij,sjk->sik", tile_data, vec_blocks, preferred_element_type=jnp.float32
        )
        term = jnp.einsum("ls,sik->lik", onehot, products, precision=lax.Precision.HIGHEST)
        term = term.reshape(row_blocks * block_size, width)
        return lax.psum_scatter(
            term.astype(jnp.bfloat16), "col", scatter_dimension=0, tiled=True
        ).astype(jnp.float32)

    previous = vectors
    applied = apply_tiles(vectors)
    current = ((applied - center_value * previous.astype(jnp.float32)) / half_width).astype(
        jnp.bfloat16
    )
    for repeat in range(DEGREE - 1):
        applied = apply_tiles(current)
        following = (
            2.0 * (applied - center_value * current.astype(jnp.float32)) / half_width
            - previous.astype(jnp.float32)
        ).astype(jnp.bfloat16)
        previous, current = (current, following)
    return current


def solution(mesh):
    n_row, n_col = mesh.shape["row"], mesh.shape["col"]
    paired = n_col == 2 and n_row & (n_row - 1) == 0
    return jax.shard_map(
        on_pair if paired else on_any,
        mesh=mesh,
        in_specs=(
            P(("row", "col"), "vec"),
            P("row", "col", None, None, None),
            P("row", "col", None),
            P("row", "col", None),
            P("row", "col"),
        ),
        out_specs=P(("row", "col"), "vec"),
        check_vma=False,
    )
```

```python
import functools

import jax
import jax.numpy as jnp
from jax import lax
from jax.experimental import pallas as pl
from jax.experimental.pallas import tpu as pltpu
from jax.sharding import PartitionSpec as P

DEGREE = 3

center_value = 0.5
half_width = 2.0

VMEM = pltpu.VMEM
SMEM = pltpu.SMEM
HBM = pltpu.HBM
DMA = pltpu.SemaphoreType.DMA
LANES = 128
UNROLL = 2
HEAD = 8


def spec(space):
    return pl.BlockSpec(memory_space=space)


def params(mib):
    return pltpu.CompilerParams(vmem_limit_bytes=mib * 1024 * 1024)


def round_up(n, step):
    return (n + step - 1) // step * step


def turn(row, n_row):
    half = n_row // 2
    return 2 * (row % half) + row // half


def plan_kernel(n_row, piece_blocks, sent_at, load_at, place, wanted, rows_a, cols_a, used_a, meta_b, out):
    slot_count = rows_a.shape[0]
    first_row = place[1] * piece_blocks

    def write(at, one, two, three):
        out[at] = one
        out[at + 1] = two
        out[at + 2] = three

    def scan(row_of, col_of, used, at, sent, load):
        def step(s, carry):
            at, sent, load = carry
            row = row_of(s) - first_row
            mine = ((row >= 0) & (row < piece_blocks)).astype(jnp.int32)
            piece = turn(col_of(s) // piece_blocks, n_row)
            write(HEAD + 3 * at, s, row, piece)
            out[load_at + load] = s
            before = sent
            for k in range(n_row):
                write(sent_at + 3 * sent, load, k, piece)
                sent = sent + jnp.where(wanted[k, 0] == row, mine, 0)
            return at + mine, sent, load + (sent > before).astype(jnp.int32)

        at, sent, load = lax.fori_loop(0, used, step, (at, sent, load))
        for _ in range(UNROLL):
            write(HEAD + 3 * at, 0, piece_blocks, 0)
            write(sent_at + 3 * sent, 0, n_row, 0)
            at = at + jnp.where(at % UNROLL == 0, 0, 1)
            sent = sent + jnp.where(sent % UNROLL == 0, 0, 1)
        return at, sent, load

    zero = jnp.int32(0)
    at, sent, load = scan(
        lambda s: rows_a[s], lambda s: cols_a[s], used_a[0], zero, zero, zero
    )
    out[0] = at
    out[2] = sent
    out[4] = load
    at, sent, load = scan(
        lambda s: meta_b[s],
        lambda s: meta_b[slot_count + s],
        meta_b[2 * slot_count],
        at,
        sent,
        load,
    )
    out[1] = at
    out[3] = sent
    out[5] = load


def pick_kernel(n_row, block_size, wanted, vectors, out, sem):
    def copy(k):
        at = pl.multiple_of(wanted[k, 0] * block_size, block_size)
        return pltpu.make_async_copy(vectors.at[pl.ds(at, block_size)], out.at[k], sem.at[k])

    for k in range(n_row):
        copy(k).start()
    for k in range(n_row):
        copy(k).wait()


def load_kernel(base, stride, ends, plan, tile_a, tile_b, blocks, sems):
    mid, end = plan[ends], plan[ends + 1]

    def copy(tile, i):
        slot = plan[base + stride * i]
        return pltpu.make_async_copy(tile.at[slot], blocks.at[i], sems.at[i])

    @pl.loop(0, mid)
    def _(i):
        copy(tile_a, i).start()

    @pl.loop(mid, end)
    def _(i):
        copy(tile_b, i).start()

    @pl.loop(0, end)
    def _(i):
        copy(tile_a, i).wait()


def add_products(plan, base, ends, blocks, pieces, total):
    mid, end = plan[ends], plan[ends + 1]

    def run(piece_ref, begin, end):
        @pl.loop(begin // UNROLL, end // UNROLL)
        def _(j):
            for u in range(UNROLL):
                i = UNROLL * j + u
                at = base + 3 * i
                block = blocks[i if base == HEAD else plan[at]]
                total[plan[at + 1]] += jnp.dot(
                    block, piece_ref[plan[at + 2]], preferred_element_type=jnp.float32
                )

    run(pieces[0], 0, mid)
    run(pieces[1], mid, end)


def sent_kernel(first, sent_at, plan, blocks, pieces, others, current, *rest):
    if first:
        out, total = rest
    else:
        previous, out, total = rest
    n_row = out.shape[0]
    for k in range(n_row):
        value = -center_value * current[k].astype(jnp.float32)
        if not first:
            value = value - previous[k].astype(jnp.float32)
        total[k] = value
    add_products(plan, sent_at, 2, blocks, (pieces, others), total)
    for k in range(n_row):
        value = total[k]
        out[k] = (value / half_width if first else value).astype(jnp.bfloat16)


def early_kernel(plan, blocks, p1, p2, o1, o2, vectors, base, vec, total, own, sems, row_sems):
    width = vectors.shape[1]
    piece_blocks, block_size, _ = base.shape
    copies = [
        pltpu.make_async_copy(
            source, vec.at[side, :, :, pl.ds(step * width, width)], sems.at[2 * side + step]
        )
        for side, step, source in ((0, 0, p1), (0, 1, p2), (1, 0, o1), (1, 1, o2))
    ]
    copies.append(pltpu.make_async_copy(vectors, own, sems.at[4]))
    for copy in copies:
        copy.start()
    copies[-1].wait()

    @pl.loop(0, piece_blocks)
    def _(b):
        at = pl.ds(pl.multiple_of(b * block_size, block_size), block_size)
        value = own[at, :].astype(jnp.float32)
        total[b, :, :width] = -center_value * value
        total[b, :, width:] = -value

    for copy in copies[:-1]:
        copy.wait()
    add_products(plan, HEAD, 0, blocks, (vec.at[0], vec.at[1]), total)

    def put(b):
        return pltpu.make_async_copy(total.at[b, :, pl.ds(0, width)], base.at[b], row_sems.at[b])

    @pl.loop(0, piece_blocks)
    def _(b):
        first = (total[b, :, :width] / half_width).astype(jnp.bfloat16).astype(jnp.float32)
        second = total[b, :, width:] - center_value * first
        second = second.astype(jnp.bfloat16).astype(jnp.float32)
        total[b, :, :width] = -center_value * second - first
        put(b).start()

    @pl.loop(0, piece_blocks)
    def _(b):
        put(b).wait()


def last_kernel(plan, blocks, pieces, others, base, out, start, total, own, base_sem, row_sems):
    piece_blocks, block_size, _ = base.shape
    base_copy = pltpu.make_async_copy(base, start, base_sem)
    base_copy.start()

    @pl.loop(0, piece_blocks)
    def _(b):
        total[b] = jnp.zeros(total.shape[1:], jnp.float32)

    add_products(plan, HEAD, 0, blocks, (pieces, others), total)
    base_copy.wait()

    def put(b):
        at = pl.ds(pl.multiple_of(b * block_size, block_size), block_size)
        return pltpu.make_async_copy(own.at[at], out.at[at], row_sems.at[b])

    @pl.loop(0, piece_blocks)
    def _(b):
        at = pl.ds(pl.multiple_of(b * block_size, block_size), block_size)
        own[at, :] = (total[b] + start[b]).astype(jnp.bfloat16)
        put(b).start()

    @pl.loop(0, piece_blocks)
    def _(b):
        put(b).wait()


def after(value, *others):
    return lax.optimization_barrier((value, *others))[0]


def call(kernel, out, args, spaces, scratch, mib, name, estimate=None):
    args = [
        pltpu.with_memory_space_constraint(arg, space) if space in (VMEM, HBM) or tied else arg
        for arg, (space, tied) in zip(args, spaces)
    ]
    shape, dtype, out_space = out
    return pl.pallas_call(
        kernel,
        out_shape=out_space(shape, dtype),
        in_specs=[spec(space) for space, _ in spaces],
        out_specs=spec(out_space),
        scratch_shapes=scratch,
        compiler_params=params(mib),
        cost_estimate=estimate,
        name=name,
    )(*args)


HERE = (VMEM, True)
FAR = (HBM, True)
LIST = (SMEM, True)
SCALARS = (SMEM, False)
ANYWHERE = (pl.ANY, False)


def on_pair(vectors, tile_blocks, block_rows, block_cols, counts):
    n_row = lax.axis_size("row")
    tile = tile_blocks[0, 0]
    slot_rows = block_rows[0, 0]
    slot_cols = block_cols[0, 0]
    used = counts[0]
    slot_count, block_size, _ = tile.shape
    width = vectors.shape[1]
    piece_blocks = vectors.shape[0] // block_size
    place = jnp.stack([lax.axis_index("row"), lax.axis_index("col")]).astype(jnp.int32)

    across = functools.partial(lax.ppermute, axis_name="col", perm=[(0, 1), (1, 0)])
    meta = across(jnp.concatenate([slot_rows, slot_cols, used]))

    needed = jnp.max(
        jnp.where(
            turn(slot_cols[None, :] // piece_blocks, n_row) == jnp.arange(n_row)[:, None],
            slot_cols[None, :] % piece_blocks,
            0,
        ),
        axis=1,
        keepdims=True,
    )
    exchange = functools.partial(
        lax.all_to_all,
        axis_name="row",
        split_axis=0,
        concat_axis=0,
        axis_index_groups=[sorted(range(n_row), key=lambda row: turn(row, n_row))],
        tiled=True,
    )
    wanted = after(exchange(jnp.broadcast_to(needed, (n_row, LANES))), meta, place)
    sent_shape = (n_row, block_size, width)
    sent = call(
        functools.partial(pick_kernel, n_row, block_size),
        (sent_shape, jnp.bfloat16, VMEM),
        (wanted, vectors),
        (SCALARS, FAR),
        [DMA((n_row,))],
        2,
        "pick",
    )
    tile_other = across(after(tile, sent))

    capacity = 2 * round_up(slot_count, UNROLL)
    sent_at = HEAD + 3 * (capacity + 1)
    load_at = sent_at + 3 * (2 * n_row * n_row + 2 * UNROLL + 1)
    plan_size = load_at + 2 * slot_count + 1
    plan = call(
        functools.partial(plan_kernel, n_row, piece_blocks, sent_at, load_at),
        ((plan_size,), jnp.int32, SMEM),
        (place, wanted, slot_rows, slot_cols, used, meta),
        (SCALARS,) * 6,
        [],
        2,
        "plan",
    )
    def load(base, stride, ends, cue):
        return call(
            functools.partial(load_kernel, base, stride, ends),
            ((capacity, block_size, block_size), jnp.bfloat16, VMEM),
            (after(plan, cue), tile, tile_other),
            (LIST, FAR, ANYWHERE),
            [DMA((capacity,))],
            2,
            "load",
        )

    def cost(products, rows):
        size = block_size * width
        return pl.CostEstimate(
            flops=2 * products * block_size * size,
            bytes_accessed=2 * (products * block_size * block_size + 3 * rows * size),
            transcendentals=0,
        )

    def sent_blocks(blocks, *args):
        return call(
            functools.partial(sent_kernel, len(args) == 3, sent_at),
            (sent_shape, jnp.bfloat16, VMEM),
            (plan, blocks, *args),
            (LIST,) + (HERE,) * (1 + len(args)),
            [VMEM((n_row + 1, block_size, width), jnp.float32)],
            4,
            "sent",
            cost(n_row, n_row),
        )

    base_shape = (piece_blocks, block_size, width)

    def early(blocks, *pieces):
        return call(
            early_kernel,
            (base_shape, jnp.float32, HBM),
            (plan, blocks, *pieces, vectors),
            (LIST,) + (HERE,) * 5 + (FAR,),
            [
                VMEM((2, n_row, block_size, 2 * width), jnp.bfloat16),
                VMEM((piece_blocks + 1, block_size, 2 * width), jnp.float32),
                VMEM(vectors.shape, jnp.bfloat16),
                DMA((5,)),
                DMA((piece_blocks,)),
            ],
            18,
            "early",
            cost(2 * slot_count, 2 * piece_blocks),
        )

    def last(blocks, *args):
        return call(
            last_kernel,
            (vectors.shape, jnp.bfloat16, HBM),
            (plan, blocks, *args),
            (LIST,) + (HERE,) * 3 + (FAR,),
            [
                VMEM(base_shape, jnp.float32),
                VMEM((piece_blocks + 1, block_size, width), jnp.float32),
                VMEM(vectors.shape, jnp.bfloat16),
                DMA,
                DMA((piece_blocks,)),
            ],
            14,
            "last",
            cost(slot_count, piece_blocks),
        )

    p1 = after(exchange(sent), plan)
    o1 = across(p1)
    blocks = load(load_at, 1, 4, p1)
    first_sent = sent_blocks(blocks, p1, o1, sent)
    p2 = exchange(first_sent)
    o2 = across(p2)
    second_sent = sent_blocks(blocks, p2, o2, first_sent, sent)
    base = early(load(HEAD, 3, 0, second_sent), p1, p2, o1, o2)
    p3 = after(exchange(second_sent), base)
    return last(load(HEAD, 3, 0, p3), p3, across(p3), base)


def on_any(vectors, tile_blocks, block_rows, block_cols, counts):
    n_row = lax.axis_size("row")
    n_col = lax.axis_size("col")
    tile_data = tile_blocks[0, 0]
    slot_rows = block_rows[0, 0]
    slot_cols = block_cols[0, 0]
    used = counts[0, 0]
    block_size = tile_data.shape[-1]
    width = vectors.shape[1]
    piece_blocks = vectors.shape[0] // block_size
    row_blocks = piece_blocks * n_col
    slot_count = tile_data.shape[0]
    live = (jnp.arange(slot_count) < used).astype(jnp.float32)
    onehot = (slot_rows[None, :] == jnp.arange(row_blocks)[:, None]).astype(jnp.float32) * live[
        None, :
    ]
    source_piece = slot_cols // piece_blocks
    offset = slot_cols % piece_blocks
    needed = jnp.max(
        jnp.where(source_piece[None, :] == jnp.arange(n_row)[:, None], offset[None, :], 0), axis=1
    )
    wanted = lax.all_to_all(
        needed.reshape(n_row, 1), "row", split_axis=0, concat_axis=0, tiled=True
    ).reshape(n_row)

    def apply_tiles(current):
        own_blocks = current.reshape(piece_blocks, block_size, width)
        outgoing = jnp.take(own_blocks, wanted, axis=0)
        received = lax.all_to_all(outgoing, "row", split_axis=0, concat_axis=0, tiled=True)
        vec_blocks = jnp.take(received, source_piece, axis=0)
        products = jnp.einsum(
            "sij,sjk->sik", tile_data, vec_blocks, preferred_element_type=jnp.float32
        )
        term = jnp.einsum("ls,sik->lik", onehot, products, precision=lax.Precision.HIGHEST)
        term = term.reshape(row_blocks * block_size, width)
        return lax.psum_scatter(
            term.astype(jnp.bfloat16), "col", scatter_dimension=0, tiled=True
        ).astype(jnp.float32)

    previous = vectors
    applied = apply_tiles(vectors)
    current = ((applied - center_value * previous.astype(jnp.float32)) / half_width).astype(
        jnp.bfloat16
    )
    for repeat in range(DEGREE - 1):
        applied = apply_tiles(current)
        following = (
            2.0 * (applied - center_value * current.astype(jnp.float32)) / half_width
            - previous.astype(jnp.float32)
        ).astype(jnp.bfloat16)
        previous, current = (current, following)
    return current


def solution(mesh):
    n_row, n_col = mesh.shape["row"], mesh.shape["col"]
    paired = n_col == 2 and n_row % 2 == 0
    return jax.shard_map(
        on_pair if paired else on_any,
        mesh=mesh,
        in_specs=(
            P(("row", "col"), "vec"),
            P("row", "col", None, None, None),
            P("row", "col", None),
            P("row", "col", None),
            P("row", "col"),
        ),
        out_specs=P(("row", "col"), "vec"),
        check_vma=False,
    )
```

```python
import functools

import jax
import jax.numpy as jnp
from jax import lax
from jax.experimental import pallas as pl
from jax.experimental.pallas import tpu as pltpu
from jax.sharding import PartitionSpec as P

DEGREE = 3

center_value = 0.5
half_width = 2.0

VMEM = pltpu.VMEM
SMEM = pltpu.SMEM
HBM = pltpu.HBM
DMA = pltpu.SemaphoreType.DMA
LANES = 128
UNROLL = 2
HEAD = 8


def spec(space):
    return pl.BlockSpec(memory_space=space)


def params(mib):
    return pltpu.CompilerParams(vmem_limit_bytes=mib * 1024 * 1024)


def round_up(n, step):
    return (n + step - 1) // step * step


def plan_kernel(n_row, piece_blocks, sent_at, load_at, place, wanted, rows_a, cols_a, used_a, meta_b, out):
    slot_count = rows_a.shape[0]
    first_row = place[1] * piece_blocks

    def write(at, one, two, three):
        out[at] = one
        out[at + 1] = two
        out[at + 2] = three

    def scan(row_of, col_of, used, at, sent, load):
        def step(s, carry):
            at, sent, load = carry
            row = row_of(s) - first_row
            mine = ((row >= 0) & (row < piece_blocks)).astype(jnp.int32)
            piece = col_of(s) // piece_blocks
            write(HEAD + 3 * at, s, row, piece)
            out[load_at + load] = s
            before = sent
            for k in range(n_row):
                write(sent_at + 3 * sent, load, k, piece)
                sent = sent + jnp.where(wanted[k, 0] == row, mine, 0)
            return at + mine, sent, load + (sent > before).astype(jnp.int32)

        at, sent, load = lax.fori_loop(0, used, step, (at, sent, load))
        for _ in range(UNROLL):
            write(HEAD + 3 * at, 0, piece_blocks, 0)
            write(sent_at + 3 * sent, 0, n_row, 0)
            at = at + jnp.where(at % UNROLL == 0, 0, 1)
            sent = sent + jnp.where(sent % UNROLL == 0, 0, 1)
        return at, sent, load

    zero = jnp.int32(0)
    at, sent, load = scan(
        lambda s: rows_a[s], lambda s: cols_a[s], used_a[0], zero, zero, zero
    )
    out[0] = at
    out[2] = sent
    out[4] = load
    at, sent, load = scan(
        lambda s: meta_b[s],
        lambda s: meta_b[slot_count + s],
        meta_b[2 * slot_count],
        at,
        sent,
        load,
    )
    out[1] = at
    out[3] = sent
    out[5] = load


def pick_kernel(n_row, block_size, wanted, vectors, out, held, in_sems, out_sems):
    def fetch(k):
        at = pl.multiple_of(wanted[k, 0] * block_size, block_size)
        return pltpu.make_async_copy(vectors.at[pl.ds(at, block_size)], held.at[k], in_sems.at[k])

    def put(k):
        return pltpu.make_async_copy(held.at[k], out.at[k], out_sems.at[k])

    for k in range(n_row):
        fetch(k).start()
    for k in range(n_row):
        fetch(k).wait()
        put(k).start()
    for k in range(n_row):
        put(k).wait()


def load_kernel(base, stride, ends, plan, tile_a, tile_b, blocks, sems):
    mid, end = plan[ends], plan[ends + 1]

    def copy(tile, i):
        slot = plan[base + stride * i]
        return pltpu.make_async_copy(tile.at[slot], blocks.at[i], sems.at[i])

    @pl.loop(0, mid)
    def _(i):
        copy(tile_a, i).start()

    @pl.loop(mid, end)
    def _(i):
        copy(tile_b, i).start()

    @pl.loop(0, end)
    def _(i):
        copy(tile_a, i).wait()


def add_products(plan, base, ends, blocks, pieces, total):
    mid, end = plan[ends], plan[ends + 1]

    def run(piece_ref, begin, end):
        @pl.loop(begin // UNROLL, end // UNROLL)
        def _(j):
            for u in range(UNROLL):
                i = UNROLL * j + u
                at = base + 3 * i
                block = blocks[i if base == HEAD else plan[at]]
                total[plan[at + 1]] += jnp.dot(
                    block, piece_ref[plan[at + 2]], preferred_element_type=jnp.float32
                )

    run(pieces[0], 0, mid)
    run(pieces[1], mid, end)


def sent_kernel(first, sent_at, plan, blocks, pieces, others, picked, *rest):
    if first:
        out, total, held, held_sem = rest
    else:
        current, out, total, held, held_sem, ready, out_sems = rest
    n_row = out.shape[0]
    copy = pltpu.make_async_copy(picked, held, held_sem)
    copy.start()
    for k in range(n_row):
        if first:
            total[k] = jnp.zeros(total.shape[1:], jnp.float32)
        else:
            total[k] = -center_value * current[k].astype(jnp.float32)
    add_products(plan, sent_at, 2, blocks, (pieces, others), total)
    copy.wait()
    if first:
        for k in range(n_row):
            value = total[k] - center_value * held[k].astype(jnp.float32)
            out[k] = (value / half_width).astype(jnp.bfloat16)
        return

    def put(k):
        return pltpu.make_async_copy(ready.at[k], out.at[k], out_sems.at[k])

    for k in range(n_row):
        ready[k] = (total[k] - held[k].astype(jnp.float32)).astype(jnp.bfloat16)
        put(k).start()
    for k in range(n_row):
        put(k).wait()


def early_kernel(plan, blocks, p1, p2, o1, o2, vectors, base, vec, total, own, sems, row_sems):
    width = vectors.shape[1]
    piece_blocks, block_size, _ = base.shape
    copies = [
        pltpu.make_async_copy(
            source, vec.at[side, :, :, pl.ds(step * width, width)], sems.at[2 * side + step]
        )
        for side, step, source in ((0, 0, p1), (0, 1, p2), (1, 0, o1), (1, 1, o2))
    ]
    copies.append(pltpu.make_async_copy(vectors, own, sems.at[4]))
    for copy in copies:
        copy.start()
    copies[-1].wait()

    @pl.loop(0, piece_blocks)
    def _(b):
        at = pl.ds(pl.multiple_of(b * block_size, block_size), block_size)
        value = own[at, :].astype(jnp.float32)
        total[b, :, :width] = -center_value * value
        total[b, :, width:] = -value

    for copy in copies[:-1]:
        copy.wait()
    add_products(plan, HEAD, 0, blocks, (vec.at[0], vec.at[1]), total)

    def put(b):
        return pltpu.make_async_copy(total.at[b, :, pl.ds(0, width)], base.at[b], row_sems.at[b])

    @pl.loop(0, piece_blocks)
    def _(b):
        first = (total[b, :, :width] / half_width).astype(jnp.bfloat16).astype(jnp.float32)
        second = total[b, :, width:] - center_value * first
        second = second.astype(jnp.bfloat16).astype(jnp.float32)
        total[b, :, :width] = -center_value * second - first
        put(b).start()

    @pl.loop(0, piece_blocks)
    def _(b):
        put(b).wait()


def last_kernel(plan, blocks, pieces, others, base, out, start, total, own, base_sem, row_sems):
    piece_blocks, block_size, _ = base.shape
    base_copy = pltpu.make_async_copy(base, start, base_sem)
    base_copy.start()

    @pl.loop(0, piece_blocks)
    def _(b):
        total[b] = jnp.zeros(total.shape[1:], jnp.float32)

    add_products(plan, HEAD, 0, blocks, (pieces, others), total)
    base_copy.wait()

    def put(b):
        at = pl.ds(pl.multiple_of(b * block_size, block_size), block_size)
        return pltpu.make_async_copy(own.at[at], out.at[at], row_sems.at[b])

    @pl.loop(0, piece_blocks)
    def _(b):
        at = pl.ds(pl.multiple_of(b * block_size, block_size), block_size)
        own[at, :] = (total[b] + start[b]).astype(jnp.bfloat16)
        put(b).start()

    @pl.loop(0, piece_blocks)
    def _(b):
        put(b).wait()


def after(value, *others):
    return lax.optimization_barrier((value, *others))[0]


def call(kernel, out, args, spaces, scratch, mib, name, estimate=None):
    args = [
        pltpu.with_memory_space_constraint(arg, space) if space in (VMEM, HBM) or tied else arg
        for arg, (space, tied) in zip(args, spaces)
    ]
    shape, dtype, out_space = out
    return pl.pallas_call(
        kernel,
        out_shape=out_space(shape, dtype),
        in_specs=[spec(space) for space, _ in spaces],
        out_specs=spec(out_space),
        scratch_shapes=scratch,
        compiler_params=params(mib),
        cost_estimate=estimate,
        name=name,
    )(*args)


HERE = (VMEM, True)
FAR = (HBM, True)
LIST = (SMEM, True)
SCALARS = (SMEM, False)
ANYWHERE = (pl.ANY, False)


def on_pair(vectors, tile_blocks, block_rows, block_cols, counts):
    n_row = lax.axis_size("row")
    tile = tile_blocks[0, 0]
    slot_rows = block_rows[0, 0]
    slot_cols = block_cols[0, 0]
    used = counts[0]
    slot_count, block_size, _ = tile.shape
    width = vectors.shape[1]
    piece_blocks = vectors.shape[0] // block_size
    place = jnp.stack([lax.axis_index("row"), lax.axis_index("col")]).astype(jnp.int32)

    across = functools.partial(lax.ppermute, axis_name="col", perm=[(0, 1), (1, 0)])
    meta = across(jnp.concatenate([slot_rows, slot_cols, used]))

    needed = jnp.max(
        jnp.where(
            slot_cols[None, :] // piece_blocks == jnp.arange(n_row)[:, None],
            slot_cols[None, :] % piece_blocks,
            0,
        ),
        axis=1,
        keepdims=True,
    )
    exchange = functools.partial(
        lax.all_to_all, axis_name="row", split_axis=0, concat_axis=0, tiled=True
    )
    wanted = after(exchange(jnp.broadcast_to(needed, (n_row, LANES))), meta, place)
    sent_shape = (n_row, block_size, width)
    sent = call(
        functools.partial(pick_kernel, n_row, block_size),
        (sent_shape, jnp.bfloat16, HBM),
        (wanted, vectors),
        (SCALARS, FAR),
        [VMEM(sent_shape, jnp.bfloat16), DMA((n_row,)), DMA((n_row,))],
        2,
        "pick",
    )
    tile_other = across(after(tile, sent))

    capacity = 2 * round_up(slot_count, UNROLL)
    sent_at = HEAD + 3 * (capacity + 1)
    load_at = sent_at + 3 * (2 * n_row * n_row + 2 * UNROLL + 1)
    plan_size = load_at + 2 * slot_count + 1
    plan = call(
        functools.partial(plan_kernel, n_row, piece_blocks, sent_at, load_at),
        ((plan_size,), jnp.int32, SMEM),
        (place, wanted, slot_rows, slot_cols, used, meta),
        (SCALARS,) * 6,
        [],
        2,
        "plan",
    )
    def load(base, stride, ends, cue):
        return call(
            functools.partial(load_kernel, base, stride, ends),
            ((capacity, block_size, block_size), jnp.bfloat16, VMEM),
            (after(plan, cue), tile, tile_other),
            (LIST, FAR, ANYWHERE),
            [DMA((capacity,))],
            2,
            "load",
        )

    def cost(products, rows):
        size = block_size * width
        return pl.CostEstimate(
            flops=2 * products * block_size * size,
            bytes_accessed=2 * (products * block_size * block_size + 3 * rows * size),
            transcendentals=0,
        )

    def sent_blocks(blocks, *args):
        first = len(args) == 3
        held = [VMEM(sent_shape, jnp.bfloat16), DMA]
        staged = [] if first else [VMEM(sent_shape, jnp.bfloat16), DMA((n_row,))]
        return call(
            functools.partial(sent_kernel, first, sent_at),
            (sent_shape, jnp.bfloat16, VMEM if first else HBM),
            (plan, blocks, *args),
            (LIST, HERE, HERE, HERE, FAR) + (HERE,) * (len(args) - 3),
            [VMEM((n_row + 1, block_size, width), jnp.float32)] + held + staged,
            4,
            "sent",
            cost(n_row, n_row),
        )

    base_shape = (piece_blocks, block_size, width)

    def early(blocks, *pieces):
        return call(
            early_kernel,
            (base_shape, jnp.float32, HBM),
            (plan, blocks, *pieces, vectors),
            (LIST,) + (HERE,) * 5 + (FAR,),
            [
                VMEM((2, n_row, block_size, 2 * width), jnp.bfloat16),
                VMEM((piece_blocks + 1, block_size, 2 * width), jnp.float32),
                VMEM(vectors.shape, jnp.bfloat16),
                DMA((5,)),
                DMA((piece_blocks,)),
            ],
            18,
            "early",
            cost(2 * slot_count, 2 * piece_blocks),
        )

    def last(blocks, *args):
        return call(
            last_kernel,
            (vectors.shape, jnp.bfloat16, HBM),
            (plan, blocks, *args),
            (LIST,) + (HERE,) * 3 + (FAR,),
            [
                VMEM(base_shape, jnp.float32),
                VMEM((piece_blocks + 1, block_size, width), jnp.float32),
                VMEM(vectors.shape, jnp.bfloat16),
                DMA,
                DMA((piece_blocks,)),
            ],
            14,
            "last",
            cost(slot_count, piece_blocks),
        )

    p1 = after(exchange(sent), plan)
    o1 = across(p1)
    blocks = load(load_at, 1, 4, p1)
    first_sent = sent_blocks(blocks, p1, o1, sent)
    p2 = exchange(first_sent)
    o2 = across(p2)
    second_sent = sent_blocks(blocks, p2, o2, sent, first_sent)
    base = early(load(HEAD, 3, 0, second_sent), p1, p2, o1, o2)
    p3 = after(exchange(second_sent), base)
    return last(load(HEAD, 3, 0, p3), p3, across(p3), base)


def on_any(vectors, tile_blocks, block_rows, block_cols, counts):
    n_row = lax.axis_size("row")
    n_col = lax.axis_size("col")
    tile_data = tile_blocks[0, 0]
    slot_rows = block_rows[0, 0]
    slot_cols = block_cols[0, 0]
    used = counts[0, 0]
    block_size = tile_data.shape[-1]
    width = vectors.shape[1]
    piece_blocks = vectors.shape[0] // block_size
    row_blocks = piece_blocks * n_col
    slot_count = tile_data.shape[0]
    live = (jnp.arange(slot_count) < used).astype(jnp.float32)
    onehot = (slot_rows[None, :] == jnp.arange(row_blocks)[:, None]).astype(jnp.float32) * live[
        None, :
    ]
    source_piece = slot_cols // piece_blocks
    offset = slot_cols % piece_blocks
    needed = jnp.max(
        jnp.where(source_piece[None, :] == jnp.arange(n_row)[:, None], offset[None, :], 0), axis=1
    )
    wanted = lax.all_to_all(
        needed.reshape(n_row, 1), "row", split_axis=0, concat_axis=0, tiled=True
    ).reshape(n_row)

    def apply_tiles(current):
        own_blocks = current.reshape(piece_blocks, block_size, width)
        outgoing = jnp.take(own_blocks, wanted, axis=0)
        received = lax.all_to_all(outgoing, "row", split_axis=0, concat_axis=0, tiled=True)
        vec_blocks = jnp.take(received, source_piece, axis=0)
        products = jnp.einsum(
            "sij,sjk->sik", tile_data, vec_blocks, preferred_element_type=jnp.float32
        )
        term = jnp.einsum("ls,sik->lik", onehot, products, precision=lax.Precision.HIGHEST)
        term = term.reshape(row_blocks * block_size, width)
        return lax.psum_scatter(
            term.astype(jnp.bfloat16), "col", scatter_dimension=0, tiled=True
        ).astype(jnp.float32)

    previous = vectors
    applied = apply_tiles(vectors)
    current = ((applied - center_value * previous.astype(jnp.float32)) / half_width).astype(
        jnp.bfloat16
    )
    for repeat in range(DEGREE - 1):
        applied = apply_tiles(current)
        following = (
            2.0 * (applied - center_value * current.astype(jnp.float32)) / half_width
            - previous.astype(jnp.float32)
        ).astype(jnp.bfloat16)
        previous, current = (current, following)
    return current


def solution(mesh):
    n_row, n_col = mesh.shape["row"], mesh.shape["col"]
    paired = n_col == 2 and n_row & (n_row - 1) == 0
    return jax.shard_map(
        on_pair if paired else on_any,
        mesh=mesh,
        in_specs=(
            P(("row", "col"), "vec"),
            P("row", "col", None, None, None),
            P("row", "col", None),
            P("row", "col", None),
            P("row", "col"),
        ),
        out_specs=P(("row", "col"), "vec"),
        check_vma=False,
    )
```

```python
import functools

import jax
import jax.numpy as jnp
from jax import lax
from jax.experimental import pallas as pl
from jax.experimental.pallas import tpu as pltpu
from jax.sharding import PartitionSpec as P

DEGREE = 3

center_value = 0.5
half_width = 2.0

VMEM = pltpu.VMEM
SMEM = pltpu.SMEM
HBM = pltpu.HBM
DMA = pltpu.SemaphoreType.DMA
LANES = 128
UNROLL = 2
HEAD = 8
STRIDE = 4
FIRST = 1
LAST = 2


def spec(space):
    return pl.BlockSpec(memory_space=space)


def params(mib):
    return pltpu.CompilerParams(vmem_limit_bytes=mib * 1024 * 1024)


def round_up(n, step):
    return (n + step - 1) // step * step


def plan_kernel(
    n_row, piece_blocks, sent_at, load_at, bare_at, place, wanted, rows_a, cols_a, used_a, meta_b, out, seen
):
    slot_count = rows_a.shape[0]
    first_row = place[1] * piece_blocks

    def scan(row_of, col_of, used, at, sent, load):
        def step(s, carry):
            at, sent, load = carry
            row = row_of(s) - first_row
            inside = (row >= 0) & (row < piece_blocks)
            mine = inside.astype(jnp.int32)
            piece = col_of(s) // piece_blocks
            kept = jnp.where(inside, row, piece_blocks)
            entry = HEAD + STRIDE * at
            out[entry] = s
            out[entry + 1] = row
            out[entry + 2] = piece
            out[entry + 3] = jnp.where(seen[kept] == 0, FIRST, 0)
            seen[kept] = entry
            out[load_at + load] = s
            before = sent
            for k in range(n_row):
                out[sent_at + STRIDE * sent] = load
                out[sent_at + STRIDE * sent + 1] = k
                out[sent_at + STRIDE * sent + 2] = piece
                sent = sent + jnp.where(wanted[k, 0] == row, mine, 0)
            return at + mine, sent, load + (sent > before).astype(jnp.int32)

        at, sent, load = lax.fori_loop(0, used, step, (at, sent, load))
        for _ in range(UNROLL):
            for base, end, spare in ((HEAD, at, piece_blocks), (sent_at, sent, n_row)):
                entry = base + STRIDE * end
                out[entry] = 0
                out[entry + 1] = spare
                out[entry + 2] = 0
                out[entry + 3] = 0
            at = at + jnp.where(at % UNROLL == 0, 0, 1)
            sent = sent + jnp.where(sent % UNROLL == 0, 0, 1)
        return at, sent, load

    for b in range(piece_blocks + 1):
        seen[b] = 0
    zero = jnp.int32(0)
    at, sent, load = scan(
        lambda s: rows_a[s], lambda s: cols_a[s], used_a[0], zero, zero, zero
    )
    out[0] = at
    out[2] = sent
    out[4] = load
    at, sent, load = scan(
        lambda s: meta_b[s],
        lambda s: meta_b[slot_count + s],
        meta_b[2 * slot_count],
        at,
        sent,
        load,
    )
    out[1] = at
    out[3] = sent
    out[5] = load

    def close(b, bare):
        entry = seen[b]
        out[bare_at + bare] = b

        @pl.when(entry > 0)
        def _():
            out[entry + 3] = out[entry + 3] + LAST

        return bare + jnp.where(entry == 0, 1, 0)

    out[6] = lax.fori_loop(0, piece_blocks, close, zero)


def pick_kernel(n_row, block_size, wanted, vectors, out, held, in_sems, out_sems):
    def fetch(k):
        at = pl.multiple_of(wanted[k, 0] * block_size, block_size)
        return pltpu.make_async_copy(vectors.at[pl.ds(at, block_size)], held.at[k], in_sems.at[k])

    def put(k):
        return pltpu.make_async_copy(held.at[k], out.at[k], out_sems.at[k])

    for k in range(n_row):
        fetch(k).start()
    for k in range(n_row):
        fetch(k).wait()
        put(k).start()
    for k in range(n_row):
        put(k).wait()


def load_kernel(base, stride, ends, plan, tile_a, tile_b, blocks, sems):
    mid, end = plan[ends], plan[ends + 1]

    def copy(tile, i):
        slot = plan[base + stride * i]
        return pltpu.make_async_copy(tile.at[slot], blocks.at[i], sems.at[i])

    @pl.loop(0, mid)
    def _(i):
        copy(tile_a, i).start()

    @pl.loop(mid, end)
    def _(i):
        copy(tile_b, i).start()

    @pl.loop(0, end)
    def _(i):
        copy(tile_a, i).wait()


def each_product(plan, base, ends, blocks, pieces, use):
    mid, end = plan[ends], plan[ends + 1]

    def run(piece_ref, begin, end):
        @pl.loop(begin // UNROLL, end // UNROLL)
        def _(j):
            for u in range(UNROLL):
                i = UNROLL * j + u
                entry = base + STRIDE * i
                block = blocks[i if base == HEAD else plan[entry]]
                use(
                    entry,
                    jnp.dot(block, piece_ref[plan[entry + 2]], preferred_element_type=jnp.float32),
                )

    run(pieces[0], 0, mid)
    run(pieces[1], mid, end)


def add_products(plan, base, ends, blocks, pieces, total):
    def use(entry, value):
        total[plan[entry + 1]] += value

    each_product(plan, base, ends, blocks, pieces, use)


def sent_kernel(first, sent_at, plan, blocks, pieces, others, picked, *rest):
    if first:
        out, total, held, held_sem = rest
    else:
        current, out, total, held, held_sem, ready, out_sems = rest
    n_row = out.shape[0]
    copy = pltpu.make_async_copy(picked, held, held_sem)
    copy.start()
    for k in range(n_row):
        if first:
            total[k] = jnp.zeros(total.shape[1:], jnp.float32)
        else:
            total[k] = -center_value * current[k].astype(jnp.float32)
    add_products(plan, sent_at, 2, blocks, (pieces, others), total)
    copy.wait()
    if first:
        for k in range(n_row):
            value = total[k] - center_value * held[k].astype(jnp.float32)
            out[k] = (value / half_width).astype(jnp.bfloat16)
        return

    def put(k):
        return pltpu.make_async_copy(ready.at[k], out.at[k], out_sems.at[k])

    for k in range(n_row):
        ready[k] = (total[k] - held[k].astype(jnp.float32)).astype(jnp.bfloat16)
        put(k).start()
    for k in range(n_row):
        put(k).wait()


def early_kernel(plan, blocks, p1, p2, o1, o2, vectors, base, vec, total, own, sems):
    width = vectors.shape[1]
    piece_blocks, block_size, _ = base.shape
    copies = [
        pltpu.make_async_copy(
            source, vec.at[side, :, :, pl.ds(step * width, width)], sems.at[2 * side + step]
        )
        for side, step, source in ((0, 0, p1), (0, 1, p2), (1, 0, o1), (1, 1, o2))
    ]
    copies.append(pltpu.make_async_copy(vectors, own, sems.at[4]))
    for copy in copies:
        copy.start()
    copies[-1].wait()

    @pl.loop(0, piece_blocks)
    def _(b):
        at = pl.ds(pl.multiple_of(b * block_size, block_size), block_size)
        value = own[at, :].astype(jnp.float32)
        total[b, :, :width] = -center_value * value
        total[b, :, width:] = -value

    for copy in copies[:-1]:
        copy.wait()
    add_products(plan, HEAD, 0, blocks, (vec.at[0], vec.at[1]), total)

    @pl.loop(0, piece_blocks)
    def _(b):
        first = (total[b, :, :width] / half_width).astype(jnp.bfloat16).astype(jnp.float32)
        second = total[b, :, width:] - center_value * first
        second = second.astype(jnp.bfloat16).astype(jnp.float32)
        base[b] = (-center_value * second - first).astype(jnp.bfloat16)


def last_kernel(bare_at, plan, blocks, pieces, others, base, out, total, own, row_sems):
    piece_blocks = base.shape[0]

    def put(source, b):
        return pltpu.make_async_copy(source.at[b], out.at[b], row_sems.at[b])

    @pl.loop(0, plan[6])
    def _(i):
        b = plan[bare_at + i]
        put(base, b).start()

    def use(entry, value):
        row = plan[entry + 1]
        marks = plan[entry + 3]
        start = base[jnp.minimum(row, piece_blocks - 1)].astype(jnp.float32)
        value = jnp.where(lax.rem(marks, LAST) == FIRST, start, total[row]) + value
        total[row] = value
        own[row] = value.astype(jnp.bfloat16)

        @pl.when(marks >= LAST)
        def _():
            put(own, row).start()

    each_product(plan, HEAD, 0, blocks, (pieces, others), use)

    @pl.loop(0, piece_blocks)
    def _(b):
        put(own, b).wait()


def after(value, *others):
    return lax.optimization_barrier((value, *others))[0]


def call(kernel, out, args, spaces, scratch, mib, name, estimate=None):
    args = [
        pltpu.with_memory_space_constraint(arg, space) if space in (VMEM, HBM) or tied else arg
        for arg, (space, tied) in zip(args, spaces)
    ]
    shape, dtype, out_space = out
    return pl.pallas_call(
        kernel,
        out_shape=out_space(shape, dtype),
        in_specs=[spec(space) for space, _ in spaces],
        out_specs=spec(out_space),
        scratch_shapes=scratch,
        compiler_params=params(mib),
        cost_estimate=estimate,
        name=name,
    )(*args)


HERE = (VMEM, True)
FAR = (HBM, True)
LIST = (SMEM, True)
SCALARS = (SMEM, False)
ANYWHERE = (pl.ANY, False)


def on_pair(vectors, tile_blocks, block_rows, block_cols, counts):
    n_row = lax.axis_size("row")
    tile = tile_blocks[0, 0]
    slot_rows = block_rows[0, 0]
    slot_cols = block_cols[0, 0]
    used = counts[0]
    slot_count, block_size, _ = tile.shape
    width = vectors.shape[1]
    piece_blocks = vectors.shape[0] // block_size
    place = jnp.stack([lax.axis_index("row"), lax.axis_index("col")]).astype(jnp.int32)

    across = functools.partial(lax.ppermute, axis_name="col", perm=[(0, 1), (1, 0)])

    needed = jnp.max(
        jnp.where(
            slot_cols[None, :] // piece_blocks == jnp.arange(n_row)[:, None],
            slot_cols[None, :] % piece_blocks,
            0,
        ),
        axis=1,
        keepdims=True,
    )
    exchange = functools.partial(
        lax.all_to_all, axis_name="row", split_axis=0, concat_axis=0, tiled=True
    )
    wanted = exchange(jnp.broadcast_to(needed, (n_row, LANES)))
    sent_shape = (n_row, block_size, width)
    sent = call(
        functools.partial(pick_kernel, n_row, block_size),
        (sent_shape, jnp.bfloat16, HBM),
        (wanted, vectors),
        (SCALARS, FAR),
        [VMEM(sent_shape, jnp.bfloat16), DMA((n_row,)), DMA((n_row,))],
        2,
        "pick",
    )
    tile_other = across(after(tile, sent))
    meta = across(after(jnp.concatenate([slot_rows, slot_cols, used]), sent))

    capacity = 2 * round_up(slot_count, UNROLL)
    sent_at = HEAD + STRIDE * (capacity + 1)
    load_at = sent_at + STRIDE * (2 * n_row * n_row + 2 * UNROLL + 1)
    bare_at = load_at + 2 * slot_count + 1
    plan_size = bare_at + piece_blocks
    plan = call(
        functools.partial(plan_kernel, n_row, piece_blocks, sent_at, load_at, bare_at),
        ((plan_size,), jnp.int32, SMEM),
        (place, wanted, slot_rows, slot_cols, used, meta),
        (SCALARS,) * 6,
        [SMEM((piece_blocks + 1,), jnp.int32)],
        2,
        "plan",
    )
    def load(base, stride, ends, cue):
        return call(
            functools.partial(load_kernel, base, stride, ends),
            ((capacity, block_size, block_size), jnp.bfloat16, VMEM),
            (after(plan, cue), tile, tile_other),
            (LIST, FAR, ANYWHERE),
            [DMA((capacity,))],
            2,
            "load",
        )

    def cost(products, rows):
        size = block_size * width
        return pl.CostEstimate(
            flops=2 * products * block_size * size,
            bytes_accessed=2 * (products * block_size * block_size + 3 * rows * size),
            transcendentals=0,
        )

    def sent_blocks(blocks, *args):
        first = len(args) == 3
        held = [VMEM(sent_shape, jnp.bfloat16), DMA]
        staged = [] if first else [VMEM(sent_shape, jnp.bfloat16), DMA((n_row,))]
        return call(
            functools.partial(sent_kernel, first, sent_at),
            (sent_shape, jnp.bfloat16, VMEM if first else HBM),
            (plan, blocks, *args),
            (LIST, HERE, HERE, HERE, FAR) + (HERE,) * (len(args) - 3),
            [VMEM((n_row + 1, block_size, width), jnp.float32)] + held + staged,
            4,
            "sent",
            cost(n_row, n_row),
        )

    base_shape = (piece_blocks, block_size, width)

    def early(blocks, *pieces):
        return call(
            early_kernel,
            (base_shape, jnp.bfloat16, VMEM),
            (plan, blocks, *pieces, vectors),
            (LIST,) + (HERE,) * 5 + (FAR,),
            [
                VMEM((2, n_row, block_size, 2 * width), jnp.bfloat16),
                VMEM((piece_blocks + 1, block_size, 2 * width), jnp.float32),
                VMEM(vectors.shape, jnp.bfloat16),
                DMA((5,)),
            ],
            18,
            "early",
            cost(2 * slot_count, 2 * piece_blocks),
        )

    def last(blocks, *args):
        rows = (piece_blocks + 1, block_size, width)
        out = call(
            functools.partial(last_kernel, bare_at),
            (base_shape, jnp.bfloat16, HBM),
            (plan, blocks, *args),
            (LIST,) + (HERE,) * 4,
            [VMEM(rows, jnp.float32), VMEM(rows, jnp.bfloat16), DMA((piece_blocks,))],
            8,
            "last",
            cost(slot_count, piece_blocks),
        )
        return out.reshape(vectors.shape)

    p1 = after(exchange(sent), plan)
    o1 = across(p1)
    blocks = load(load_at, 1, 4, p1)
    first_sent = sent_blocks(blocks, p1, o1, sent)
    p2 = exchange(first_sent)
    o2 = across(p2)
    second_sent = sent_blocks(blocks, p2, o2, sent, first_sent)
    base = early(load(HEAD, STRIDE, 0, second_sent), p1, p2, o1, o2)
    p3 = after(exchange(second_sent), base)
    return last(load(HEAD, STRIDE, 0, p3), p3, across(p3), base)


def on_any(vectors, tile_blocks, block_rows, block_cols, counts):
    n_row = lax.axis_size("row")
    n_col = lax.axis_size("col")
    tile_data = tile_blocks[0, 0]
    slot_rows = block_rows[0, 0]
    slot_cols = block_cols[0, 0]
    used = counts[0, 0]
    block_size = tile_data.shape[-1]
    width = vectors.shape[1]
    piece_blocks = vectors.shape[0] // block_size
    row_blocks = piece_blocks * n_col
    slot_count = tile_data.shape[0]
    live = (jnp.arange(slot_count) < used).astype(jnp.float32)
    onehot = (slot_rows[None, :] == jnp.arange(row_blocks)[:, None]).astype(jnp.float32) * live[
        None, :
    ]
    source_piece = slot_cols // piece_blocks
    offset = slot_cols % piece_blocks
    needed = jnp.max(
        jnp.where(source_piece[None, :] == jnp.arange(n_row)[:, None], offset[None, :], 0), axis=1
    )
    wanted = lax.all_to_all(
        needed.reshape(n_row, 1), "row", split_axis=0, concat_axis=0, tiled=True
    ).reshape(n_row)

    def apply_tiles(current):
        own_blocks = current.reshape(piece_blocks, block_size, width)
        outgoing = jnp.take(own_blocks, wanted, axis=0)
        received = lax.all_to_all(outgoing, "row", split_axis=0, concat_axis=0, tiled=True)
        vec_blocks = jnp.take(received, source_piece, axis=0)
        products = jnp.einsum(
            "sij,sjk->sik", tile_data, vec_blocks, preferred_element_type=jnp.float32
        )
        term = jnp.einsum("ls,sik->lik", onehot, products, precision=lax.Precision.HIGHEST)
        term = term.reshape(row_blocks * block_size, width)
        return lax.psum_scatter(
            term.astype(jnp.bfloat16), "col", scatter_dimension=0, tiled=True
        ).astype(jnp.float32)

    previous = vectors
    applied = apply_tiles(vectors)
    current = ((applied - center_value * previous.astype(jnp.float32)) / half_width).astype(
        jnp.bfloat16
    )
    for repeat in range(DEGREE - 1):
        applied = apply_tiles(current)
        following = (
            2.0 * (applied - center_value * current.astype(jnp.float32)) / half_width
            - previous.astype(jnp.float32)
        ).astype(jnp.bfloat16)
        previous, current = (current, following)
    return current


def solution(mesh):
    n_row, n_col = mesh.shape["row"], mesh.shape["col"]
    paired = n_col == 2 and n_row & (n_row - 1) == 0
    return jax.shard_map(
        on_pair if paired else on_any,
        mesh=mesh,
        in_specs=(
            P(("row", "col"), "vec"),
            P("row", "col", None, None, None),
            P("row", "col", None),
            P("row", "col", None),
            P("row", "col"),
        ),
        out_specs=P(("row", "col"), "vec"),
        check_vma=False,
    )
```

```python
import functools

import jax
import jax.numpy as jnp
from jax import lax
from jax.experimental import pallas as pl
from jax.experimental.pallas import tpu as pltpu
from jax.sharding import PartitionSpec as P

DEGREE = 3

center_value = 0.5
half_width = 2.0

VMEM = pltpu.VMEM
SMEM = pltpu.SMEM
HBM = pltpu.HBM
DMA = pltpu.SemaphoreType.DMA
LANES = 128
UNROLL = 2
HEAD = 8
STRIDE = 4
FIRST = 1
LAST = 2


def spec(space):
    return pl.BlockSpec(memory_space=space)


def params(mib):
    return pltpu.CompilerParams(vmem_limit_bytes=mib * 1024 * 1024)


def round_up(n, step):
    return (n + step - 1) // step * step


def plan_kernel(
    n_row, piece_blocks, sent_at, load_at, bare_at, place, wanted, rows_a, cols_a, used_a, meta_b, out, seen
):
    slot_count = rows_a.shape[0]
    first_row = place[1] * piece_blocks

    def scan(row_of, col_of, used, at, sent, load):
        def step(s, carry):
            at, sent, load = carry
            row = row_of(s) - first_row
            inside = (row >= 0) & (row < piece_blocks)
            mine = inside.astype(jnp.int32)
            piece = col_of(s) // piece_blocks
            kept = jnp.where(inside, row, piece_blocks)
            entry = HEAD + STRIDE * at
            out[entry] = s
            out[entry + 1] = row
            out[entry + 2] = piece
            out[entry + 3] = jnp.where(seen[kept] == 0, FIRST, 0)
            seen[kept] = entry
            out[load_at + load] = s
            before = sent
            for k in range(n_row):
                out[sent_at + STRIDE * sent] = load
                out[sent_at + STRIDE * sent + 1] = k
                out[sent_at + STRIDE * sent + 2] = piece
                sent = sent + jnp.where(wanted[k, 0] == row, mine, 0)
            return at + mine, sent, load + (sent > before).astype(jnp.int32)

        at, sent, load = lax.fori_loop(0, used, step, (at, sent, load))
        for _ in range(UNROLL):
            for base, end, spare in ((HEAD, at, piece_blocks), (sent_at, sent, n_row)):
                entry = base + STRIDE * end
                out[entry] = 0
                out[entry + 1] = spare
                out[entry + 2] = 0
                out[entry + 3] = 0
            at = at + jnp.where(at % UNROLL == 0, 0, 1)
            sent = sent + jnp.where(sent % UNROLL == 0, 0, 1)
        return at, sent, load

    for b in range(piece_blocks + 1):
        seen[b] = 0
    zero = jnp.int32(0)
    at, sent, load = scan(
        lambda s: rows_a[s], lambda s: cols_a[s], used_a[0], zero, zero, zero
    )
    out[0] = at
    out[2] = sent
    out[4] = load
    at, sent, load = scan(
        lambda s: meta_b[s],
        lambda s: meta_b[slot_count + s],
        meta_b[2 * slot_count],
        at,
        sent,
        load,
    )
    out[1] = at
    out[3] = sent
    out[5] = load

    def close(b, bare):
        entry = seen[b]
        out[bare_at + bare] = b

        @pl.when(entry > 0)
        def _():
            out[entry + 3] = out[entry + 3] + LAST

        return bare + jnp.where(entry == 0, 1, 0)

    out[6] = lax.fori_loop(0, piece_blocks, close, zero)


def pick_kernel(n_row, block_size, wanted, vectors, out, held, in_sems, out_sems):
    def fetch(k):
        at = pl.multiple_of(wanted[k, 0] * block_size, block_size)
        return pltpu.make_async_copy(vectors.at[pl.ds(at, block_size)], held.at[k], in_sems.at[k])

    def put(k):
        return pltpu.make_async_copy(held.at[k], out.at[k], out_sems.at[k])

    for k in range(n_row):
        fetch(k).start()
    for k in range(n_row):
        fetch(k).wait()
        put(k).start()
    for k in range(n_row):
        put(k).wait()


def load_kernel(base, stride, ends, plan, tile_a, tile_b, blocks, sems):
    mid, end = plan[ends], plan[ends + 1]

    def copy(tile, i):
        slot = plan[base + stride * i]
        return pltpu.make_async_copy(tile.at[slot], blocks.at[i], sems.at[i])

    @pl.loop(0, mid)
    def _(i):
        copy(tile_a, i).start()

    @pl.loop(mid, end)
    def _(i):
        copy(tile_b, i).start()

    @pl.loop(0, end)
    def _(i):
        copy(tile_a, i).wait()


def load_both_kernel(base, stride, ends, plan, tile_a, tile_b, array, blocks, held, sems, held_sem):
    copy = pltpu.make_async_copy(array, held, held_sem)
    copy.start()
    load_kernel(base, stride, ends, plan, tile_a, tile_b, blocks, sems)
    copy.wait()


def each_product(plan, base, ends, blocks, pieces, use, then=None):
    mid, end = plan[ends], plan[ends + 1]

    def run(piece_ref, begin, end):
        @pl.loop(begin // UNROLL, end // UNROLL)
        def _(j):
            for u in range(UNROLL):
                i = UNROLL * j + u
                entry = base + STRIDE * i
                block = blocks[i if base == HEAD else plan[entry]]
                use(
                    entry,
                    jnp.dot(block, piece_ref[plan[entry + 2]], preferred_element_type=jnp.float32),
                )
            if then is not None:
                for u in range(UNROLL):
                    then(base + STRIDE * (UNROLL * j + u))

    run(pieces[0], 0, mid)
    run(pieces[1], mid, end)


def add_products(plan, base, ends, blocks, pieces, total):
    def use(entry, value):
        total[plan[entry + 1]] += value

    each_product(plan, base, ends, blocks, pieces, use)


def sent_kernel(first, sent_at, plan, blocks, pieces, others, picked, *rest):
    if first:
        out, total, held, held_sem = rest
    else:
        current, out, total, held, held_sem, ready, out_sems = rest
    n_row = out.shape[0]
    copy = pltpu.make_async_copy(picked, held, held_sem)
    copy.start()
    for k in range(n_row):
        if first:
            total[k] = jnp.zeros(total.shape[1:], jnp.float32)
        else:
            total[k] = -center_value * current[k].astype(jnp.float32)
    add_products(plan, sent_at, 2, blocks, (pieces, others), total)
    copy.wait()
    if first:
        for k in range(n_row):
            value = total[k] - center_value * held[k].astype(jnp.float32)
            out[k] = (value / half_width).astype(jnp.bfloat16)
        return

    def put(k):
        return pltpu.make_async_copy(ready.at[k], out.at[k], out_sems.at[k])

    for k in range(n_row):
        ready[k] = (total[k] - held[k].astype(jnp.float32)).astype(jnp.bfloat16)
        put(k).start()
    for k in range(n_row):
        put(k).wait()


def early_kernel(plan, blocks, p1, p2, o1, o2, vectors, base, vec, total, own, sems, row_sems):
    width = vectors.shape[1]
    piece_blocks, block_size, _ = base.shape
    copies = [
        pltpu.make_async_copy(
            source, vec.at[side, :, :, pl.ds(step * width, width)], sems.at[2 * side + step]
        )
        for side, step, source in ((0, 0, p1), (0, 1, p2), (1, 0, o1), (1, 1, o2))
    ]
    copies.append(pltpu.make_async_copy(vectors, own, sems.at[4]))
    for copy in copies:
        copy.start()
    copies[-1].wait()

    def rows(b):
        return pl.ds(pl.multiple_of(b * block_size, block_size), block_size)

    def put(b):
        return pltpu.make_async_copy(own.at[rows(b)], base.at[b], row_sems.at[b])

    @pl.loop(0, piece_blocks)
    def _(b):
        value = own[rows(b), :].astype(jnp.float32)
        total[b, :, :width] = -center_value * value
        total[b, :, width:] = -value

    for copy in copies[:-1]:
        copy.wait()
    add_products(plan, HEAD, 0, blocks, (vec.at[0], vec.at[1]), total)

    @pl.loop(0, piece_blocks)
    def _(b):
        first = (total[b, :, :width] / half_width).astype(jnp.bfloat16).astype(jnp.float32)
        second = total[b, :, width:] - center_value * first
        second = second.astype(jnp.bfloat16).astype(jnp.float32)
        own[rows(b), :] = (-center_value * second - first).astype(jnp.bfloat16)
        put(b).start()

    @pl.loop(0, piece_blocks)
    def _(b):
        put(b).wait()


def last_kernel(bare_at, plan, blocks, pieces, others, base, out, total, own, row_sems):
    piece_blocks = base.shape[0]

    def put(source, b):
        return pltpu.make_async_copy(source.at[b], out.at[b], row_sems.at[b])

    @pl.loop(0, plan[6])
    def _(i):
        b = plan[bare_at + i]
        put(base, b).start()

    def use(entry, value):
        row = plan[entry + 1]
        marks = plan[entry + 3]
        start = base[jnp.minimum(row, piece_blocks - 1)].astype(jnp.float32)
        value = jnp.where(lax.rem(marks, LAST) == FIRST, start, total[row]) + value
        total[row] = value
        own[row] = value.astype(jnp.bfloat16)

    def then(entry):
        @pl.when(plan[entry + 3] >= LAST)
        def _():
            put(own, plan[entry + 1]).start()

    each_product(plan, HEAD, 0, blocks, (pieces, others), use, then)

    @pl.loop(0, piece_blocks)
    def _(b):
        put(own, b).wait()


def after(value, *others):
    return lax.optimization_barrier((value, *others))[0]


def call(kernel, out, args, spaces, scratch, mib, name, estimate=None):
    args = [
        pltpu.with_memory_space_constraint(arg, space) if space in (VMEM, HBM) or tied else arg
        for arg, (space, tied) in zip(args, spaces)
    ]
    return pl.pallas_call(
        kernel,
        out_shape=[space(shape, dtype) for shape, dtype, space in out],
        in_specs=[spec(space) for space, _ in spaces],
        out_specs=[spec(space) for _, _, space in out],
        scratch_shapes=scratch,
        compiler_params=params(mib),
        cost_estimate=estimate,
        name=name,
    )(*args)


HERE = (VMEM, True)
FAR = (HBM, True)
LIST = (SMEM, True)
SCALARS = (SMEM, False)
ANYWHERE = (pl.ANY, False)


def on_pair(vectors, tile_blocks, block_rows, block_cols, counts):
    n_row = lax.axis_size("row")
    tile = tile_blocks[0, 0]
    slot_rows = block_rows[0, 0]
    slot_cols = block_cols[0, 0]
    used = counts[0]
    slot_count, block_size, _ = tile.shape
    width = vectors.shape[1]
    piece_blocks = vectors.shape[0] // block_size
    place = jnp.stack([lax.axis_index("row"), lax.axis_index("col")]).astype(jnp.int32)

    across = functools.partial(lax.ppermute, axis_name="col", perm=[(0, 1), (1, 0)])

    needed = jnp.max(
        jnp.where(
            slot_cols[None, :] // piece_blocks == jnp.arange(n_row)[:, None],
            slot_cols[None, :] % piece_blocks,
            0,
        ),
        axis=1,
        keepdims=True,
    )
    exchange = functools.partial(
        lax.all_to_all, axis_name="row", split_axis=0, concat_axis=0, tiled=True
    )
    wanted = exchange(jnp.broadcast_to(needed, (n_row, LANES)))
    sent_shape = (n_row, block_size, width)
    (sent,) = call(
        functools.partial(pick_kernel, n_row, block_size),
        [(sent_shape, jnp.bfloat16, HBM)],
        (wanted, vectors),
        (SCALARS, FAR),
        [VMEM(sent_shape, jnp.bfloat16), DMA((n_row,)), DMA((n_row,))],
        2,
        "pick",
    )
    tile_other = across(after(tile, sent))
    meta = across(after(jnp.concatenate([slot_rows, slot_cols, used]), sent))

    capacity = 2 * round_up(slot_count, UNROLL)
    sent_at = HEAD + STRIDE * (capacity + 1)
    load_at = sent_at + STRIDE * (2 * n_row * n_row + 2 * UNROLL + 1)
    bare_at = load_at + 2 * slot_count + 1
    plan_size = bare_at + piece_blocks
    (plan,) = call(
        functools.partial(plan_kernel, n_row, piece_blocks, sent_at, load_at, bare_at),
        [((plan_size,), jnp.int32, SMEM)],
        (place, wanted, slot_rows, slot_cols, used, meta),
        (SCALARS,) * 6,
        [SMEM((piece_blocks + 1,), jnp.int32)],
        2,
        "plan",
    )
    def load(base, stride, ends, cue, *array):
        kernel = load_both_kernel if array else load_kernel
        return call(
            functools.partial(kernel, base, stride, ends),
            [((capacity, block_size, block_size), jnp.bfloat16, VMEM)]
            + [(held.shape, held.dtype, VMEM) for held in array],
            (after(plan, cue), tile, tile_other, *array),
            (LIST, FAR, ANYWHERE) + (FAR,) * len(array),
            [DMA((capacity,))] + [DMA] * len(array),
            2,
            "load",
        )

    def cost(products, rows):
        size = block_size * width
        return pl.CostEstimate(
            flops=2 * products * block_size * size,
            bytes_accessed=2 * (products * block_size * block_size + 3 * rows * size),
            transcendentals=0,
        )

    def sent_blocks(blocks, *args):
        first = len(args) == 3
        held = [VMEM(sent_shape, jnp.bfloat16), DMA]
        staged = [] if first else [VMEM(sent_shape, jnp.bfloat16), DMA((n_row,))]
        return call(
            functools.partial(sent_kernel, first, sent_at),
            [(sent_shape, jnp.bfloat16, VMEM if first else HBM)],
            (plan, blocks, *args),
            (LIST, HERE, HERE, HERE, FAR) + (HERE,) * (len(args) - 3),
            [VMEM((n_row + 1, block_size, width), jnp.float32)] + held + staged,
            4,
            "sent",
            cost(n_row, n_row),
        )[0]

    base_shape = (piece_blocks, block_size, width)

    def early(blocks, *pieces):
        return call(
            early_kernel,
            [(base_shape, jnp.bfloat16, HBM)],
            (plan, blocks, *pieces, vectors),
            (LIST,) + (HERE,) * 5 + (FAR,),
            [
                VMEM((2, n_row, block_size, 2 * width), jnp.bfloat16),
                VMEM((piece_blocks + 1, block_size, 2 * width), jnp.float32),
                VMEM(vectors.shape, jnp.bfloat16),
                DMA((5,)),
                DMA((piece_blocks,)),
            ],
            18,
            "early",
            cost(2 * slot_count, 2 * piece_blocks),
        )[0]

    def last(blocks, *args):
        rows = (piece_blocks + 1, block_size, width)
        (out,) = call(
            functools.partial(last_kernel, bare_at),
            [(base_shape, jnp.bfloat16, HBM)],
            (plan, blocks, *args),
            (LIST,) + (HERE,) * 4,
            [VMEM(rows, jnp.float32), VMEM(rows, jnp.bfloat16), DMA((piece_blocks,))],
            8,
            "last",
            cost(slot_count, piece_blocks),
        )
        return out.reshape(vectors.shape)

    p1 = after(exchange(sent), plan)
    o1 = across(p1)
    (blocks,) = load(load_at, 1, 4, p1)
    first_sent = sent_blocks(blocks, p1, o1, sent)
    p2 = exchange(first_sent)
    o2 = across(p2)
    second_sent = sent_blocks(blocks, p2, o2, sent, first_sent)
    (blocks,) = load(HEAD, STRIDE, 0, second_sent)
    base = early(blocks, p1, p2, o1, o2)
    p3 = after(exchange(second_sent), base)
    o3 = across(p3)
    blocks, base = load(HEAD, STRIDE, 0, p3, base)
    return last(blocks, p3, o3, base)


def on_any(vectors, tile_blocks, block_rows, block_cols, counts):
    n_row = lax.axis_size("row")
    n_col = lax.axis_size("col")
    tile_data = tile_blocks[0, 0]
    slot_rows = block_rows[0, 0]
    slot_cols = block_cols[0, 0]
    used = counts[0, 0]
    block_size = tile_data.shape[-1]
    width = vectors.shape[1]
    piece_blocks = vectors.shape[0] // block_size
    row_blocks = piece_blocks * n_col
    slot_count = tile_data.shape[0]
    live = (jnp.arange(slot_count) < used).astype(jnp.float32)
    onehot = (slot_rows[None, :] == jnp.arange(row_blocks)[:, None]).astype(jnp.float32) * live[
        None, :
    ]
    source_piece = slot_cols // piece_blocks
    offset = slot_cols % piece_blocks
    needed = jnp.max(
        jnp.where(source_piece[None, :] == jnp.arange(n_row)[:, None], offset[None, :], 0), axis=1
    )
    wanted = lax.all_to_all(
        needed.reshape(n_row, 1), "row", split_axis=0, concat_axis=0, tiled=True
    ).reshape(n_row)

    def apply_tiles(current):
        own_blocks = current.reshape(piece_blocks, block_size, width)
        outgoing = jnp.take(own_blocks, wanted, axis=0)
        received = lax.all_to_all(outgoing, "row", split_axis=0, concat_axis=0, tiled=True)
        vec_blocks = jnp.take(received, source_piece, axis=0)
        products = jnp.einsum(
            "sij,sjk->sik", tile_data, vec_blocks, preferred_element_type=jnp.float32
        )
        term = jnp.einsum("ls,sik->lik", onehot, products, precision=lax.Precision.HIGHEST)
        term = term.reshape(row_blocks * block_size, width)
        return lax.psum_scatter(
            term.astype(jnp.bfloat16), "col", scatter_dimension=0, tiled=True
        ).astype(jnp.float32)

    previous = vectors
    applied = apply_tiles(vectors)
    current = ((applied - center_value * previous.astype(jnp.float32)) / half_width).astype(
        jnp.bfloat16
    )
    for repeat in range(DEGREE - 1):
        applied = apply_tiles(current)
        following = (
            2.0 * (applied - center_value * current.astype(jnp.float32)) / half_width
            - previous.astype(jnp.float32)
        ).astype(jnp.bfloat16)
        previous, current = (current, following)
    return current


def solution(mesh):
    n_row, n_col = mesh.shape["row"], mesh.shape["col"]
    paired = n_col == 2 and n_row & (n_row - 1) == 0
    return jax.shard_map(
        on_pair if paired else on_any,
        mesh=mesh,
        in_specs=(
            P(("row", "col"), "vec"),
            P("row", "col", None, None, None),
            P("row", "col", None),
            P("row", "col", None),
            P("row", "col"),
        ),
        out_specs=P(("row", "col"), "vec"),
        check_vma=False,
    )
```

```python
import functools

import jax
import jax.numpy as jnp
from jax import lax
from jax.experimental import pallas as pl
from jax.experimental.pallas import tpu as pltpu
from jax.sharding import PartitionSpec as P

DEGREE = 3

center_value = 0.5
half_width = 2.0

VMEM = pltpu.VMEM
SMEM = pltpu.SMEM
HBM = pltpu.HBM
DMA = pltpu.SemaphoreType.DMA
LANES = 128
FEW = 2
MANY = 4
HEAD = 8
STRIDE = 4
FIRST = 1
LAST = 2


def spec(space):
    return pl.BlockSpec(memory_space=space)


def params(mib):
    return pltpu.CompilerParams(vmem_limit_bytes=mib * 1024 * 1024)


def round_up(n, step):
    return (n + step - 1) // step * step


def plan_kernel(
    n_row, piece_blocks, sent_at, load_at, bare_at, place, wanted, rows_a, cols_a, used_a, meta_b, out, seen
):
    slot_count = rows_a.shape[0]
    first_row = place[1] * piece_blocks

    def scan(row_of, col_of, used, at, sent, load):
        def step(s, carry):
            at, sent, load = carry
            row = row_of(s) - first_row
            inside = (row >= 0) & (row < piece_blocks)
            mine = inside.astype(jnp.int32)
            piece = col_of(s) // piece_blocks
            kept = jnp.where(inside, row, piece_blocks)
            entry = HEAD + STRIDE * at
            out[entry] = s
            out[entry + 1] = row
            out[entry + 2] = piece
            out[entry + 3] = jnp.where(seen[kept] == 0, FIRST, 0)
            seen[kept] = entry
            out[load_at + load] = s
            before = sent
            for k in range(n_row):
                out[sent_at + STRIDE * sent] = load
                out[sent_at + STRIDE * sent + 1] = k
                out[sent_at + STRIDE * sent + 2] = piece
                sent = sent + jnp.where(wanted[k, 0] == row, mine, 0)
            return at + mine, sent, load + (sent > before).astype(jnp.int32)

        at, sent, load = lax.fori_loop(0, used, step, (at, sent, load))
        for _ in range(MANY):
            for base, end, spare in ((HEAD, at, piece_blocks), (sent_at, sent, n_row)):
                entry = base + STRIDE * end
                out[entry] = 0
                out[entry + 1] = spare
                out[entry + 2] = 0
                out[entry + 3] = 0
            at = at + jnp.where(at % MANY == 0, 0, 1)
            sent = sent + jnp.where(sent % FEW == 0, 0, 1)
        return at, sent, load

    for b in range(piece_blocks + 1):
        seen[b] = 0
    zero = jnp.int32(0)
    at, sent, load = scan(
        lambda s: rows_a[s], lambda s: cols_a[s], used_a[0], zero, zero, zero
    )
    out[0] = at
    out[2] = sent
    out[4] = load
    at, sent, load = scan(
        lambda s: meta_b[s],
        lambda s: meta_b[slot_count + s],
        meta_b[2 * slot_count],
        at,
        sent,
        load,
    )
    out[1] = at
    out[3] = sent
    out[5] = load

    def close(b, bare):
        entry = seen[b]
        out[bare_at + bare] = b

        @pl.when(entry > 0)
        def _():
            out[entry + 3] = out[entry + 3] + LAST

        return bare + jnp.where(entry == 0, 1, 0)

    out[6] = lax.fori_loop(0, piece_blocks, close, zero)


def pick_kernel(n_row, block_size, wanted, vectors, out, held, in_sems, out_sems):
    def fetch(k):
        at = pl.multiple_of(wanted[k, 0] * block_size, block_size)
        return pltpu.make_async_copy(vectors.at[pl.ds(at, block_size)], held.at[k], in_sems.at[k])

    def put(k):
        return pltpu.make_async_copy(held.at[k], out.at[k], out_sems.at[k])

    for k in range(n_row):
        fetch(k).start()
    for k in range(n_row):
        fetch(k).wait()
        put(k).start()
    for k in range(n_row):
        put(k).wait()


def load_kernel(base, stride, ends, plan, tile_a, tile_b, blocks, sems):
    mid, end = plan[ends], plan[ends + 1]

    def copy(tile, i):
        slot = plan[base + stride * i]
        return pltpu.make_async_copy(tile.at[slot], blocks.at[i], sems.at[i])

    @pl.loop(0, mid)
    def _(i):
        copy(tile_a, i).start()

    @pl.loop(mid, end)
    def _(i):
        copy(tile_b, i).start()

    @pl.loop(0, end)
    def _(i):
        copy(tile_a, i).wait()


def load_both_kernel(base, stride, ends, plan, tile_a, tile_b, array, blocks, held, sems, held_sem):
    copy = pltpu.make_async_copy(array, held, held_sem)
    copy.start()
    load_kernel(base, stride, ends, plan, tile_a, tile_b, blocks, sems)
    copy.wait()


def each_product(plan, base, ends, blocks, pieces, use, then=None):
    mid, end = plan[ends], plan[ends + 1]
    unroll = MANY if base == HEAD else FEW

    def run(piece_ref, begin, end):
        @pl.loop(begin // unroll, end // unroll)
        def _(j):
            for u in range(unroll):
                i = unroll * j + u
                entry = base + STRIDE * i
                block = blocks[i if base == HEAD else plan[entry]]
                use(
                    entry,
                    jnp.dot(block, piece_ref[plan[entry + 2]], preferred_element_type=jnp.float32),
                )
            if then is not None:
                for u in range(unroll):
                    then(base + STRIDE * (unroll * j + u))

    run(pieces[0], 0, mid)
    run(pieces[1], mid, end)


def add_products(plan, base, ends, blocks, pieces, total):
    def use(entry, value):
        total[plan[entry + 1]] += value

    each_product(plan, base, ends, blocks, pieces, use)


def sent_kernel(first, sent_at, plan, blocks, pieces, others, picked, *rest):
    if first:
        out, total, held, held_sem = rest
    else:
        current, out, total, held, held_sem, ready, out_sems = rest
    n_row = out.shape[0]
    copy = pltpu.make_async_copy(picked, held, held_sem)
    copy.start()
    for k in range(n_row):
        if first:
            total[k] = jnp.zeros(total.shape[1:], jnp.float32)
        else:
            total[k] = -center_value * current[k].astype(jnp.float32)
    add_products(plan, sent_at, 2, blocks, (pieces, others), total)
    copy.wait()
    if first:
        for k in range(n_row):
            value = total[k] - center_value * held[k].astype(jnp.float32)
            out[k] = (value / half_width).astype(jnp.bfloat16)
        return

    def put(k):
        return pltpu.make_async_copy(ready.at[k], out.at[k], out_sems.at[k])

    for k in range(n_row):
        ready[k] = (total[k] - held[k].astype(jnp.float32)).astype(jnp.bfloat16)
        put(k).start()
    for k in range(n_row):
        put(k).wait()


def early_kernel(plan, blocks, p1, p2, o1, o2, vectors, base, vec, total, own, sems, row_sems):
    width = vectors.shape[1]
    piece_blocks, block_size, _ = base.shape
    copies = [
        pltpu.make_async_copy(
            source, vec.at[side, :, :, pl.ds(step * width, width)], sems.at[2 * side + step]
        )
        for side, step, source in ((0, 0, p1), (0, 1, p2), (1, 0, o1), (1, 1, o2))
    ]
    copies.append(pltpu.make_async_copy(vectors, own, sems.at[4]))
    for copy in copies:
        copy.start()
    copies[-1].wait()

    def rows(b):
        return pl.ds(pl.multiple_of(b * block_size, block_size), block_size)

    def put(b):
        return pltpu.make_async_copy(own.at[rows(b)], base.at[b], row_sems.at[b])

    @pl.loop(0, piece_blocks)
    def _(b):
        value = own[rows(b), :].astype(jnp.float32)
        total[b, :, :width] = -center_value * value
        total[b, :, width:] = -value

    for copy in copies[:-1]:
        copy.wait()
    add_products(plan, HEAD, 0, blocks, (vec.at[0], vec.at[1]), total)

    @pl.loop(0, piece_blocks)
    def _(b):
        first = (total[b, :, :width] / half_width).astype(jnp.bfloat16).astype(jnp.float32)
        second = total[b, :, width:] - center_value * first
        second = second.astype(jnp.bfloat16).astype(jnp.float32)
        own[rows(b), :] = (-center_value * second - first).astype(jnp.bfloat16)
        put(b).start()

    @pl.loop(0, piece_blocks)
    def _(b):
        put(b).wait()


def last_kernel(bare_at, plan, blocks, pieces, others, base, out, total, own, row_sems):
    piece_blocks = base.shape[0]

    def put(source, b):
        return pltpu.make_async_copy(source.at[b], out.at[b], row_sems.at[b])

    @pl.loop(0, plan[6])
    def _(i):
        b = plan[bare_at + i]
        put(base, b).start()

    def use(entry, value):
        row = plan[entry + 1]
        marks = plan[entry + 3]
        start = base[jnp.minimum(row, piece_blocks - 1)].astype(jnp.float32)
        value = jnp.where(lax.rem(marks, LAST) == FIRST, start, total[row]) + value
        total[row] = value
        own[row] = value.astype(jnp.bfloat16)

    def then(entry):
        @pl.when(plan[entry + 3] >= LAST)
        def _():
            put(own, plan[entry + 1]).start()

    each_product(plan, HEAD, 0, blocks, (pieces, others), use, then)

    @pl.loop(0, piece_blocks)
    def _(b):
        put(own, b).wait()


def after(value, *others):
    return lax.optimization_barrier((value, *others))[0]


def call(kernel, out, args, spaces, scratch, mib, name, estimate=None):
    args = [
        pltpu.with_memory_space_constraint(arg, space) if space in (VMEM, HBM) or tied else arg
        for arg, (space, tied) in zip(args, spaces)
    ]
    return pl.pallas_call(
        kernel,
        out_shape=[space(shape, dtype) for shape, dtype, space in out],
        in_specs=[spec(space) for space, _ in spaces],
        out_specs=[spec(space) for _, _, space in out],
        scratch_shapes=scratch,
        compiler_params=params(mib),
        cost_estimate=estimate,
        name=name,
    )(*args)


HERE = (VMEM, True)
FAR = (HBM, True)
LIST = (SMEM, True)
SCALARS = (SMEM, False)
ANYWHERE = (pl.ANY, False)


def on_pair(vectors, tile_blocks, block_rows, block_cols, counts):
    n_row = lax.axis_size("row")
    tile = tile_blocks[0, 0]
    slot_rows = block_rows[0, 0]
    slot_cols = block_cols[0, 0]
    used = counts[0]
    slot_count, block_size, _ = tile.shape
    width = vectors.shape[1]
    piece_blocks = vectors.shape[0] // block_size
    place = jnp.stack([lax.axis_index("row"), lax.axis_index("col")]).astype(jnp.int32)

    across = functools.partial(lax.ppermute, axis_name="col", perm=[(0, 1), (1, 0)])

    needed = jnp.max(
        jnp.where(
            slot_cols[None, :] // piece_blocks == jnp.arange(n_row)[:, None],
            slot_cols[None, :] % piece_blocks,
            0,
        ),
        axis=1,
        keepdims=True,
    )
    exchange = functools.partial(
        lax.all_to_all, axis_name="row", split_axis=0, concat_axis=0, tiled=True
    )
    wanted = exchange(jnp.broadcast_to(needed, (n_row, LANES)))
    sent_shape = (n_row, block_size, width)
    (sent,) = call(
        functools.partial(pick_kernel, n_row, block_size),
        [(sent_shape, jnp.bfloat16, HBM)],
        (wanted, vectors),
        (SCALARS, FAR),
        [VMEM(sent_shape, jnp.bfloat16), DMA((n_row,)), DMA((n_row,))],
        2,
        "pick",
    )
    tile_other = across(after(tile, sent))
    meta = across(after(jnp.concatenate([slot_rows, slot_cols, used]), sent))

    capacity = 2 * round_up(slot_count, MANY)
    sent_at = HEAD + STRIDE * (capacity + 1)
    load_at = sent_at + STRIDE * (2 * n_row * n_row + 2 * FEW + 1)
    bare_at = load_at + 2 * slot_count + 1
    plan_size = bare_at + piece_blocks
    (plan,) = call(
        functools.partial(plan_kernel, n_row, piece_blocks, sent_at, load_at, bare_at),
        [((plan_size,), jnp.int32, SMEM)],
        (place, wanted, slot_rows, slot_cols, used, meta),
        (SCALARS,) * 6,
        [SMEM((piece_blocks + 1,), jnp.int32)],
        2,
        "plan",
    )
    def load(base, stride, ends, cue, *array):
        kernel = load_both_kernel if array else load_kernel
        return call(
            functools.partial(kernel, base, stride, ends),
            [((capacity, block_size, block_size), jnp.bfloat16, VMEM)]
            + [(held.shape, held.dtype, VMEM) for held in array],
            (after(plan, cue), tile, tile_other, *array),
            (LIST, FAR, ANYWHERE) + (FAR,) * len(array),
            [DMA((capacity,))] + [DMA] * len(array),
            2,
            "load",
        )

    def cost(products, rows):
        size = block_size * width
        return pl.CostEstimate(
            flops=2 * products * block_size * size,
            bytes_accessed=2 * (products * block_size * block_size + 3 * rows * size),
            transcendentals=0,
        )

    def sent_blocks(blocks, *args):
        first = len(args) == 3
        held = [VMEM(sent_shape, jnp.bfloat16), DMA]
        staged = [] if first else [VMEM(sent_shape, jnp.bfloat16), DMA((n_row,))]
        return call(
            functools.partial(sent_kernel, first, sent_at),
            [(sent_shape, jnp.bfloat16, VMEM if first else HBM)],
            (plan, blocks, *args),
            (LIST, HERE, HERE, HERE, FAR) + (HERE,) * (len(args) - 3),
            [VMEM((n_row + 1, block_size, width), jnp.float32)] + held + staged,
            4,
            "sent",
            cost(n_row, n_row),
        )[0]

    base_shape = (piece_blocks, block_size, width)

    def early(blocks, *pieces):
        return call(
            early_kernel,
            [(base_shape, jnp.bfloat16, HBM)],
            (plan, blocks, *pieces, vectors),
            (LIST,) + (HERE,) * 5 + (FAR,),
            [
                VMEM((2, n_row, block_size, 2 * width), jnp.bfloat16),
                VMEM((piece_blocks + 1, block_size, 2 * width), jnp.float32),
                VMEM(vectors.shape, jnp.bfloat16),
                DMA((5,)),
                DMA((piece_blocks,)),
            ],
            18,
            "early",
            cost(2 * slot_count, 2 * piece_blocks),
        )[0]

    def last(blocks, *args):
        rows = (piece_blocks + 1, block_size, width)
        (out,) = call(
            functools.partial(last_kernel, bare_at),
            [(base_shape, jnp.bfloat16, HBM)],
            (plan, blocks, *args),
            (LIST,) + (HERE,) * 4,
            [VMEM(rows, jnp.float32), VMEM(rows, jnp.bfloat16), DMA((piece_blocks,))],
            8,
            "last",
            cost(slot_count, piece_blocks),
        )
        return out.reshape(vectors.shape)

    p1 = after(exchange(sent), plan)
    o1 = across(p1)
    (blocks,) = load(load_at, 1, 4, p1)
    first_sent = sent_blocks(blocks, p1, o1, sent)
    p2 = exchange(first_sent)
    o2 = across(p2)
    second_sent = sent_blocks(blocks, p2, o2, sent, first_sent)
    (blocks,) = load(HEAD, STRIDE, 0, second_sent)
    base = early(blocks, p1, p2, o1, o2)
    p3 = after(exchange(second_sent), base)
    o3 = across(p3)
    blocks, base = load(HEAD, STRIDE, 0, p3, base)
    return last(blocks, p3, o3, base)


def on_any(vectors, tile_blocks, block_rows, block_cols, counts):
    n_row = lax.axis_size("row")
    n_col = lax.axis_size("col")
    tile_data = tile_blocks[0, 0]
    slot_rows = block_rows[0, 0]
    slot_cols = block_cols[0, 0]
    used = counts[0, 0]
    block_size = tile_data.shape[-1]
    width = vectors.shape[1]
    piece_blocks = vectors.shape[0] // block_size
    row_blocks = piece_blocks * n_col
    slot_count = tile_data.shape[0]
    live = (jnp.arange(slot_count) < used).astype(jnp.float32)
    onehot = (slot_rows[None, :] == jnp.arange(row_blocks)[:, None]).astype(jnp.float32) * live[
        None, :
    ]
    source_piece = slot_cols // piece_blocks
    offset = slot_cols % piece_blocks
    needed = jnp.max(
        jnp.where(source_piece[None, :] == jnp.arange(n_row)[:, None], offset[None, :], 0), axis=1
    )
    wanted = lax.all_to_all(
        needed.reshape(n_row, 1), "row", split_axis=0, concat_axis=0, tiled=True
    ).reshape(n_row)

    def apply_tiles(current):
        own_blocks = current.reshape(piece_blocks, block_size, width)
        outgoing = jnp.take(own_blocks, wanted, axis=0)
        received = lax.all_to_all(outgoing, "row", split_axis=0, concat_axis=0, tiled=True)
        vec_blocks = jnp.take(received, source_piece, axis=0)
        products = jnp.einsum(
            "sij,sjk->sik", tile_data, vec_blocks, preferred_element_type=jnp.float32
        )
        term = jnp.einsum("ls,sik->lik", onehot, products, precision=lax.Precision.HIGHEST)
        term = term.reshape(row_blocks * block_size, width)
        return lax.psum_scatter(
            term.astype(jnp.bfloat16), "col", scatter_dimension=0, tiled=True
        ).astype(jnp.float32)

    previous = vectors
    applied = apply_tiles(vectors)
    current = ((applied - center_value * previous.astype(jnp.float32)) / half_width).astype(
        jnp.bfloat16
    )
    for repeat in range(DEGREE - 1):
        applied = apply_tiles(current)
        following = (
            2.0 * (applied - center_value * current.astype(jnp.float32)) / half_width
            - previous.astype(jnp.float32)
        ).astype(jnp.bfloat16)
        previous, current = (current, following)
    return current


def solution(mesh):
    n_row, n_col = mesh.shape["row"], mesh.shape["col"]
    paired = n_col == 2 and n_row & (n_row - 1) == 0
    return jax.shard_map(
        on_pair if paired else on_any,
        mesh=mesh,
        in_specs=(
            P(("row", "col"), "vec"),
            P("row", "col", None, None, None),
            P("row", "col", None),
            P("row", "col", None),
            P("row", "col"),
        ),
        out_specs=P(("row", "col"), "vec"),
        check_vma=False,
    )
```

```python
import functools

import jax
import jax.numpy as jnp
from jax import lax
from jax.experimental import pallas as pl
from jax.experimental.pallas import tpu as pltpu
from jax.sharding import PartitionSpec as P

DEGREE = 3

center_value = 0.5
half_width = 2.0

VMEM = pltpu.VMEM
SMEM = pltpu.SMEM
HBM = pltpu.HBM
DMA = pltpu.SemaphoreType.DMA
LANES = 128
FEW = 4
MANY = 4
HEAD = 8
STRIDE = 4
FIRST = 1
LAST = 2


def spec(space):
    return pl.BlockSpec(memory_space=space)


def params(mib):
    return pltpu.CompilerParams(vmem_limit_bytes=mib * 1024 * 1024)


def round_up(n, step):
    return (n + step - 1) // step * step


def plan_kernel(
    n_row, piece_blocks, sent_at, load_at, bare_at, place, wanted, rows_a, cols_a, used_a, meta_b, out, seen
):
    slot_count = rows_a.shape[0]
    first_row = place[1] * piece_blocks

    def scan(row_of, col_of, used, at, sent, load):
        def step(s, carry):
            at, sent, load = carry
            row = row_of(s) - first_row
            inside = (row >= 0) & (row < piece_blocks)
            mine = inside.astype(jnp.int32)
            piece = col_of(s) // piece_blocks
            kept = jnp.where(inside, row, piece_blocks)
            entry = HEAD + STRIDE * at
            out[entry] = s
            out[entry + 1] = row
            out[entry + 2] = piece
            out[entry + 3] = jnp.where(seen[kept] == 0, FIRST, 0)
            seen[kept] = entry
            out[load_at + load] = s
            before = sent
            for k in range(n_row):
                out[sent_at + STRIDE * sent] = load
                out[sent_at + STRIDE * sent + 1] = k
                out[sent_at + STRIDE * sent + 2] = piece
                sent = sent + jnp.where(wanted[k, 0] == row, mine, 0)
            return at + mine, sent, load + (sent > before).astype(jnp.int32)

        at, sent, load = lax.fori_loop(0, used, step, (at, sent, load))
        for _ in range(MANY):
            for base, end, spare in ((HEAD, at, piece_blocks), (sent_at, sent, n_row)):
                entry = base + STRIDE * end
                out[entry] = 0
                out[entry + 1] = spare
                out[entry + 2] = 0
                out[entry + 3] = 0
            at = at + jnp.where(at % MANY == 0, 0, 1)
            sent = sent + jnp.where(sent % FEW == 0, 0, 1)
        return at, sent, load

    for b in range(piece_blocks + 1):
        seen[b] = 0
    zero = jnp.int32(0)
    at, sent, load = scan(
        lambda s: rows_a[s], lambda s: cols_a[s], used_a[0], zero, zero, zero
    )
    out[0] = at
    out[2] = sent
    out[4] = load
    at, sent, load = scan(
        lambda s: meta_b[s],
        lambda s: meta_b[slot_count + s],
        meta_b[2 * slot_count],
        at,
        sent,
        load,
    )
    out[1] = at
    out[3] = sent
    out[5] = load

    def close(b, bare):
        entry = seen[b]
        out[bare_at + bare] = b

        @pl.when(entry > 0)
        def _():
            out[entry + 3] = out[entry + 3] + LAST

        return bare + jnp.where(entry == 0, 1, 0)

    out[6] = lax.fori_loop(0, piece_blocks, close, zero)


def pick_kernel(n_row, block_size, wanted, vectors, out, held, in_sems, out_sems):
    def fetch(k):
        at = pl.multiple_of(wanted[k, 0] * block_size, block_size)
        return pltpu.make_async_copy(vectors.at[pl.ds(at, block_size)], held.at[k], in_sems.at[k])

    def put(k):
        return pltpu.make_async_copy(held.at[k], out.at[k], out_sems.at[k])

    for k in range(n_row):
        fetch(k).start()
    for k in range(n_row):
        fetch(k).wait()
        put(k).start()
    for k in range(n_row):
        put(k).wait()


def load_kernel(base, stride, ends, plan, tile_a, tile_b, blocks, sems):
    mid, end = plan[ends], plan[ends + 1]

    def copy(tile, i):
        slot = plan[base + stride * i]
        return pltpu.make_async_copy(tile.at[slot], blocks.at[i], sems.at[i])

    @pl.loop(0, mid)
    def _(i):
        copy(tile_a, i).start()

    @pl.loop(mid, end)
    def _(i):
        copy(tile_b, i).start()

    @pl.loop(0, end)
    def _(i):
        copy(tile_a, i).wait()


def load_both_kernel(base, stride, ends, plan, tile_a, tile_b, array, blocks, held, sems, held_sem):
    copy = pltpu.make_async_copy(array, held, held_sem)
    copy.start()
    load_kernel(base, stride, ends, plan, tile_a, tile_b, blocks, sems)
    copy.wait()


def each_product(plan, base, ends, blocks, pieces, use, then=None):
    mid, end = plan[ends], plan[ends + 1]
    unroll = MANY if base == HEAD else FEW

    def run(piece_ref, begin, end):
        @pl.loop(begin // unroll, end // unroll)
        def _(j):
            for u in range(unroll):
                i = unroll * j + u
                entry = base + STRIDE * i
                block = blocks[i if base == HEAD else plan[entry]]
                use(
                    entry,
                    jnp.dot(block, piece_ref[plan[entry + 2]], preferred_element_type=jnp.float32),
                )
            if then is not None:
                for u in range(unroll):
                    then(base + STRIDE * (unroll * j + u))

    run(pieces[0], 0, mid)
    run(pieces[1], mid, end)


def add_products(plan, base, ends, blocks, pieces, total):
    def use(entry, value):
        total[plan[entry + 1]] += value

    each_product(plan, base, ends, blocks, pieces, use)


def sent_kernel(first, sent_at, plan, blocks, pieces, others, picked, *rest):
    if first:
        out, total, held, held_sem = rest
    else:
        current, out, total, held, held_sem, ready, out_sems = rest
    n_row = out.shape[0]
    copy = pltpu.make_async_copy(picked, held, held_sem)
    copy.start()
    for k in range(n_row):
        if first:
            total[k] = jnp.zeros(total.shape[1:], jnp.float32)
        else:
            total[k] = -center_value * current[k].astype(jnp.float32)
    add_products(plan, sent_at, 2, blocks, (pieces, others), total)
    copy.wait()
    if first:
        for k in range(n_row):
            value = total[k] - center_value * held[k].astype(jnp.float32)
            out[k] = (value / half_width).astype(jnp.bfloat16)
        return

    def put(k):
        return pltpu.make_async_copy(ready.at[k], out.at[k], out_sems.at[k])

    for k in range(n_row):
        ready[k] = (total[k] - held[k].astype(jnp.float32)).astype(jnp.bfloat16)
        put(k).start()
    for k in range(n_row):
        put(k).wait()


def early_kernel(plan, blocks, p1, p2, o1, o2, vectors, base, vec, total, own, sems, row_sems):
    width = vectors.shape[1]
    piece_blocks, block_size, _ = base.shape
    copies = [
        pltpu.make_async_copy(
            source, vec.at[side, :, :, pl.ds(step * width, width)], sems.at[2 * side + step]
        )
        for side, step, source in ((0, 0, p1), (0, 1, p2), (1, 0, o1), (1, 1, o2))
    ]
    copies.append(pltpu.make_async_copy(vectors, own, sems.at[4]))
    for copy in copies:
        copy.start()
    copies[-1].wait()

    def rows(b):
        return pl.ds(pl.multiple_of(b * block_size, block_size), block_size)

    def put(b):
        return pltpu.make_async_copy(own.at[rows(b)], base.at[b], row_sems.at[b])

    @pl.loop(0, piece_blocks)
    def _(b):
        value = own[rows(b), :].astype(jnp.float32)
        total[b, :, :width] = -center_value * value
        total[b, :, width:] = -value

    for copy in copies[:-1]:
        copy.wait()
    add_products(plan, HEAD, 0, blocks, (vec.at[0], vec.at[1]), total)

    @pl.loop(0, piece_blocks)
    def _(b):
        first = (total[b, :, :width] / half_width).astype(jnp.bfloat16).astype(jnp.float32)
        second = total[b, :, width:] - center_value * first
        second = second.astype(jnp.bfloat16).astype(jnp.float32)
        own[rows(b), :] = (-center_value * second - first).astype(jnp.bfloat16)
        put(b).start()

    @pl.loop(0, piece_blocks)
    def _(b):
        put(b).wait()


def last_kernel(bare_at, plan, blocks, pieces, others, base, out, total, own, row_sems):
    piece_blocks = base.shape[0]

    def put(source, b):
        return pltpu.make_async_copy(source.at[b], out.at[b], row_sems.at[b])

    @pl.loop(0, plan[6])
    def _(i):
        b = plan[bare_at + i]
        put(base, b).start()

    def use(entry, value):
        row = plan[entry + 1]
        marks = plan[entry + 3]
        start = base[jnp.minimum(row, piece_blocks - 1)].astype(jnp.float32)
        value = jnp.where(lax.rem(marks, LAST) == FIRST, start, total[row]) + value
        total[row] = value
        own[row] = value.astype(jnp.bfloat16)

    def then(entry):
        @pl.when(plan[entry + 3] >= LAST)
        def _():
            put(own, plan[entry + 1]).start()

    each_product(plan, HEAD, 0, blocks, (pieces, others), use, then)

    @pl.loop(0, piece_blocks)
    def _(b):
        put(own, b).wait()


def after(value, *others):
    return lax.optimization_barrier((value, *others))[0]


def call(kernel, out, args, spaces, scratch, mib, name, estimate=None):
    args = [
        pltpu.with_memory_space_constraint(arg, space) if space in (VMEM, HBM) or tied else arg
        for arg, (space, tied) in zip(args, spaces)
    ]
    return pl.pallas_call(
        kernel,
        out_shape=[space(shape, dtype) for shape, dtype, space in out],
        in_specs=[spec(space) for space, _ in spaces],
        out_specs=[spec(space) for _, _, space in out],
        scratch_shapes=scratch,
        compiler_params=params(mib),
        cost_estimate=estimate,
        name=name,
    )(*args)


HERE = (VMEM, True)
FAR = (HBM, True)
LIST = (SMEM, True)
SCALARS = (SMEM, False)
ANYWHERE = (pl.ANY, False)


def on_pair(vectors, tile_blocks, block_rows, block_cols, counts):
    n_row = lax.axis_size("row")
    tile = tile_blocks[0, 0]
    slot_rows = block_rows[0, 0]
    slot_cols = block_cols[0, 0]
    used = counts[0]
    slot_count, block_size, _ = tile.shape
    width = vectors.shape[1]
    piece_blocks = vectors.shape[0] // block_size
    place = jnp.stack([lax.axis_index("row"), lax.axis_index("col")]).astype(jnp.int32)

    across = functools.partial(lax.ppermute, axis_name="col", perm=[(0, 1), (1, 0)])

    needed = jnp.max(
        jnp.where(
            slot_cols[None, :] // piece_blocks == jnp.arange(n_row)[:, None],
            slot_cols[None, :] % piece_blocks,
            0,
        ),
        axis=1,
        keepdims=True,
    )
    exchange = functools.partial(
        lax.all_to_all, axis_name="row", split_axis=0, concat_axis=0, tiled=True
    )
    wanted = exchange(jnp.broadcast_to(needed, (n_row, LANES)))
    sent_shape = (n_row, block_size, width)
    (sent,) = call(
        functools.partial(pick_kernel, n_row, block_size),
        [(sent_shape, jnp.bfloat16, HBM)],
        (wanted, vectors),
        (SCALARS, FAR),
        [VMEM(sent_shape, jnp.bfloat16), DMA((n_row,)), DMA((n_row,))],
        2,
        "pick",
    )
    tile_other = across(tile)
    meta = across(after(jnp.concatenate([slot_rows, slot_cols, used]), sent))

    capacity = 2 * round_up(slot_count, MANY)
    sent_at = HEAD + STRIDE * (capacity + 1)
    load_at = sent_at + STRIDE * (2 * n_row * n_row + 2 * FEW + 1)
    bare_at = load_at + 2 * slot_count + 1
    plan_size = bare_at + piece_blocks
    (plan,) = call(
        functools.partial(plan_kernel, n_row, piece_blocks, sent_at, load_at, bare_at),
        [((plan_size,), jnp.int32, SMEM)],
        (place, wanted, slot_rows, slot_cols, used, meta),
        (SCALARS,) * 6,
        [SMEM((piece_blocks + 1,), jnp.int32)],
        2,
        "plan",
    )
    def load(base, stride, ends, cue, *array):
        kernel = load_both_kernel if array else load_kernel
        return call(
            functools.partial(kernel, base, stride, ends),
            [((capacity, block_size, block_size), jnp.bfloat16, VMEM)]
            + [(held.shape, held.dtype, VMEM) for held in array],
            (after(plan, cue), tile, tile_other, *array),
            (LIST, FAR, ANYWHERE) + (FAR,) * len(array),
            [DMA((capacity,))] + [DMA] * len(array),
            2,
            "load",
        )

    def cost(products, rows):
        size = block_size * width
        return pl.CostEstimate(
            flops=2 * products * block_size * size,
            bytes_accessed=2 * (products * block_size * block_size + 3 * rows * size),
            transcendentals=0,
        )

    def sent_blocks(blocks, *args):
        first = len(args) == 3
        held = [VMEM(sent_shape, jnp.bfloat16), DMA]
        staged = [] if first else [VMEM(sent_shape, jnp.bfloat16), DMA((n_row,))]
        return call(
            functools.partial(sent_kernel, first, sent_at),
            [(sent_shape, jnp.bfloat16, VMEM if first else HBM)],
            (plan, blocks, *args),
            (LIST, HERE, HERE, HERE, FAR) + (HERE,) * (len(args) - 3),
            [VMEM((n_row + 1, block_size, width), jnp.float32)] + held + staged,
            4,
            "sent",
            cost(n_row, n_row),
        )[0]

    base_shape = (piece_blocks, block_size, width)

    def early(blocks, *pieces):
        return call(
            early_kernel,
            [(base_shape, jnp.bfloat16, HBM)],
            (plan, blocks, *pieces, vectors),
            (LIST,) + (HERE,) * 5 + (FAR,),
            [
                VMEM((2, n_row, block_size, 2 * width), jnp.bfloat16),
                VMEM((piece_blocks + 1, block_size, 2 * width), jnp.float32),
                VMEM(vectors.shape, jnp.bfloat16),
                DMA((5,)),
                DMA((piece_blocks,)),
            ],
            18,
            "early",
            cost(2 * slot_count, 2 * piece_blocks),
        )[0]

    def last(blocks, *args):
        rows = (piece_blocks + 1, block_size, width)
        (out,) = call(
            functools.partial(last_kernel, bare_at),
            [(base_shape, jnp.bfloat16, HBM)],
            (plan, blocks, *args),
            (LIST,) + (HERE,) * 4,
            [VMEM(rows, jnp.float32), VMEM(rows, jnp.bfloat16), DMA((piece_blocks,))],
            8,
            "last",
            cost(slot_count, piece_blocks),
        )
        return out.reshape(vectors.shape)

    p1 = after(exchange(sent), plan)
    o1 = across(p1)
    (blocks,) = load(load_at, 1, 4, p1)
    first_sent = sent_blocks(blocks, p1, o1, sent)
    p2 = exchange(first_sent)
    o2 = across(p2)
    second_sent = sent_blocks(blocks, p2, o2, sent, first_sent)
    (blocks,) = load(HEAD, STRIDE, 0, second_sent)
    base = early(blocks, p1, p2, o1, o2)
    p3 = after(exchange(second_sent), base)
    o3 = across(p3)
    blocks, base = load(HEAD, STRIDE, 0, p3, base)
    return last(blocks, p3, o3, base)


def on_any(vectors, tile_blocks, block_rows, block_cols, counts):
    n_row = lax.axis_size("row")
    n_col = lax.axis_size("col")
    tile_data = tile_blocks[0, 0]
    slot_rows = block_rows[0, 0]
    slot_cols = block_cols[0, 0]
    used = counts[0, 0]
    block_size = tile_data.shape[-1]
    width = vectors.shape[1]
    piece_blocks = vectors.shape[0] // block_size
    row_blocks = piece_blocks * n_col
    slot_count = tile_data.shape[0]
    live = (jnp.arange(slot_count) < used).astype(jnp.float32)
    onehot = (slot_rows[None, :] == jnp.arange(row_blocks)[:, None]).astype(jnp.float32) * live[
        None, :
    ]
    source_piece = slot_cols // piece_blocks
    offset = slot_cols % piece_blocks
    needed = jnp.max(
        jnp.where(source_piece[None, :] == jnp.arange(n_row)[:, None], offset[None, :], 0), axis=1
    )
    wanted = lax.all_to_all(
        needed.reshape(n_row, 1), "row", split_axis=0, concat_axis=0, tiled=True
    ).reshape(n_row)

    def apply_tiles(current):
        own_blocks = current.reshape(piece_blocks, block_size, width)
        outgoing = jnp.take(own_blocks, wanted, axis=0)
        received = lax.all_to_all(outgoing, "row", split_axis=0, concat_axis=0, tiled=True)
        vec_blocks = jnp.take(received, source_piece, axis=0)
        products = jnp.einsum(
            "sij,sjk->sik", tile_data, vec_blocks, preferred_element_type=jnp.float32
        )
        term = jnp.einsum("ls,sik->lik", onehot, products, precision=lax.Precision.HIGHEST)
        term = term.reshape(row_blocks * block_size, width)
        return lax.psum_scatter(
            term.astype(jnp.bfloat16), "col", scatter_dimension=0, tiled=True
        ).astype(jnp.float32)

    previous = vectors
    applied = apply_tiles(vectors)
    current = ((applied - center_value * previous.astype(jnp.float32)) / half_width).astype(
        jnp.bfloat16
    )
    for repeat in range(DEGREE - 1):
        applied = apply_tiles(current)
        following = (
            2.0 * (applied - center_value * current.astype(jnp.float32)) / half_width
            - previous.astype(jnp.float32)
        ).astype(jnp.bfloat16)
        previous, current = (current, following)
    return current


def solution(mesh):
    n_row, n_col = mesh.shape["row"], mesh.shape["col"]
    paired = n_col == 2 and n_row & (n_row - 1) == 0
    return jax.shard_map(
        on_pair if paired else on_any,
        mesh=mesh,
        in_specs=(
            P(("row", "col"), "vec"),
            P("row", "col", None, None, None),
            P("row", "col", None),
            P("row", "col", None),
            P("row", "col"),
        ),
        out_specs=P(("row", "col"), "vec"),
        check_vma=False,
    )
```

```python
import functools

import jax
import jax.numpy as jnp
from jax import lax
from jax.experimental import pallas as pl
from jax.experimental.pallas import tpu as pltpu
from jax.sharding import PartitionSpec as P

DEGREE = 3

center_value = 0.5
half_width = 2.0

VMEM = pltpu.VMEM
SMEM = pltpu.SMEM
HBM = pltpu.HBM
DMA = pltpu.SemaphoreType.DMA
LANES = 128
FEW = 4
MANY = 4
HEAD = 8
STRIDE = 4
FIRST = 1
LAST = 2


def spec(space):
    return pl.BlockSpec(memory_space=space)


def params(mib):
    return pltpu.CompilerParams(vmem_limit_bytes=mib * 1024 * 1024)


def round_up(n, step):
    return (n + step - 1) // step * step


def plan_kernel(
    n_row,
    piece_blocks,
    sent_at,
    load_at,
    bare_at,
    place,
    wanted_a,
    wanted_b,
    rows_a,
    cols_a,
    used_a,
    meta_b,
    out,
    seen,
):
    slot_count = rows_a.shape[0]
    own_half = place[1]

    def scan(row_of, col_of, used, at, sent, load):
        def step(s, carry):
            at, sent, load = carry
            half = row_of(s) // piece_blocks
            row = row_of(s) - half * piece_blocks
            inside = half == own_half
            piece = col_of(s) // piece_blocks
            kept = jnp.where(inside, row, piece_blocks)
            entry = HEAD + STRIDE * at
            out[entry] = s
            out[entry + 1] = row
            out[entry + 2] = piece
            out[entry + 3] = jnp.where(seen[kept] == 0, FIRST, 0)
            seen[kept] = entry
            out[load_at + load] = s
            before = sent
            for k in range(n_row):
                out[sent_at + STRIDE * sent] = load
                out[sent_at + STRIDE * sent + 1] = 2 * k + half
                out[sent_at + STRIDE * sent + 2] = piece
                asked = jnp.where(inside, wanted_a[k, 0], wanted_b[k, 0])
                sent = sent + (asked == row).astype(jnp.int32)
            return at + inside.astype(jnp.int32), sent, load + (sent > before).astype(jnp.int32)

        at, sent, load = lax.fori_loop(0, used, step, (at, sent, load))
        for _ in range(MANY):
            for base, end, spare in ((HEAD, at, piece_blocks), (sent_at, sent, 2 * n_row)):
                entry = base + STRIDE * end
                out[entry] = 0
                out[entry + 1] = spare
                out[entry + 2] = 0
                out[entry + 3] = 0
            at = at + jnp.where(at % MANY == 0, 0, 1)
            sent = sent + jnp.where(sent % FEW == 0, 0, 1)
        return at, sent, load

    for b in range(piece_blocks + 1):
        seen[b] = 0
    zero = jnp.int32(0)
    at, sent, load = scan(
        lambda s: rows_a[s], lambda s: cols_a[s], used_a[0], zero, zero, zero
    )
    out[0] = at
    out[2] = sent
    out[4] = load
    at, sent, load = scan(
        lambda s: meta_b[s],
        lambda s: meta_b[slot_count + s],
        meta_b[2 * slot_count],
        at,
        sent,
        load,
    )
    out[1] = at
    out[3] = sent
    out[5] = load

    def close(b, bare):
        entry = seen[b]
        out[bare_at + bare] = b

        @pl.when(entry > 0)
        def _():
            out[entry + 3] = out[entry + 3] + LAST

        return bare + jnp.where(entry == 0, 1, 0)

    out[6] = lax.fori_loop(0, piece_blocks, close, zero)
    out[7] = own_half


def pick_kernel(n_row, block_size, wanted, vectors, out, held, in_sems, out_sems):
    def fetch(k):
        at = pl.multiple_of(wanted[k, 0] * block_size, block_size)
        return pltpu.make_async_copy(vectors.at[pl.ds(at, block_size)], held.at[k], in_sems.at[k])

    def put(k):
        return pltpu.make_async_copy(held.at[k], out.at[k], out_sems.at[k])

    for k in range(n_row):
        fetch(k).start()
    for k in range(n_row):
        fetch(k).wait()
        put(k).start()
    for k in range(n_row):
        put(k).wait()


def load_kernel(base, stride, ends, plan, tile_a, tile_b, blocks, sems):
    mid, end = plan[ends], plan[ends + 1]

    def copy(tile, i):
        slot = plan[base + stride * i]
        return pltpu.make_async_copy(tile.at[slot], blocks.at[i], sems.at[i])

    @pl.loop(0, mid)
    def _(i):
        copy(tile_a, i).start()

    @pl.loop(mid, end)
    def _(i):
        copy(tile_b, i).start()

    @pl.loop(0, end)
    def _(i):
        copy(tile_a, i).wait()


def load_both_kernel(base, stride, ends, plan, tile_a, tile_b, array, blocks, held, sems, held_sem):
    copy = pltpu.make_async_copy(array, held, held_sem)
    copy.start()
    load_kernel(base, stride, ends, plan, tile_a, tile_b, blocks, sems)
    copy.wait()


def each_product(plan, base, ends, blocks, pieces, use, then=None):
    mid, end = plan[ends], plan[ends + 1]
    unroll = MANY if base == HEAD else FEW

    def run(piece_ref, begin, end):
        @pl.loop(begin // unroll, end // unroll)
        def _(j):
            for u in range(unroll):
                i = unroll * j + u
                entry = base + STRIDE * i
                block = blocks[i if base == HEAD else plan[entry]]
                use(
                    entry,
                    jnp.dot(block, piece_ref[plan[entry + 2]], preferred_element_type=jnp.float32),
                )
            if then is not None:
                for u in range(unroll):
                    then(base + STRIDE * (unroll * j + u))

    run(pieces[0], 0, mid)
    run(pieces[1], mid, end)


def add_products(plan, base, ends, blocks, pieces, total):
    def use(entry, value):
        total[plan[entry + 1]] += value

    each_product(plan, base, ends, blocks, pieces, use)


def lanes_of(shape, half):
    column = lax.broadcasted_iota(jnp.int32, shape, 1)
    return (column // (shape[1] // 2)) == half


def only_half(vec, side, pieces, half):
    keep = jnp.where(lanes_of((1, vec.shape[-1]), half), 1.0, 0.0).astype(jnp.bfloat16)
    for p in range(vec.shape[1]):
        vec[side, p] = pieces[p] * keep


def joined(total, k):
    one, two = total[2 * k], total[2 * k + 1]
    low = lanes_of(one.shape, 0)
    return jnp.where(low, one, two) + pltpu.roll(
        jnp.where(low, two, one), one.shape[1] // 2, axis=1
    )


def first_sent_kernel(
    sent_at, plan, blocks, pieces, others, picked, picked_b, out, start, vec, total, held, held_sems
):
    n_row = out.shape[0]
    half = plan[7]
    copies = [
        pltpu.make_async_copy(source, held.at[i], held_sems.at[i])
        for i, source in enumerate((picked, picked_b))
    ]
    for copy in copies:
        copy.start()
    only_half(vec, 0, pieces, half)
    only_half(vec, 1, others, half)
    total[...] = jnp.zeros_like(total)
    add_products(plan, sent_at, 2, blocks, (vec.at[0], vec.at[1]), total)
    for copy in copies:
        copy.wait()
    mine = lanes_of(out.shape[1:], half)
    for k in range(n_row):
        own = held[0, k].astype(jnp.float32)
        other = pltpu.roll(held[1, k].astype(jnp.float32), out.shape[2] // 2, axis=1)
        value = jnp.where(mine, own, other)
        start[k] = value.astype(jnp.bfloat16)
        out[k] = ((joined(total, k) - center_value * value) / half_width).astype(jnp.bfloat16)


def second_sent_kernel(
    sent_at, plan, blocks, pieces, previous, current, out, vec, total, ready, out_sems
):
    n_row = out.shape[0]
    half = plan[7]
    only_half(vec, 0, pieces, half)
    only_half(vec, 1, pieces, 1 - half)
    total[...] = jnp.zeros_like(total)
    add_products(plan, sent_at, 2, blocks, (vec.at[0], vec.at[1]), total)

    def put(k):
        return pltpu.make_async_copy(ready.at[k], out.at[k], out_sems.at[k])

    for k in range(n_row):
        value = joined(total, k) - center_value * current[k].astype(jnp.float32)
        ready[k] = (value - previous[k].astype(jnp.float32)).astype(jnp.bfloat16)
        put(k).start()
    for k in range(n_row):
        put(k).wait()


def whole_columns(half, mine, other, vec, at):
    n_row, _, width = mine.shape
    middle = width // 2

    def merge(lower, upper, sides):
        @pl.loop(0, n_row)
        def _(p):
            for side, column in sides:
                part = slice(column * middle, (column + 1) * middle)
                vec[side, p, :, at : at + middle] = lower[p, :, part]
                vec[side, p, :, at + middle : at + width] = upper[p, :, part]

    @pl.when(half == 0)
    def _():
        merge(mine, other, ((0, 0), (1, 1)))

    @pl.when(half == 1)
    def _():
        merge(other, mine, ((0, 1), (1, 0)))


def early_kernel(
    plan, blocks, pieces, others, mine, other, vectors, base, vec, total, own, sems, row_sems
):
    width = vectors.shape[1]
    piece_blocks, block_size, _ = base.shape
    copies = [
        pltpu.make_async_copy(source, vec.at[side, :, :, pl.ds(0, width)], sems.at[side])
        for side, source in enumerate((pieces, others))
    ]
    copies.append(pltpu.make_async_copy(vectors, own, sems.at[2]))
    for copy in copies:
        copy.start()
    whole_columns(plan[7], mine, other, vec, width)
    copies[-1].wait()

    def rows(b):
        return pl.ds(pl.multiple_of(b * block_size, block_size), block_size)

    def put(b):
        return pltpu.make_async_copy(own.at[rows(b)], base.at[b], row_sems.at[b])

    @pl.loop(0, piece_blocks)
    def _(b):
        value = own[rows(b), :].astype(jnp.float32)
        total[b, :, :width] = -center_value * value
        total[b, :, width:] = -value

    for copy in copies[:-1]:
        copy.wait()
    add_products(plan, HEAD, 0, blocks, (vec.at[0], vec.at[1]), total)

    @pl.loop(0, piece_blocks)
    def _(b):
        first = (total[b, :, :width] / half_width).astype(jnp.bfloat16).astype(jnp.float32)
        second = total[b, :, width:] - center_value * first
        second = second.astype(jnp.bfloat16).astype(jnp.float32)
        own[rows(b), :] = (-center_value * second - first).astype(jnp.bfloat16)
        put(b).start()

    @pl.loop(0, piece_blocks)
    def _(b):
        put(b).wait()


def last_kernel(bare_at, plan, blocks, mine, other, base, out, vec, total, own, row_sems):
    piece_blocks = base.shape[0]

    def put(source, b):
        return pltpu.make_async_copy(source.at[b], out.at[b], row_sems.at[b])

    @pl.loop(0, plan[6])
    def _(i):
        b = plan[bare_at + i]
        put(base, b).start()

    whole_columns(plan[7], mine, other, vec, 0)

    def use(entry, value):
        row = plan[entry + 1]
        marks = plan[entry + 3]
        start = base[jnp.minimum(row, piece_blocks - 1)].astype(jnp.float32)
        value = jnp.where(lax.rem(marks, LAST) == FIRST, start, total[row]) + value
        total[row] = value
        own[row] = value.astype(jnp.bfloat16)

    def then(entry):
        @pl.when(plan[entry + 3] >= LAST)
        def _():
            put(own, plan[entry + 1]).start()

    each_product(plan, HEAD, 0, blocks, (vec.at[0], vec.at[1]), use, then)

    @pl.loop(0, piece_blocks)
    def _(b):
        put(own, b).wait()


def after(value, *others):
    return lax.optimization_barrier((value, *others))[0]


def call(kernel, out, args, spaces, scratch, mib, name, estimate=None):
    args = [
        pltpu.with_memory_space_constraint(arg, space) if space in (VMEM, HBM) or tied else arg
        for arg, (space, tied) in zip(args, spaces)
    ]
    return pl.pallas_call(
        kernel,
        out_shape=[space(shape, dtype) for shape, dtype, space in out],
        in_specs=[spec(space) for space, _ in spaces],
        out_specs=[spec(space) for _, _, space in out],
        scratch_shapes=scratch,
        compiler_params=params(mib),
        cost_estimate=estimate,
        name=name,
    )(*args)


HERE = (VMEM, True)
FAR = (HBM, True)
LIST = (SMEM, True)
SCALARS = (SMEM, False)
ANYWHERE = (pl.ANY, False)


def on_pair(vectors, tile_blocks, block_rows, block_cols, counts):
    n_row = lax.axis_size("row")
    tile = tile_blocks[0, 0]
    slot_rows = block_rows[0, 0]
    slot_cols = block_cols[0, 0]
    used = counts[0]
    slot_count, block_size, _ = tile.shape
    width = vectors.shape[1]
    piece_blocks = vectors.shape[0] // block_size
    place = jnp.stack([lax.axis_index("row"), lax.axis_index("col")]).astype(jnp.int32)

    across = functools.partial(lax.ppermute, axis_name="col", perm=[(0, 1), (1, 0)])

    needed = jnp.max(
        jnp.where(
            slot_cols[None, :] // piece_blocks == jnp.arange(n_row)[:, None],
            slot_cols[None, :] % piece_blocks,
            0,
        ),
        axis=1,
        keepdims=True,
    )
    exchange = functools.partial(
        lax.all_to_all, axis_name="row", split_axis=0, concat_axis=0, tiled=True
    )
    wanted = exchange(jnp.broadcast_to(needed, (n_row, LANES)))
    sent_shape = (n_row, block_size, width)
    (sent,) = call(
        functools.partial(pick_kernel, n_row, block_size),
        [(sent_shape, jnp.bfloat16, HBM)],
        (wanted, vectors),
        (SCALARS, FAR),
        [VMEM(sent_shape, jnp.bfloat16), DMA((n_row,)), DMA((n_row,))],
        2,
        "pick",
    )
    tile_other = across(tile)
    wanted_other = across(after(wanted, sent))
    meta = across(after(jnp.concatenate([slot_rows, slot_cols, used]), sent))
    sent_other = across(sent)

    capacity = 2 * round_up(slot_count, MANY)
    sent_at = HEAD + STRIDE * (capacity + 1)
    load_at = sent_at + STRIDE * (4 * n_row * n_row + 2 * FEW + 1)
    bare_at = load_at + 2 * slot_count + 1
    plan_size = bare_at + piece_blocks
    (plan,) = call(
        functools.partial(plan_kernel, n_row, piece_blocks, sent_at, load_at, bare_at),
        [((plan_size,), jnp.int32, SMEM)],
        (place, wanted, wanted_other, slot_rows, slot_cols, used, meta),
        (SCALARS,) * 7,
        [SMEM((piece_blocks + 1,), jnp.int32)],
        2,
        "plan",
    )
    def load(base, stride, ends, cue, *array):
        kernel = load_both_kernel if array else load_kernel
        return call(
            functools.partial(kernel, base, stride, ends),
            [((capacity, block_size, block_size), jnp.bfloat16, VMEM)]
            + [(held.shape, held.dtype, VMEM) for held in array],
            (after(plan, cue), tile, tile_other, *array),
            (LIST, FAR, ANYWHERE) + (FAR,) * len(array),
            [DMA((capacity,))] + [DMA] * len(array),
            2,
            "load",
        )

    def cost(products, rows):
        size = block_size * width
        return pl.CostEstimate(
            flops=2 * products * block_size * size,
            bytes_accessed=2 * (products * block_size * block_size + 3 * rows * size),
            transcendentals=0,
        )

    sums = [
        VMEM((2, n_row, block_size, width), jnp.bfloat16),
        VMEM((2 * n_row + 1, block_size, width), jnp.float32),
    ]

    def first_blocks(*args):
        return call(
            functools.partial(first_sent_kernel, sent_at),
            [(sent_shape, jnp.bfloat16, VMEM)] * 2,
            (plan, *args),
            (LIST, HERE, HERE, HERE, FAR, FAR),
            sums + [VMEM((2, *sent_shape), jnp.bfloat16), DMA((2,))],
            8,
            "sent",
            cost(n_row, n_row),
        )

    def second_blocks(*args):
        return call(
            functools.partial(second_sent_kernel, sent_at),
            [(sent_shape, jnp.bfloat16, HBM)],
            (plan, *args),
            (LIST, HERE, HERE, HERE, HERE),
            sums + [VMEM(sent_shape, jnp.bfloat16), DMA((n_row,))],
            8,
            "sent",
            cost(n_row, n_row),
        )[0]

    base_shape = (piece_blocks, block_size, width)

    def early(blocks, *pieces):
        return call(
            early_kernel,
            [(base_shape, jnp.bfloat16, HBM)],
            (plan, blocks, *pieces, vectors),
            (LIST,) + (HERE,) * 5 + (FAR,),
            [
                VMEM((2, n_row, block_size, 2 * width), jnp.bfloat16),
                VMEM((piece_blocks + 1, block_size, 2 * width), jnp.float32),
                VMEM(vectors.shape, jnp.bfloat16),
                DMA((3,)),
                DMA((piece_blocks,)),
            ],
            18,
            "early",
            cost(2 * slot_count, 2 * piece_blocks),
        )[0]

    def last(blocks, *args):
        rows = (piece_blocks + 1, block_size, width)
        (out,) = call(
            functools.partial(last_kernel, bare_at),
            [(base_shape, jnp.bfloat16, HBM)],
            (plan, blocks, *args),
            (LIST,) + (HERE,) * 4,
            [
                VMEM((2, n_row, block_size, width), jnp.bfloat16),
                VMEM(rows, jnp.float32),
                VMEM(rows, jnp.bfloat16),
                DMA((piece_blocks,)),
            ],
            9,
            "last",
            cost(slot_count, piece_blocks),
        )
        return out.reshape(vectors.shape)

    p1 = after(exchange(sent), plan, sent_other)
    o1 = across(p1)
    (blocks,) = load(load_at, 1, 4, p1)
    first_sent, start = first_blocks(blocks, p1, o1, sent, sent_other)
    q2 = exchange(first_sent)
    second_sent = second_blocks(blocks, q2, start, first_sent)
    (blocks,) = load(HEAD, STRIDE, 0, second_sent)
    base = early(blocks, p1, o1, q2, across(after(q2, second_sent)))
    q3 = after(exchange(second_sent), base)
    q3_other = across(q3)
    blocks, base = load(HEAD, STRIDE, 0, q3, base)
    return last(blocks, q3, q3_other, base)


def on_any(vectors, tile_blocks, block_rows, block_cols, counts):
    n_row = lax.axis_size("row")
    n_col = lax.axis_size("col")
    tile_data = tile_blocks[0, 0]
    slot_rows = block_rows[0, 0]
    slot_cols = block_cols[0, 0]
    used = counts[0, 0]
    block_size = tile_data.shape[-1]
    width = vectors.shape[1]
    piece_blocks = vectors.shape[0] // block_size
    row_blocks = piece_blocks * n_col
    slot_count = tile_data.shape[0]
    live = (jnp.arange(slot_count) < used).astype(jnp.float32)
    onehot = (slot_rows[None, :] == jnp.arange(row_blocks)[:, None]).astype(jnp.float32) * live[
        None, :
    ]
    source_piece = slot_cols // piece_blocks
    offset = slot_cols % piece_blocks
    needed = jnp.max(
        jnp.where(source_piece[None, :] == jnp.arange(n_row)[:, None], offset[None, :], 0), axis=1
    )
    wanted = lax.all_to_all(
        needed.reshape(n_row, 1), "row", split_axis=0, concat_axis=0, tiled=True
    ).reshape(n_row)

    def apply_tiles(current):
        own_blocks = current.reshape(piece_blocks, block_size, width)
        outgoing = jnp.take(own_blocks, wanted, axis=0)
        received = lax.all_to_all(outgoing, "row", split_axis=0, concat_axis=0, tiled=True)
        vec_blocks = jnp.take(received, source_piece, axis=0)
        products = jnp.einsum(
            "sij,sjk->sik", tile_data, vec_blocks, preferred_element_type=jnp.float32
        )
        term = jnp.einsum("ls,sik->lik", onehot, products, precision=lax.Precision.HIGHEST)
        term = term.reshape(row_blocks * block_size, width)
        return lax.psum_scatter(
            term.astype(jnp.bfloat16), "col", scatter_dimension=0, tiled=True
        ).astype(jnp.float32)

    previous = vectors
    applied = apply_tiles(vectors)
    current = ((applied - center_value * previous.astype(jnp.float32)) / half_width).astype(
        jnp.bfloat16
    )
    for repeat in range(DEGREE - 1):
        applied = apply_tiles(current)
        following = (
            2.0 * (applied - center_value * current.astype(jnp.float32)) / half_width
            - previous.astype(jnp.float32)
        ).astype(jnp.bfloat16)
        previous, current = (current, following)
    return current


def solution(mesh):
    n_row, n_col = mesh.shape["row"], mesh.shape["col"]
    paired = n_col == 2 and n_row & (n_row - 1) == 0
    return jax.shard_map(
        on_pair if paired else on_any,
        mesh=mesh,
        in_specs=(
            P(("row", "col"), "vec"),
            P("row", "col", None, None, None),
            P("row", "col", None),
            P("row", "col", None),
            P("row", "col"),
        ),
        out_specs=P(("row", "col"), "vec"),
        check_vma=False,
    )
```

```python
import functools

import jax
import jax.numpy as jnp
from jax import lax
from jax.experimental import pallas as pl
from jax.experimental.pallas import tpu as pltpu
from jax.sharding import PartitionSpec as P

DEGREE = 3

center_value = 0.5
half_width = 2.0

VMEM = pltpu.VMEM
SMEM = pltpu.SMEM
HBM = pltpu.HBM
DMA = pltpu.SemaphoreType.DMA
LANES = 128
FEW = 4
MANY = 4
HEAD = 8
STRIDE = 4
FIRST = 1
LAST = 2


def spec(space):
    return pl.BlockSpec(memory_space=space)


def params(mib):
    return pltpu.CompilerParams(vmem_limit_bytes=mib * 1024 * 1024)


def round_up(n, step):
    return (n + step - 1) // step * step


def plan_kernel(
    n_row,
    piece_blocks,
    sent_at,
    load_at,
    bare_at,
    place,
    wanted_a,
    wanted_b,
    rows_a,
    cols_a,
    used_a,
    meta_b,
    out,
    seen,
):
    slot_count = rows_a.shape[0]
    own_half = place[1]

    def scan(row_of, col_of, used, at, sent, load):
        def step(s, carry):
            at, sent, load = carry
            half = row_of(s) // piece_blocks
            row = row_of(s) - half * piece_blocks
            inside = half == own_half
            piece = col_of(s) // piece_blocks
            kept = jnp.where(inside, row, piece_blocks)
            entry = HEAD + STRIDE * at
            out[entry] = s
            out[entry + 1] = row
            out[entry + 2] = piece
            out[entry + 3] = jnp.where(seen[kept] == 0, FIRST, 0)
            seen[kept] = entry
            out[load_at + load] = s
            before = sent
            for k in range(n_row):
                out[sent_at + STRIDE * sent] = load
                out[sent_at + STRIDE * sent + 1] = 2 * k + half
                out[sent_at + STRIDE * sent + 2] = piece
                asked = jnp.where(inside, wanted_a[k, 0], wanted_b[k, 0])
                sent = sent + (asked == row).astype(jnp.int32)
            return at + inside.astype(jnp.int32), sent, load + (sent > before).astype(jnp.int32)

        at, sent, load = lax.fori_loop(0, used, step, (at, sent, load))
        for _ in range(MANY):
            for base, end, spare in ((HEAD, at, piece_blocks), (sent_at, sent, 2 * n_row)):
                entry = base + STRIDE * end
                out[entry] = 0
                out[entry + 1] = spare
                out[entry + 2] = 0
                out[entry + 3] = 0
            at = at + jnp.where(at % MANY == 0, 0, 1)
            sent = sent + jnp.where(sent % FEW == 0, 0, 1)
        return at, sent, load

    for b in range(piece_blocks + 1):
        seen[b] = 0
    zero = jnp.int32(0)
    at, sent, load = scan(
        lambda s: rows_a[s], lambda s: cols_a[s], used_a[0], zero, zero, zero
    )
    out[0] = at
    out[2] = sent
    out[4] = load
    at, sent, load = scan(
        lambda s: meta_b[s],
        lambda s: meta_b[slot_count + s],
        meta_b[2 * slot_count],
        at,
        sent,
        load,
    )
    out[1] = at
    out[3] = sent
    out[5] = load

    def close(b, bare):
        entry = seen[b]
        out[bare_at + bare] = b

        @pl.when(entry > 0)
        def _():
            out[entry + 3] = out[entry + 3] + LAST

        return bare + jnp.where(entry == 0, 1, 0)

    out[6] = lax.fori_loop(0, piece_blocks, close, zero)
    out[7] = own_half


def pick_kernel(n_row, block_size, wanted, vectors, out, held, in_sems, out_sems):
    def fetch(k):
        at = pl.multiple_of(wanted[k, 0] * block_size, block_size)
        return pltpu.make_async_copy(vectors.at[pl.ds(at, block_size)], held.at[k], in_sems.at[k])

    def put(k):
        return pltpu.make_async_copy(held.at[k], out.at[k], out_sems.at[k])

    for k in range(n_row):
        fetch(k).start()
    for k in range(n_row):
        fetch(k).wait()
        put(k).start()
    for k in range(n_row):
        put(k).wait()


def load_kernel(base, stride, ends, plan, tile_a, tile_b, blocks, sems):
    mid, end = plan[ends], plan[ends + 1]

    def copy(tile, i):
        slot = plan[base + stride * i]
        return pltpu.make_async_copy(tile.at[slot], blocks.at[i], sems.at[i])

    @pl.loop(0, mid)
    def _(i):
        copy(tile_a, i).start()

    @pl.loop(mid, end)
    def _(i):
        copy(tile_b, i).start()

    @pl.loop(0, end)
    def _(i):
        copy(tile_a, i).wait()


def load_both_kernel(base, stride, ends, plan, tile_a, tile_b, array, blocks, held, sems, held_sem):
    copy = pltpu.make_async_copy(array, held, held_sem)
    copy.start()
    load_kernel(base, stride, ends, plan, tile_a, tile_b, blocks, sems)
    copy.wait()


def each_product(plan, base, ends, blocks, pieces, use, then=None, before=None):
    mid, end = plan[ends], plan[ends + 1]
    unroll = MANY if base == HEAD else FEW

    def run(piece_ref, begin, end):
        @pl.loop(begin // unroll, end // unroll)
        def _(j):
            if before is not None:
                for u in range(unroll):
                    before(unroll * j + u)
            for u in range(unroll):
                i = unroll * j + u
                entry = base + STRIDE * i
                block = blocks[i if base == HEAD else plan[entry]]
                use(
                    entry,
                    jnp.dot(block, piece_ref[plan[entry + 2]], preferred_element_type=jnp.float32),
                )
            if then is not None:
                for u in range(unroll):
                    then(base + STRIDE * (unroll * j + u))

    run(pieces[0], 0, mid)
    run(pieces[1], mid, end)


def add_products(plan, base, ends, blocks, pieces, total):
    def use(entry, value):
        total[plan[entry + 1]] += value

    each_product(plan, base, ends, blocks, pieces, use)


def lanes_of(shape, half):
    column = lax.broadcasted_iota(jnp.int32, shape, 1)
    return (column // (shape[1] // 2)) == half


def only_half(vec, side, pieces, half):
    keep = jnp.where(lanes_of((1, vec.shape[-1]), half), 1.0, 0.0).astype(jnp.bfloat16)
    for p in range(vec.shape[1]):
        vec[side, p] = pieces[p] * keep


def joined(total, k):
    one, two = total[2 * k], total[2 * k + 1]
    low = lanes_of(one.shape, 0)
    return jnp.where(low, one, two) + pltpu.roll(
        jnp.where(low, two, one), one.shape[1] // 2, axis=1
    )


def first_sent_kernel(
    sent_at, plan, blocks, pieces, others, picked, picked_b, out, start, vec, total, held, held_sems
):
    n_row = out.shape[0]
    half = plan[7]
    copies = [
        pltpu.make_async_copy(source, held.at[i], held_sems.at[i])
        for i, source in enumerate((picked, picked_b))
    ]
    for copy in copies:
        copy.start()
    only_half(vec, 0, pieces, half)
    only_half(vec, 1, others, half)
    total[...] = jnp.zeros_like(total)
    add_products(plan, sent_at, 2, blocks, (vec.at[0], vec.at[1]), total)
    for copy in copies:
        copy.wait()
    mine = lanes_of(out.shape[1:], half)
    for k in range(n_row):
        own = held[0, k].astype(jnp.float32)
        other = pltpu.roll(held[1, k].astype(jnp.float32), out.shape[2] // 2, axis=1)
        value = jnp.where(mine, own, other)
        start[k] = value.astype(jnp.bfloat16)
        out[k] = ((joined(total, k) - center_value * value) / half_width).astype(jnp.bfloat16)


def second_sent_kernel(
    sent_at, plan, blocks, pieces, previous, current, out, vec, total, ready, out_sems
):
    n_row = out.shape[0]
    half = plan[7]
    only_half(vec, 0, pieces, half)
    only_half(vec, 1, pieces, 1 - half)
    total[...] = jnp.zeros_like(total)
    add_products(plan, sent_at, 2, blocks, (vec.at[0], vec.at[1]), total)

    def put(k):
        return pltpu.make_async_copy(ready.at[k], out.at[k], out_sems.at[k])

    for k in range(n_row):
        value = joined(total, k) - center_value * current[k].astype(jnp.float32)
        ready[k] = (value - previous[k].astype(jnp.float32)).astype(jnp.bfloat16)
        put(k).start()
    for k in range(n_row):
        put(k).wait()


def whole_columns(half, mine, other, vec, at):
    n_row, _, width = mine.shape
    middle = width // 2

    def merge(lower, upper, sides):
        @pl.loop(0, n_row)
        def _(p):
            for side, column in sides:
                part = slice(column * middle, (column + 1) * middle)
                vec[side, p, :, at : at + middle] = lower[p, :, part]
                vec[side, p, :, at + middle : at + width] = upper[p, :, part]

    @pl.when(half == 0)
    def _():
        merge(mine, other, ((0, 0), (1, 1)))

    @pl.when(half == 1)
    def _():
        merge(other, mine, ((0, 1), (1, 0)))


def rows(b, block_size):
    return pl.ds(pl.multiple_of(b * block_size, block_size), block_size)


def first_kernel(
    which, plan, tile_a, tile_b, pieces, others, vectors, *rest
):
    out, total, own, blocks, own_sem, sems, row_sems = rest[-7:]
    piece_blocks, block_size, _ = out.shape

    def fetch(tile, i):
        slot = plan[HEAD + STRIDE * i]
        return pltpu.make_async_copy(tile.at[slot], blocks.at[i], sems.at[i])

    def put(b):
        return pltpu.make_async_copy(own.at[rows(b, block_size)], out.at[b], row_sems.at[b])

    @pl.when(plan[7] == which)
    def _():
        copy = pltpu.make_async_copy(vectors, own, own_sem)
        copy.start()

        @pl.loop(0, plan[0])
        def _(i):
            fetch(tile_a, i).start()

        @pl.loop(plan[0], plan[1])
        def _(i):
            fetch(tile_b, i).start()

        copy.wait()

        @pl.loop(0, piece_blocks)
        def _(b):
            total[b] = -center_value * own[rows(b, block_size), :].astype(jnp.float32)

        def use(entry, value):
            total[plan[entry + 1]] += value

        each_product(
            plan,
            HEAD,
            0,
            blocks,
            (pieces, others),
            use,
            before=lambda i: fetch(tile_a, i).wait(),
        )

        @pl.loop(0, piece_blocks)
        def _(b):
            own[rows(b, block_size), :] = (total[b] / half_width).astype(jnp.bfloat16)
            put(b).start()

        @pl.loop(0, piece_blocks)
        def _(b):
            put(b).wait()


def early_kernel(
    plan, blocks, mine, other, first, vectors, base, vec, total, own, older, sems, row_sems
):
    piece_blocks, block_size, _ = base.shape
    copies = [
        pltpu.make_async_copy(vectors, older, sems.at[0]),
        pltpu.make_async_copy(first, own, sems.at[1]),
    ]
    for copy in copies:
        copy.start()
    whole_columns(plan[7], mine, other, vec, 0)
    for copy in copies:
        copy.wait()

    def put(b):
        return pltpu.make_async_copy(own.at[b], base.at[b], row_sems.at[b])

    @pl.loop(0, piece_blocks)
    def _(b):
        total[b] = -center_value * own[b].astype(jnp.float32) - older[
            rows(b, block_size), :
        ].astype(jnp.float32)

    add_products(plan, HEAD, 0, blocks, (vec.at[0], vec.at[1]), total)

    @pl.loop(0, piece_blocks)
    def _(b):
        second = total[b].astype(jnp.bfloat16).astype(jnp.float32)
        own[b] = (-center_value * second - own[b].astype(jnp.float32)).astype(jnp.bfloat16)
        put(b).start()

    @pl.loop(0, piece_blocks)
    def _(b):
        put(b).wait()


def last_kernel(bare_at, plan, blocks, mine, other, base, out, vec, total, own, row_sems):
    piece_blocks = base.shape[0]

    def put(source, b):
        return pltpu.make_async_copy(source.at[b], out.at[b], row_sems.at[b])

    @pl.loop(0, plan[6])
    def _(i):
        b = plan[bare_at + i]
        put(base, b).start()

    whole_columns(plan[7], mine, other, vec, 0)

    def use(entry, value):
        row = plan[entry + 1]
        marks = plan[entry + 3]
        start = base[jnp.minimum(row, piece_blocks - 1)].astype(jnp.float32)
        value = jnp.where(lax.rem(marks, LAST) == FIRST, start, total[row]) + value
        total[row] = value
        own[row] = value.astype(jnp.bfloat16)

    def then(entry):
        @pl.when(plan[entry + 3] >= LAST)
        def _():
            put(own, plan[entry + 1]).start()

    each_product(plan, HEAD, 0, blocks, (vec.at[0], vec.at[1]), use, then)

    @pl.loop(0, piece_blocks)
    def _(b):
        put(own, b).wait()


def after(value, *others):
    return lax.optimization_barrier((value, *others))[0]


def call(kernel, out, args, spaces, scratch, mib, name, estimate=None, aliases=None):
    args = [
        pltpu.with_memory_space_constraint(arg, space) if space in (VMEM, HBM) or tied else arg
        for arg, (space, tied) in zip(args, spaces)
    ]
    return pl.pallas_call(
        kernel,
        out_shape=[space(shape, dtype) for shape, dtype, space in out],
        in_specs=[spec(space) for space, _ in spaces],
        out_specs=[spec(space) for _, _, space in out],
        scratch_shapes=scratch,
        compiler_params=params(mib),
        cost_estimate=estimate,
        input_output_aliases=aliases or {},
        name=name,
    )(*args)


HERE = (VMEM, True)
FAR = (HBM, True)
LIST = (SMEM, True)
SCALARS = (SMEM, False)
ANYWHERE = (pl.ANY, False)


def on_pair(vectors, tile_blocks, block_rows, block_cols, counts):
    n_row = lax.axis_size("row")
    tile = tile_blocks[0, 0]
    slot_rows = block_rows[0, 0]
    slot_cols = block_cols[0, 0]
    used = counts[0]
    slot_count, block_size, _ = tile.shape
    width = vectors.shape[1]
    piece_blocks = vectors.shape[0] // block_size
    place = jnp.stack([lax.axis_index("row"), lax.axis_index("col")]).astype(jnp.int32)

    across = functools.partial(lax.ppermute, axis_name="col", perm=[(0, 1), (1, 0)])

    needed = jnp.max(
        jnp.where(
            slot_cols[None, :] // piece_blocks == jnp.arange(n_row)[:, None],
            slot_cols[None, :] % piece_blocks,
            0,
        ),
        axis=1,
        keepdims=True,
    )
    exchange = functools.partial(
        lax.all_to_all, axis_name="row", split_axis=0, concat_axis=0, tiled=True
    )
    wanted = exchange(jnp.broadcast_to(needed, (n_row, LANES)))
    sent_shape = (n_row, block_size, width)
    (sent,) = call(
        functools.partial(pick_kernel, n_row, block_size),
        [(sent_shape, jnp.bfloat16, HBM)],
        (wanted, vectors),
        (SCALARS, FAR),
        [VMEM(sent_shape, jnp.bfloat16), DMA((n_row,)), DMA((n_row,))],
        2,
        "pick",
    )
    tile_other = across(tile)
    wanted_other = across(after(wanted, sent))
    meta = across(after(jnp.concatenate([slot_rows, slot_cols, used]), sent))
    sent_other = across(sent)

    capacity = 2 * round_up(slot_count, MANY)
    sent_at = HEAD + STRIDE * (capacity + 1)
    load_at = sent_at + STRIDE * (4 * n_row * n_row + 2 * FEW + 1)
    bare_at = load_at + 2 * slot_count + 1
    plan_size = bare_at + piece_blocks
    (plan,) = call(
        functools.partial(plan_kernel, n_row, piece_blocks, sent_at, load_at, bare_at),
        [((plan_size,), jnp.int32, SMEM)],
        (place, wanted, wanted_other, slot_rows, slot_cols, used, meta),
        (SCALARS,) * 7,
        [SMEM((piece_blocks + 1,), jnp.int32)],
        2,
        "plan",
    )
    def load(base, stride, ends, cue, *array):
        kernel = load_both_kernel if array else load_kernel
        return call(
            functools.partial(kernel, base, stride, ends),
            [((capacity, block_size, block_size), jnp.bfloat16, VMEM)]
            + [(held.shape, held.dtype, VMEM) for held in array],
            (after(plan, cue), tile, tile_other, *array),
            (LIST, FAR, ANYWHERE) + (FAR,) * len(array),
            [DMA((capacity,))] + [DMA] * len(array),
            2,
            "load",
        )

    def cost(products, rows):
        size = block_size * width
        return pl.CostEstimate(
            flops=2 * products * block_size * size,
            bytes_accessed=2 * (products * block_size * block_size + 3 * rows * size),
            transcendentals=0,
        )

    sums = [
        VMEM((2, n_row, block_size, width), jnp.bfloat16),
        VMEM((2 * n_row + 1, block_size, width), jnp.float32),
    ]

    def first_blocks(*args):
        return call(
            functools.partial(first_sent_kernel, sent_at),
            [(sent_shape, jnp.bfloat16, VMEM)] * 2,
            (plan, *args),
            (LIST, HERE, HERE, HERE, FAR, FAR),
            sums + [VMEM((2, *sent_shape), jnp.bfloat16), DMA((2,))],
            8,
            "sent",
            cost(n_row, n_row),
        )

    def second_blocks(*args):
        return call(
            functools.partial(second_sent_kernel, sent_at),
            [(sent_shape, jnp.bfloat16, HBM)],
            (plan, *args),
            (LIST, HERE, HERE, HERE, HERE),
            sums + [VMEM(sent_shape, jnp.bfloat16), DMA((n_row,))],
            8,
            "sent",
            cost(n_row, n_row),
        )[0]

    base_shape = (piece_blocks, block_size, width)

    def first_rows(which, cue, *args):
        return call(
            functools.partial(first_kernel, which),
            [(base_shape, jnp.bfloat16, HBM)],
            (after(plan, cue), tile, tile_other, *args),
            (LIST, FAR, ANYWHERE, HERE, HERE, FAR) + (FAR,) * (len(args) - 3),
            [
                VMEM((piece_blocks + 1, block_size, width), jnp.float32),
                VMEM(vectors.shape, jnp.bfloat16),
                VMEM((capacity, block_size, block_size), jnp.bfloat16),
                DMA,
                DMA((capacity,)),
                DMA((piece_blocks,)),
            ],
            18,
            "first",
            cost(slot_count, 2 * piece_blocks),
            {6: 0} if len(args) > 3 else None,
        )[0]

    def early(*args):
        return call(
            early_kernel,
            [(base_shape, jnp.bfloat16, HBM)],
            (plan, *args),
            (LIST, HERE, HERE, HERE, FAR, FAR),
            [
                VMEM((2, n_row, block_size, width), jnp.bfloat16),
                VMEM((piece_blocks + 1, block_size, width), jnp.float32),
                VMEM(base_shape, jnp.bfloat16),
                VMEM(vectors.shape, jnp.bfloat16),
                DMA((2,)),
                DMA((piece_blocks,)),
            ],
            12,
            "early",
            cost(slot_count, 2 * piece_blocks),
        )[0]

    def last(blocks, *args):
        rows = (piece_blocks + 1, block_size, width)
        (out,) = call(
            functools.partial(last_kernel, bare_at),
            [(base_shape, jnp.bfloat16, HBM)],
            (plan, blocks, *args),
            (LIST,) + (HERE,) * 4,
            [
                VMEM((2, n_row, block_size, width), jnp.bfloat16),
                VMEM(rows, jnp.float32),
                VMEM(rows, jnp.bfloat16),
                DMA((piece_blocks,)),
            ],
            9,
            "last",
            cost(slot_count, piece_blocks),
        )
        return out.reshape(vectors.shape)

    p1 = after(exchange(sent), plan, sent_other)
    o1 = across(p1)
    (blocks,) = load(load_at, 1, 4, p1)
    first_sent, start = first_blocks(blocks, p1, o1, sent, sent_other)
    first = first_rows(0, first_sent, p1, o1, vectors)
    q2 = exchange(after(first_sent, first))
    second_sent = second_blocks(blocks, q2, start, first_sent)
    first = first_rows(1, second_sent, p1, o1, vectors, first)
    q2_other = across(after(q2, first))
    (blocks,) = load(HEAD, STRIDE, 0, first)
    base = early(blocks, q2, q2_other, first, vectors)
    q3 = after(exchange(second_sent), base)
    q3_other = across(q3)
    blocks, base = load(HEAD, STRIDE, 0, q3, base)
    return last(blocks, q3, q3_other, base)


def on_any(vectors, tile_blocks, block_rows, block_cols, counts):
    n_row = lax.axis_size("row")
    n_col = lax.axis_size("col")
    tile_data = tile_blocks[0, 0]
    slot_rows = block_rows[0, 0]
    slot_cols = block_cols[0, 0]
    used = counts[0, 0]
    block_size = tile_data.shape[-1]
    width = vectors.shape[1]
    piece_blocks = vectors.shape[0] // block_size
    row_blocks = piece_blocks * n_col
    slot_count = tile_data.shape[0]
    live = (jnp.arange(slot_count) < used).astype(jnp.float32)
    onehot = (slot_rows[None, :] == jnp.arange(row_blocks)[:, None]).astype(jnp.float32) * live[
        None, :
    ]
    source_piece = slot_cols // piece_blocks
    offset = slot_cols % piece_blocks
    needed = jnp.max(
        jnp.where(source_piece[None, :] == jnp.arange(n_row)[:, None], offset[None, :], 0), axis=1
    )
    wanted = lax.all_to_all(
        needed.reshape(n_row, 1), "row", split_axis=0, concat_axis=0, tiled=True
    ).reshape(n_row)

    def apply_tiles(current):
        own_blocks = current.reshape(piece_blocks, block_size, width)
        outgoing = jnp.take(own_blocks, wanted, axis=0)
        received = lax.all_to_all(outgoing, "row", split_axis=0, concat_axis=0, tiled=True)
        vec_blocks = jnp.take(received, source_piece, axis=0)
        products = jnp.einsum(
            "sij,sjk->sik", tile_data, vec_blocks, preferred_element_type=jnp.float32
        )
        term = jnp.einsum("ls,sik->lik", onehot, products, precision=lax.Precision.HIGHEST)
        term = term.reshape(row_blocks * block_size, width)
        return lax.psum_scatter(
            term.astype(jnp.bfloat16), "col", scatter_dimension=0, tiled=True
        ).astype(jnp.float32)

    previous = vectors
    applied = apply_tiles(vectors)
    current = ((applied - center_value * previous.astype(jnp.float32)) / half_width).astype(
        jnp.bfloat16
    )
    for repeat in range(DEGREE - 1):
        applied = apply_tiles(current)
        following = (
            2.0 * (applied - center_value * current.astype(jnp.float32)) / half_width
            - previous.astype(jnp.float32)
        ).astype(jnp.bfloat16)
        previous, current = (current, following)
    return current


def solution(mesh):
    n_row, n_col = mesh.shape["row"], mesh.shape["col"]
    paired = n_col == 2 and n_row & (n_row - 1) == 0
    return jax.shard_map(
        on_pair if paired else on_any,
        mesh=mesh,
        in_specs=(
            P(("row", "col"), "vec"),
            P("row", "col", None, None, None),
            P("row", "col", None),
            P("row", "col", None),
            P("row", "col"),
        ),
        out_specs=P(("row", "col"), "vec"),
        check_vma=False,
    )
```

```python
import functools

import jax
import jax.numpy as jnp
from jax import lax
from jax.experimental import pallas as pl
from jax.experimental.pallas import tpu as pltpu
from jax.sharding import PartitionSpec as P

DEGREE = 3

center_value = 0.5
half_width = 2.0

VMEM = pltpu.VMEM
SMEM = pltpu.SMEM
HBM = pltpu.HBM
DMA = pltpu.SemaphoreType.DMA
LANES = 128
FEW = 4
MANY = 4
HEAD = 8
STRIDE = 4
FIRST = 1
LAST = 2


def spec(space):
    return pl.BlockSpec(memory_space=space)


def params(mib):
    return pltpu.CompilerParams(vmem_limit_bytes=mib * 1024 * 1024)


def round_up(n, step):
    return (n + step - 1) // step * step


def plan_kernel(
    n_row, piece_blocks, sent_at, load_at, bare_at, size, place, wanted_a, wanted_b, meta_a, meta_b, out, seen
):
    slot_count = (meta_a.shape[0] - 1) // 2

    def scan(base, own_half, meta, asked_own, asked_other, at, sent, load):
        def step(s, carry):
            at, sent, load = carry
            half = meta[s] // piece_blocks
            row = meta[s] - half * piece_blocks
            inside = half == own_half
            piece = meta[slot_count + s] // piece_blocks
            kept = jnp.where(inside, row, piece_blocks)
            entry = HEAD + STRIDE * at
            out[base + entry] = s
            out[base + entry + 1] = row
            out[base + entry + 2] = piece
            out[base + entry + 3] = jnp.where(seen[kept] == 0, FIRST, 0)
            seen[kept] = entry
            out[base + load_at + load] = s
            side = jnp.where(inside, 0, 1)
            before = sent
            for k in range(n_row):
                out[base + sent_at + STRIDE * sent] = load
                out[base + sent_at + STRIDE * sent + 1] = 2 * k + side
                out[base + sent_at + STRIDE * sent + 2] = piece
                asked = jnp.where(inside, asked_own[k, 0], asked_other[k, 0])
                sent = sent + (asked == row).astype(jnp.int32)
            return at + inside.astype(jnp.int32), sent, load + (sent > before).astype(jnp.int32)

        at, sent, load = lax.fori_loop(0, meta[2 * slot_count], step, (at, sent, load))
        for _ in range(MANY):
            for start, end, spare in ((HEAD, at, piece_blocks), (sent_at, sent, 2 * n_row)):
                entry = base + start + STRIDE * end
                out[entry] = 0
                out[entry + 1] = spare
                out[entry + 2] = 0
                out[entry + 3] = 0
            at = at + jnp.where(at % MANY == 0, 0, 1)
            sent = sent + jnp.where(sent % FEW == 0, 0, 1)
        return at, sent, load

    def lists(base, own_half, meta_own, meta_other, asked_own, asked_other):
        for b in range(piece_blocks + 1):
            seen[b] = 0
        ends = (jnp.int32(0),) * 3
        for tile, meta in enumerate((meta_own, meta_other)):
            ends = scan(base, own_half, meta, asked_own, asked_other, *ends)
            for i, end in enumerate(ends):
                out[base + 2 * i + tile] = end

        def close(b, bare):
            entry = seen[b]
            out[base + bare_at + bare] = b

            @pl.when(entry > 0)
            def _():
                out[base + entry + 3] = out[base + entry + 3] + LAST

            return bare + jnp.where(entry == 0, 1, 0)

        out[base + 6] = lax.fori_loop(0, piece_blocks, close, jnp.int32(0))
        out[base + 7] = own_half

    @pl.when(place[1] == 0)
    def _():
        lists(0, 0, meta_a, meta_b, wanted_a, wanted_b)
        lists(size, 1, meta_b, meta_a, wanted_b, wanted_a)


def settle_kernel(place, own, handed, out):
    @pl.when(place[1] == 0)
    def _():
        @pl.loop(0, out.shape[0])
        def _(i):
            out[i] = own[i]

    @pl.when(place[1] != 0)
    def _():
        @pl.loop(0, out.shape[0])
        def _(i):
            out[i] = handed[i]


def pick_kernel(n_row, block_size, wanted, vectors, out, held, in_sems, out_sems):
    def fetch(k):
        at = pl.multiple_of(wanted[k, 0] * block_size, block_size)
        return pltpu.make_async_copy(vectors.at[pl.ds(at, block_size)], held.at[k], in_sems.at[k])

    def put(k):
        return pltpu.make_async_copy(held.at[k], out.at[k], out_sems.at[k])

    for k in range(n_row):
        fetch(k).start()
    for k in range(n_row):
        fetch(k).wait()
        put(k).start()
    for k in range(n_row):
        put(k).wait()


def pack_kernel(place, picked, picked_b, out, held, in_sems, out_sems):
    n_row, _, width = picked.shape
    middle = width // 2

    def fetch(source, side, k):
        return pltpu.make_async_copy(source.at[k], held.at[side, k], in_sems.at[side, k])

    def put(k):
        return pltpu.make_async_copy(held.at[0, k], out.at[k], out_sems.at[k])

    for k in range(n_row):
        fetch(picked, 0, k).start()
        fetch(picked_b, 1, k).start()
    for k in range(n_row):
        fetch(picked, 0, k).wait()
        fetch(picked_b, 1, k).wait()
        for half in range(2):

            @pl.when(place[1] == half)
            def _():
                part = slice(half * middle, (half + 1) * middle)
                held[0, k] = jnp.concatenate([held[0, k, :, part], held[1, k, :, part]], axis=1)

        put(k).start()
    for k in range(n_row):
        put(k).wait()


def load_kernel(base, stride, ends, plan, tile_a, tile_b, blocks, sems):
    mid, end = plan[ends], plan[ends + 1]

    def copy(tile, i):
        slot = plan[base + stride * i]
        return pltpu.make_async_copy(tile.at[slot], blocks.at[i], sems.at[i])

    @pl.loop(0, mid)
    def _(i):
        copy(tile_a, i).start()

    @pl.loop(mid, end)
    def _(i):
        copy(tile_b, i).start()

    @pl.loop(0, end)
    def _(i):
        copy(tile_a, i).wait()


def load_both_kernel(base, stride, ends, plan, tile_a, tile_b, array, blocks, held, sems, held_sem):
    copy = pltpu.make_async_copy(array, held, held_sem)
    copy.start()
    load_kernel(base, stride, ends, plan, tile_a, tile_b, blocks, sems)
    copy.wait()


def each_product(plan, base, ends, blocks, pieces, use, then=None):
    mid, end = plan[ends], plan[ends + 1]
    unroll = MANY if base == HEAD else FEW

    def run(piece_ref, begin, end):
        @pl.loop(begin // unroll, end // unroll)
        def _(j):
            for u in range(unroll):
                i = unroll * j + u
                entry = base + STRIDE * i
                block = blocks[i if base == HEAD else plan[entry]]
                use(
                    entry,
                    jnp.dot(block, piece_ref[plan[entry + 2]], preferred_element_type=jnp.float32),
                )
            if then is not None:
                for u in range(unroll):
                    then(base + STRIDE * (unroll * j + u))

    run(pieces[0], 0, mid)
    run(pieces[1], mid, end)


def add_products(plan, base, ends, blocks, pieces, total):
    def use(entry, value):
        total[plan[entry + 1]] += value

    each_product(plan, base, ends, blocks, pieces, use)


def split_sides(pieces, vec):
    middle = vec.shape[-1] // 2
    column = lax.broadcasted_iota(jnp.int32, (1, vec.shape[-1]), 1)
    for side in range(2):
        keep = jnp.where((column // middle) == side, 1.0, 0.0).astype(jnp.bfloat16)
        for p in range(vec.shape[1]):
            vec[side, p] = pieces[p] * keep


def joined(total, k):
    one, two = total[2 * k], total[2 * k + 1]
    low = lax.broadcasted_iota(jnp.int32, one.shape, 1) < one.shape[1] // 2
    return jnp.where(low, one, two) + pltpu.roll(
        jnp.where(low, two, one), one.shape[1] // 2, axis=1
    )


def first_sent_kernel(
    sent_at, load_at, plan, tile_a, tile_b, pieces, start, out, blocks, vec, total, held, held_sem, sems
):
    n_row = out.shape[0]
    mid, end = plan[4], plan[5]

    def fetch(tile, i):
        return pltpu.make_async_copy(tile.at[plan[load_at + i]], blocks.at[i], sems.at[i])

    @pl.loop(0, mid)
    def _(i):
        fetch(tile_a, i).start()

    @pl.loop(mid, end)
    def _(i):
        fetch(tile_b, i).start()

    copy = pltpu.make_async_copy(start, held, held_sem)
    copy.start()
    split_sides(pieces, vec)
    total[...] = jnp.zeros_like(total)

    @pl.loop(0, end)
    def _(i):
        fetch(tile_a, i).wait()

    add_products(plan, sent_at, 2, blocks, (vec.at[0], vec.at[1]), total)
    copy.wait()
    for k in range(n_row):
        value = joined(total, k) - center_value * held[k].astype(jnp.float32)
        out[k] = (value / half_width).astype(jnp.bfloat16)


def second_sent_kernel(
    sent_at, plan, blocks, pieces, current, previous, out, vec, total, held, held_sem, ready, out_sems
):
    n_row = out.shape[0]
    copy = pltpu.make_async_copy(previous, held, held_sem)
    copy.start()
    split_sides(pieces, vec)
    total[...] = jnp.zeros_like(total)
    add_products(plan, sent_at, 2, blocks, (vec.at[0], vec.at[1]), total)
    copy.wait()

    def put(k):
        return pltpu.make_async_copy(ready.at[k], out.at[k], out_sems.at[k])

    for k in range(n_row):
        value = joined(total, k) - center_value * current[k].astype(jnp.float32)
        ready[k] = (value - held[k].astype(jnp.float32)).astype(jnp.bfloat16)
        put(k).start()
    for k in range(n_row):
        put(k).wait()


def whole_columns(half, mine, other, vec, at):
    n_row, _, width = mine.shape
    middle = width // 2

    @pl.when(half == 0)
    def _():
        @pl.loop(0, n_row)
        def _(p):
            one, two = mine[p], other[p]
            vec[0, p, :, at : at + width] = jnp.concatenate([one[:, :middle], two[:, middle:]], axis=1)
            vec[1, p, :, at : at + width] = jnp.concatenate([one[:, middle:], two[:, :middle]], axis=1)

    @pl.when(half != 0)
    def _():
        @pl.loop(0, n_row)
        def _(p):
            one, two = mine[p], other[p]
            vec[0, p, :, at : at + width] = jnp.concatenate([two[:, middle:], one[:, :middle]], axis=1)
            vec[1, p, :, at : at + width] = jnp.concatenate([two[:, :middle], one[:, middle:]], axis=1)


def early_kernel(plan, blocks, q1, q1_other, q2, q2_other, vectors, base, vec, total, own, sem, row_sems):
    width = vectors.shape[1]
    piece_blocks, block_size, _ = base.shape
    copy = pltpu.make_async_copy(vectors, own, sem)
    copy.start()
    whole_columns(plan[7], q1, q1_other, vec, 0)
    whole_columns(plan[7], q2, q2_other, vec, width)
    copy.wait()

    def rows(b):
        return pl.ds(pl.multiple_of(b * block_size, block_size), block_size)

    def put(b):
        return pltpu.make_async_copy(own.at[rows(b)], base.at[b], row_sems.at[b])

    @pl.loop(0, piece_blocks)
    def _(b):
        value = own[rows(b), :].astype(jnp.float32)
        total[b, :, :width] = -center_value * value
        total[b, :, width:] = -value

    add_products(plan, HEAD, 0, blocks, (vec.at[0], vec.at[1]), total)

    @pl.loop(0, piece_blocks)
    def _(b):
        first = (total[b, :, :width] / half_width).astype(jnp.bfloat16).astype(jnp.float32)
        second = total[b, :, width:] - center_value * first
        second = second.astype(jnp.bfloat16).astype(jnp.float32)
        own[rows(b), :] = (-center_value * second - first).astype(jnp.bfloat16)
        put(b).start()

    @pl.loop(0, piece_blocks)
    def _(b):
        put(b).wait()


def last_kernel(bare_at, plan, blocks, mine, other, base, out, vec, total, own, row_sems):
    piece_blocks = base.shape[0]

    def put(source, b):
        return pltpu.make_async_copy(source.at[b], out.at[b], row_sems.at[b])

    @pl.loop(0, plan[6])
    def _(i):
        b = plan[bare_at + i]
        put(base, b).start()

    whole_columns(plan[7], mine, other, vec, 0)

    def use(entry, value):
        row = plan[entry + 1]
        marks = plan[entry + 3]
        start = base[jnp.minimum(row, piece_blocks - 1)].astype(jnp.float32)
        value = jnp.where(lax.rem(marks, LAST) == FIRST, start, total[row]) + value
        total[row] = value
        own[row] = value.astype(jnp.bfloat16)

    def then(entry):
        @pl.when(plan[entry + 3] >= LAST)
        def _():
            put(own, plan[entry + 1]).start()

    each_product(plan, HEAD, 0, blocks, (vec.at[0], vec.at[1]), use, then)

    @pl.loop(0, piece_blocks)
    def _(b):
        put(own, b).wait()


def after(value, *others):
    return lax.optimization_barrier((value, *others))[0]


def call(kernel, out, args, spaces, scratch, mib, name, estimate=None):
    args = [
        pltpu.with_memory_space_constraint(arg, space) if space in (VMEM, HBM) or tied else arg
        for arg, (space, tied) in zip(args, spaces)
    ]
    return pl.pallas_call(
        kernel,
        out_shape=[space(shape, dtype) for shape, dtype, space in out],
        in_specs=[spec(space) for space, _ in spaces],
        out_specs=[spec(space) for _, _, space in out],
        scratch_shapes=scratch,
        compiler_params=params(mib),
        cost_estimate=estimate,
        name=name,
    )(*args)


HERE = (VMEM, True)
FAR = (HBM, True)
LIST = (SMEM, True)
SCALARS = (SMEM, False)
ANYWHERE = (pl.ANY, False)


def on_pair(vectors, tile_blocks, block_rows, block_cols, counts):
    n_row = lax.axis_size("row")
    tile = tile_blocks[0, 0]
    slot_rows = block_rows[0, 0]
    slot_cols = block_cols[0, 0]
    used = counts[0]
    slot_count, block_size, _ = tile.shape
    width = vectors.shape[1]
    piece_blocks = vectors.shape[0] // block_size
    place = jnp.stack([lax.axis_index("row"), lax.axis_index("col")]).astype(jnp.int32)

    across = functools.partial(lax.ppermute, axis_name="col", perm=[(0, 1), (1, 0)])

    needed = jnp.max(
        jnp.where(
            slot_cols[None, :] // piece_blocks == jnp.arange(n_row)[:, None],
            slot_cols[None, :] % piece_blocks,
            0,
        ),
        axis=1,
        keepdims=True,
    )
    exchange = functools.partial(
        lax.all_to_all, axis_name="row", split_axis=0, concat_axis=0, tiled=True
    )
    wanted = exchange(jnp.broadcast_to(needed, (n_row, LANES)))
    sent_shape = (n_row, block_size, width)
    (sent,) = call(
        functools.partial(pick_kernel, n_row, block_size),
        [(sent_shape, jnp.bfloat16, HBM)],
        (wanted, vectors),
        (SCALARS, FAR),
        [VMEM(sent_shape, jnp.bfloat16), DMA((n_row,)), DMA((n_row,))],
        2,
        "pick",
    )
    tile_other = across(tile)
    meta = jnp.concatenate([slot_rows, slot_cols, used])
    sent_other = across(sent)
    wanted_other = across(after(wanted, sent))
    meta_other = across(after(meta, sent))
    packed = call(
        pack_kernel,
        [(sent_shape, jnp.bfloat16, HBM)],
        (place, sent, sent_other),
        (SCALARS, ANYWHERE, ANYWHERE),
        [VMEM((2, *sent_shape), jnp.bfloat16), DMA((2, n_row)), DMA((n_row,))],
        4,
        "pack",
    )[0]

    capacity = 2 * round_up(slot_count, MANY)
    sent_at = HEAD + STRIDE * (capacity + 1)
    load_at = sent_at + STRIDE * (4 * n_row * n_row + 2 * FEW + 1)
    bare_at = load_at + 2 * slot_count + 1
    plan_size = round_up(bare_at + piece_blocks, LANES)
    plans = call(
        functools.partial(plan_kernel, n_row, piece_blocks, sent_at, load_at, bare_at, plan_size),
        [((2 * plan_size,), jnp.int32, SMEM)],
        (place, wanted, wanted_other, meta, meta_other),
        (SCALARS,) * 5,
        [SMEM((piece_blocks + 1,), jnp.int32)],
        2,
        "plan",
    )[0]
    q1 = exchange(after(packed, plans))
    plan = call(
        settle_kernel,
        [((plan_size,), jnp.int32, SMEM)],
        (place, plans[:plan_size], across(after(plans[plan_size:], packed))),
        (SCALARS,) * 3,
        [],
        2,
        "settle",
    )[0]

    def load(base, stride, ends, cue, *array):
        kernel = load_both_kernel if array else load_kernel
        return call(
            functools.partial(kernel, base, stride, ends),
            [((capacity, block_size, block_size), jnp.bfloat16, VMEM)]
            + [(held.shape, held.dtype, VMEM) for held in array],
            (after(plan, cue), tile, tile_other, *array),
            (LIST, FAR, ANYWHERE) + (FAR,) * len(array),
            [DMA((capacity,))] + [DMA] * len(array),
            2,
            "load",
        )

    def cost(products, rows):
        size = block_size * width
        return pl.CostEstimate(
            flops=2 * products * block_size * size,
            bytes_accessed=2 * (products * block_size * block_size + 3 * rows * size),
            transcendentals=0,
        )

    sums = [
        VMEM((2, n_row, block_size, width), jnp.bfloat16),
        VMEM((2 * n_row + 1, block_size, width), jnp.float32),
    ]

    def first_blocks(*args):
        return call(
            functools.partial(first_sent_kernel, sent_at, load_at),
            [
                (sent_shape, jnp.bfloat16, VMEM),
                ((capacity, block_size, block_size), jnp.bfloat16, VMEM),
            ],
            (plan, tile, tile_other, *args),
            (LIST, FAR, ANYWHERE, HERE, FAR),
            sums + [VMEM(sent_shape, jnp.bfloat16), DMA, DMA((capacity,))],
            8,
            "sent",
            cost(n_row, n_row),
        )

    def second_blocks(*args):
        return call(
            functools.partial(second_sent_kernel, sent_at),
            [(sent_shape, jnp.bfloat16, HBM)],
            (plan, *args),
            (LIST, HERE, HERE, HERE, FAR),
            sums
            + [VMEM(sent_shape, jnp.bfloat16), DMA, VMEM(sent_shape, jnp.bfloat16), DMA((n_row,))],
            8,
            "sent",
            cost(n_row, n_row),
        )[0]

    base_shape = (piece_blocks, block_size, width)

    def early(*args):
        return call(
            early_kernel,
            [(base_shape, jnp.bfloat16, HBM)],
            (plan, *args),
            (LIST, HERE, HERE, HERE, HERE, HERE, FAR),
            [
                VMEM((2, n_row, block_size, 2 * width), jnp.bfloat16),
                VMEM((piece_blocks + 1, block_size, 2 * width), jnp.float32),
                VMEM(vectors.shape, jnp.bfloat16),
                DMA,
                DMA((piece_blocks,)),
            ],
            18,
            "early",
            cost(2 * slot_count, 2 * piece_blocks),
        )[0]

    def last(blocks, *args):
        rows = (piece_blocks + 1, block_size, width)
        (out,) = call(
            functools.partial(last_kernel, bare_at),
            [(base_shape, jnp.bfloat16, HBM)],
            (plan, blocks, *args),
            (LIST,) + (HERE,) * 4,
            [
                VMEM((2, n_row, block_size, width), jnp.bfloat16),
                VMEM(rows, jnp.float32),
                VMEM(rows, jnp.bfloat16),
                DMA((piece_blocks,)),
            ],
            9,
            "last",
            cost(slot_count, piece_blocks),
        )
        return out.reshape(vectors.shape)

    q1 = after(q1, plan)
    first_sent, blocks = first_blocks(q1, packed)
    q2 = exchange(first_sent)
    second_sent = second_blocks(blocks, q2, first_sent, packed)
    q1_other = across(after(q1, second_sent))
    q2_other = across(after(q2, second_sent))
    (blocks,) = load(HEAD, STRIDE, 0, second_sent)
    base = early(blocks, q1, q1_other, q2, q2_other, vectors)
    q3 = after(exchange(second_sent), base)
    q3_other = across(q3)
    blocks, base = load(HEAD, STRIDE, 0, q3, base)
    return last(blocks, q3, q3_other, base)


def on_any(vectors, tile_blocks, block_rows, block_cols, counts):
    n_row = lax.axis_size("row")
    n_col = lax.axis_size("col")
    tile_data = tile_blocks[0, 0]
    slot_rows = block_rows[0, 0]
    slot_cols = block_cols[0, 0]
    used = counts[0, 0]
    block_size = tile_data.shape[-1]
    width = vectors.shape[1]
    piece_blocks = vectors.shape[0] // block_size
    row_blocks = piece_blocks * n_col
    slot_count = tile_data.shape[0]
    live = (jnp.arange(slot_count) < used).astype(jnp.float32)
    onehot = (slot_rows[None, :] == jnp.arange(row_blocks)[:, None]).astype(jnp.float32) * live[
        None, :
    ]
    source_piece = slot_cols // piece_blocks
    offset = slot_cols % piece_blocks
    needed = jnp.max(
        jnp.where(source_piece[None, :] == jnp.arange(n_row)[:, None], offset[None, :], 0), axis=1
    )
    wanted = lax.all_to_all(
        needed.reshape(n_row, 1), "row", split_axis=0, concat_axis=0, tiled=True
    ).reshape(n_row)

    def apply_tiles(current):
        own_blocks = current.reshape(piece_blocks, block_size, width)
        outgoing = jnp.take(own_blocks, wanted, axis=0)
        received = lax.all_to_all(outgoing, "row", split_axis=0, concat_axis=0, tiled=True)
        vec_blocks = jnp.take(received, source_piece, axis=0)
        products = jnp.einsum(
            "sij,sjk->sik", tile_data, vec_blocks, preferred_element_type=jnp.float32
        )
        term = jnp.einsum("ls,sik->lik", onehot, products, precision=lax.Precision.HIGHEST)
        term = term.reshape(row_blocks * block_size, width)
        return lax.psum_scatter(
            term.astype(jnp.bfloat16), "col", scatter_dimension=0, tiled=True
        ).astype(jnp.float32)

    previous = vectors
    applied = apply_tiles(vectors)
    current = ((applied - center_value * previous.astype(jnp.float32)) / half_width).astype(
        jnp.bfloat16
    )
    for repeat in range(DEGREE - 1):
        applied = apply_tiles(current)
        following = (
            2.0 * (applied - center_value * current.astype(jnp.float32)) / half_width
            - previous.astype(jnp.float32)
        ).astype(jnp.bfloat16)
        previous, current = (current, following)
    return current


def solution(mesh):
    n_row, n_col = mesh.shape["row"], mesh.shape["col"]
    paired = n_col == 2 and n_row & (n_row - 1) == 0
    return jax.shard_map(
        on_pair if paired else on_any,
        mesh=mesh,
        in_specs=(
            P(("row", "col"), "vec"),
            P("row", "col", None, None, None),
            P("row", "col", None),
            P("row", "col", None),
            P("row", "col"),
        ),
        out_specs=P(("row", "col"), "vec"),
        check_vma=False,
    )
```

```python
import functools

import jax
import jax.numpy as jnp
from jax import lax
from jax.experimental import pallas as pl
from jax.experimental.pallas import tpu as pltpu
from jax.sharding import PartitionSpec as P

DEGREE = 3

center_value = 0.5
half_width = 2.0

VMEM = pltpu.VMEM
SMEM = pltpu.SMEM
HBM = pltpu.HBM
DMA = pltpu.SemaphoreType.DMA
LANES = 128
FEW = 4
MANY = 4
HEAD = 8
STRIDE = 4
FIRST = 1
LAST = 2


def spec(space):
    return pl.BlockSpec(memory_space=space)


def params(mib):
    return pltpu.CompilerParams(vmem_limit_bytes=mib * 1024 * 1024)


def round_up(n, step):
    return (n + step - 1) // step * step


def plan_kernel(
    n_row,
    piece_blocks,
    sent_at,
    load_at,
    bare_at,
    place,
    wanted_a,
    wanted_b,
    meta_a,
    meta_b,
    own,
    other,
    out,
    seen,
    sems,
):
    slot_count = (meta_a.shape[0] - 1) // 2
    size = own.shape[0]

    def scan(base, own_half, meta, asked_own, asked_other, at, sent, load):
        def step(s, carry):
            at, sent, load = carry
            half = meta[s] // piece_blocks
            row = meta[s] - half * piece_blocks
            inside = half == own_half
            piece = meta[slot_count + s] // piece_blocks
            kept = jnp.where(inside, row, piece_blocks)
            entry = HEAD + STRIDE * at
            out[base + entry] = s
            out[base + entry + 1] = row
            out[base + entry + 2] = piece
            out[base + entry + 3] = jnp.where(seen[kept] == 0, FIRST, 0)
            seen[kept] = entry
            out[base + load_at + load] = s
            side = jnp.where(inside, 0, 1)
            before = sent
            for k in range(n_row):
                out[base + sent_at + STRIDE * sent] = load
                out[base + sent_at + STRIDE * sent + 1] = 2 * k + side
                out[base + sent_at + STRIDE * sent + 2] = piece
                asked = jnp.where(inside, asked_own[k, 0], asked_other[k, 0])
                sent = sent + (asked == row).astype(jnp.int32)
            return at + inside.astype(jnp.int32), sent, load + (sent > before).astype(jnp.int32)

        at, sent, load = lax.fori_loop(0, meta[2 * slot_count], step, (at, sent, load))
        for _ in range(MANY):
            for start, end, spare in ((HEAD, at, piece_blocks), (sent_at, sent, 2 * n_row)):
                entry = base + start + STRIDE * end
                out[entry] = 0
                out[entry + 1] = spare
                out[entry + 2] = 0
                out[entry + 3] = 0
            at = at + jnp.where(at % MANY == 0, 0, 1)
            sent = sent + jnp.where(sent % FEW == 0, 0, 1)
        return at, sent, load

    def lists(base, own_half, meta_own, meta_other, asked_own, asked_other):
        for b in range(piece_blocks + 1):
            seen[b] = 0
        ends = (jnp.int32(0),) * 3
        for tile, meta in enumerate((meta_own, meta_other)):
            ends = scan(base, own_half, meta, asked_own, asked_other, *ends)
            for i, end in enumerate(ends):
                out[base + 2 * i + tile] = end

        def close(b, bare):
            entry = seen[b]
            out[base + bare_at + bare] = b

            @pl.when(entry > 0)
            def _():
                out[base + entry + 3] = out[base + entry + 3] + LAST

            return bare + jnp.where(entry == 0, 1, 0)

        out[base + 6] = lax.fori_loop(0, piece_blocks, close, jnp.int32(0))
        out[base + 7] = own_half

    @pl.when(place[1] == 0)
    def _():
        lists(0, 0, meta_a, meta_b, wanted_a, wanted_b)
        copy = pltpu.make_async_copy(out.at[pl.ds(0, size)], own, sems.at[0])
        copy.start()
        lists(size, 1, meta_b, meta_a, wanted_b, wanted_a)
        handed = pltpu.make_async_copy(out.at[pl.ds(size, size)], other, sems.at[1])
        handed.start()
        copy.wait()
        handed.wait()


def settle_kernel(place, own, handed, out, sem):
    for half, source in enumerate((own, handed)):

        @pl.when(place[1] == half)
        def _():
            copy = pltpu.make_async_copy(source, out, sem)
            copy.start()
            copy.wait()


def pick_kernel(n_row, block_size, wanted, vectors, out, sems):
    def fetch(k):
        at = pl.multiple_of(wanted[k, 0] * block_size, block_size)
        return pltpu.make_async_copy(vectors.at[pl.ds(at, block_size)], out.at[k], sems.at[k])

    for k in range(n_row):
        fetch(k).start()
    for k in range(n_row):
        fetch(k).wait()


def pack_kernel(place, picked, picked_b, out, held, sems):
    n_row, _, width = picked.shape
    middle = width // 2

    def put(k):
        return pltpu.make_async_copy(held.at[k], out.at[k], sems.at[k])

    for half in range(2):

        @pl.when(place[1] == half)
        def _():
            part = slice(half * middle, (half + 1) * middle)
            for k in range(n_row):
                held[k] = jnp.concatenate([picked[k, :, part], picked_b[k, :, part]], axis=1)
                put(k).start()

    for k in range(n_row):
        put(k).wait()


def load_kernel(base, stride, ends, plan, tile_a, tile_b, blocks, sems):
    mid, end = plan[ends], plan[ends + 1]

    def copy(tile, i):
        slot = plan[base + stride * i]
        return pltpu.make_async_copy(tile.at[slot], blocks.at[i], sems.at[i])

    @pl.loop(0, mid)
    def _(i):
        copy(tile_a, i).start()

    @pl.loop(mid, end)
    def _(i):
        copy(tile_b, i).start()

    @pl.loop(0, end)
    def _(i):
        copy(tile_a, i).wait()


def load_both_kernel(base, stride, ends, plan, tile_a, tile_b, array, blocks, held, sems, held_sem):
    copy = pltpu.make_async_copy(array, held, held_sem)
    copy.start()
    load_kernel(base, stride, ends, plan, tile_a, tile_b, blocks, sems)
    copy.wait()


def each_product(plan, base, ends, blocks, pieces, use, then=None):
    mid, end = plan[ends], plan[ends + 1]
    unroll = MANY if base == HEAD else FEW

    def run(piece_ref, begin, end):
        @pl.loop(begin // unroll, end // unroll)
        def _(j):
            for u in range(unroll):
                i = unroll * j + u
                entry = base + STRIDE * i
                block = blocks[i if base == HEAD else plan[entry]]
                use(
                    entry,
                    jnp.dot(block, piece_ref[plan[entry + 2]], preferred_element_type=jnp.float32),
                )
            if then is not None:
                for u in range(unroll):
                    then(base + STRIDE * (unroll * j + u))

    run(pieces[0], 0, mid)
    run(pieces[1], mid, end)


def add_products(plan, base, ends, blocks, pieces, total):
    def use(entry, value):
        total[plan[entry + 1]] += value

    each_product(plan, base, ends, blocks, pieces, use)


def split_sides(pieces, vec):
    middle = vec.shape[-1] // 2
    column = lax.broadcasted_iota(jnp.int32, (1, vec.shape[-1]), 1)
    for side in range(2):
        keep = jnp.where((column // middle) == side, 1.0, 0.0).astype(jnp.bfloat16)
        for p in range(vec.shape[1]):
            vec[side, p] = pieces[p] * keep


def joined(total, k):
    one, two = total[2 * k], total[2 * k + 1]
    low = lax.broadcasted_iota(jnp.int32, one.shape, 1) < one.shape[1] // 2
    return jnp.where(low, one, two) + pltpu.roll(
        jnp.where(low, two, one), one.shape[1] // 2, axis=1
    )


def first_sent_kernel(
    sent_at, load_at, plan, tile_a, tile_b, pieces, start, out, blocks, vec, total, held, held_sem, sems
):
    n_row = out.shape[0]
    mid, end = plan[4], plan[5]

    def fetch(tile, i):
        return pltpu.make_async_copy(tile.at[plan[load_at + i]], blocks.at[i], sems.at[i])

    @pl.loop(0, mid)
    def _(i):
        fetch(tile_a, i).start()

    @pl.loop(mid, end)
    def _(i):
        fetch(tile_b, i).start()

    copy = pltpu.make_async_copy(start, held, held_sem)
    copy.start()
    split_sides(pieces, vec)
    total[...] = jnp.zeros_like(total)

    @pl.loop(0, end)
    def _(i):
        fetch(tile_a, i).wait()

    add_products(plan, sent_at, 2, blocks, (vec.at[0], vec.at[1]), total)
    copy.wait()
    for k in range(n_row):
        value = joined(total, k) - center_value * held[k].astype(jnp.float32)
        out[k] = (value / half_width).astype(jnp.bfloat16)


def second_sent_kernel(
    sent_at, plan, blocks, pieces, current, previous, out, vec, total, held, held_sem, ready, out_sems
):
    n_row = out.shape[0]
    copy = pltpu.make_async_copy(previous, held, held_sem)
    copy.start()
    split_sides(pieces, vec)
    total[...] = jnp.zeros_like(total)
    add_products(plan, sent_at, 2, blocks, (vec.at[0], vec.at[1]), total)
    copy.wait()

    def put(k):
        return pltpu.make_async_copy(ready.at[k], out.at[k], out_sems.at[k])

    for k in range(n_row):
        value = joined(total, k) - center_value * current[k].astype(jnp.float32)
        ready[k] = (value - held[k].astype(jnp.float32)).astype(jnp.bfloat16)
        put(k).start()
    for k in range(n_row):
        put(k).wait()


def whole_columns(half, mine, other, vec, at):
    n_row, _, width = mine.shape
    middle = width // 2

    @pl.when(half == 0)
    def _():
        @pl.loop(0, n_row)
        def _(p):
            one, two = mine[p], other[p]
            vec[0, p, :, at : at + width] = jnp.concatenate([one[:, :middle], two[:, middle:]], axis=1)
            vec[1, p, :, at : at + width] = jnp.concatenate([one[:, middle:], two[:, :middle]], axis=1)

    @pl.when(half != 0)
    def _():
        @pl.loop(0, n_row)
        def _(p):
            one, two = mine[p], other[p]
            vec[0, p, :, at : at + width] = jnp.concatenate([two[:, middle:], one[:, :middle]], axis=1)
            vec[1, p, :, at : at + width] = jnp.concatenate([two[:, :middle], one[:, middle:]], axis=1)


def early_kernel(plan, blocks, q1, q1_other, q2, q2_other, vectors, base, vec, total, own, sem, row_sems):
    width = vectors.shape[1]
    piece_blocks, block_size, _ = base.shape
    copy = pltpu.make_async_copy(vectors, own, sem)
    copy.start()
    whole_columns(plan[7], q1, q1_other, vec, 0)
    whole_columns(plan[7], q2, q2_other, vec, width)
    copy.wait()

    def rows(b):
        return pl.ds(pl.multiple_of(b * block_size, block_size), block_size)

    def put(b):
        return pltpu.make_async_copy(own.at[rows(b)], base.at[b], row_sems.at[b])

    @pl.loop(0, piece_blocks)
    def _(b):
        value = own[rows(b), :].astype(jnp.float32)
        total[b, :, :width] = -center_value * value
        total[b, :, width:] = -value

    add_products(plan, HEAD, 0, blocks, (vec.at[0], vec.at[1]), total)

    @pl.loop(0, piece_blocks)
    def _(b):
        first = (total[b, :, :width] / half_width).astype(jnp.bfloat16).astype(jnp.float32)
        second = total[b, :, width:] - center_value * first
        second = second.astype(jnp.bfloat16).astype(jnp.float32)
        own[rows(b), :] = (-center_value * second - first).astype(jnp.bfloat16)
        put(b).start()

    @pl.loop(0, piece_blocks)
    def _(b):
        put(b).wait()


def last_kernel(bare_at, plan, blocks, mine, other, base, out, vec, total, own, row_sems):
    piece_blocks = base.shape[0]

    def put(source, b):
        return pltpu.make_async_copy(source.at[b], out.at[b], row_sems.at[b])

    @pl.loop(0, plan[6])
    def _(i):
        b = plan[bare_at + i]
        put(base, b).start()

    whole_columns(plan[7], mine, other, vec, 0)

    def use(entry, value):
        row = plan[entry + 1]
        marks = plan[entry + 3]
        start = base[jnp.minimum(row, piece_blocks - 1)].astype(jnp.float32)
        value = jnp.where(lax.rem(marks, LAST) == FIRST, start, total[row]) + value
        total[row] = value
        own[row] = value.astype(jnp.bfloat16)

    def then(entry):
        @pl.when(plan[entry + 3] >= LAST)
        def _():
            put(own, plan[entry + 1]).start()

    each_product(plan, HEAD, 0, blocks, (vec.at[0], vec.at[1]), use, then)

    @pl.loop(0, piece_blocks)
    def _(b):
        put(own, b).wait()


def after(value, *others):
    return lax.optimization_barrier((value, *others))[0]


def call(kernel, out, args, spaces, scratch, mib, name, estimate=None):
    args = [
        pltpu.with_memory_space_constraint(arg, space) if space in (VMEM, HBM) or tied else arg
        for arg, (space, tied) in zip(args, spaces)
    ]
    return pl.pallas_call(
        kernel,
        out_shape=[space(shape, dtype) for shape, dtype, space in out],
        in_specs=[spec(space) for space, _ in spaces],
        out_specs=[spec(space) for _, _, space in out],
        scratch_shapes=scratch,
        compiler_params=params(mib),
        cost_estimate=estimate,
        name=name,
    )(*args)


HERE = (VMEM, True)
FAR = (HBM, True)
LIST = (SMEM, True)
SCALARS = (SMEM, False)
ANYWHERE = (pl.ANY, False)


def on_pair(vectors, tile_blocks, block_rows, block_cols, counts):
    n_row = lax.axis_size("row")
    tile = tile_blocks[0, 0]
    slot_rows = block_rows[0, 0]
    slot_cols = block_cols[0, 0]
    used = counts[0]
    slot_count, block_size, _ = tile.shape
    width = vectors.shape[1]
    piece_blocks = vectors.shape[0] // block_size
    place = jnp.stack([lax.axis_index("row"), lax.axis_index("col")]).astype(jnp.int32)

    across = functools.partial(lax.ppermute, axis_name="col", perm=[(0, 1), (1, 0)])

    needed = jnp.max(
        jnp.where(
            slot_cols[None, :] // piece_blocks == jnp.arange(n_row)[:, None],
            slot_cols[None, :] % piece_blocks,
            0,
        ),
        axis=1,
        keepdims=True,
    )
    exchange = functools.partial(
        lax.all_to_all, axis_name="row", split_axis=0, concat_axis=0, tiled=True
    )
    meta = jnp.concatenate([slot_rows, slot_cols, used])
    meta_other = across(meta)
    wanted = after(exchange(jnp.broadcast_to(needed, (n_row, LANES))), meta_other, place)
    sent_shape = (n_row, block_size, width)
    (sent,) = call(
        functools.partial(pick_kernel, n_row, block_size),
        [(sent_shape, jnp.bfloat16, VMEM)],
        (wanted, vectors),
        (SCALARS, FAR),
        [DMA((n_row,))],
        2,
        "pick",
    )
    tile_other = across(tile)
    sent_other = across(sent)
    wanted_other = across(after(wanted, sent))
    packed = call(
        pack_kernel,
        [(sent_shape, jnp.bfloat16, HBM)],
        (place, sent, sent_other),
        (SCALARS, HERE, HERE),
        [VMEM(sent_shape, jnp.bfloat16), DMA((n_row,))],
        4,
        "pack",
    )[0]

    capacity = 2 * round_up(slot_count, MANY)
    sent_at = HEAD + STRIDE * (capacity + 1)
    load_at = sent_at + STRIDE * (4 * n_row * n_row + 2 * FEW + 1)
    bare_at = load_at + 2 * slot_count + 1
    plan_size = round_up(bare_at + piece_blocks, 8 * LANES)
    own_list, other_list = call(
        functools.partial(plan_kernel, n_row, piece_blocks, sent_at, load_at, bare_at),
        [((plan_size,), jnp.int32, HBM)] * 2,
        (place, wanted, wanted_other, meta, meta_other),
        (SCALARS,) * 5,
        [SMEM((2 * plan_size,), jnp.int32), SMEM((piece_blocks + 1,), jnp.int32), DMA((2,))],
        2,
        "plan",
    )
    q1 = exchange(after(packed, own_list))
    plan = call(
        settle_kernel,
        [((plan_size,), jnp.int32, SMEM)],
        (place, own_list, across(after(other_list, packed))),
        (SCALARS, ANYWHERE, ANYWHERE),
        [DMA],
        2,
        "settle",
    )[0]

    def load(base, stride, ends, cue, *array):
        kernel = load_both_kernel if array else load_kernel
        return call(
            functools.partial(kernel, base, stride, ends),
            [((capacity, block_size, block_size), jnp.bfloat16, VMEM)]
            + [(held.shape, held.dtype, VMEM) for held in array],
            (after(plan, cue), tile, tile_other, *array),
            (LIST, FAR, ANYWHERE) + (FAR,) * len(array),
            [DMA((capacity,))] + [DMA] * len(array),
            2,
            "load",
        )

    def cost(products, rows):
        size = block_size * width
        return pl.CostEstimate(
            flops=2 * products * block_size * size,
            bytes_accessed=2 * (products * block_size * block_size + 3 * rows * size),
            transcendentals=0,
        )

    sums = [
        VMEM((2, n_row, block_size, width), jnp.bfloat16),
        VMEM((2 * n_row + 1, block_size, width), jnp.float32),
    ]

    def first_blocks(*args):
        return call(
            functools.partial(first_sent_kernel, sent_at, load_at),
            [
                (sent_shape, jnp.bfloat16, VMEM),
                ((capacity, block_size, block_size), jnp.bfloat16, VMEM),
            ],
            (plan, tile, tile_other, *args),
            (LIST, FAR, ANYWHERE, HERE, FAR),
            sums + [VMEM(sent_shape, jnp.bfloat16), DMA, DMA((capacity,))],
            8,
            "sent",
            cost(n_row, n_row),
        )

    def second_blocks(*args):
        return call(
            functools.partial(second_sent_kernel, sent_at),
            [(sent_shape, jnp.bfloat16, HBM)],
            (plan, *args),
            (LIST, HERE, HERE, HERE, FAR),
            sums
            + [VMEM(sent_shape, jnp.bfloat16), DMA, VMEM(sent_shape, jnp.bfloat16), DMA((n_row,))],
            8,
            "sent",
            cost(n_row, n_row),
        )[0]

    base_shape = (piece_blocks, block_size, width)

    def early(*args):
        return call(
            early_kernel,
            [(base_shape, jnp.bfloat16, HBM)],
            (plan, *args),
            (LIST, HERE, HERE, HERE, HERE, HERE, FAR),
            [
                VMEM((2, n_row, block_size, 2 * width), jnp.bfloat16),
                VMEM((piece_blocks + 1, block_size, 2 * width), jnp.float32),
                VMEM(vectors.shape, jnp.bfloat16),
                DMA,
                DMA((piece_blocks,)),
            ],
            18,
            "early",
            cost(2 * slot_count, 2 * piece_blocks),
        )[0]

    def last(blocks, *args):
        rows = (piece_blocks + 1, block_size, width)
        (out,) = call(
            functools.partial(last_kernel, bare_at),
            [(base_shape, jnp.bfloat16, HBM)],
            (plan, blocks, *args),
            (LIST,) + (HERE,) * 4,
            [
                VMEM((2, n_row, block_size, width), jnp.bfloat16),
                VMEM(rows, jnp.float32),
                VMEM(rows, jnp.bfloat16),
                DMA((piece_blocks,)),
            ],
            9,
            "last",
            cost(slot_count, piece_blocks),
        )
        return out.reshape(vectors.shape)

    q1 = after(q1, plan)
    first_sent, blocks = first_blocks(q1, packed)
    q2 = exchange(first_sent)
    second_sent = second_blocks(blocks, q2, first_sent, packed)
    q1_other = across(after(q1, second_sent))
    q2_other = across(after(q2, second_sent))
    (blocks,) = load(HEAD, STRIDE, 0, second_sent)
    base = early(blocks, q1, q1_other, q2, q2_other, vectors)
    q3 = after(exchange(second_sent), base)
    q3_other = across(q3)
    blocks, base = load(HEAD, STRIDE, 0, q3, base)
    return last(blocks, q3, q3_other, base)


def on_any(vectors, tile_blocks, block_rows, block_cols, counts):
    n_row = lax.axis_size("row")
    n_col = lax.axis_size("col")
    tile_data = tile_blocks[0, 0]
    slot_rows = block_rows[0, 0]
    slot_cols = block_cols[0, 0]
    used = counts[0, 0]
    block_size = tile_data.shape[-1]
    width = vectors.shape[1]
    piece_blocks = vectors.shape[0] // block_size
    row_blocks = piece_blocks * n_col
    slot_count = tile_data.shape[0]
    live = (jnp.arange(slot_count) < used).astype(jnp.float32)
    onehot = (slot_rows[None, :] == jnp.arange(row_blocks)[:, None]).astype(jnp.float32) * live[
        None, :
    ]
    source_piece = slot_cols // piece_blocks
    offset = slot_cols % piece_blocks
    needed = jnp.max(
        jnp.where(source_piece[None, :] == jnp.arange(n_row)[:, None], offset[None, :], 0), axis=1
    )
    wanted = lax.all_to_all(
        needed.reshape(n_row, 1), "row", split_axis=0, concat_axis=0, tiled=True
    ).reshape(n_row)

    def apply_tiles(current):
        own_blocks = current.reshape(piece_blocks, block_size, width)
        outgoing = jnp.take(own_blocks, wanted, axis=0)
        received = lax.all_to_all(outgoing, "row", split_axis=0, concat_axis=0, tiled=True)
        vec_blocks = jnp.take(received, source_piece, axis=0)
        products = jnp.einsum(
            "sij,sjk->sik", tile_data, vec_blocks, preferred_element_type=jnp.float32
        )
        term = jnp.einsum("ls,sik->lik", onehot, products, precision=lax.Precision.HIGHEST)
        term = term.reshape(row_blocks * block_size, width)
        return lax.psum_scatter(
            term.astype(jnp.bfloat16), "col", scatter_dimension=0, tiled=True
        ).astype(jnp.float32)

    previous = vectors
    applied = apply_tiles(vectors)
    current = ((applied - center_value * previous.astype(jnp.float32)) / half_width).astype(
        jnp.bfloat16
    )
    for repeat in range(DEGREE - 1):
        applied = apply_tiles(current)
        following = (
            2.0 * (applied - center_value * current.astype(jnp.float32)) / half_width
            - previous.astype(jnp.float32)
        ).astype(jnp.bfloat16)
        previous, current = (current, following)
    return current


def solution(mesh):
    n_row, n_col = mesh.shape["row"], mesh.shape["col"]
    paired = n_col == 2 and n_row & (n_row - 1) == 0
    return jax.shard_map(
        on_pair if paired else on_any,
        mesh=mesh,
        in_specs=(
            P(("row", "col"), "vec"),
            P("row", "col", None, None, None),
            P("row", "col", None),
            P("row", "col", None),
            P("row", "col"),
        ),
        out_specs=P(("row", "col"), "vec"),
        check_vma=False,
    )
```

```python
import functools

import jax
import jax.numpy as jnp
from jax import lax
from jax.experimental import pallas as pl
from jax.experimental.pallas import tpu as pltpu
from jax.sharding import PartitionSpec as P

DEGREE = 3

center_value = 0.5
half_width = 2.0

VMEM = pltpu.VMEM
SMEM = pltpu.SMEM
HBM = pltpu.HBM
DMA = pltpu.SemaphoreType.DMA
LANES = 128
FEW = 4
MANY = 4
HEAD = 8
STRIDE = 4
FIRST = 1
LAST = 2


def spec(space):
    return pl.BlockSpec(memory_space=space)


def params(mib):
    return pltpu.CompilerParams(vmem_limit_bytes=mib * 1024 * 1024)


def round_up(n, step):
    return (n + step - 1) // step * step


def plan_kernel(
    n_row,
    piece_blocks,
    sent_at,
    load_at,
    bare_at,
    place,
    wanted_a,
    wanted_b,
    meta_a,
    meta_b,
    own,
    other,
    out,
    seen,
    asked,
    sems,
):
    slot_count = (meta_a.shape[0] - 1) // 2
    size = own.shape[0]

    def scan(base, own_half, meta, at, sent, load):
        used = meta[2 * slot_count]

        def step(s, carry):
            at, sent, load = carry
            half = meta[s] // piece_blocks
            row = meta[s] - half * piece_blocks
            live = s < used
            inside = live & (half == own_half)
            piece = meta[slot_count + s] // piece_blocks
            kept = jnp.where(inside, row, piece_blocks)
            entry = HEAD + STRIDE * at
            out[base + entry] = s
            out[base + entry + 1] = row
            out[base + entry + 2] = piece
            out[base + entry + 3] = jnp.where(seen[kept] == 0, FIRST, 0)
            seen[kept] = entry
            out[base + load_at + load] = s
            sought = jnp.where(live, row, -1)
            hits = [(asked[half * n_row + k] == sought).astype(jnp.int32) for k in range(n_row)]
            found = sum(hits)

            @pl.when(found > 0)
            def _():
                side = jnp.where(inside, 0, 1)
                place = sent
                for k in range(n_row):
                    entry = base + sent_at + STRIDE * place
                    out[entry] = load
                    out[entry + 1] = 2 * k + side
                    out[entry + 2] = piece
                    out[entry + 3] = jnp.where(place == sent, FIRST, 0)
                    place = place + hits[k]

            return (
                at + inside.astype(jnp.int32),
                sent + found,
                load + (found > 0).astype(jnp.int32),
            )

        at, sent, load = lax.fori_loop(0, slot_count, step, (at, sent, load))
        for _ in range(MANY):
            for start, end, spare in ((HEAD, at, piece_blocks), (sent_at, sent, 2 * n_row)):
                entry = base + start + STRIDE * end
                out[entry] = 0
                out[entry + 1] = spare
                out[entry + 2] = 0
                out[entry + 3] = 0
            at = at + jnp.where(at % MANY == 0, 0, 1)
            sent = sent + jnp.where(sent % FEW == 0, 0, 1)
        return at, sent, load

    def lists(base, own_half, meta_own, meta_other):
        for b in range(piece_blocks + 1):
            seen[b] = 0
        ends = (jnp.int32(0),) * 3
        for tile, meta in enumerate((meta_own, meta_other)):
            ends = scan(base, own_half, meta, *ends)
            for i, end in enumerate(ends):
                out[base + 2 * i + tile] = end

        def close(b, bare):
            entry = seen[b]
            out[base + bare_at + bare] = b

            @pl.when(entry > 0)
            def _():
                out[base + entry + 3] = out[base + entry + 3] + LAST

            return bare + jnp.where(entry == 0, 1, 0)

        out[base + 6] = lax.fori_loop(0, piece_blocks, close, jnp.int32(0))
        out[base + 7] = own_half

    @pl.when(place[1] == 0)
    def _():
        for k in range(n_row):
            asked[k] = wanted_a[k, 0]
            asked[n_row + k] = wanted_b[k, 0]
        lists(0, 0, meta_a, meta_b)
        copy = pltpu.make_async_copy(out.at[pl.ds(0, size)], own, sems.at[0])
        copy.start()
        lists(size, 1, meta_b, meta_a)
        handed = pltpu.make_async_copy(out.at[pl.ds(size, size)], other, sems.at[1])
        handed.start()
        copy.wait()
        handed.wait()


def settle_kernel(place, own, handed, out, sem):
    for half, source in enumerate((own, handed)):

        @pl.when(place[1] == half)
        def _():
            copy = pltpu.make_async_copy(source, out, sem)
            copy.start()
            copy.wait()


def pick_kernel(n_row, block_size, wanted, vectors, out, sems):
    def fetch(k):
        at = pl.multiple_of(wanted[k, 0] * block_size, block_size)
        return pltpu.make_async_copy(vectors.at[pl.ds(at, block_size)], out.at[k], sems.at[k])

    for k in range(n_row):
        fetch(k).start()
    for k in range(n_row):
        fetch(k).wait()


def pack_kernel(place, picked, picked_b, out, held, sems):
    n_row, _, width = picked.shape
    middle = width // 2

    def put(k):
        return pltpu.make_async_copy(held.at[k], out.at[k], sems.at[k])

    for half in range(2):

        @pl.when(place[1] == half)
        def _():
            part = slice(half * middle, (half + 1) * middle)
            for k in range(n_row):
                held[k] = jnp.concatenate([picked[k, :, part], picked_b[k, :, part]], axis=1)
                put(k).start()

    for k in range(n_row):
        put(k).wait()


def fetches(plan, base, stride, ends, tile_a, tile_b, blocks, sems):
    mid, end = plan[ends], plan[ends + 1]

    def copy(tile, i):
        slot = plan[base + stride * i]
        return pltpu.make_async_copy(tile.at[slot], blocks.at[i], sems.at[i])

    def start():
        @pl.loop(0, mid)
        def _(i):
            copy(tile_a, i).start()

        @pl.loop(mid, end)
        def _(i):
            copy(tile_b, i).start()

    def wait(i):
        copy(tile_a, i).wait()

    return start, wait


def load_kernel(plan, tile_a, array, blocks, held, sems, held_sem):
    def copy(i):
        return pltpu.make_async_copy(
            tile_a.at[plan[HEAD + STRIDE * i]], blocks.at[i], sems.at[i]
        )

    whole = pltpu.make_async_copy(array, held, held_sem)
    whole.start()

    @pl.loop(0, plan[0])
    def _(i):
        copy(i).start()

    @pl.loop(0, plan[0])
    def _(i):
        copy(i).wait()

    whole.wait()


def each_product(plan, base, ends, block_of, pieces, use, then=None, before=None):
    mid, end = plan[ends], plan[ends + 1]
    unroll = MANY if base == HEAD else FEW

    def run(side, begin, end):
        @pl.loop(begin // unroll, end // unroll)
        def _(j):
            step = [(unroll * j + u, base + STRIDE * (unroll * j + u)) for u in range(unroll)]
            if before is not None:
                for i, entry in step:
                    before(side, i, entry)
            for i, entry in step:
                block = block_of(side, i, entry)
                piece = pieces[side][plan[entry + 2]]
                use(entry, jnp.dot(block, piece, preferred_element_type=jnp.float32))
            if then is not None:
                for i, entry in step:
                    then(entry)

    run(0, 0, mid)
    run(1, mid, end)


def add_products(plan, base, ends, block_of, pieces, total, before=None):
    def use(entry, value):
        total[plan[entry + 1]] += value

    each_product(plan, base, ends, block_of, pieces, use, before=before)


def split_sides(pieces, vec):
    middle = vec.shape[-1] // 2
    column = lax.broadcasted_iota(jnp.int32, (1, vec.shape[-1]), 1)
    for side in range(2):
        keep = jnp.where((column // middle) == side, 1.0, 0.0).astype(jnp.bfloat16)
        for p in range(vec.shape[1]):
            vec[side, p] = pieces[p] * keep


def joined(total, k):
    one, two = total[2 * k], total[2 * k + 1]
    low = lax.broadcasted_iota(jnp.int32, one.shape, 1) < one.shape[1] // 2
    return jnp.where(low, one, two) + pltpu.roll(
        jnp.where(low, two, one), one.shape[1] // 2, axis=1
    )


def first_sent_kernel(
    sent_at, load_at, plan, tile_a, tile_b, pieces, start, out, blocks, vec, total, held, held_sem, sems
):
    n_row = out.shape[0]
    begin, wait = fetches(plan, load_at, 1, 4, tile_a, tile_b, blocks, sems)
    begin()
    copy = pltpu.make_async_copy(start, held, held_sem)
    copy.start()
    split_sides(pieces, vec)
    total[...] = jnp.zeros_like(total)

    def before(side, i, entry):
        @pl.when(plan[entry + 3] == FIRST)
        def _():
            wait(plan[entry])

    add_products(
        plan,
        sent_at,
        2,
        lambda side, i, entry: blocks[plan[entry]],
        (vec.at[0], vec.at[1]),
        total,
        before,
    )
    copy.wait()
    for k in range(n_row):
        value = joined(total, k) - center_value * held[k].astype(jnp.float32)
        out[k] = (value / half_width).astype(jnp.bfloat16)


def second_sent_kernel(
    sent_at, plan, blocks, pieces, current, previous, out, vec, total, held, held_sem, ready, out_sems
):
    n_row = out.shape[0]
    copy = pltpu.make_async_copy(previous, held, held_sem)
    copy.start()
    split_sides(pieces, vec)
    total[...] = jnp.zeros_like(total)
    add_products(
        plan,
        sent_at,
        2,
        lambda side, i, entry: blocks[plan[entry]],
        (vec.at[0], vec.at[1]),
        total,
    )
    copy.wait()

    def put(k):
        return pltpu.make_async_copy(ready.at[k], out.at[k], out_sems.at[k])

    for k in range(n_row):
        value = joined(total, k) - center_value * current[k].astype(jnp.float32)
        ready[k] = (value - held[k].astype(jnp.float32)).astype(jnp.bfloat16)
        put(k).start()
    for k in range(n_row):
        put(k).wait()


def whole_columns(half, mine, other, vec, at):
    n_row, _, width = mine.shape
    middle = width // 2

    @pl.when(half == 0)
    def _():
        @pl.loop(0, n_row)
        def _(p):
            one, two = mine[p], other[p]
            vec[0, p, :, at : at + width] = jnp.concatenate([one[:, :middle], two[:, middle:]], axis=1)
            vec[1, p, :, at : at + width] = jnp.concatenate([one[:, middle:], two[:, :middle]], axis=1)

    @pl.when(half != 0)
    def _():
        @pl.loop(0, n_row)
        def _(p):
            one, two = mine[p], other[p]
            vec[0, p, :, at : at + width] = jnp.concatenate([two[:, middle:], one[:, :middle]], axis=1)
            vec[1, p, :, at : at + width] = jnp.concatenate([two[:, :middle], one[:, middle:]], axis=1)


def early_kernel(
    plan,
    tile_a,
    tile_b,
    q1,
    q1_other,
    q2,
    q2_other,
    vectors,
    base,
    vec,
    total,
    own,
    blocks,
    sem,
    sems,
    row_sems,
):
    width = vectors.shape[1]
    piece_blocks, block_size, _ = base.shape
    copy = pltpu.make_async_copy(vectors, own, sem)
    copy.start()
    begin, wait = fetches(plan, HEAD, STRIDE, 0, tile_a, tile_b, blocks, sems)
    begin()
    whole_columns(plan[7], q1, q1_other, vec, 0)
    whole_columns(plan[7], q2, q2_other, vec, width)
    copy.wait()

    def rows(b):
        return pl.ds(pl.multiple_of(b * block_size, block_size), block_size)

    def put(b):
        return pltpu.make_async_copy(own.at[rows(b)], base.at[b], row_sems.at[b])

    @pl.loop(0, piece_blocks)
    def _(b):
        value = own[rows(b), :].astype(jnp.float32)
        total[b, :, :width] = -center_value * value
        total[b, :, width:] = -value

    add_products(
        plan,
        HEAD,
        0,
        lambda side, i, entry: blocks[i],
        (vec.at[0], vec.at[1]),
        total,
        lambda side, i, entry: wait(i),
    )

    @pl.loop(0, piece_blocks)
    def _(b):
        first = (total[b, :, :width] / half_width).astype(jnp.bfloat16).astype(jnp.float32)
        second = total[b, :, width:] - center_value * first
        second = second.astype(jnp.bfloat16).astype(jnp.float32)
        own[rows(b), :] = (-center_value * second - first).astype(jnp.bfloat16)
        put(b).start()

    @pl.loop(0, piece_blocks)
    def _(b):
        put(b).wait()


def last_kernel(
    bare_at, plan, blocks, tile_b, mine, other, base, out, vec, total, own, blocks_b, sems, row_sems
):
    piece_blocks = base.shape[0]
    mid = plan[0]

    def fetch(i):
        slot = plan[HEAD + STRIDE * i]
        return pltpu.make_async_copy(tile_b.at[slot], blocks_b.at[i - mid], sems.at[i - mid])

    @pl.loop(mid, plan[1])
    def _(i):
        fetch(i).start()

    def put(source, b):
        return pltpu.make_async_copy(source.at[b], out.at[b], row_sems.at[b])

    @pl.loop(0, plan[6])
    def _(i):
        b = plan[bare_at + i]
        put(base, b).start()

    whole_columns(plan[7], mine, other, vec, 0)

    def use(entry, value):
        row = plan[entry + 1]
        marks = plan[entry + 3]
        start = base[jnp.minimum(row, piece_blocks - 1)].astype(jnp.float32)
        value = jnp.where(lax.rem(marks, LAST) == FIRST, start, total[row]) + value
        total[row] = value
        own[row] = value.astype(jnp.bfloat16)

    def then(entry):
        @pl.when(plan[entry + 3] >= LAST)
        def _():
            put(own, plan[entry + 1]).start()

    def block_of(side, i, entry):
        return blocks[i] if side == 0 else blocks_b[i - mid]

    def before(side, i, entry):
        if side == 1:
            fetch(i).wait()

    each_product(plan, HEAD, 0, block_of, (vec.at[0], vec.at[1]), use, then, before)

    @pl.loop(0, piece_blocks)
    def _(b):
        put(own, b).wait()


def after(value, *others):
    return lax.optimization_barrier((value, *others))[0]


def call(kernel, out, args, spaces, scratch, mib, name, estimate=None):
    args = [
        pltpu.with_memory_space_constraint(arg, space) if space in (VMEM, HBM) or tied else arg
        for arg, (space, tied) in zip(args, spaces)
    ]
    return pl.pallas_call(
        kernel,
        out_shape=[space(shape, dtype) for shape, dtype, space in out],
        in_specs=[spec(space) for space, _ in spaces],
        out_specs=[spec(space) for _, _, space in out],
        scratch_shapes=scratch,
        compiler_params=params(mib),
        cost_estimate=estimate,
        name=name,
    )(*args)


HERE = (VMEM, True)
FAR = (HBM, True)
LIST = (SMEM, True)
SCALARS = (SMEM, False)
ANYWHERE = (pl.ANY, False)


def on_pair(vectors, tile_blocks, block_rows, block_cols, counts):
    n_row = lax.axis_size("row")
    tile = tile_blocks[0, 0]
    slot_rows = block_rows[0, 0]
    slot_cols = block_cols[0, 0]
    used = counts[0]
    slot_count, block_size, _ = tile.shape
    width = vectors.shape[1]
    piece_blocks = vectors.shape[0] // block_size
    place = jnp.stack([lax.axis_index("row"), lax.axis_index("col")]).astype(jnp.int32)

    across = functools.partial(lax.ppermute, axis_name="col", perm=[(0, 1), (1, 0)])

    needed = jnp.max(
        jnp.where(
            slot_cols[None, :] // piece_blocks == jnp.arange(n_row)[:, None],
            slot_cols[None, :] % piece_blocks,
            0,
        ),
        axis=1,
        keepdims=True,
    )
    exchange = functools.partial(
        lax.all_to_all, axis_name="row", split_axis=0, concat_axis=0, tiled=True
    )
    meta = jnp.concatenate([slot_rows, slot_cols, used])
    meta_other = across(meta)
    wanted = after(exchange(jnp.broadcast_to(needed, (n_row, LANES))), meta_other, place)
    sent_shape = (n_row, block_size, width)
    (sent,) = call(
        functools.partial(pick_kernel, n_row, block_size),
        [(sent_shape, jnp.bfloat16, VMEM)],
        (wanted, vectors),
        (SCALARS, FAR),
        [DMA((n_row,))],
        2,
        "pick",
    )
    tile_other = across(tile)
    sent_other = across(sent)
    wanted_other = across(after(wanted, sent))
    packed = call(
        pack_kernel,
        [(sent_shape, jnp.bfloat16, HBM)],
        (place, sent, sent_other),
        (SCALARS, HERE, HERE),
        [VMEM(sent_shape, jnp.bfloat16), DMA((n_row,))],
        4,
        "pack",
    )[0]

    capacity = 2 * round_up(slot_count, MANY)
    sent_at = HEAD + STRIDE * (capacity + 1)
    load_at = sent_at + STRIDE * (4 * n_row * n_row + 2 * FEW + 1)
    bare_at = load_at + 2 * slot_count + 1
    plan_size = round_up(bare_at + piece_blocks, 8 * LANES)
    own_list, other_list = call(
        functools.partial(plan_kernel, n_row, piece_blocks, sent_at, load_at, bare_at),
        [((plan_size,), jnp.int32, HBM)] * 2,
        (place, wanted, after(wanted_other, packed), meta, meta_other),
        (SCALARS,) * 5,
        [
            SMEM((2 * plan_size,), jnp.int32),
            SMEM((piece_blocks + 1,), jnp.int32),
            SMEM((2 * n_row,), jnp.int32),
            DMA((2,)),
        ],
        2,
        "plan",
    )
    q1 = exchange(after(packed, own_list))
    plan = call(
        settle_kernel,
        [((plan_size,), jnp.int32, SMEM)],
        (place, own_list, across(after(other_list, packed))),
        (SCALARS, ANYWHERE, ANYWHERE),
        [DMA],
        2,
        "settle",
    )[0]

    def load(cue, array):
        return call(
            load_kernel,
            [
                ((capacity // 2, block_size, block_size), jnp.bfloat16, VMEM),
                (array.shape, array.dtype, VMEM),
            ],
            (after(plan, cue), tile, array),
            (LIST, FAR, FAR),
            [DMA((capacity // 2,)), DMA],
            2,
            "load",
        )

    def cost(products, rows):
        size = block_size * width
        return pl.CostEstimate(
            flops=2 * products * block_size * size,
            bytes_accessed=2 * (products * block_size * block_size + 3 * rows * size),
            transcendentals=0,
        )

    sums = [
        VMEM((2, n_row, block_size, width), jnp.bfloat16),
        VMEM((2 * n_row + 1, block_size, width), jnp.float32),
    ]

    def first_blocks(*args):
        return call(
            functools.partial(first_sent_kernel, sent_at, load_at),
            [
                (sent_shape, jnp.bfloat16, VMEM),
                ((capacity, block_size, block_size), jnp.bfloat16, VMEM),
            ],
            (plan, tile, tile_other, *args),
            (LIST, FAR, ANYWHERE, HERE, FAR),
            sums + [VMEM(sent_shape, jnp.bfloat16), DMA, DMA((capacity,))],
            8,
            "sent",
            cost(n_row, n_row),
        )

    def second_blocks(*args):
        return call(
            functools.partial(second_sent_kernel, sent_at),
            [(sent_shape, jnp.bfloat16, HBM)],
            (plan, *args),
            (LIST, HERE, HERE, HERE, FAR),
            sums
            + [VMEM(sent_shape, jnp.bfloat16), DMA, VMEM(sent_shape, jnp.bfloat16), DMA((n_row,))],
            8,
            "sent",
            cost(n_row, n_row),
        )[0]

    base_shape = (piece_blocks, block_size, width)

    def early(*args):
        return call(
            early_kernel,
            [(base_shape, jnp.bfloat16, HBM)],
            (plan, tile, tile_other, *args),
            (LIST, FAR, ANYWHERE, HERE, HERE, HERE, HERE, FAR),
            [
                VMEM((2, n_row, block_size, 2 * width), jnp.bfloat16),
                VMEM((piece_blocks + 1, block_size, 2 * width), jnp.float32),
                VMEM(vectors.shape, jnp.bfloat16),
                VMEM((capacity, block_size, block_size), jnp.bfloat16),
                DMA,
                DMA((capacity,)),
                DMA((piece_blocks,)),
            ],
            28,
            "early",
            cost(2 * slot_count, 2 * piece_blocks),
        )[0]

    def last(blocks, *args):
        rows = (piece_blocks + 1, block_size, width)
        (out,) = call(
            functools.partial(last_kernel, bare_at),
            [(base_shape, jnp.bfloat16, HBM)],
            (plan, blocks, tile_other, *args),
            (LIST, HERE, ANYWHERE, HERE, HERE, HERE),
            [
                VMEM((2, n_row, block_size, width), jnp.bfloat16),
                VMEM(rows, jnp.float32),
                VMEM(rows, jnp.bfloat16),
                VMEM((capacity // 2, block_size, block_size), jnp.bfloat16),
                DMA((capacity // 2,)),
                DMA((piece_blocks,)),
            ],
            14,
            "last",
            cost(slot_count, piece_blocks),
        )
        return out.reshape(vectors.shape)

    q1 = after(q1, plan)
    first_sent, blocks = first_blocks(q1, packed)
    q2 = exchange(first_sent)
    second_sent = second_blocks(blocks, q2, first_sent, packed)
    q1_other = across(after(q1, second_sent))
    q2_other = across(after(q2, second_sent))
    base = early(q1, q1_other, q2, q2_other, vectors)
    q3 = after(exchange(second_sent), base)
    q3_other = across(q3)
    blocks, base = load(q3, base)
    return last(blocks, q3, q3_other, base)


def on_any(vectors, tile_blocks, block_rows, block_cols, counts):
    n_row = lax.axis_size("row")
    n_col = lax.axis_size("col")
    tile_data = tile_blocks[0, 0]
    slot_rows = block_rows[0, 0]
    slot_cols = block_cols[0, 0]
    used = counts[0, 0]
    block_size = tile_data.shape[-1]
    width = vectors.shape[1]
    piece_blocks = vectors.shape[0] // block_size
    row_blocks = piece_blocks * n_col
    slot_count = tile_data.shape[0]
    live = (jnp.arange(slot_count) < used).astype(jnp.float32)
    onehot = (slot_rows[None, :] == jnp.arange(row_blocks)[:, None]).astype(jnp.float32) * live[
        None, :
    ]
    source_piece = slot_cols // piece_blocks
    offset = slot_cols % piece_blocks
    needed = jnp.max(
        jnp.where(source_piece[None, :] == jnp.arange(n_row)[:, None], offset[None, :], 0), axis=1
    )
    wanted = lax.all_to_all(
        needed.reshape(n_row, 1), "row", split_axis=0, concat_axis=0, tiled=True
    ).reshape(n_row)

    def apply_tiles(current):
        own_blocks = current.reshape(piece_blocks, block_size, width)
        outgoing = jnp.take(own_blocks, wanted, axis=0)
        received = lax.all_to_all(outgoing, "row", split_axis=0, concat_axis=0, tiled=True)
        vec_blocks = jnp.take(received, source_piece, axis=0)
        products = jnp.einsum(
            "sij,sjk->sik", tile_data, vec_blocks, preferred_element_type=jnp.float32
        )
        term = jnp.einsum("ls,sik->lik", onehot, products, precision=lax.Precision.HIGHEST)
        term = term.reshape(row_blocks * block_size, width)
        return lax.psum_scatter(
            term.astype(jnp.bfloat16), "col", scatter_dimension=0, tiled=True
        ).astype(jnp.float32)

    previous = vectors
    applied = apply_tiles(vectors)
    current = ((applied - center_value * previous.astype(jnp.float32)) / half_width).astype(
        jnp.bfloat16
    )
    for repeat in range(DEGREE - 1):
        applied = apply_tiles(current)
        following = (
            2.0 * (applied - center_value * current.astype(jnp.float32)) / half_width
            - previous.astype(jnp.float32)
        ).astype(jnp.bfloat16)
        previous, current = (current, following)
    return current


def solution(mesh):
    n_row, n_col = mesh.shape["row"], mesh.shape["col"]
    paired = n_col == 2 and n_row & (n_row - 1) == 0
    return jax.shard_map(
        on_pair if paired else on_any,
        mesh=mesh,
        in_specs=(
            P(("row", "col"), "vec"),
            P("row", "col", None, None, None),
            P("row", "col", None),
            P("row", "col", None),
            P("row", "col"),
        ),
        out_specs=P(("row", "col"), "vec"),
        check_vma=False,
    )
```

```python
import functools
import typing

import jax
import jax.numpy as jnp
from jax import lax
from jax.experimental import pallas as pl
from jax.experimental.pallas import tpu as pltpu
from jax.sharding import PartitionSpec as P

DEGREE = 3

center_value = 0.5
half_width = 2.0

VMEM = pltpu.VMEM
SMEM = pltpu.SMEM
HBM = pltpu.HBM
DMA = pltpu.SemaphoreType.DMA
LANES = 128
FEW = 4
MANY = 4
HEAD = 8
STRIDE = 4
FIRST = 1
LAST = 2


def spec(space):
    return pl.BlockSpec(memory_space=space)


def params(mib):
    return pltpu.CompilerParams(vmem_limit_bytes=mib * 1024 * 1024)


def round_up(n, step):
    return (n + step - 1) // step * step


class Layout(typing.NamedTuple):
    slots: int
    sends: int
    loads: int
    sent_at: int
    load_at: int
    bare_at: int
    size: int


def layout_for(slot_count, n_row, piece_blocks):
    slots = round_up(slot_count, MANY) + MANY
    sends = round_up(2 * n_row * n_row, FEW) + FEW
    sent_at = HEAD + STRIDE * 2 * slots
    load_at = sent_at + STRIDE * 2 * sends
    bare_at = load_at + 2 * (slot_count + 1)
    size = round_up(bare_at + piece_blocks, 8 * LANES)
    return Layout(slots, sends, slot_count + 1, sent_at, load_at, bare_at, size)


def plan_kernel(
    n_row,
    piece_blocks,
    lay,
    place,
    wanted_a,
    wanted_b,
    meta_a,
    meta_b,
    own,
    other,
    out,
    count,
    asked,
    sems,
):
    slot_count = (meta_a.shape[0] - 1) // 2

    def put(at, *values):
        for i, value in enumerate(values):
            out[at + i] = value

    def scan(tile, meta):
        used = meta[2 * slot_count]

        def step(s, carry):
            ends, sent, load = carry
            row = meta[s]
            piece = meta[slot_count + s] // piece_blocks
            live = s < used
            half = row // piece_blocks
            local = row - half * piece_blocks
            lower = half == 0
            part = jnp.where(lower, tile, 1 - tile)
            at = HEAD + STRIDE * (part * lay.slots + jnp.where(lower, ends[0], ends[1]))
            base = half * lay.size
            put(base + at, s, local, piece)
            found = jnp.where(live, count[row], 0)

            @pl.when(found > 0)
            def _():
                for core in range(2):
                    mine = tile if core == 0 else 1 - tile
                    side = half if core == 0 else 1 - half
                    first = core * lay.size
                    out[first + lay.load_at + mine * lay.loads + load] = s

                    @pl.loop(0, found)
                    def _(j):
                        put(
                            first + lay.sent_at + STRIDE * (mine * lay.sends + sent + j),
                            mine * lay.loads + load,
                            2 * asked[row * n_row + j] + side,
                            piece,
                            jnp.where(j == 0, FIRST, 0),
                        )

            one = live.astype(jnp.int32)
            ends = (ends[0] + jnp.where(lower, one, 0), ends[1] + jnp.where(lower, 0, one))
            return ends, sent + found, load + jnp.where(found > 0, 1, 0)

        zero = jnp.int32(0)
        ends, sent, load = lax.fori_loop(0, slot_count, step, ((zero, zero), zero, zero))
        for core in range(2):
            mine = tile if core == 0 else 1 - tile
            base = core * lay.size
            for i, (at, begin, end, unit, spare) in enumerate(
                (
                    (HEAD, mine * lay.slots, ends[core], MANY, piece_blocks),
                    (lay.sent_at, mine * lay.sends, sent, FEW, 2 * n_row),
                )
            ):
                for u in range(unit - 1):
                    put(base + at + STRIDE * (begin + end + u), 0, spare, 0, 0)
                out[base + 2 * i + mine] = begin + (end + unit - 1) // unit * unit
            out[base + 4 + mine] = mine * lay.loads + load

    @pl.when(place[1] == 0)
    def _():
        for row in range(2 * piece_blocks):
            count[row] = 0
        for half, wanted in enumerate((wanted_a, wanted_b)):
            for k in range(n_row):
                row = half * piece_blocks + wanted[k, 0]
                number = count[row]
                asked[row * n_row + number] = k
                count[row] = number + 1
        scan(0, meta_a)
        scan(1, meta_b)
        copies = [
            pltpu.make_async_copy(out.at[pl.ds(core * lay.size, lay.size)], target, sems.at[core])
            for core, target in enumerate((own, other))
        ]
        for copy in copies:
            copy.start()
        for copy in copies:
            copy.wait()


def settle_kernel(piece_blocks, lay, place, own, handed, out, seen, sem):
    for half, source in enumerate((own, handed)):

        @pl.when(place[1] == half)
        def _():
            copy = pltpu.make_async_copy(source, out, sem)
            copy.start()
            copy.wait()

    for b in range(piece_blocks + 1):
        seen[b] = 0
    for part in range(2):

        @pl.loop(part * lay.slots, out[part])
        def _(i):
            entry = HEAD + STRIDE * i
            row = out[entry + 1]
            out[entry + 3] = jnp.where(seen[row] == 0, FIRST, 0)
            seen[row] = entry

    def close(b, bare):
        entry = seen[b]
        out[lay.bare_at + bare] = b

        @pl.when(entry > 0)
        def _():
            out[entry + 3] = out[entry + 3] + LAST

        return bare + jnp.where(entry == 0, 1, 0)

    out[6] = lax.fori_loop(0, piece_blocks, close, jnp.int32(0))
    out[7] = place[1]


def pick_kernel(n_row, block_size, wanted, vectors, out, sems):
    def fetch(k):
        at = pl.multiple_of(wanted[k, 0] * block_size, block_size)
        return pltpu.make_async_copy(vectors.at[pl.ds(at, block_size)], out.at[k], sems.at[k])

    for k in range(n_row):
        fetch(k).start()
    for k in range(n_row):
        fetch(k).wait()


def pack_kernel(place, picked, picked_b, out, held, sems):
    n_row, _, width = picked.shape
    middle = width // 2

    def put(k):
        return pltpu.make_async_copy(held.at[k], out.at[k], sems.at[k])

    for half in range(2):

        @pl.when(place[1] == half)
        def _():
            part = slice(half * middle, (half + 1) * middle)
            for k in range(n_row):
                held[k] = jnp.concatenate([picked[k, :, part], picked_b[k, :, part]], axis=1)
                put(k).start()

    for k in range(n_row):
        put(k).wait()


def fetches(plan, base, stride, ends, part, tiles, blocks, sems):
    def copy(tile, i):
        slot = plan[base + stride * i]
        return pltpu.make_async_copy(tile.at[slot], blocks.at[i], sems.at[i])

    def start():
        for side, tile in enumerate(tiles):

            @pl.loop(side * part, plan[ends + side])
            def _(i):
                copy(tile, i).start()

    def wait(i):
        copy(tiles[0], i).wait()

    return start, wait


def load_kernel(plan, tile_a, array, blocks, held, sems, held_sem):
    whole = pltpu.make_async_copy(array, held, held_sem)
    whole.start()
    start, wait = fetches(plan, HEAD, STRIDE, 0, 0, (tile_a,), blocks, sems)
    start()

    @pl.loop(0, plan[0])
    def _(i):
        wait(i)

    whole.wait()


def each_product(plan, base, ends, part, block_of, pieces, use, then=None, before=None):
    unroll = MANY if base == HEAD else FEW

    for side in range(2):

        @pl.loop(side * part // unroll, plan[ends + side] // unroll)
        def _(j):
            step = [(unroll * j + u, base + STRIDE * (unroll * j + u)) for u in range(unroll)]
            if before is not None:
                for i, entry in step:
                    before(side, i, entry)
            for i, entry in step:
                block = block_of(side, i, entry)
                piece = pieces[side][plan[entry + 2]]
                use(entry, jnp.dot(block, piece, preferred_element_type=jnp.float32))
            if then is not None:
                for i, entry in step:
                    then(entry)


def add_products(plan, base, ends, part, block_of, pieces, total, before=None):
    def use(entry, value):
        total[plan[entry + 1]] += value

    each_product(plan, base, ends, part, block_of, pieces, use, before=before)


def split_sides(pieces, vec):
    middle = vec.shape[-1] // 2
    column = lax.broadcasted_iota(jnp.int32, (1, vec.shape[-1]), 1)
    for side in range(2):
        keep = jnp.where((column // middle) == side, 1.0, 0.0).astype(jnp.bfloat16)
        for p in range(vec.shape[1]):
            vec[side, p] = pieces[p] * keep


def joined(total, k):
    one, two = total[2 * k], total[2 * k + 1]
    low = lax.broadcasted_iota(jnp.int32, one.shape, 1) < one.shape[1] // 2
    return jnp.where(low, one, two) + pltpu.roll(
        jnp.where(low, two, one), one.shape[1] // 2, axis=1
    )


def first_sent_kernel(
    lay, plan, tile_a, tile_b, pieces, start, out, blocks, vec, total, held, held_sem, sems
):
    n_row = out.shape[0]
    begin, wait = fetches(plan, lay.load_at, 1, 4, lay.loads, (tile_a, tile_b), blocks, sems)
    begin()
    copy = pltpu.make_async_copy(start, held, held_sem)
    copy.start()
    split_sides(pieces, vec)
    total[...] = jnp.zeros_like(total)

    def before(side, i, entry):
        @pl.when(plan[entry + 3] == FIRST)
        def _():
            wait(plan[entry])

    add_products(
        plan,
        lay.sent_at,
        2,
        lay.sends,
        lambda side, i, entry: blocks[plan[entry]],
        (vec.at[0], vec.at[1]),
        total,
        before,
    )
    copy.wait()
    for k in range(n_row):
        value = joined(total, k) - center_value * held[k].astype(jnp.float32)
        out[k] = (value / half_width).astype(jnp.bfloat16)


def second_sent_kernel(
    lay, plan, blocks, pieces, current, previous, out, vec, total, held, held_sem, ready, out_sems
):
    n_row = out.shape[0]
    copy = pltpu.make_async_copy(previous, held, held_sem)
    copy.start()
    split_sides(pieces, vec)
    total[...] = jnp.zeros_like(total)
    add_products(
        plan,
        lay.sent_at,
        2,
        lay.sends,
        lambda side, i, entry: blocks[plan[entry]],
        (vec.at[0], vec.at[1]),
        total,
    )
    copy.wait()

    def put(k):
        return pltpu.make_async_copy(ready.at[k], out.at[k], out_sems.at[k])

    for k in range(n_row):
        value = joined(total, k) - center_value * current[k].astype(jnp.float32)
        ready[k] = (value - held[k].astype(jnp.float32)).astype(jnp.bfloat16)
        put(k).start()
    for k in range(n_row):
        put(k).wait()


def whole_columns(half, mine, other, vec, at):
    n_row, _, width = mine.shape
    middle = width // 2

    @pl.when(half == 0)
    def _():
        @pl.loop(0, n_row)
        def _(p):
            one, two = mine[p], other[p]
            vec[0, p, :, at : at + width] = jnp.concatenate([one[:, :middle], two[:, middle:]], axis=1)
            vec[1, p, :, at : at + width] = jnp.concatenate([one[:, middle:], two[:, :middle]], axis=1)

    @pl.when(half != 0)
    def _():
        @pl.loop(0, n_row)
        def _(p):
            one, two = mine[p], other[p]
            vec[0, p, :, at : at + width] = jnp.concatenate([two[:, middle:], one[:, :middle]], axis=1)
            vec[1, p, :, at : at + width] = jnp.concatenate([two[:, :middle], one[:, middle:]], axis=1)


def early_kernel(
    lay,
    plan,
    tile_a,
    tile_b,
    q1,
    q1_other,
    q2,
    q2_other,
    vectors,
    base,
    vec,
    total,
    own,
    blocks,
    sem,
    sems,
    row_sems,
):
    width = vectors.shape[1]
    piece_blocks, block_size, _ = base.shape
    copy = pltpu.make_async_copy(vectors, own, sem)
    copy.start()
    begin, wait = fetches(plan, HEAD, STRIDE, 0, lay.slots, (tile_a, tile_b), blocks, sems)
    begin()
    whole_columns(plan[7], q1, q1_other, vec, 0)
    whole_columns(plan[7], q2, q2_other, vec, width)
    copy.wait()

    def rows(b):
        return pl.ds(pl.multiple_of(b * block_size, block_size), block_size)

    def put(b):
        return pltpu.make_async_copy(own.at[rows(b)], base.at[b], row_sems.at[b])

    @pl.loop(0, piece_blocks)
    def _(b):
        value = own[rows(b), :].astype(jnp.float32)
        total[b, :, :width] = -center_value * value
        total[b, :, width:] = -value

    add_products(
        plan,
        HEAD,
        0,
        lay.slots,
        lambda side, i, entry: blocks[i],
        (vec.at[0], vec.at[1]),
        total,
        lambda side, i, entry: wait(i),
    )

    @pl.loop(0, piece_blocks)
    def _(b):
        first = (total[b, :, :width] / half_width).astype(jnp.bfloat16).astype(jnp.float32)
        second = total[b, :, width:] - center_value * first
        second = second.astype(jnp.bfloat16).astype(jnp.float32)
        own[rows(b), :] = (-center_value * second - first).astype(jnp.bfloat16)
        put(b).start()

    @pl.loop(0, piece_blocks)
    def _(b):
        put(b).wait()


def last_kernel(
    lay, plan, blocks, tile_b, mine, other, base, out, vec, total, own, blocks_b, sems, row_sems
):
    piece_blocks = base.shape[0]
    begin = lay.slots

    def fetch(i):
        slot = plan[HEAD + STRIDE * i]
        return pltpu.make_async_copy(tile_b.at[slot], blocks_b.at[i - begin], sems.at[i - begin])

    @pl.loop(begin, plan[1])
    def _(i):
        fetch(i).start()

    def put(source, b):
        return pltpu.make_async_copy(source.at[b], out.at[b], row_sems.at[b])

    @pl.loop(0, plan[6])
    def _(i):
        b = plan[lay.bare_at + i]
        put(base, b).start()

    whole_columns(plan[7], mine, other, vec, 0)

    def use(entry, value):
        row = plan[entry + 1]
        marks = plan[entry + 3]
        start = base[jnp.minimum(row, piece_blocks - 1)].astype(jnp.float32)
        value = jnp.where(lax.rem(marks, LAST) == FIRST, start, total[row]) + value
        total[row] = value
        own[row] = value.astype(jnp.bfloat16)

    def then(entry):
        @pl.when(plan[entry + 3] >= LAST)
        def _():
            put(own, plan[entry + 1]).start()

    def block_of(side, i, entry):
        return blocks[i] if side == 0 else blocks_b[i - begin]

    def before(side, i, entry):
        if side == 1:
            fetch(i).wait()

    each_product(
        plan, HEAD, 0, lay.slots, block_of, (vec.at[0], vec.at[1]), use, then, before
    )

    @pl.loop(0, piece_blocks)
    def _(b):
        put(own, b).wait()


def after(value, *others):
    return lax.optimization_barrier((value, *others))[0]


def call(kernel, out, args, spaces, scratch, mib, name, estimate=None):
    args = [
        pltpu.with_memory_space_constraint(arg, space) if space in (VMEM, HBM) or tied else arg
        for arg, (space, tied) in zip(args, spaces)
    ]
    return pl.pallas_call(
        kernel,
        out_shape=[space(shape, dtype) for shape, dtype, space in out],
        in_specs=[spec(space) for space, _ in spaces],
        out_specs=[spec(space) for _, _, space in out],
        scratch_shapes=scratch,
        compiler_params=params(mib),
        cost_estimate=estimate,
        name=name,
    )(*args)


HERE = (VMEM, True)
FAR = (HBM, True)
LIST = (SMEM, True)
SCALARS = (SMEM, False)
ANYWHERE = (pl.ANY, False)


def on_pair(vectors, tile_blocks, block_rows, block_cols, counts):
    n_row = lax.axis_size("row")
    tile = tile_blocks[0, 0]
    slot_rows = block_rows[0, 0]
    slot_cols = block_cols[0, 0]
    used = counts[0]
    slot_count, block_size, _ = tile.shape
    width = vectors.shape[1]
    piece_blocks = vectors.shape[0] // block_size
    place = jnp.stack([lax.axis_index("row"), lax.axis_index("col")]).astype(jnp.int32)

    across = functools.partial(lax.ppermute, axis_name="col", perm=[(0, 1), (1, 0)])

    needed = jnp.max(
        jnp.where(
            slot_cols[None, :] // piece_blocks == jnp.arange(n_row)[:, None],
            slot_cols[None, :] % piece_blocks,
            0,
        ),
        axis=1,
        keepdims=True,
    )
    exchange = functools.partial(
        lax.all_to_all, axis_name="row", split_axis=0, concat_axis=0, tiled=True
    )
    meta = jnp.concatenate([slot_rows, slot_cols, used])
    meta_other = across(meta)
    wanted = after(exchange(jnp.broadcast_to(needed, (n_row, LANES))), meta_other, place)
    sent_shape = (n_row, block_size, width)
    (sent,) = call(
        functools.partial(pick_kernel, n_row, block_size),
        [(sent_shape, jnp.bfloat16, VMEM)],
        (wanted, vectors),
        (SCALARS, FAR),
        [DMA((n_row,))],
        2,
        "pick",
    )
    tile_other = across(tile)
    sent_other = across(sent)
    wanted_other = across(after(wanted, sent))
    packed = call(
        pack_kernel,
        [(sent_shape, jnp.bfloat16, HBM)],
        (place, sent, sent_other),
        (SCALARS, HERE, HERE),
        [VMEM(sent_shape, jnp.bfloat16), DMA((n_row,))],
        4,
        "pack",
    )[0]

    lay = layout_for(slot_count, n_row, piece_blocks)
    list_shape = ((lay.size,), jnp.int32)
    own_list, other_list = call(
        functools.partial(plan_kernel, n_row, piece_blocks, lay),
        [(*list_shape, HBM)] * 2,
        (place, wanted, after(wanted_other, packed), meta, meta_other),
        (SCALARS,) * 5,
        [
            SMEM((2 * lay.size,), jnp.int32),
            SMEM((2 * piece_blocks,), jnp.int32),
            SMEM((2 * piece_blocks * n_row,), jnp.int32),
            DMA((2,)),
        ],
        2,
        "plan",
    )
    q1 = exchange(after(packed, own_list))
    plan = call(
        functools.partial(settle_kernel, piece_blocks, lay),
        [(*list_shape, SMEM)],
        (place, own_list, across(after(other_list, packed))),
        (SCALARS, ANYWHERE, ANYWHERE),
        [SMEM((piece_blocks + 1,), jnp.int32), DMA],
        2,
        "settle",
    )[0]

    def load(cue, array):
        return call(
            load_kernel,
            [
                ((lay.slots, block_size, block_size), jnp.bfloat16, VMEM),
                (array.shape, array.dtype, VMEM),
            ],
            (after(plan, cue), tile, array),
            (LIST, FAR, FAR),
            [DMA((lay.slots,)), DMA],
            2,
            "load",
        )

    def cost(products, rows):
        size = block_size * width
        return pl.CostEstimate(
            flops=2 * products * block_size * size,
            bytes_accessed=2 * (products * block_size * block_size + 3 * rows * size),
            transcendentals=0,
        )

    sums = [
        VMEM((2, n_row, block_size, width), jnp.bfloat16),
        VMEM((2 * n_row + 1, block_size, width), jnp.float32),
    ]

    def first_blocks(*args):
        return call(
            functools.partial(first_sent_kernel, lay),
            [
                (sent_shape, jnp.bfloat16, VMEM),
                ((2 * lay.loads, block_size, block_size), jnp.bfloat16, VMEM),
            ],
            (plan, tile, tile_other, *args),
            (LIST, FAR, ANYWHERE, HERE, FAR),
            sums + [VMEM(sent_shape, jnp.bfloat16), DMA, DMA((2 * lay.loads,))],
            8,
            "sent",
            cost(n_row, n_row),
        )

    def second_blocks(*args):
        return call(
            functools.partial(second_sent_kernel, lay),
            [(sent_shape, jnp.bfloat16, HBM)],
            (plan, *args),
            (LIST, HERE, HERE, HERE, FAR),
            sums
            + [VMEM(sent_shape, jnp.bfloat16), DMA, VMEM(sent_shape, jnp.bfloat16), DMA((n_row,))],
            8,
            "sent",
            cost(n_row, n_row),
        )[0]

    base_shape = (piece_blocks, block_size, width)

    def early(*args):
        return call(
            functools.partial(early_kernel, lay),
            [(base_shape, jnp.bfloat16, HBM)],
            (plan, tile, tile_other, *args),
            (LIST, FAR, ANYWHERE, HERE, HERE, HERE, HERE, FAR),
            [
                VMEM((2, n_row, block_size, 2 * width), jnp.bfloat16),
                VMEM((piece_blocks + 1, block_size, 2 * width), jnp.float32),
                VMEM(vectors.shape, jnp.bfloat16),
                VMEM((2 * lay.slots, block_size, block_size), jnp.bfloat16),
                DMA,
                DMA((2 * lay.slots,)),
                DMA((piece_blocks,)),
            ],
            28,
            "early",
            cost(2 * slot_count, 2 * piece_blocks),
        )[0]

    def last(blocks, *args):
        rows = (piece_blocks + 1, block_size, width)
        (out,) = call(
            functools.partial(last_kernel, lay),
            [(base_shape, jnp.bfloat16, HBM)],
            (plan, blocks, tile_other, *args),
            (LIST, HERE, ANYWHERE, HERE, HERE, HERE),
            [
                VMEM((2, n_row, block_size, width), jnp.bfloat16),
                VMEM(rows, jnp.float32),
                VMEM(rows, jnp.bfloat16),
                VMEM((lay.slots, block_size, block_size), jnp.bfloat16),
                DMA((lay.slots,)),
                DMA((piece_blocks,)),
            ],
            14,
            "last",
            cost(slot_count, piece_blocks),
        )
        return out.reshape(vectors.shape)

    q1 = after(q1, plan)
    first_sent, blocks = first_blocks(q1, packed)
    q2 = exchange(first_sent)
    second_sent = second_blocks(blocks, q2, first_sent, packed)
    q1_other = across(after(q1, second_sent))
    q2_other = across(after(q2, second_sent))
    base = early(q1, q1_other, q2, q2_other, vectors)
    q3 = after(exchange(second_sent), base)
    q3_other = across(q3)
    blocks, base = load(q3, base)
    return last(blocks, q3, q3_other, base)


def on_any(vectors, tile_blocks, block_rows, block_cols, counts):
    n_row = lax.axis_size("row")
    n_col = lax.axis_size("col")
    tile_data = tile_blocks[0, 0]
    slot_rows = block_rows[0, 0]
    slot_cols = block_cols[0, 0]
    used = counts[0, 0]
    block_size = tile_data.shape[-1]
    width = vectors.shape[1]
    piece_blocks = vectors.shape[0] // block_size
    row_blocks = piece_blocks * n_col
    slot_count = tile_data.shape[0]
    live = (jnp.arange(slot_count) < used).astype(jnp.float32)
    onehot = (slot_rows[None, :] == jnp.arange(row_blocks)[:, None]).astype(jnp.float32) * live[
        None, :
    ]
    source_piece = slot_cols // piece_blocks
    offset = slot_cols % piece_blocks
    needed = jnp.max(
        jnp.where(source_piece[None, :] == jnp.arange(n_row)[:, None], offset[None, :], 0), axis=1
    )
    wanted = lax.all_to_all(
        needed.reshape(n_row, 1), "row", split_axis=0, concat_axis=0, tiled=True
    ).reshape(n_row)

    def apply_tiles(current):
        own_blocks = current.reshape(piece_blocks, block_size, width)
        outgoing = jnp.take(own_blocks, wanted, axis=0)
        received = lax.all_to_all(outgoing, "row", split_axis=0, concat_axis=0, tiled=True)
        vec_blocks = jnp.take(received, source_piece, axis=0)
        products = jnp.einsum(
            "sij,sjk->sik", tile_data, vec_blocks, preferred_element_type=jnp.float32
        )
        term = jnp.einsum("ls,sik->lik", onehot, products, precision=lax.Precision.HIGHEST)
        term = term.reshape(row_blocks * block_size, width)
        return lax.psum_scatter(
            term.astype(jnp.bfloat16), "col", scatter_dimension=0, tiled=True
        ).astype(jnp.float32)

    previous = vectors
    applied = apply_tiles(vectors)
    current = ((applied - center_value * previous.astype(jnp.float32)) / half_width).astype(
        jnp.bfloat16
    )
    for repeat in range(DEGREE - 1):
        applied = apply_tiles(current)
        following = (
            2.0 * (applied - center_value * current.astype(jnp.float32)) / half_width
            - previous.astype(jnp.float32)
        ).astype(jnp.bfloat16)
        previous, current = (current, following)
    return current


def solution(mesh):
    n_row, n_col = mesh.shape["row"], mesh.shape["col"]
    paired = n_col == 2 and n_row & (n_row - 1) == 0
    return jax.shard_map(
        on_pair if paired else on_any,
        mesh=mesh,
        in_specs=(
            P(("row", "col"), "vec"),
            P("row", "col", None, None, None),
            P("row", "col", None),
            P("row", "col", None),
            P("row", "col"),
        ),
        out_specs=P(("row", "col"), "vec"),
        check_vma=False,
    )
```

```python
import functools
import typing

import jax
import jax.numpy as jnp
from jax import lax
from jax.experimental import pallas as pl
from jax.experimental.pallas import tpu as pltpu
from jax.sharding import PartitionSpec as P

DEGREE = 3

center_value = 0.5
half_width = 2.0

VMEM = pltpu.VMEM
SMEM = pltpu.SMEM
HBM = pltpu.HBM
DMA = pltpu.SemaphoreType.DMA
LANES = 128
FEW = 4
MANY = 4
HEAD = 8
STRIDE = 4
FIRST = 1
LAST = 2


def spec(space):
    return pl.BlockSpec(memory_space=space)


def params(mib):
    return pltpu.CompilerParams(vmem_limit_bytes=mib * 1024 * 1024)


def round_up(n, step):
    return (n + step - 1) // step * step


class Layout(typing.NamedTuple):
    slots: int
    sends: int
    loads: int
    sent_at: int
    load_at: int
    bare_at: int
    size: int


def layout_for(slot_count, n_row, piece_blocks):
    slots = round_up(slot_count, MANY) + MANY
    sends = round_up(2 * n_row * n_row, FEW) + FEW
    sent_at = HEAD + STRIDE * 2 * slots
    load_at = sent_at + STRIDE * 2 * sends
    bare_at = load_at + 2 * (slot_count + 1)
    size = round_up(bare_at + piece_blocks, 8 * LANES)
    return Layout(slots, sends, slot_count + 1, sent_at, load_at, bare_at, size)


def plan_kernel(
    n_row,
    piece_blocks,
    lay,
    place,
    wanted_a,
    wanted_b,
    meta_a,
    meta_b,
    own,
    other,
    out,
    count,
    asked,
    seen,
    sems,
):
    slot_count = (meta_a.shape[0] - 1) // 2

    def put(at, *values):
        for i, value in enumerate(values):
            out[at + i] = value

    def scan(tile, meta):
        used = meta[2 * slot_count]

        def step(s, carry):
            ends, sent, load = carry
            row = meta[s]
            piece = meta[slot_count + s] // piece_blocks
            live = s < used
            half = row // piece_blocks
            local = row - half * piece_blocks
            lower = half == 0
            part = jnp.where(lower, tile, 1 - tile)
            at = HEAD + STRIDE * (part * lay.slots + jnp.where(lower, ends[0], ends[1]))
            base = half * lay.size
            put(base + at, s, local, piece)
            found = jnp.where(live, count[row], 0)

            @pl.when(found > 0)
            def _():
                for core in range(2):
                    mine = tile if core == 0 else 1 - tile
                    side = half if core == 0 else 1 - half
                    first = core * lay.size
                    out[first + lay.load_at + mine * lay.loads + load] = s

                    @pl.loop(0, found)
                    def _(j):
                        put(
                            first + lay.sent_at + STRIDE * (mine * lay.sends + sent + j),
                            mine * lay.loads + load,
                            2 * asked[row * n_row + j] + side,
                            piece,
                            jnp.where(j == 0, FIRST, 0),
                        )

            one = live.astype(jnp.int32)
            ends = (ends[0] + jnp.where(lower, one, 0), ends[1] + jnp.where(lower, 0, one))
            return ends, sent + found, load + jnp.where(found > 0, 1, 0)

        zero = jnp.int32(0)
        ends, sent, load = lax.fori_loop(0, slot_count, step, ((zero, zero), zero, zero))
        for core in range(2):
            mine = tile if core == 0 else 1 - tile
            base = core * lay.size
            for i, (at, begin, end, unit, spare) in enumerate(
                (
                    (HEAD, mine * lay.slots, ends[core], MANY, piece_blocks),
                    (lay.sent_at, mine * lay.sends, sent, FEW, 2 * n_row),
                )
            ):
                for u in range(unit - 1):
                    put(base + at + STRIDE * (begin + end + u), 0, spare, 0, 0)
                out[base + 2 * i + mine] = begin + (end + unit - 1) // unit * unit
            out[base + 4 + mine] = mine * lay.loads + load

    def mark(core):
        base = core * lay.size
        for b in range(piece_blocks + 1):
            seen[b] = 0
        for part in range(2):

            @pl.loop(part * lay.slots, out[base + part])
            def _(i):
                entry = base + HEAD + STRIDE * i
                row = out[entry + 1]
                out[entry + 3] = jnp.where(seen[row] == 0, FIRST, 0)
                seen[row] = entry

        def close(b, bare):
            entry = seen[b]
            out[base + lay.bare_at + bare] = b

            @pl.when(entry > 0)
            def _():
                out[entry + 3] = out[entry + 3] + LAST

            return bare + jnp.where(entry == 0, 1, 0)

        out[base + 6] = lax.fori_loop(0, piece_blocks, close, jnp.int32(0))
        out[base + 7] = core

    @pl.when(place[1] == 0)
    def _():
        for row in range(2 * piece_blocks):
            count[row] = 0
        for half, wanted in enumerate((wanted_a, wanted_b)):
            for k in range(n_row):
                row = half * piece_blocks + wanted[k, 0]
                number = count[row]
                asked[row * n_row + number] = k
                count[row] = number + 1
        scan(0, meta_a)
        scan(1, meta_b)
        for core in range(2):
            mark(core)
        copies = [
            pltpu.make_async_copy(out.at[pl.ds(core * lay.size, lay.size)], target, sems.at[core])
            for core, target in enumerate((own, other))
        ]
        for copy in copies:
            copy.start()
        for copy in copies:
            copy.wait()


def settle_kernel(place, own, handed, out, sem):
    for half, source in enumerate((own, handed)):

        @pl.when(place[1] == half)
        def _():
            copy = pltpu.make_async_copy(source, out, sem)
            copy.start()
            copy.wait()


def pick_kernel(n_row, block_size, wanted, vectors, out, sems):
    def fetch(k):
        at = pl.multiple_of(wanted[k, 0] * block_size, block_size)
        return pltpu.make_async_copy(vectors.at[pl.ds(at, block_size)], out.at[k], sems.at[k])

    for k in range(n_row):
        fetch(k).start()
    for k in range(n_row):
        fetch(k).wait()


def pack_kernel(place, picked, picked_b, out, held, sems):
    n_row, _, width = picked.shape
    middle = width // 2

    def put(k):
        return pltpu.make_async_copy(held.at[k], out.at[k], sems.at[k])

    for half in range(2):

        @pl.when(place[1] == half)
        def _():
            part = slice(half * middle, (half + 1) * middle)
            for k in range(n_row):
                held[k] = jnp.concatenate([picked[k, :, part], picked_b[k, :, part]], axis=1)
                put(k).start()

    for k in range(n_row):
        put(k).wait()


def fetches(plan, base, stride, ends, part, tiles, blocks, sems):
    def copy(tile, i):
        slot = plan[base + stride * i]
        return pltpu.make_async_copy(tile.at[slot], blocks.at[i], sems.at[i])

    def start():
        for side, tile in enumerate(tiles):

            @pl.loop(side * part, plan[ends + side])
            def _(i):
                copy(tile, i).start()

    def wait(i):
        copy(tiles[0], i).wait()

    return start, wait


def load_kernel(plan, tile_a, array, blocks, held, sems, held_sem):
    whole = pltpu.make_async_copy(array, held, held_sem)
    whole.start()
    start, wait = fetches(plan, HEAD, STRIDE, 0, 0, (tile_a,), blocks, sems)
    start()

    @pl.loop(0, plan[0])
    def _(i):
        wait(i)

    whole.wait()


def each_product(plan, base, ends, part, block_of, pieces, use, then=None, before=None):
    unroll = MANY if base == HEAD else FEW

    for side in range(2):

        @pl.loop(side * part // unroll, plan[ends + side] // unroll)
        def _(j):
            step = [(unroll * j + u, base + STRIDE * (unroll * j + u)) for u in range(unroll)]
            if before is not None:
                for i, entry in step:
                    before(side, i, entry)
            for i, entry in step:
                block = block_of(side, i, entry)
                piece = pieces[side][plan[entry + 2]]
                use(entry, jnp.dot(block, piece, preferred_element_type=jnp.float32))
            if then is not None:
                for i, entry in step:
                    then(entry)


def add_products(plan, base, ends, part, block_of, pieces, total, before=None):
    def use(entry, value):
        total[plan[entry + 1]] += value

    each_product(plan, base, ends, part, block_of, pieces, use, before=before)


def split_sides(pieces, vec):
    middle = vec.shape[-1] // 2
    column = lax.broadcasted_iota(jnp.int32, (1, vec.shape[-1]), 1)
    for side in range(2):
        keep = jnp.where((column // middle) == side, 1.0, 0.0).astype(jnp.bfloat16)
        for p in range(vec.shape[1]):
            vec[side, p] = pieces[p] * keep


def joined(total, k):
    one, two = total[2 * k], total[2 * k + 1]
    low = lax.broadcasted_iota(jnp.int32, one.shape, 1) < one.shape[1] // 2
    return jnp.where(low, one, two) + pltpu.roll(
        jnp.where(low, two, one), one.shape[1] // 2, axis=1
    )


def first_sent_kernel(
    lay, plan, tile_a, tile_b, pieces, start, out, blocks, vec, total, held, held_sem, sems
):
    n_row = out.shape[0]
    begin, wait = fetches(plan, lay.load_at, 1, 4, lay.loads, (tile_a, tile_b), blocks, sems)
    begin()
    copy = pltpu.make_async_copy(start, held, held_sem)
    copy.start()
    split_sides(pieces, vec)
    total[...] = jnp.zeros_like(total)

    def before(side, i, entry):
        @pl.when(plan[entry + 3] == FIRST)
        def _():
            wait(plan[entry])

    add_products(
        plan,
        lay.sent_at,
        2,
        lay.sends,
        lambda side, i, entry: blocks[plan[entry]],
        (vec.at[0], vec.at[1]),
        total,
        before,
    )
    copy.wait()
    for k in range(n_row):
        value = joined(total, k) - center_value * held[k].astype(jnp.float32)
        out[k] = (value / half_width).astype(jnp.bfloat16)


def second_sent_kernel(
    lay, plan, blocks, pieces, current, previous, out, vec, total, held, held_sem, ready, out_sems
):
    n_row = out.shape[0]
    copy = pltpu.make_async_copy(previous, held, held_sem)
    copy.start()
    split_sides(pieces, vec)
    total[...] = jnp.zeros_like(total)
    add_products(
        plan,
        lay.sent_at,
        2,
        lay.sends,
        lambda side, i, entry: blocks[plan[entry]],
        (vec.at[0], vec.at[1]),
        total,
    )
    copy.wait()

    def put(k):
        return pltpu.make_async_copy(ready.at[k], out.at[k], out_sems.at[k])

    for k in range(n_row):
        value = joined(total, k) - center_value * current[k].astype(jnp.float32)
        ready[k] = (value - held[k].astype(jnp.float32)).astype(jnp.bfloat16)
        put(k).start()
    for k in range(n_row):
        put(k).wait()


def whole_columns(half, mine, other, vec, at):
    n_row, _, width = mine.shape
    middle = width // 2

    @pl.when(half == 0)
    def _():
        @pl.loop(0, n_row)
        def _(p):
            one, two = mine[p], other[p]
            vec[0, p, :, at : at + width] = jnp.concatenate([one[:, :middle], two[:, middle:]], axis=1)
            vec[1, p, :, at : at + width] = jnp.concatenate([one[:, middle:], two[:, :middle]], axis=1)

    @pl.when(half != 0)
    def _():
        @pl.loop(0, n_row)
        def _(p):
            one, two = mine[p], other[p]
            vec[0, p, :, at : at + width] = jnp.concatenate([two[:, middle:], one[:, :middle]], axis=1)
            vec[1, p, :, at : at + width] = jnp.concatenate([two[:, :middle], one[:, middle:]], axis=1)


def early_kernel(
    lay,
    plan,
    tile_a,
    tile_b,
    q1,
    q1_other,
    q2,
    q2_other,
    vectors,
    base,
    vec,
    total,
    own,
    blocks,
    sem,
    sems,
    row_sems,
):
    width = vectors.shape[1]
    piece_blocks, block_size, _ = base.shape
    copy = pltpu.make_async_copy(vectors, own, sem)
    copy.start()
    begin, wait = fetches(plan, HEAD, STRIDE, 0, lay.slots, (tile_a, tile_b), blocks, sems)
    begin()
    whole_columns(plan[7], q1, q1_other, vec, 0)
    whole_columns(plan[7], q2, q2_other, vec, width)
    copy.wait()

    def rows(b):
        return pl.ds(pl.multiple_of(b * block_size, block_size), block_size)

    def put(b):
        return pltpu.make_async_copy(own.at[rows(b)], base.at[b], row_sems.at[b])

    @pl.loop(0, piece_blocks)
    def _(b):
        value = own[rows(b), :].astype(jnp.float32)
        total[b, :, :width] = -center_value * value
        total[b, :, width:] = -value

    add_products(
        plan,
        HEAD,
        0,
        lay.slots,
        lambda side, i, entry: blocks[i],
        (vec.at[0], vec.at[1]),
        total,
        lambda side, i, entry: wait(i),
    )

    @pl.loop(0, piece_blocks)
    def _(b):
        first = (total[b, :, :width] / half_width).astype(jnp.bfloat16).astype(jnp.float32)
        second = total[b, :, width:] - center_value * first
        second = second.astype(jnp.bfloat16).astype(jnp.float32)
        own[rows(b), :] = (-center_value * second - first).astype(jnp.bfloat16)
        put(b).start()

    @pl.loop(0, piece_blocks)
    def _(b):
        put(b).wait()


def last_kernel(
    lay, plan, blocks, tile_b, mine, other, base, out, vec, total, own, blocks_b, sems, row_sems
):
    piece_blocks = base.shape[0]
    begin = lay.slots

    def fetch(i):
        slot = plan[HEAD + STRIDE * i]
        return pltpu.make_async_copy(tile_b.at[slot], blocks_b.at[i - begin], sems.at[i - begin])

    @pl.loop(begin, plan[1])
    def _(i):
        fetch(i).start()

    def put(source, b):
        return pltpu.make_async_copy(source.at[b], out.at[b], row_sems.at[b])

    @pl.loop(0, plan[6])
    def _(i):
        b = plan[lay.bare_at + i]
        put(base, b).start()

    whole_columns(plan[7], mine, other, vec, 0)

    def use(entry, value):
        row = plan[entry + 1]
        marks = plan[entry + 3]
        start = base[jnp.minimum(row, piece_blocks - 1)].astype(jnp.float32)
        value = jnp.where(lax.rem(marks, LAST) == FIRST, start, total[row]) + value
        total[row] = value
        own[row] = value.astype(jnp.bfloat16)

    def then(entry):
        @pl.when(plan[entry + 3] >= LAST)
        def _():
            put(own, plan[entry + 1]).start()

    def block_of(side, i, entry):
        return blocks[i] if side == 0 else blocks_b[i - begin]

    def before(side, i, entry):
        if side == 1:
            fetch(i).wait()

    each_product(
        plan, HEAD, 0, lay.slots, block_of, (vec.at[0], vec.at[1]), use, then, before
    )

    @pl.loop(0, piece_blocks)
    def _(b):
        put(own, b).wait()


def after(value, *others):
    return lax.optimization_barrier((value, *others))[0]


def call(kernel, out, args, spaces, scratch, mib, name, estimate=None):
    args = [
        pltpu.with_memory_space_constraint(arg, space) if space in (VMEM, HBM) or tied else arg
        for arg, (space, tied) in zip(args, spaces)
    ]
    return pl.pallas_call(
        kernel,
        out_shape=[space(shape, dtype) for shape, dtype, space in out],
        in_specs=[spec(space) for space, _ in spaces],
        out_specs=[spec(space) for _, _, space in out],
        scratch_shapes=scratch,
        compiler_params=params(mib),
        cost_estimate=estimate,
        name=name,
    )(*args)


HERE = (VMEM, True)
FAR = (HBM, True)
LIST = (SMEM, True)
SCALARS = (SMEM, False)
ANYWHERE = (pl.ANY, False)


def on_pair(vectors, tile_blocks, block_rows, block_cols, counts):
    n_row = lax.axis_size("row")
    tile = tile_blocks[0, 0]
    slot_rows = block_rows[0, 0]
    slot_cols = block_cols[0, 0]
    used = counts[0]
    slot_count, block_size, _ = tile.shape
    width = vectors.shape[1]
    piece_blocks = vectors.shape[0] // block_size
    place = jnp.stack([lax.axis_index("row"), lax.axis_index("col")]).astype(jnp.int32)

    across = functools.partial(lax.ppermute, axis_name="col", perm=[(0, 1), (1, 0)])

    needed = jnp.max(
        jnp.where(
            slot_cols[None, :] // piece_blocks == jnp.arange(n_row)[:, None],
            slot_cols[None, :] % piece_blocks,
            0,
        ),
        axis=1,
        keepdims=True,
    )
    exchange = functools.partial(
        lax.all_to_all, axis_name="row", split_axis=0, concat_axis=0, tiled=True
    )
    meta = jnp.concatenate([slot_rows, slot_cols, used])
    meta_other = across(meta)
    wanted = after(exchange(jnp.broadcast_to(needed, (n_row, LANES))), meta_other, place)
    sent_shape = (n_row, block_size, width)
    (sent,) = call(
        functools.partial(pick_kernel, n_row, block_size),
        [(sent_shape, jnp.bfloat16, VMEM)],
        (wanted, vectors),
        (SCALARS, FAR),
        [DMA((n_row,))],
        2,
        "pick",
    )
    tile_other = across(tile)
    sent_other = across(sent)
    wanted_other = across(after(wanted, sent))
    packed = call(
        pack_kernel,
        [(sent_shape, jnp.bfloat16, HBM)],
        (place, sent, sent_other),
        (SCALARS, HERE, HERE),
        [VMEM(sent_shape, jnp.bfloat16), DMA((n_row,))],
        4,
        "pack",
    )[0]

    lay = layout_for(slot_count, n_row, piece_blocks)
    list_shape = ((lay.size,), jnp.int32)
    own_list, other_list = call(
        functools.partial(plan_kernel, n_row, piece_blocks, lay),
        [(*list_shape, HBM)] * 2,
        (place, wanted, after(wanted_other, packed), meta, meta_other),
        (SCALARS,) * 5,
        [
            SMEM((2 * lay.size,), jnp.int32),
            SMEM((2 * piece_blocks,), jnp.int32),
            SMEM((2 * piece_blocks * n_row,), jnp.int32),
            SMEM((piece_blocks + 1,), jnp.int32),
            DMA((2,)),
        ],
        2,
        "plan",
    )
    q1 = exchange(after(packed, own_list))
    plan = call(
        settle_kernel,
        [(*list_shape, SMEM)],
        (place, own_list, across(after(other_list, packed))),
        (SCALARS, ANYWHERE, ANYWHERE),
        [DMA],
        2,
        "settle",
    )[0]

    def load(cue, array):
        return call(
            load_kernel,
            [
                ((lay.slots, block_size, block_size), jnp.bfloat16, VMEM),
                (array.shape, array.dtype, VMEM),
            ],
            (after(plan, cue), tile, array),
            (LIST, FAR, FAR),
            [DMA((lay.slots,)), DMA],
            2,
            "load",
        )

    def cost(products, rows):
        size = block_size * width
        return pl.CostEstimate(
            flops=2 * products * block_size * size,
            bytes_accessed=2 * (products * block_size * block_size + 3 * rows * size),
            transcendentals=0,
        )

    sums = [
        VMEM((2, n_row, block_size, width), jnp.bfloat16),
        VMEM((2 * n_row + 1, block_size, width), jnp.float32),
    ]

    def first_blocks(*args):
        return call(
            functools.partial(first_sent_kernel, lay),
            [
                (sent_shape, jnp.bfloat16, VMEM),
                ((2 * lay.loads, block_size, block_size), jnp.bfloat16, VMEM),
            ],
            (plan, tile, tile_other, *args),
            (LIST, FAR, ANYWHERE, HERE, FAR),
            sums + [VMEM(sent_shape, jnp.bfloat16), DMA, DMA((2 * lay.loads,))],
            8,
            "sent",
            cost(n_row, n_row),
        )

    def second_blocks(*args):
        return call(
            functools.partial(second_sent_kernel, lay),
            [(sent_shape, jnp.bfloat16, HBM)],
            (plan, *args),
            (LIST, HERE, HERE, HERE, FAR),
            sums
            + [VMEM(sent_shape, jnp.bfloat16), DMA, VMEM(sent_shape, jnp.bfloat16), DMA((n_row,))],
            8,
            "sent",
            cost(n_row, n_row),
        )[0]

    base_shape = (piece_blocks, block_size, width)

    def early(*args):
        return call(
            functools.partial(early_kernel, lay),
            [(base_shape, jnp.bfloat16, HBM)],
            (plan, tile, tile_other, *args),
            (LIST, FAR, ANYWHERE, HERE, HERE, HERE, HERE, FAR),
            [
                VMEM((2, n_row, block_size, 2 * width), jnp.bfloat16),
                VMEM((piece_blocks + 1, block_size, 2 * width), jnp.float32),
                VMEM(vectors.shape, jnp.bfloat16),
                VMEM((2 * lay.slots, block_size, block_size), jnp.bfloat16),
                DMA,
                DMA((2 * lay.slots,)),
                DMA((piece_blocks,)),
            ],
            28,
            "early",
            cost(2 * slot_count, 2 * piece_blocks),
        )[0]

    def last(blocks, *args):
        rows = (piece_blocks + 1, block_size, width)
        (out,) = call(
            functools.partial(last_kernel, lay),
            [(base_shape, jnp.bfloat16, HBM)],
            (plan, blocks, tile_other, *args),
            (LIST, HERE, ANYWHERE, HERE, HERE, HERE),
            [
                VMEM((2, n_row, block_size, width), jnp.bfloat16),
                VMEM(rows, jnp.float32),
                VMEM(rows, jnp.bfloat16),
                VMEM((lay.slots, block_size, block_size), jnp.bfloat16),
                DMA((lay.slots,)),
                DMA((piece_blocks,)),
            ],
            14,
            "last",
            cost(slot_count, piece_blocks),
        )
        return out.reshape(vectors.shape)

    q1 = after(q1, plan)
    first_sent, blocks = first_blocks(q1, packed)
    q2 = exchange(first_sent)
    second_sent = second_blocks(blocks, q2, first_sent, packed)
    q1_other = across(after(q1, second_sent))
    q2_other = across(after(q2, second_sent))
    base = early(q1, q1_other, q2, q2_other, vectors)
    q3 = after(exchange(second_sent), base)
    q3_other = across(q3)
    blocks, base = load(q3, base)
    return last(blocks, q3, q3_other, base)


def on_any(vectors, tile_blocks, block_rows, block_cols, counts):
    n_row = lax.axis_size("row")
    n_col = lax.axis_size("col")
    tile_data = tile_blocks[0, 0]
    slot_rows = block_rows[0, 0]
    slot_cols = block_cols[0, 0]
    used = counts[0, 0]
    block_size = tile_data.shape[-1]
    width = vectors.shape[1]
    piece_blocks = vectors.shape[0] // block_size
    row_blocks = piece_blocks * n_col
    slot_count = tile_data.shape[0]
    live = (jnp.arange(slot_count) < used).astype(jnp.float32)
    onehot = (slot_rows[None, :] == jnp.arange(row_blocks)[:, None]).astype(jnp.float32) * live[
        None, :
    ]
    source_piece = slot_cols // piece_blocks
    offset = slot_cols % piece_blocks
    needed = jnp.max(
        jnp.where(source_piece[None, :] == jnp.arange(n_row)[:, None], offset[None, :], 0), axis=1
    )
    wanted = lax.all_to_all(
        needed.reshape(n_row, 1), "row", split_axis=0, concat_axis=0, tiled=True
    ).reshape(n_row)

    def apply_tiles(current):
        own_blocks = current.reshape(piece_blocks, block_size, width)
        outgoing = jnp.take(own_blocks, wanted, axis=0)
        received = lax.all_to_all(outgoing, "row", split_axis=0, concat_axis=0, tiled=True)
        vec_blocks = jnp.take(received, source_piece, axis=0)
        products = jnp.einsum(
            "sij,sjk->sik", tile_data, vec_blocks, preferred_element_type=jnp.float32
        )
        term = jnp.einsum("ls,sik->lik", onehot, products, precision=lax.Precision.HIGHEST)
        term = term.reshape(row_blocks * block_size, width)
        return lax.psum_scatter(
            term.astype(jnp.bfloat16), "col", scatter_dimension=0, tiled=True
        ).astype(jnp.float32)

    previous = vectors
    applied = apply_tiles(vectors)
    current = ((applied - center_value * previous.astype(jnp.float32)) / half_width).astype(
        jnp.bfloat16
    )
    for repeat in range(DEGREE - 1):
        applied = apply_tiles(current)
        following = (
            2.0 * (applied - center_value * current.astype(jnp.float32)) / half_width
            - previous.astype(jnp.float32)
        ).astype(jnp.bfloat16)
        previous, current = (current, following)
    return current


def solution(mesh):
    n_row, n_col = mesh.shape["row"], mesh.shape["col"]
    paired = n_col == 2 and n_row & (n_row - 1) == 0
    return jax.shard_map(
        on_pair if paired else on_any,
        mesh=mesh,
        in_specs=(
            P(("row", "col"), "vec"),
            P("row", "col", None, None, None),
            P("row", "col", None),
            P("row", "col", None),
            P("row", "col"),
        ),
        out_specs=P(("row", "col"), "vec"),
        check_vma=False,
    )
```

```python
import functools
import typing

import jax
import jax.numpy as jnp
from jax import lax
from jax.experimental import pallas as pl
from jax.experimental.pallas import tpu as pltpu
from jax.sharding import PartitionSpec as P

DEGREE = 3

center_value = 0.5
half_width = 2.0

VMEM = pltpu.VMEM
SMEM = pltpu.SMEM
HBM = pltpu.HBM
DMA = pltpu.SemaphoreType.DMA
LANES = 128
FEW = 4
MANY = 4
HEAD = 8
STRIDE = 4
FIRST = 1
LAST = 2


def spec(space):
    return pl.BlockSpec(memory_space=space)


def params(mib):
    return pltpu.CompilerParams(vmem_limit_bytes=mib * 1024 * 1024)


def round_up(n, step):
    return (n + step - 1) // step * step


class Layout(typing.NamedTuple):
    slots: int
    sends: int
    loads: int
    sent_at: int
    load_at: int
    bare_at: int
    size: int


def layout_for(slot_count, n_row, piece_blocks):
    slots = round_up(slot_count, MANY) + MANY
    sends = round_up(2 * n_row * n_row, FEW) + FEW
    sent_at = HEAD + STRIDE * 2 * slots
    load_at = sent_at + STRIDE * 2 * sends
    bare_at = load_at + 2 * (slot_count + 1)
    size = round_up(bare_at + piece_blocks, 8 * LANES)
    return Layout(slots, sends, slot_count + 1, sent_at, load_at, bare_at, size)


def plan_kernel(
    n_row,
    piece_blocks,
    lay,
    place,
    wanted_a,
    wanted_b,
    rows_a,
    cols_a,
    used_a,
    rows_b,
    cols_b,
    used_b,
    own,
    other,
    out,
    count,
    asked,
    seen,
    sems,
):
    slot_count = rows_a.shape[0]

    def put(at, *values):
        for i, value in enumerate(values):
            out[at + i] = value

    def scan(tile, rows, cols, used):

        def step(s, carry):
            ends, sent, load = carry
            row = rows[s]
            piece = cols[s] // piece_blocks
            live = s < used[0]
            half = row // piece_blocks
            local = row - half * piece_blocks
            lower = half == 0
            part = jnp.where(lower, tile, 1 - tile)
            at = HEAD + STRIDE * (part * lay.slots + jnp.where(lower, ends[0], ends[1]))
            base = half * lay.size
            put(base + at, s, local, piece)
            found = jnp.where(live, count[row], 0)

            @pl.when(found > 0)
            def _():
                for core in range(2):
                    mine = tile if core == 0 else 1 - tile
                    side = half if core == 0 else 1 - half
                    first = core * lay.size
                    out[first + lay.load_at + mine * lay.loads + load] = s

                    @pl.loop(0, found)
                    def _(j):
                        put(
                            first + lay.sent_at + STRIDE * (mine * lay.sends + sent + j),
                            mine * lay.loads + load,
                            2 * asked[row * n_row + j] + side,
                            piece,
                            jnp.where(j == 0, FIRST, 0),
                        )

            one = live.astype(jnp.int32)
            ends = (ends[0] + jnp.where(lower, one, 0), ends[1] + jnp.where(lower, 0, one))
            return ends, sent + found, load + jnp.where(found > 0, 1, 0)

        zero = jnp.int32(0)
        ends, sent, load = lax.fori_loop(0, slot_count, step, ((zero, zero), zero, zero))
        for core in range(2):
            mine = tile if core == 0 else 1 - tile
            base = core * lay.size
            for i, (at, begin, end, unit, spare) in enumerate(
                (
                    (HEAD, mine * lay.slots, ends[core], MANY, piece_blocks),
                    (lay.sent_at, mine * lay.sends, sent, FEW, 2 * n_row),
                )
            ):
                for u in range(unit - 1):
                    put(base + at + STRIDE * (begin + end + u), 0, spare, 0, 0)
                out[base + 2 * i + mine] = begin + (end + unit - 1) // unit * unit
            out[base + 4 + mine] = mine * lay.loads + load

    def mark(core):
        base = core * lay.size
        for b in range(piece_blocks + 1):
            seen[b] = 0
        for part in range(2):

            @pl.loop(part * lay.slots, out[base + part])
            def _(i):
                entry = base + HEAD + STRIDE * i
                row = out[entry + 1]
                out[entry + 3] = jnp.where(seen[row] == 0, FIRST, 0)
                seen[row] = entry

        def close(b, bare):
            entry = seen[b]
            out[base + lay.bare_at + bare] = b

            @pl.when(entry > 0)
            def _():
                out[entry + 3] = out[entry + 3] + LAST

            return bare + jnp.where(entry == 0, 1, 0)

        out[base + 6] = lax.fori_loop(0, piece_blocks, close, jnp.int32(0))
        out[base + 7] = core

    @pl.when(place[1] == 0)
    def _():
        for row in range(2 * piece_blocks):
            count[row] = 0
        for half, wanted in enumerate((wanted_a, wanted_b)):
            for k in range(n_row):
                row = half * piece_blocks + wanted[k, 0]
                number = count[row]
                asked[row * n_row + number] = k
                count[row] = number + 1
        scan(0, rows_a, cols_a, used_a)
        scan(1, rows_b, cols_b, used_b)
        for core in range(2):
            mark(core)
        copies = [
            pltpu.make_async_copy(out.at[pl.ds(core * lay.size, lay.size)], target, sems.at[core])
            for core, target in enumerate((own, other))
        ]
        for copy in copies:
            copy.start()
        for copy in copies:
            copy.wait()


def settle_kernel(place, own, handed, out, sem):
    for half, source in enumerate((own, handed)):

        @pl.when(place[1] == half)
        def _():
            copy = pltpu.make_async_copy(source, out, sem)
            copy.start()
            copy.wait()


def pick_kernel(n_row, block_size, wanted, vectors, out, sems):
    def fetch(k):
        at = pl.multiple_of(wanted[k, 0] * block_size, block_size)
        return pltpu.make_async_copy(vectors.at[pl.ds(at, block_size)], out.at[k], sems.at[k])

    for k in range(n_row):
        fetch(k).start()
    for k in range(n_row):
        fetch(k).wait()


def pack_kernel(place, picked, picked_b, out, held, sems):
    n_row, _, width = picked.shape
    middle = width // 2

    def put(k):
        return pltpu.make_async_copy(held.at[k], out.at[k], sems.at[k])

    for half in range(2):

        @pl.when(place[1] == half)
        def _():
            part = slice(half * middle, (half + 1) * middle)
            for k in range(n_row):
                held[k] = jnp.concatenate([picked[k, :, part], picked_b[k, :, part]], axis=1)
                put(k).start()

    for k in range(n_row):
        put(k).wait()


def fetches(plan, base, stride, ends, part, tiles, blocks, sems):
    def copy(tile, i):
        slot = plan[base + stride * i]
        return pltpu.make_async_copy(tile.at[slot], blocks.at[i], sems.at[i])

    def start():
        for side, tile in enumerate(tiles):

            @pl.loop(side * part, plan[ends + side])
            def _(i):
                copy(tile, i).start()

    def wait(i):
        copy(tiles[0], i).wait()

    return start, wait


def load_kernel(plan, tile_a, array, blocks, held, sems, held_sem):
    whole = pltpu.make_async_copy(array, held, held_sem)
    whole.start()
    start, wait = fetches(plan, HEAD, STRIDE, 0, 0, (tile_a,), blocks, sems)
    start()

    @pl.loop(0, plan[0])
    def _(i):
        wait(i)

    whole.wait()


def each_product(plan, base, ends, part, block_of, pieces, use, then=None, before=None):
    unroll = MANY if base == HEAD else FEW

    for side in range(2):

        @pl.loop(side * part // unroll, plan[ends + side] // unroll)
        def _(j):
            step = [(unroll * j + u, base + STRIDE * (unroll * j + u)) for u in range(unroll)]
            if before is not None:
                for i, entry in step:
                    before(side, i, entry)
            for i, entry in step:
                block = block_of(side, i, entry)
                piece = pieces[side][plan[entry + 2]]
                use(entry, jnp.dot(block, piece, preferred_element_type=jnp.float32))
            if then is not None:
                for i, entry in step:
                    then(entry)


def add_products(plan, base, ends, part, block_of, pieces, total, before=None):
    def use(entry, value):
        total[plan[entry + 1]] += value

    each_product(plan, base, ends, part, block_of, pieces, use, before=before)


def split_sides(pieces, vec):
    middle = vec.shape[-1] // 2
    column = lax.broadcasted_iota(jnp.int32, (1, vec.shape[-1]), 1)
    for side in range(2):
        keep = jnp.where((column // middle) == side, 1.0, 0.0).astype(jnp.bfloat16)
        for p in range(vec.shape[1]):
            vec[side, p] = pieces[p] * keep


def joined(total, k):
    one, two = total[2 * k], total[2 * k + 1]
    low = lax.broadcasted_iota(jnp.int32, one.shape, 1) < one.shape[1] // 2
    return jnp.where(low, one, two) + pltpu.roll(
        jnp.where(low, two, one), one.shape[1] // 2, axis=1
    )


def first_sent_kernel(
    lay, plan, tile_a, tile_b, pieces, start, out, blocks, vec, total, held, held_sem, sems
):
    n_row = out.shape[0]
    begin, wait = fetches(plan, lay.load_at, 1, 4, lay.loads, (tile_a, tile_b), blocks, sems)
    begin()
    copy = pltpu.make_async_copy(start, held, held_sem)
    copy.start()
    split_sides(pieces, vec)
    total[...] = jnp.zeros_like(total)

    def before(side, i, entry):
        @pl.when(plan[entry + 3] == FIRST)
        def _():
            wait(plan[entry])

    add_products(
        plan,
        lay.sent_at,
        2,
        lay.sends,
        lambda side, i, entry: blocks[plan[entry]],
        (vec.at[0], vec.at[1]),
        total,
        before,
    )
    copy.wait()
    for k in range(n_row):
        value = joined(total, k) - center_value * held[k].astype(jnp.float32)
        out[k] = (value / half_width).astype(jnp.bfloat16)


def second_sent_kernel(
    lay, plan, blocks, pieces, current, previous, out, vec, total, held, held_sem, ready, out_sems
):
    n_row = out.shape[0]
    copy = pltpu.make_async_copy(previous, held, held_sem)
    copy.start()
    split_sides(pieces, vec)
    total[...] = jnp.zeros_like(total)
    add_products(
        plan,
        lay.sent_at,
        2,
        lay.sends,
        lambda side, i, entry: blocks[plan[entry]],
        (vec.at[0], vec.at[1]),
        total,
    )
    copy.wait()

    def put(k):
        return pltpu.make_async_copy(ready.at[k], out.at[k], out_sems.at[k])

    for k in range(n_row):
        value = joined(total, k) - center_value * current[k].astype(jnp.float32)
        ready[k] = (value - held[k].astype(jnp.float32)).astype(jnp.bfloat16)
        put(k).start()
    for k in range(n_row):
        put(k).wait()


def whole_columns(half, mine, other, vec, at):
    n_row, _, width = mine.shape
    middle = width // 2

    @pl.when(half == 0)
    def _():
        for p in range(n_row):
            one, two = mine[p], other[p]
            vec[0, p, :, at : at + width] = jnp.concatenate([one[:, :middle], two[:, middle:]], axis=1)
            vec[1, p, :, at : at + width] = jnp.concatenate([one[:, middle:], two[:, :middle]], axis=1)

    @pl.when(half != 0)
    def _():
        for p in range(n_row):
            one, two = mine[p], other[p]
            vec[0, p, :, at : at + width] = jnp.concatenate([two[:, middle:], one[:, :middle]], axis=1)
            vec[1, p, :, at : at + width] = jnp.concatenate([two[:, :middle], one[:, middle:]], axis=1)


def early_kernel(
    lay,
    plan,
    tile_a,
    tile_b,
    q1,
    q1_other,
    q2,
    q2_other,
    vectors,
    base,
    vec,
    total,
    own,
    blocks,
    sem,
    sems,
    row_sems,
):
    width = vectors.shape[1]
    piece_blocks, block_size, _ = base.shape
    copy = pltpu.make_async_copy(vectors, own, sem)
    copy.start()
    begin, wait = fetches(plan, HEAD, STRIDE, 0, lay.slots, (tile_a, tile_b), blocks, sems)
    begin()
    whole_columns(plan[7], q1, q1_other, vec, 0)
    whole_columns(plan[7], q2, q2_other, vec, width)
    copy.wait()

    def rows(b):
        return pl.ds(pl.multiple_of(b * block_size, block_size), block_size)

    def put(b):
        return pltpu.make_async_copy(own.at[rows(b)], base.at[b], row_sems.at[b])

    @pl.loop(0, piece_blocks)
    def _(b):
        value = own[rows(b), :].astype(jnp.float32)
        total[b, :, :width] = -center_value * value
        total[b, :, width:] = -value

    add_products(
        plan,
        HEAD,
        0,
        lay.slots,
        lambda side, i, entry: blocks[i],
        (vec.at[0], vec.at[1]),
        total,
        lambda side, i, entry: wait(i),
    )

    @pl.loop(0, piece_blocks)
    def _(b):
        first = (total[b, :, :width] / half_width).astype(jnp.bfloat16).astype(jnp.float32)
        second = total[b, :, width:] - center_value * first
        second = second.astype(jnp.bfloat16).astype(jnp.float32)
        own[rows(b), :] = (-center_value * second - first).astype(jnp.bfloat16)
        put(b).start()

    @pl.loop(0, piece_blocks)
    def _(b):
        put(b).wait()


def last_kernel(
    lay, plan, blocks, tile_b, mine, other, base, out, vec, total, own, blocks_b, sems, row_sems
):
    piece_blocks = base.shape[0]
    begin = lay.slots

    def fetch(i):
        slot = plan[HEAD + STRIDE * i]
        return pltpu.make_async_copy(tile_b.at[slot], blocks_b.at[i - begin], sems.at[i - begin])

    @pl.loop(begin, plan[1])
    def _(i):
        fetch(i).start()

    def put(source, b):
        return pltpu.make_async_copy(source.at[b], out.at[b], row_sems.at[b])

    @pl.loop(0, plan[6])
    def _(i):
        b = plan[lay.bare_at + i]
        put(base, b).start()

    whole_columns(plan[7], mine, other, vec, 0)

    def use(entry, value):
        row = plan[entry + 1]
        marks = plan[entry + 3]
        start = base[jnp.minimum(row, piece_blocks - 1)].astype(jnp.float32)
        value = jnp.where(lax.rem(marks, LAST) == FIRST, start, total[row]) + value
        total[row] = value
        own[row] = value.astype(jnp.bfloat16)

    def then(entry):
        @pl.when(plan[entry + 3] >= LAST)
        def _():
            put(own, plan[entry + 1]).start()

    def block_of(side, i, entry):
        return blocks[i] if side == 0 else blocks_b[i - begin]

    def before(side, i, entry):
        if side == 1:
            fetch(i).wait()

    each_product(
        plan, HEAD, 0, lay.slots, block_of, (vec.at[0], vec.at[1]), use, then, before
    )

    @pl.loop(0, piece_blocks)
    def _(b):
        put(own, b).wait()


def after(value, *others):
    return lax.optimization_barrier((value, *others))[0]


def call(kernel, out, args, spaces, scratch, mib, name, estimate=None):
    args = [
        pltpu.with_memory_space_constraint(arg, space) if space in (VMEM, HBM) or tied else arg
        for arg, (space, tied) in zip(args, spaces)
    ]
    return pl.pallas_call(
        kernel,
        out_shape=[space(shape, dtype) for shape, dtype, space in out],
        in_specs=[spec(space) for space, _ in spaces],
        out_specs=[spec(space) for _, _, space in out],
        scratch_shapes=scratch,
        compiler_params=params(mib),
        cost_estimate=estimate,
        name=name,
    )(*args)


HERE = (VMEM, True)
FAR = (HBM, True)
LIST = (SMEM, True)
SCALARS = (SMEM, False)
ANYWHERE = (pl.ANY, False)


def on_pair(vectors, tile_blocks, block_rows, block_cols, counts):
    n_row = lax.axis_size("row")
    tile = tile_blocks[0, 0]
    slot_rows = block_rows[0, 0]
    slot_cols = block_cols[0, 0]
    used = counts[0]
    slot_count, block_size, _ = tile.shape
    width = vectors.shape[1]
    piece_blocks = vectors.shape[0] // block_size
    place = jnp.stack([lax.axis_index("row"), lax.axis_index("col")]).astype(jnp.int32)

    across = functools.partial(lax.ppermute, axis_name="col", perm=[(0, 1), (1, 0)])

    needed = jnp.max(
        jnp.where(
            slot_cols[None, :] // piece_blocks == jnp.arange(n_row)[:, None],
            slot_cols[None, :] % piece_blocks,
            0,
        ),
        axis=1,
        keepdims=True,
    )
    exchange = functools.partial(
        lax.all_to_all, axis_name="row", split_axis=0, concat_axis=0, tiled=True
    )
    wanted = exchange(jnp.broadcast_to(needed, (n_row, LANES)))
    sent_shape = (n_row, block_size, width)
    (sent,) = call(
        functools.partial(pick_kernel, n_row, block_size),
        [(sent_shape, jnp.bfloat16, VMEM)],
        (wanted, vectors),
        (SCALARS, FAR),
        [DMA((n_row,))],
        2,
        "pick",
    )
    tile_other = across(tile)
    sent_other = across(sent)
    wanted_other = across(after(wanted, sent))
    slots = (slot_rows, slot_cols, used)
    slots_other = [across(after(array, sent)) for array in slots]
    packed = call(
        pack_kernel,
        [(sent_shape, jnp.bfloat16, HBM)],
        (place, sent, sent_other),
        (SCALARS, HERE, HERE),
        [VMEM(sent_shape, jnp.bfloat16), DMA((n_row,))],
        4,
        "pack",
    )[0]

    lay = layout_for(slot_count, n_row, piece_blocks)
    list_shape = ((lay.size,), jnp.int32)
    own_list, other_list = call(
        functools.partial(plan_kernel, n_row, piece_blocks, lay),
        [(*list_shape, HBM)] * 2,
        (place, wanted, after(wanted_other, packed), *slots, *slots_other),
        (SCALARS,) * 9,
        [
            SMEM((2 * lay.size,), jnp.int32),
            SMEM((2 * piece_blocks,), jnp.int32),
            SMEM((2 * piece_blocks * n_row,), jnp.int32),
            SMEM((piece_blocks + 1,), jnp.int32),
            DMA((2,)),
        ],
        2,
        "plan",
    )
    q1 = exchange(after(packed, own_list))
    plan = call(
        settle_kernel,
        [(*list_shape, SMEM)],
        (place, own_list, across(after(other_list, packed))),
        (SCALARS, ANYWHERE, ANYWHERE),
        [DMA],
        2,
        "settle",
    )[0]

    def load(cue, array):
        return call(
            load_kernel,
            [
                ((lay.slots, block_size, block_size), jnp.bfloat16, VMEM),
                (array.shape, array.dtype, VMEM),
            ],
            (after(plan, cue), tile, array),
            (LIST, FAR, FAR),
            [DMA((lay.slots,)), DMA],
            2,
            "load",
        )

    def cost(products, rows):
        size = block_size * width
        return pl.CostEstimate(
            flops=2 * products * block_size * size,
            bytes_accessed=2 * (products * block_size * block_size + 3 * rows * size),
            transcendentals=0,
        )

    sums = [
        VMEM((2, n_row, block_size, width), jnp.bfloat16),
        VMEM((2 * n_row + 1, block_size, width), jnp.float32),
    ]

    def first_blocks(*args):
        return call(
            functools.partial(first_sent_kernel, lay),
            [
                (sent_shape, jnp.bfloat16, VMEM),
                ((2 * lay.loads, block_size, block_size), jnp.bfloat16, VMEM),
            ],
            (plan, tile, tile_other, *args),
            (LIST, FAR, ANYWHERE, HERE, FAR),
            sums + [VMEM(sent_shape, jnp.bfloat16), DMA, DMA((2 * lay.loads,))],
            8,
            "sent",
            cost(n_row, n_row),
        )

    def second_blocks(*args):
        return call(
            functools.partial(second_sent_kernel, lay),
            [(sent_shape, jnp.bfloat16, HBM)],
            (plan, *args),
            (LIST, HERE, HERE, HERE, FAR),
            sums
            + [VMEM(sent_shape, jnp.bfloat16), DMA, VMEM(sent_shape, jnp.bfloat16), DMA((n_row,))],
            8,
            "sent",
            cost(n_row, n_row),
        )[0]

    base_shape = (piece_blocks, block_size, width)

    def early(*args):
        return call(
            functools.partial(early_kernel, lay),
            [(base_shape, jnp.bfloat16, HBM)],
            (plan, tile, tile_other, *args),
            (LIST, FAR, ANYWHERE, HERE, HERE, HERE, HERE, FAR),
            [
                VMEM((2, n_row, block_size, 2 * width), jnp.bfloat16),
                VMEM((piece_blocks + 1, block_size, 2 * width), jnp.float32),
                VMEM(vectors.shape, jnp.bfloat16),
                VMEM((2 * lay.slots, block_size, block_size), jnp.bfloat16),
                DMA,
                DMA((2 * lay.slots,)),
                DMA((piece_blocks,)),
            ],
            28,
            "early",
            cost(2 * slot_count, 2 * piece_blocks),
        )[0]

    def last(blocks, *args):
        rows = (piece_blocks + 1, block_size, width)
        (out,) = call(
            functools.partial(last_kernel, lay),
            [(base_shape, jnp.bfloat16, HBM)],
            (plan, blocks, tile_other, *args),
            (LIST, HERE, ANYWHERE, HERE, HERE, HERE),
            [
                VMEM((2, n_row, block_size, width), jnp.bfloat16),
                VMEM(rows, jnp.float32),
                VMEM(rows, jnp.bfloat16),
                VMEM((lay.slots, block_size, block_size), jnp.bfloat16),
                DMA((lay.slots,)),
                DMA((piece_blocks,)),
            ],
            14,
            "last",
            cost(slot_count, piece_blocks),
        )
        return out.reshape(vectors.shape)

    q1 = after(q1, plan)
    first_sent, blocks = first_blocks(q1, packed)
    q2 = exchange(first_sent)
    second_sent = second_blocks(blocks, q2, first_sent, packed)
    q1_other = across(after(q1, second_sent))
    q2_other = across(after(q2, second_sent))
    base = early(q1, q1_other, q2, q2_other, vectors)
    q3 = after(exchange(second_sent), base)
    q3_other = across(q3)
    blocks, base = load(q3, base)
    return last(blocks, q3, q3_other, base)


def on_any(vectors, tile_blocks, block_rows, block_cols, counts):
    n_row = lax.axis_size("row")
    n_col = lax.axis_size("col")
    tile_data = tile_blocks[0, 0]
    slot_rows = block_rows[0, 0]
    slot_cols = block_cols[0, 0]
    used = counts[0, 0]
    block_size = tile_data.shape[-1]
    width = vectors.shape[1]
    piece_blocks = vectors.shape[0] // block_size
    row_blocks = piece_blocks * n_col
    slot_count = tile_data.shape[0]
    live = (jnp.arange(slot_count) < used).astype(jnp.float32)
    onehot = (slot_rows[None, :] == jnp.arange(row_blocks)[:, None]).astype(jnp.float32) * live[
        None, :
    ]
    source_piece = slot_cols // piece_blocks
    offset = slot_cols % piece_blocks
    needed = jnp.max(
        jnp.where(source_piece[None, :] == jnp.arange(n_row)[:, None], offset[None, :], 0), axis=1
    )
    wanted = lax.all_to_all(
        needed.reshape(n_row, 1), "row", split_axis=0, concat_axis=0, tiled=True
    ).reshape(n_row)

    def apply_tiles(current):
        own_blocks = current.reshape(piece_blocks, block_size, width)
        outgoing = jnp.take(own_blocks, wanted, axis=0)
        received = lax.all_to_all(outgoing, "row", split_axis=0, concat_axis=0, tiled=True)
        vec_blocks = jnp.take(received, source_piece, axis=0)
        products = jnp.einsum(
            "sij,sjk->sik", tile_data, vec_blocks, preferred_element_type=jnp.float32
        )
        term = jnp.einsum("ls,sik->lik", onehot, products, precision=lax.Precision.HIGHEST)
        term = term.reshape(row_blocks * block_size, width)
        return lax.psum_scatter(
            term.astype(jnp.bfloat16), "col", scatter_dimension=0, tiled=True
        ).astype(jnp.float32)

    previous = vectors
    applied = apply_tiles(vectors)
    current = ((applied - center_value * previous.astype(jnp.float32)) / half_width).astype(
        jnp.bfloat16
    )
    for repeat in range(DEGREE - 1):
        applied = apply_tiles(current)
        following = (
            2.0 * (applied - center_value * current.astype(jnp.float32)) / half_width
            - previous.astype(jnp.float32)
        ).astype(jnp.bfloat16)
        previous, current = (current, following)
    return current


def solution(mesh):
    n_row, n_col = mesh.shape["row"], mesh.shape["col"]
    paired = n_col == 2 and n_row & (n_row - 1) == 0
    return jax.shard_map(
        on_pair if paired else on_any,
        mesh=mesh,
        in_specs=(
            P(("row", "col"), "vec"),
            P("row", "col", None, None, None),
            P("row", "col", None),
            P("row", "col", None),
            P("row", "col"),
        ),
        out_specs=P(("row", "col"), "vec"),
        check_vma=False,
    )
```

```python
import functools
import typing

import jax
import jax.numpy as jnp
from jax import lax
from jax.experimental import pallas as pl
from jax.experimental.pallas import tpu as pltpu
from jax.sharding import PartitionSpec as P

DEGREE = 3

center_value = 0.5
half_width = 2.0

VMEM = pltpu.VMEM
SMEM = pltpu.SMEM
HBM = pltpu.HBM
DMA = pltpu.SemaphoreType.DMA
LANES = 128
FEW = 4
MANY = 4
HEAD = 8
STRIDE = 4
FIRST = 1
LAST = 2


def spec(space):
    return pl.BlockSpec(memory_space=space)


def params(mib):
    return pltpu.CompilerParams(vmem_limit_bytes=mib * 1024 * 1024)


def round_up(n, step):
    return (n + step - 1) // step * step


class Layout(typing.NamedTuple):
    slots: int
    sends: int
    loads: int
    sent_at: int
    load_at: int
    bare_at: int
    size: int


def layout_for(slot_count, n_row, piece_blocks):
    slots = round_up(slot_count, MANY) + MANY
    sends = round_up(2 * n_row * n_row, FEW) + FEW
    sent_at = HEAD + STRIDE * 2 * slots
    load_at = sent_at + STRIDE * 2 * sends
    bare_at = load_at + 2 * (slot_count + 1)
    size = round_up(bare_at + piece_blocks, 8 * LANES)
    return Layout(slots, sends, slot_count + 1, sent_at, load_at, bare_at, size)


def plan_kernel(
    n_row,
    piece_blocks,
    lay,
    place,
    wanted_a,
    wanted_b,
    rows_a,
    cols_a,
    used_a,
    rows_b,
    cols_b,
    used_b,
    own,
    other,
    out,
    asked,
    seen,
    sems,
):
    slot_count = rows_a.shape[0]

    def put(at, *values):
        for i, value in enumerate(values):
            out[at + i] = value

    def scan(tile, rows, cols, used):

        def step(s, carry):
            ends, sent, load = carry
            row = rows[s]
            piece = cols[s] // piece_blocks
            live = s < used[0]
            half = row // piece_blocks
            local = row - half * piece_blocks
            lower = half == 0
            part = jnp.where(lower, tile, 1 - tile)
            at = HEAD + STRIDE * (part * lay.slots + jnp.where(lower, ends[0], ends[1]))
            base = half * lay.size
            put(base + at, s, local, piece)
            sought = jnp.where(live, local, -1)
            hits = [(asked[half * n_row + k] == sought).astype(jnp.int32) for k in range(n_row)]
            found = sum(hits)

            @pl.when(found > 0)
            def _():
                for core in range(2):
                    mine = tile if core == 0 else 1 - tile
                    side = half if core == 0 else 1 - half
                    first = core * lay.size
                    out[first + lay.load_at + mine * lay.loads + load] = s

                    place = sent
                    for k in range(n_row):
                        put(
                            first + lay.sent_at + STRIDE * (mine * lay.sends + place),
                            mine * lay.loads + load,
                            2 * k + side,
                            piece,
                            jnp.where(place == sent, FIRST, 0),
                        )
                        place = place + hits[k]

            one = live.astype(jnp.int32)
            ends = (ends[0] + jnp.where(lower, one, 0), ends[1] + jnp.where(lower, 0, one))
            return ends, sent + found, load + jnp.where(found > 0, 1, 0)

        zero = jnp.int32(0)
        ends, sent, load = lax.fori_loop(0, slot_count, step, ((zero, zero), zero, zero))
        for core in range(2):
            mine = tile if core == 0 else 1 - tile
            base = core * lay.size
            for i, (at, begin, end, unit, spare) in enumerate(
                (
                    (HEAD, mine * lay.slots, ends[core], MANY, piece_blocks),
                    (lay.sent_at, mine * lay.sends, sent, FEW, 2 * n_row),
                )
            ):
                for u in range(unit - 1):
                    put(base + at + STRIDE * (begin + end + u), 0, spare, 0, 0)
                out[base + 2 * i + mine] = begin + (end + unit - 1) // unit * unit
            out[base + 4 + mine] = mine * lay.loads + load

    def mark(core):
        base = core * lay.size
        for b in range(piece_blocks + 1):
            seen[b] = 0
        for part in range(2):

            @pl.loop(part * lay.slots, out[base + part])
            def _(i):
                entry = base + HEAD + STRIDE * i
                row = out[entry + 1]
                out[entry + 3] = jnp.where(seen[row] == 0, FIRST, 0)
                seen[row] = entry

        def close(b, bare):
            entry = seen[b]
            out[base + lay.bare_at + bare] = b

            @pl.when(entry > 0)
            def _():
                out[entry + 3] = out[entry + 3] + LAST

            return bare + jnp.where(entry == 0, 1, 0)

        out[base + 6] = lax.fori_loop(0, piece_blocks, close, jnp.int32(0))
        out[base + 7] = core

    @pl.when(place[1] == 0)
    def _():
        for half, wanted in enumerate((wanted_a, wanted_b)):
            for k in range(n_row):
                asked[half * n_row + k] = wanted[k, 0]
        scan(0, rows_a, cols_a, used_a)
        scan(1, rows_b, cols_b, used_b)
        for core in range(2):
            mark(core)
        copies = [
            pltpu.make_async_copy(out.at[pl.ds(core * lay.size, lay.size)], target, sems.at[core])
            for core, target in enumerate((own, other))
        ]
        for copy in copies:
            copy.start()
        for copy in copies:
            copy.wait()


def settle_kernel(place, own, handed, out, sem):
    for half, source in enumerate((own, handed)):

        @pl.when(place[1] == half)
        def _():
            copy = pltpu.make_async_copy(source, out, sem)
            copy.start()
            copy.wait()


def pick_kernel(n_row, block_size, wanted, vectors, out, sems):
    def fetch(k):
        at = pl.multiple_of(wanted[k, 0] * block_size, block_size)
        return pltpu.make_async_copy(vectors.at[pl.ds(at, block_size)], out.at[k], sems.at[k])

    for k in range(n_row):
        fetch(k).start()
    for k in range(n_row):
        fetch(k).wait()


def pack_kernel(place, picked, picked_b, out, held, sems):
    n_row, _, width = picked.shape
    middle = width // 2

    def put(k):
        return pltpu.make_async_copy(held.at[k], out.at[k], sems.at[k])

    for half in range(2):

        @pl.when(place[1] == half)
        def _():
            part = slice(half * middle, (half + 1) * middle)
            for k in range(n_row):
                held[k] = jnp.concatenate([picked[k, :, part], picked_b[k, :, part]], axis=1)
                put(k).start()

    for k in range(n_row):
        put(k).wait()


def fetches(plan, base, stride, ends, part, tiles, blocks, sems):
    def copy(tile, i):
        slot = plan[base + stride * i]
        return pltpu.make_async_copy(tile.at[slot], blocks.at[i], sems.at[i])

    def start():
        for side, tile in enumerate(tiles):

            @pl.loop(side * part, plan[ends + side])
            def _(i):
                copy(tile, i).start()

    def wait(i):
        copy(tiles[0], i).wait()

    return start, wait


def load_kernel(plan, tile_a, array, blocks, held, sems, held_sem):
    whole = pltpu.make_async_copy(array, held, held_sem)
    whole.start()
    start, wait = fetches(plan, HEAD, STRIDE, 0, 0, (tile_a,), blocks, sems)
    start()

    @pl.loop(0, plan[0])
    def _(i):
        wait(i)

    whole.wait()


def each_product(plan, base, ends, part, block_of, pieces, use, then=None, before=None):
    unroll = MANY if base == HEAD else FEW

    for side in range(2):

        @pl.loop(side * part // unroll, plan[ends + side] // unroll)
        def _(j):
            step = [(unroll * j + u, base + STRIDE * (unroll * j + u)) for u in range(unroll)]
            if before is not None:
                for i, entry in step:
                    before(side, i, entry)
            for i, entry in step:
                block = block_of(side, i, entry)
                piece = pieces[side][plan[entry + 2]]
                use(entry, jnp.dot(block, piece, preferred_element_type=jnp.float32))
            if then is not None:
                for i, entry in step:
                    then(entry)


def add_products(plan, base, ends, part, block_of, pieces, total, before=None):
    def use(entry, value):
        total[plan[entry + 1]] += value

    each_product(plan, base, ends, part, block_of, pieces, use, before=before)


def split_sides(pieces, vec):
    middle = vec.shape[-1] // 2
    column = lax.broadcasted_iota(jnp.int32, (1, vec.shape[-1]), 1)
    for side in range(2):
        keep = jnp.where((column // middle) == side, 1.0, 0.0).astype(jnp.bfloat16)
        for p in range(vec.shape[1]):
            vec[side, p] = pieces[p] * keep


def joined(total, k):
    one, two = total[2 * k], total[2 * k + 1]
    low = lax.broadcasted_iota(jnp.int32, one.shape, 1) < one.shape[1] // 2
    return jnp.where(low, one, two) + pltpu.roll(
        jnp.where(low, two, one), one.shape[1] // 2, axis=1
    )


def first_sent_kernel(
    lay, plan, tile_a, tile_b, pieces, start, out, blocks, vec, total, held, held_sem, sems
):
    n_row = out.shape[0]
    begin, wait = fetches(plan, lay.load_at, 1, 4, lay.loads, (tile_a, tile_b), blocks, sems)
    begin()
    copy = pltpu.make_async_copy(start, held, held_sem)
    copy.start()
    split_sides(pieces, vec)
    total[...] = jnp.zeros_like(total)

    def before(side, i, entry):
        @pl.when(plan[entry + 3] == FIRST)
        def _():
            wait(plan[entry])

    add_products(
        plan,
        lay.sent_at,
        2,
        lay.sends,
        lambda side, i, entry: blocks[plan[entry]],
        (vec.at[0], vec.at[1]),
        total,
        before,
    )
    copy.wait()
    for k in range(n_row):
        value = joined(total, k) - center_value * held[k].astype(jnp.float32)
        out[k] = (value / half_width).astype(jnp.bfloat16)


def second_sent_kernel(
    lay, plan, blocks, pieces, current, previous, out, vec, total, held, held_sem, ready, out_sems
):
    n_row = out.shape[0]
    copy = pltpu.make_async_copy(previous, held, held_sem)
    copy.start()
    split_sides(pieces, vec)
    total[...] = jnp.zeros_like(total)
    add_products(
        plan,
        lay.sent_at,
        2,
        lay.sends,
        lambda side, i, entry: blocks[plan[entry]],
        (vec.at[0], vec.at[1]),
        total,
    )
    copy.wait()

    def put(k):
        return pltpu.make_async_copy(ready.at[k], out.at[k], out_sems.at[k])

    for k in range(n_row):
        value = joined(total, k) - center_value * current[k].astype(jnp.float32)
        ready[k] = (value - held[k].astype(jnp.float32)).astype(jnp.bfloat16)
        put(k).start()
    for k in range(n_row):
        put(k).wait()


def whole_columns(half, mine, other, vec, at):
    n_row, _, width = mine.shape
    middle = width // 2

    @pl.when(half == 0)
    def _():
        for p in range(n_row):
            one, two = mine[p], other[p]
            vec[0, p, :, at : at + width] = jnp.concatenate([one[:, :middle], two[:, middle:]], axis=1)
            vec[1, p, :, at : at + width] = jnp.concatenate([one[:, middle:], two[:, :middle]], axis=1)

    @pl.when(half != 0)
    def _():
        for p in range(n_row):
            one, two = mine[p], other[p]
            vec[0, p, :, at : at + width] = jnp.concatenate([two[:, middle:], one[:, :middle]], axis=1)
            vec[1, p, :, at : at + width] = jnp.concatenate([two[:, :middle], one[:, middle:]], axis=1)


def early_kernel(
    lay,
    plan,
    tile_a,
    tile_b,
    q1,
    q1_other,
    q2,
    q2_other,
    vectors,
    base,
    vec,
    total,
    own,
    blocks,
    sem,
    sems,
    row_sems,
):
    width = vectors.shape[1]
    piece_blocks, block_size, _ = base.shape
    copy = pltpu.make_async_copy(vectors, own, sem)
    copy.start()
    begin, wait = fetches(plan, HEAD, STRIDE, 0, lay.slots, (tile_a, tile_b), blocks, sems)
    begin()
    whole_columns(plan[7], q1, q1_other, vec, 0)
    whole_columns(plan[7], q2, q2_other, vec, width)
    copy.wait()

    def rows(b):
        return pl.ds(pl.multiple_of(b * block_size, block_size), block_size)

    def put(b):
        return pltpu.make_async_copy(own.at[rows(b)], base.at[b], row_sems.at[b])

    @pl.loop(0, piece_blocks)
    def _(b):
        value = own[rows(b), :].astype(jnp.float32)
        total[b, :, :width] = -center_value * value
        total[b, :, width:] = -value

    add_products(
        plan,
        HEAD,
        0,
        lay.slots,
        lambda side, i, entry: blocks[i],
        (vec.at[0], vec.at[1]),
        total,
        lambda side, i, entry: wait(i),
    )

    @pl.loop(0, piece_blocks)
    def _(b):
        first = (total[b, :, :width] / half_width).astype(jnp.bfloat16).astype(jnp.float32)
        second = total[b, :, width:] - center_value * first
        second = second.astype(jnp.bfloat16).astype(jnp.float32)
        own[rows(b), :] = (-center_value * second - first).astype(jnp.bfloat16)
        put(b).start()

    @pl.loop(0, piece_blocks)
    def _(b):
        put(b).wait()


def last_kernel(
    lay, plan, blocks, tile_b, mine, other, base, out, vec, total, own, blocks_b, sems, row_sems
):
    piece_blocks = base.shape[0]
    begin = lay.slots

    def fetch(i):
        slot = plan[HEAD + STRIDE * i]
        return pltpu.make_async_copy(tile_b.at[slot], blocks_b.at[i - begin], sems.at[i - begin])

    @pl.loop(begin, plan[1])
    def _(i):
        fetch(i).start()

    def put(source, b):
        return pltpu.make_async_copy(source.at[b], out.at[b], row_sems.at[b])

    @pl.loop(0, plan[6])
    def _(i):
        b = plan[lay.bare_at + i]
        put(base, b).start()

    whole_columns(plan[7], mine, other, vec, 0)

    def use(entry, value):
        row = plan[entry + 1]
        marks = plan[entry + 3]
        start = base[jnp.minimum(row, piece_blocks - 1)].astype(jnp.float32)
        value = jnp.where(lax.rem(marks, LAST) == FIRST, start, total[row]) + value
        total[row] = value
        own[row] = value.astype(jnp.bfloat16)

    def then(entry):
        @pl.when(plan[entry + 3] >= LAST)
        def _():
            put(own, plan[entry + 1]).start()

    def block_of(side, i, entry):
        return blocks[i] if side == 0 else blocks_b[i - begin]

    def before(side, i, entry):
        if side == 1:
            fetch(i).wait()

    each_product(
        plan, HEAD, 0, lay.slots, block_of, (vec.at[0], vec.at[1]), use, then, before
    )

    @pl.loop(0, piece_blocks)
    def _(b):
        put(own, b).wait()


def after(value, *others):
    return lax.optimization_barrier((value, *others))[0]


def call(kernel, out, args, spaces, scratch, mib, name, estimate=None):
    args = [
        pltpu.with_memory_space_constraint(arg, space) if space in (VMEM, HBM) or tied else arg
        for arg, (space, tied) in zip(args, spaces)
    ]
    return pl.pallas_call(
        kernel,
        out_shape=[space(shape, dtype) for shape, dtype, space in out],
        in_specs=[spec(space) for space, _ in spaces],
        out_specs=[spec(space) for _, _, space in out],
        scratch_shapes=scratch,
        compiler_params=params(mib),
        cost_estimate=estimate,
        name=name,
    )(*args)


HERE = (VMEM, True)
FAR = (HBM, True)
LIST = (SMEM, True)
SCALARS = (SMEM, False)
ANYWHERE = (pl.ANY, False)


def on_pair(vectors, tile_blocks, block_rows, block_cols, counts):
    n_row = lax.axis_size("row")
    tile = tile_blocks[0, 0]
    slot_rows = block_rows[0, 0]
    slot_cols = block_cols[0, 0]
    used = counts[0]
    slot_count, block_size, _ = tile.shape
    width = vectors.shape[1]
    piece_blocks = vectors.shape[0] // block_size
    place = jnp.stack([lax.axis_index("row"), lax.axis_index("col")]).astype(jnp.int32)

    across = functools.partial(lax.ppermute, axis_name="col", perm=[(0, 1), (1, 0)])

    needed = jnp.max(
        jnp.where(
            slot_cols[None, :] // piece_blocks == jnp.arange(n_row)[:, None],
            slot_cols[None, :] % piece_blocks,
            0,
        ),
        axis=1,
        keepdims=True,
    )
    exchange = functools.partial(
        lax.all_to_all, axis_name="row", split_axis=0, concat_axis=0, tiled=True
    )
    wanted = exchange(jnp.broadcast_to(needed, (n_row, LANES)))
    sent_shape = (n_row, block_size, width)
    (sent,) = call(
        functools.partial(pick_kernel, n_row, block_size),
        [(sent_shape, jnp.bfloat16, VMEM)],
        (wanted, vectors),
        (SCALARS, FAR),
        [DMA((n_row,))],
        2,
        "pick",
    )
    tile_other = across(tile)
    sent_other = across(sent)
    wanted_other = across(after(wanted, sent))
    slots = (slot_rows, slot_cols, used)
    slots_other = [across(after(array, sent)) for array in slots]
    packed = call(
        pack_kernel,
        [(sent_shape, jnp.bfloat16, HBM)],
        (place, sent, sent_other),
        (SCALARS, HERE, HERE),
        [VMEM(sent_shape, jnp.bfloat16), DMA((n_row,))],
        4,
        "pack",
    )[0]

    lay = layout_for(slot_count, n_row, piece_blocks)
    list_shape = ((lay.size,), jnp.int32)
    own_list, other_list = call(
        functools.partial(plan_kernel, n_row, piece_blocks, lay),
        [(*list_shape, HBM)] * 2,
        (place, wanted, after(wanted_other, packed), *slots, *slots_other),
        (SCALARS,) * 9,
        [
            SMEM((2 * lay.size,), jnp.int32),
            SMEM((2 * n_row,), jnp.int32),
            SMEM((piece_blocks + 1,), jnp.int32),
            DMA((2,)),
        ],
        2,
        "plan",
    )
    q1 = exchange(after(packed, own_list))
    plan = call(
        settle_kernel,
        [(*list_shape, SMEM)],
        (place, own_list, across(after(other_list, packed))),
        (SCALARS, ANYWHERE, ANYWHERE),
        [DMA],
        2,
        "settle",
    )[0]

    def load(cue, array):
        return call(
            load_kernel,
            [
                ((lay.slots, block_size, block_size), jnp.bfloat16, VMEM),
                (array.shape, array.dtype, VMEM),
            ],
            (after(plan, cue), tile, array),
            (LIST, FAR, FAR),
            [DMA((lay.slots,)), DMA],
            2,
            "load",
        )

    def cost(products, rows):
        size = block_size * width
        return pl.CostEstimate(
            flops=2 * products * block_size * size,
            bytes_accessed=2 * (products * block_size * block_size + 3 * rows * size),
            transcendentals=0,
        )

    sums = [
        VMEM((2, n_row, block_size, width), jnp.bfloat16),
        VMEM((2 * n_row + 1, block_size, width), jnp.float32),
    ]

    def first_blocks(*args):
        return call(
            functools.partial(first_sent_kernel, lay),
            [
                (sent_shape, jnp.bfloat16, VMEM),
                ((2 * lay.loads, block_size, block_size), jnp.bfloat16, VMEM),
            ],
            (plan, tile, tile_other, *args),
            (LIST, FAR, ANYWHERE, HERE, FAR),
            sums + [VMEM(sent_shape, jnp.bfloat16), DMA, DMA((2 * lay.loads,))],
            8,
            "sent",
            cost(n_row, n_row),
        )

    def second_blocks(*args):
        return call(
            functools.partial(second_sent_kernel, lay),
            [(sent_shape, jnp.bfloat16, HBM)],
            (plan, *args),
            (LIST, HERE, HERE, HERE, FAR),
            sums
            + [VMEM(sent_shape, jnp.bfloat16), DMA, VMEM(sent_shape, jnp.bfloat16), DMA((n_row,))],
            8,
            "sent",
            cost(n_row, n_row),
        )[0]

    base_shape = (piece_blocks, block_size, width)

    def early(*args):
        return call(
            functools.partial(early_kernel, lay),
            [(base_shape, jnp.bfloat16, HBM)],
            (plan, tile, tile_other, *args),
            (LIST, FAR, ANYWHERE, HERE, HERE, HERE, HERE, FAR),
            [
                VMEM((2, n_row, block_size, 2 * width), jnp.bfloat16),
                VMEM((piece_blocks + 1, block_size, 2 * width), jnp.float32),
                VMEM(vectors.shape, jnp.bfloat16),
                VMEM((2 * lay.slots, block_size, block_size), jnp.bfloat16),
                DMA,
                DMA((2 * lay.slots,)),
                DMA((piece_blocks,)),
            ],
            28,
            "early",
            cost(2 * slot_count, 2 * piece_blocks),
        )[0]

    def last(blocks, *args):
        rows = (piece_blocks + 1, block_size, width)
        (out,) = call(
            functools.partial(last_kernel, lay),
            [(base_shape, jnp.bfloat16, HBM)],
            (plan, blocks, tile_other, *args),
            (LIST, HERE, ANYWHERE, HERE, HERE, HERE),
            [
                VMEM((2, n_row, block_size, width), jnp.bfloat16),
                VMEM(rows, jnp.float32),
                VMEM(rows, jnp.bfloat16),
                VMEM((lay.slots, block_size, block_size), jnp.bfloat16),
                DMA((lay.slots,)),
                DMA((piece_blocks,)),
            ],
            14,
            "last",
            cost(slot_count, piece_blocks),
        )
        return out.reshape(vectors.shape)

    q1 = after(q1, plan)
    first_sent, blocks = first_blocks(q1, packed)
    q2 = exchange(first_sent)
    second_sent = second_blocks(blocks, q2, first_sent, packed)
    q1_other = across(after(q1, second_sent))
    q2_other = across(after(q2, second_sent))
    base = early(q1, q1_other, q2, q2_other, vectors)
    q3 = after(exchange(second_sent), base)
    q3_other = across(q3)
    blocks, base = load(q3, base)
    return last(blocks, q3, q3_other, base)


def on_any(vectors, tile_blocks, block_rows, block_cols, counts):
    n_row = lax.axis_size("row")
    n_col = lax.axis_size("col")
    tile_data = tile_blocks[0, 0]
    slot_rows = block_rows[0, 0]
    slot_cols = block_cols[0, 0]
    used = counts[0, 0]
    block_size = tile_data.shape[-1]
    width = vectors.shape[1]
    piece_blocks = vectors.shape[0] // block_size
    row_blocks = piece_blocks * n_col
    slot_count = tile_data.shape[0]
    live = (jnp.arange(slot_count) < used).astype(jnp.float32)
    onehot = (slot_rows[None, :] == jnp.arange(row_blocks)[:, None]).astype(jnp.float32) * live[
        None, :
    ]
    source_piece = slot_cols // piece_blocks
    offset = slot_cols % piece_blocks
    needed = jnp.max(
        jnp.where(source_piece[None, :] == jnp.arange(n_row)[:, None], offset[None, :], 0), axis=1
    )
    wanted = lax.all_to_all(
        needed.reshape(n_row, 1), "row", split_axis=0, concat_axis=0, tiled=True
    ).reshape(n_row)

    def apply_tiles(current):
        own_blocks = current.reshape(piece_blocks, block_size, width)
        outgoing = jnp.take(own_blocks, wanted, axis=0)
        received = lax.all_to_all(outgoing, "row", split_axis=0, concat_axis=0, tiled=True)
        vec_blocks = jnp.take(received, source_piece, axis=0)
        products = jnp.einsum(
            "sij,sjk->sik", tile_data, vec_blocks, preferred_element_type=jnp.float32
        )
        term = jnp.einsum("ls,sik->lik", onehot, products, precision=lax.Precision.HIGHEST)
        term = term.reshape(row_blocks * block_size, width)
        return lax.psum_scatter(
            term.astype(jnp.bfloat16), "col", scatter_dimension=0, tiled=True
        ).astype(jnp.float32)

    previous = vectors
    applied = apply_tiles(vectors)
    current = ((applied - center_value * previous.astype(jnp.float32)) / half_width).astype(
        jnp.bfloat16
    )
    for repeat in range(DEGREE - 1):
        applied = apply_tiles(current)
        following = (
            2.0 * (applied - center_value * current.astype(jnp.float32)) / half_width
            - previous.astype(jnp.float32)
        ).astype(jnp.bfloat16)
        previous, current = (current, following)
    return current


def solution(mesh):
    n_row, n_col = mesh.shape["row"], mesh.shape["col"]
    paired = n_col == 2 and n_row & (n_row - 1) == 0
    return jax.shard_map(
        on_pair if paired else on_any,
        mesh=mesh,
        in_specs=(
            P(("row", "col"), "vec"),
            P("row", "col", None, None, None),
            P("row", "col", None),
            P("row", "col", None),
            P("row", "col"),
        ),
        out_specs=P(("row", "col"), "vec"),
        check_vma=False,
    )
```

```python
import functools
import typing

import jax
import jax.numpy as jnp
from jax import lax
from jax.experimental import pallas as pl
from jax.experimental.pallas import tpu as pltpu
from jax.sharding import PartitionSpec as P

DEGREE = 3

center_value = 0.5
half_width = 2.0

VMEM = pltpu.VMEM
SMEM = pltpu.SMEM
HBM = pltpu.HBM
DMA = pltpu.SemaphoreType.DMA
LANES = 128
FEW = 4
MANY = 4
HEAD = 8
STRIDE = 4
FIRST = 1
LAST = 2


def spec(space):
    return pl.BlockSpec(memory_space=space)


def params(mib):
    return pltpu.CompilerParams(vmem_limit_bytes=mib * 1024 * 1024)


def round_up(n, step):
    return (n + step - 1) // step * step


class Layout(typing.NamedTuple):
    slots: int
    sends: int
    loads: int
    sent_at: int
    load_at: int
    bare_at: int
    size: int


def layout_for(slot_count, n_row, piece_blocks):
    slots = round_up(slot_count, MANY) + MANY
    sends = round_up(2 * n_row * n_row, FEW) + FEW
    sent_at = HEAD + STRIDE * 2 * slots
    load_at = sent_at + STRIDE * 2 * sends
    bare_at = load_at + 2 * (slot_count + 1)
    size = round_up(bare_at + piece_blocks, 8 * LANES)
    return Layout(slots, sends, slot_count + 1, sent_at, load_at, bare_at, size)


def plan_kernel(
    n_row,
    piece_blocks,
    lay,
    place,
    *rest,
):
    sources, (own, other), held = rest[:8], rest[8:10], rest[10:18]
    out, asked, seen, in_sems, sems = rest[18:]
    wanted_a, wanted_b, rows_a, cols_a, used_a, rows_b, cols_b, used_b = held
    slot_count = rows_a.shape[0]

    def put(at, *values):
        for i, value in enumerate(values):
            out[at + i] = value

    def scan(tile, rows, cols, used):

        def step(s, carry):
            ends, sent, load = carry
            row = rows[s]
            piece = cols[s] // piece_blocks
            live = s < used[0]
            half = row // piece_blocks
            local = row - half * piece_blocks
            lower = half == 0
            part = jnp.where(lower, tile, 1 - tile)
            at = HEAD + STRIDE * (part * lay.slots + jnp.where(lower, ends[0], ends[1]))
            base = half * lay.size
            put(base + at, s, local, piece)
            sought = jnp.where(live, local, -1)
            hits = [(asked[half * n_row + k] == sought).astype(jnp.int32) for k in range(n_row)]
            found = sum(hits)

            @pl.when(found > 0)
            def _():
                for core in range(2):
                    mine = tile if core == 0 else 1 - tile
                    side = half if core == 0 else 1 - half
                    first = core * lay.size
                    out[first + lay.load_at + mine * lay.loads + load] = s

                    place = sent
                    for k in range(n_row):
                        put(
                            first + lay.sent_at + STRIDE * (mine * lay.sends + place),
                            mine * lay.loads + load,
                            2 * k + side,
                            piece,
                            jnp.where(place == sent, FIRST, 0),
                        )
                        place = place + hits[k]

            one = live.astype(jnp.int32)
            ends = (ends[0] + jnp.where(lower, one, 0), ends[1] + jnp.where(lower, 0, one))
            return ends, sent + found, load + jnp.where(found > 0, 1, 0)

        zero = jnp.int32(0)
        ends, sent, load = lax.fori_loop(0, slot_count, step, ((zero, zero), zero, zero))
        for core in range(2):
            mine = tile if core == 0 else 1 - tile
            base = core * lay.size
            for i, (at, begin, end, unit, spare) in enumerate(
                (
                    (HEAD, mine * lay.slots, ends[core], MANY, piece_blocks),
                    (lay.sent_at, mine * lay.sends, sent, FEW, 2 * n_row),
                )
            ):
                for u in range(unit - 1):
                    put(base + at + STRIDE * (begin + end + u), 0, spare, 0, 0)
                out[base + 2 * i + mine] = begin + (end + unit - 1) // unit * unit
            out[base + 4 + mine] = mine * lay.loads + load

    def mark(core):
        base = core * lay.size
        for b in range(piece_blocks + 1):
            seen[b] = 0
        for part in range(2):

            @pl.loop(part * lay.slots, out[base + part])
            def _(i):
                entry = base + HEAD + STRIDE * i
                row = out[entry + 1]
                out[entry + 3] = jnp.where(seen[row] == 0, FIRST, 0)
                seen[row] = entry

        def close(b, bare):
            entry = seen[b]
            out[base + lay.bare_at + bare] = b

            @pl.when(entry > 0)
            def _():
                out[entry + 3] = out[entry + 3] + LAST

            return bare + jnp.where(entry == 0, 1, 0)

        out[base + 6] = lax.fori_loop(0, piece_blocks, close, jnp.int32(0))
        out[base + 7] = core

    @pl.when(place[1] == 0)
    def _():
        fetches = [
            pltpu.make_async_copy(source, target, in_sems.at[i])
            for i, (source, target) in enumerate(zip(sources, held))
        ]
        for fetch in fetches:
            fetch.start()
        for fetch in fetches:
            fetch.wait()
        for half, wanted in enumerate((wanted_a, wanted_b)):
            for k in range(n_row):
                asked[half * n_row + k] = wanted[k, 0]
        scan(0, rows_a, cols_a, used_a)
        scan(1, rows_b, cols_b, used_b)
        for core in range(2):
            mark(core)
        copies = [
            pltpu.make_async_copy(out.at[pl.ds(core * lay.size, lay.size)], target, sems.at[core])
            for core, target in enumerate((own, other))
        ]
        for copy in copies:
            copy.start()
        for copy in copies:
            copy.wait()


def settle_kernel(place, own, handed, out, sem):
    for half, source in enumerate((own, handed)):

        @pl.when(place[1] == half)
        def _():
            copy = pltpu.make_async_copy(source, out, sem)
            copy.start()
            copy.wait()


def pick_kernel(n_row, block_size, wanted, vectors, out, sems):
    def fetch(k):
        at = pl.multiple_of(wanted[k, 0] * block_size, block_size)
        return pltpu.make_async_copy(vectors.at[pl.ds(at, block_size)], out.at[k], sems.at[k])

    for k in range(n_row):
        fetch(k).start()
    for k in range(n_row):
        fetch(k).wait()


def pack_kernel(place, picked, picked_b, out, held, sems):
    n_row, _, width = picked.shape
    middle = width // 2

    def put(k):
        return pltpu.make_async_copy(held.at[k], out.at[k], sems.at[k])

    for half in range(2):

        @pl.when(place[1] == half)
        def _():
            part = slice(half * middle, (half + 1) * middle)
            for k in range(n_row):
                held[k] = jnp.concatenate([picked[k, :, part], picked_b[k, :, part]], axis=1)
                put(k).start()

    for k in range(n_row):
        put(k).wait()


def fetches(plan, base, stride, ends, part, tiles, blocks, sems):
    def copy(tile, i):
        slot = plan[base + stride * i]
        return pltpu.make_async_copy(tile.at[slot], blocks.at[i], sems.at[i])

    def start():
        for side, tile in enumerate(tiles):

            @pl.loop(side * part, plan[ends + side])
            def _(i):
                copy(tile, i).start()

    def wait(i):
        copy(tiles[0], i).wait()

    return start, wait


def load_kernel(plan, tile_a, array, blocks, held, sems, held_sem):
    whole = pltpu.make_async_copy(array, held, held_sem)
    whole.start()
    start, wait = fetches(plan, HEAD, STRIDE, 0, 0, (tile_a,), blocks, sems)
    start()

    @pl.loop(0, plan[0])
    def _(i):
        wait(i)

    whole.wait()


def each_product(plan, base, ends, part, block_of, pieces, use, then=None, before=None):
    unroll = MANY if base == HEAD else FEW

    for side in range(2):

        @pl.loop(side * part // unroll, plan[ends + side] // unroll)
        def _(j):
            step = [(unroll * j + u, base + STRIDE * (unroll * j + u)) for u in range(unroll)]
            if before is not None:
                for i, entry in step:
                    before(side, i, entry)
            for i, entry in step:
                block = block_of(side, i, entry)
                piece = pieces[side][plan[entry + 2]]
                use(entry, jnp.dot(block, piece, preferred_element_type=jnp.float32))
            if then is not None:
                for i, entry in step:
                    then(entry)


def add_products(plan, base, ends, part, block_of, pieces, total, before=None):
    def use(entry, value):
        total[plan[entry + 1]] += value

    each_product(plan, base, ends, part, block_of, pieces, use, before=before)


def split_sides(pieces, vec):
    middle = vec.shape[-1] // 2
    column = lax.broadcasted_iota(jnp.int32, (1, vec.shape[-1]), 1)
    for side in range(2):
        keep = jnp.where((column // middle) == side, 1.0, 0.0).astype(jnp.bfloat16)
        for p in range(vec.shape[1]):
            vec[side, p] = pieces[p] * keep


def joined(total, k):
    one, two = total[2 * k], total[2 * k + 1]
    low = lax.broadcasted_iota(jnp.int32, one.shape, 1) < one.shape[1] // 2
    return jnp.where(low, one, two) + pltpu.roll(
        jnp.where(low, two, one), one.shape[1] // 2, axis=1
    )


def first_sent_kernel(
    lay, plan, tile_a, tile_b, pieces, start, out, blocks, vec, total, held, held_sem, sems
):
    n_row = out.shape[0]
    begin, wait = fetches(plan, lay.load_at, 1, 4, lay.loads, (tile_a, tile_b), blocks, sems)
    begin()
    copy = pltpu.make_async_copy(start, held, held_sem)
    copy.start()
    split_sides(pieces, vec)
    total[...] = jnp.zeros_like(total)

    def before(side, i, entry):
        @pl.when(plan[entry + 3] == FIRST)
        def _():
            wait(plan[entry])

    add_products(
        plan,
        lay.sent_at,
        2,
        lay.sends,
        lambda side, i, entry: blocks[plan[entry]],
        (vec.at[0], vec.at[1]),
        total,
        before,
    )
    copy.wait()
    for k in range(n_row):
        value = joined(total, k) - center_value * held[k].astype(jnp.float32)
        out[k] = (value / half_width).astype(jnp.bfloat16)


def second_sent_kernel(
    lay, plan, blocks, pieces, current, previous, out, vec, total, held, held_sem, ready, out_sems
):
    n_row = out.shape[0]
    copy = pltpu.make_async_copy(previous, held, held_sem)
    copy.start()
    split_sides(pieces, vec)
    total[...] = jnp.zeros_like(total)
    add_products(
        plan,
        lay.sent_at,
        2,
        lay.sends,
        lambda side, i, entry: blocks[plan[entry]],
        (vec.at[0], vec.at[1]),
        total,
    )
    copy.wait()

    def put(k):
        return pltpu.make_async_copy(ready.at[k], out.at[k], out_sems.at[k])

    for k in range(n_row):
        value = joined(total, k) - center_value * current[k].astype(jnp.float32)
        ready[k] = (value - held[k].astype(jnp.float32)).astype(jnp.bfloat16)
        put(k).start()
    for k in range(n_row):
        put(k).wait()


def whole_columns(half, mine, other, vec, at):
    n_row, _, width = mine.shape
    middle = width // 2

    @pl.when(half == 0)
    def _():
        for p in range(n_row):
            one, two = mine[p], other[p]
            vec[0, p, :, at : at + width] = jnp.concatenate([one[:, :middle], two[:, middle:]], axis=1)
            vec[1, p, :, at : at + width] = jnp.concatenate([one[:, middle:], two[:, :middle]], axis=1)

    @pl.when(half != 0)
    def _():
        for p in range(n_row):
            one, two = mine[p], other[p]
            vec[0, p, :, at : at + width] = jnp.concatenate([two[:, middle:], one[:, :middle]], axis=1)
            vec[1, p, :, at : at + width] = jnp.concatenate([two[:, :middle], one[:, middle:]], axis=1)


def prime_kernel(vectors, total, own, sem):
    _, block_size, double = total.shape
    width = double // 2
    copy = pltpu.make_async_copy(vectors, own, sem)
    copy.start()
    copy.wait()

    @pl.loop(0, vectors.shape[0] // block_size)
    def _(b):
        at = pl.ds(pl.multiple_of(b * block_size, block_size), block_size)
        value = own[at, :].astype(jnp.float32)
        total[b, :, :width] = -center_value * value
        total[b, :, width:] = -value


def early_kernel(
    lay,
    plan,
    tile_a,
    tile_b,
    q1,
    q1_other,
    q2,
    q2_other,
    start,
    base,
    total,
    vec,
    own,
    blocks,
    sems,
    row_sems,
):
    piece_blocks, block_size, width = base.shape
    begin, wait = fetches(plan, HEAD, STRIDE, 0, lay.slots, (tile_a, tile_b), blocks, sems)
    begin()
    whole_columns(plan[7], q1, q1_other, vec, 0)
    whole_columns(plan[7], q2, q2_other, vec, width)

    def rows(b):
        return pl.ds(pl.multiple_of(b * block_size, block_size), block_size)

    def put(b):
        return pltpu.make_async_copy(own.at[rows(b)], base.at[b], row_sems.at[b])

    add_products(
        plan,
        HEAD,
        0,
        lay.slots,
        lambda side, i, entry: blocks[i],
        (vec.at[0], vec.at[1]),
        total,
        lambda side, i, entry: wait(i),
    )

    @pl.loop(0, piece_blocks)
    def _(b):
        first = (total[b, :, :width] / half_width).astype(jnp.bfloat16).astype(jnp.float32)
        second = total[b, :, width:] - center_value * first
        second = second.astype(jnp.bfloat16).astype(jnp.float32)
        own[rows(b), :] = (-center_value * second - first).astype(jnp.bfloat16)
        put(b).start()

    @pl.loop(0, piece_blocks)
    def _(b):
        put(b).wait()


def last_kernel(
    lay, plan, blocks, tile_b, mine, other, base, out, vec, total, own, blocks_b, sems, row_sems
):
    piece_blocks = base.shape[0]
    begin = lay.slots

    def fetch(i):
        slot = plan[HEAD + STRIDE * i]
        return pltpu.make_async_copy(tile_b.at[slot], blocks_b.at[i - begin], sems.at[i - begin])

    @pl.loop(begin, plan[1])
    def _(i):
        fetch(i).start()

    def put(source, b):
        return pltpu.make_async_copy(source.at[b], out.at[b], row_sems.at[b])

    @pl.loop(0, plan[6])
    def _(i):
        b = plan[lay.bare_at + i]
        put(base, b).start()

    whole_columns(plan[7], mine, other, vec, 0)

    def use(entry, value):
        row = plan[entry + 1]
        marks = plan[entry + 3]
        start = base[jnp.minimum(row, piece_blocks - 1)].astype(jnp.float32)
        value = jnp.where(lax.rem(marks, LAST) == FIRST, start, total[row]) + value
        total[row] = value
        own[row] = value.astype(jnp.bfloat16)

    def then(entry):
        @pl.when(plan[entry + 3] >= LAST)
        def _():
            put(own, plan[entry + 1]).start()

    def block_of(side, i, entry):
        return blocks[i] if side == 0 else blocks_b[i - begin]

    def before(side, i, entry):
        if side == 1:
            fetch(i).wait()

    each_product(
        plan, HEAD, 0, lay.slots, block_of, (vec.at[0], vec.at[1]), use, then, before
    )

    @pl.loop(0, piece_blocks)
    def _(b):
        put(own, b).wait()


def after(value, *others):
    return lax.optimization_barrier((value, *others))[0]


def call(kernel, out, args, spaces, scratch, mib, name, estimate=None, aliases=None):
    args = [
        pltpu.with_memory_space_constraint(arg, space) if space in (VMEM, HBM) or tied else arg
        for arg, (space, tied) in zip(args, spaces)
    ]
    return pl.pallas_call(
        kernel,
        out_shape=[space(shape, dtype) for shape, dtype, space in out],
        in_specs=[spec(space) for space, _ in spaces],
        out_specs=[spec(space) for _, _, space in out],
        scratch_shapes=scratch,
        compiler_params=params(mib),
        cost_estimate=estimate,
        input_output_aliases=aliases or {},
        name=name,
    )(*args)


HERE = (VMEM, True)
FAR = (HBM, True)
LIST = (SMEM, True)
SCALARS = (SMEM, False)
ANYWHERE = (pl.ANY, False)


def on_pair(vectors, tile_blocks, block_rows, block_cols, counts):
    n_row = lax.axis_size("row")
    tile = tile_blocks[0, 0]
    slot_rows = block_rows[0, 0]
    slot_cols = block_cols[0, 0]
    used = counts[0]
    slot_count, block_size, _ = tile.shape
    width = vectors.shape[1]
    piece_blocks = vectors.shape[0] // block_size
    place = jnp.stack([lax.axis_index("row"), lax.axis_index("col")]).astype(jnp.int32)

    across = functools.partial(lax.ppermute, axis_name="col", perm=[(0, 1), (1, 0)])

    needed = jnp.max(
        jnp.where(
            slot_cols[None, :] // piece_blocks == jnp.arange(n_row)[:, None],
            slot_cols[None, :] % piece_blocks,
            0,
        ),
        axis=1,
        keepdims=True,
    )
    exchange = functools.partial(
        lax.all_to_all, axis_name="row", split_axis=0, concat_axis=0, tiled=True
    )
    wanted = exchange(jnp.broadcast_to(needed, (n_row, LANES)))
    sent_shape = (n_row, block_size, width)
    (sent,) = call(
        functools.partial(pick_kernel, n_row, block_size),
        [(sent_shape, jnp.bfloat16, VMEM)],
        (wanted, vectors),
        (SCALARS, FAR),
        [DMA((n_row,))],
        2,
        "pick",
    )
    tile_other = across(tile)
    sent_other = across(sent)
    wanted_other = across(after(wanted, sent))
    slots = (slot_rows, slot_cols, used)
    slots_other = [across(after(array, sent)) for array in slots]
    packed = call(
        pack_kernel,
        [(sent_shape, jnp.bfloat16, HBM)],
        (place, sent, sent_other),
        (SCALARS, HERE, HERE),
        [VMEM(sent_shape, jnp.bfloat16), DMA((n_row,))],
        4,
        "pack",
    )[0]

    lay = layout_for(slot_count, n_row, piece_blocks)
    list_shape = ((lay.size,), jnp.int32)
    described = (wanted, after(wanted_other, packed), *slots, *slots_other)
    own_list, other_list = call(
        functools.partial(plan_kernel, n_row, piece_blocks, lay),
        [(*list_shape, HBM)] * 2,
        (place, *described),
        (SCALARS,) + (ANYWHERE,) * len(described),
        [SMEM(array.shape, jnp.int32) for array in described]
        + [
            SMEM((2 * lay.size,), jnp.int32),
            SMEM((2 * n_row,), jnp.int32),
            SMEM((piece_blocks + 1,), jnp.int32),
            DMA((len(described),)),
            DMA((2,)),
        ],
        2,
        "plan",
    )
    q1 = exchange(after(packed, own_list))
    plan = call(
        settle_kernel,
        [(*list_shape, SMEM)],
        (place, own_list, across(after(other_list, packed))),
        (SCALARS, ANYWHERE, ANYWHERE),
        [DMA],
        2,
        "settle",
    )[0]

    def load(cue, array):
        return call(
            load_kernel,
            [
                ((lay.slots, block_size, block_size), jnp.bfloat16, VMEM),
                (array.shape, array.dtype, VMEM),
            ],
            (after(plan, cue), tile, array),
            (LIST, FAR, FAR),
            [DMA((lay.slots,)), DMA],
            2,
            "load",
        )

    def cost(products, rows):
        size = block_size * width
        return pl.CostEstimate(
            flops=2 * products * block_size * size,
            bytes_accessed=2 * (products * block_size * block_size + 3 * rows * size),
            transcendentals=0,
        )

    sums = [
        VMEM((2, n_row, block_size, width), jnp.bfloat16),
        VMEM((2 * n_row + 1, block_size, width), jnp.float32),
    ]

    def first_blocks(*args):
        return call(
            functools.partial(first_sent_kernel, lay),
            [
                (sent_shape, jnp.bfloat16, VMEM),
                ((2 * lay.loads, block_size, block_size), jnp.bfloat16, VMEM),
            ],
            (plan, tile, tile_other, *args),
            (LIST, FAR, ANYWHERE, HERE, FAR),
            sums + [VMEM(sent_shape, jnp.bfloat16), DMA, DMA((2 * lay.loads,))],
            8,
            "sent",
            cost(n_row, n_row),
        )

    def second_blocks(*args):
        return call(
            functools.partial(second_sent_kernel, lay),
            [(sent_shape, jnp.bfloat16, HBM)],
            (plan, *args),
            (LIST, HERE, HERE, HERE, FAR),
            sums
            + [VMEM(sent_shape, jnp.bfloat16), DMA, VMEM(sent_shape, jnp.bfloat16), DMA((n_row,))],
            8,
            "sent",
            cost(n_row, n_row),
        )[0]

    base_shape = (piece_blocks, block_size, width)

    sums_shape = ((piece_blocks + 1, block_size, 2 * width), jnp.float32, VMEM)

    def early(*args):
        return call(
            functools.partial(early_kernel, lay),
            [(base_shape, jnp.bfloat16, HBM), sums_shape],
            (plan, tile, tile_other, *args),
            (LIST, FAR, ANYWHERE, HERE, HERE, HERE, HERE, HERE),
            [
                VMEM((2, n_row, block_size, 2 * width), jnp.bfloat16),
                VMEM(vectors.shape, jnp.bfloat16),
                VMEM((2 * lay.slots, block_size, block_size), jnp.bfloat16),
                DMA((2 * lay.slots,)),
                DMA((piece_blocks,)),
            ],
            18,
            "early",
            cost(2 * slot_count, 2 * piece_blocks),
            {7: 1},
        )[0]

    def last(blocks, *args):
        rows = (piece_blocks + 1, block_size, width)
        (out,) = call(
            functools.partial(last_kernel, lay),
            [(base_shape, jnp.bfloat16, HBM)],
            (plan, blocks, tile_other, *args),
            (LIST, HERE, ANYWHERE, HERE, HERE, HERE),
            [
                VMEM((2, n_row, block_size, width), jnp.bfloat16),
                VMEM(rows, jnp.float32),
                VMEM(rows, jnp.bfloat16),
                VMEM((lay.slots, block_size, block_size), jnp.bfloat16),
                DMA((lay.slots,)),
                DMA((piece_blocks,)),
            ],
            14,
            "last",
            cost(slot_count, piece_blocks),
        )
        return out.reshape(vectors.shape)

    q1 = after(q1, plan)
    first_sent, blocks = first_blocks(q1, packed)
    q2 = exchange(first_sent)
    second_sent = second_blocks(blocks, q2, first_sent, packed)
    q1_other = across(after(q1, second_sent))
    q2_other = across(after(q2, second_sent))
    (start,) = call(
        prime_kernel,
        [sums_shape],
        (after(vectors, second_sent),),
        (FAR,),
        [VMEM(vectors.shape, jnp.bfloat16), DMA],
        4,
        "prime",
        cost(0, 3 * piece_blocks),
    )
    base = early(q1, q1_other, q2, q2_other, start)
    q3 = after(exchange(second_sent), base)
    q3_other = across(q3)
    blocks, base = load(q3, base)
    return last(blocks, q3, q3_other, base)


def on_any(vectors, tile_blocks, block_rows, block_cols, counts):
    n_row = lax.axis_size("row")
    n_col = lax.axis_size("col")
    tile_data = tile_blocks[0, 0]
    slot_rows = block_rows[0, 0]
    slot_cols = block_cols[0, 0]
    used = counts[0, 0]
    block_size = tile_data.shape[-1]
    width = vectors.shape[1]
    piece_blocks = vectors.shape[0] // block_size
    row_blocks = piece_blocks * n_col
    slot_count = tile_data.shape[0]
    live = (jnp.arange(slot_count) < used).astype(jnp.float32)
    onehot = (slot_rows[None, :] == jnp.arange(row_blocks)[:, None]).astype(jnp.float32) * live[
        None, :
    ]
    source_piece = slot_cols // piece_blocks
    offset = slot_cols % piece_blocks
    needed = jnp.max(
        jnp.where(source_piece[None, :] == jnp.arange(n_row)[:, None], offset[None, :], 0), axis=1
    )
    wanted = lax.all_to_all(
        needed.reshape(n_row, 1), "row", split_axis=0, concat_axis=0, tiled=True
    ).reshape(n_row)

    def apply_tiles(current):
        own_blocks = current.reshape(piece_blocks, block_size, width)
        outgoing = jnp.take(own_blocks, wanted, axis=0)
        received = lax.all_to_all(outgoing, "row", split_axis=0, concat_axis=0, tiled=True)
        vec_blocks = jnp.take(received, source_piece, axis=0)
        products = jnp.einsum(
            "sij,sjk->sik", tile_data, vec_blocks, preferred_element_type=jnp.float32
        )
        term = jnp.einsum("ls,sik->lik", onehot, products, precision=lax.Precision.HIGHEST)
        term = term.reshape(row_blocks * block_size, width)
        return lax.psum_scatter(
            term.astype(jnp.bfloat16), "col", scatter_dimension=0, tiled=True
        ).astype(jnp.float32)

    previous = vectors
    applied = apply_tiles(vectors)
    current = ((applied - center_value * previous.astype(jnp.float32)) / half_width).astype(
        jnp.bfloat16
    )
    for repeat in range(DEGREE - 1):
        applied = apply_tiles(current)
        following = (
            2.0 * (applied - center_value * current.astype(jnp.float32)) / half_width
            - previous.astype(jnp.float32)
        ).astype(jnp.bfloat16)
        previous, current = (current, following)
    return current


def solution(mesh):
    n_row, n_col = mesh.shape["row"], mesh.shape["col"]
    paired = n_col == 2 and n_row & (n_row - 1) == 0
    return jax.shard_map(
        on_pair if paired else on_any,
        mesh=mesh,
        in_specs=(
            P(("row", "col"), "vec"),
            P("row", "col", None, None, None),
            P("row", "col", None),
            P("row", "col", None),
            P("row", "col"),
        ),
        out_specs=P(("row", "col"), "vec"),
        check_vma=False,
    )
```

```python
import functools
import typing

import jax
import jax.numpy as jnp
from jax import lax
from jax.experimental import pallas as pl
from jax.experimental.pallas import tpu as pltpu
from jax.sharding import PartitionSpec as P

DEGREE = 3

center_value = 0.5
half_width = 2.0

VMEM = pltpu.VMEM
SMEM = pltpu.SMEM
HBM = pltpu.HBM
DMA = pltpu.SemaphoreType.DMA
LANES = 128
FEW = 4
MANY = 8
HEAD = 8
STRIDE = 4
FIRST = 1
LAST = 2


def spec(space):
    return pl.BlockSpec(memory_space=space)


def params(mib):
    return pltpu.CompilerParams(vmem_limit_bytes=mib * 1024 * 1024)


def round_up(n, step):
    return (n + step - 1) // step * step


class Layout(typing.NamedTuple):
    slots: int
    sends: int
    loads: int
    sent_at: int
    load_at: int
    bare_at: int
    size: int


def layout_for(slot_count, n_row, piece_blocks):
    slots = round_up(slot_count, MANY) + MANY
    sends = round_up(2 * n_row * n_row, FEW) + FEW
    sent_at = HEAD + STRIDE * 2 * slots
    load_at = sent_at + STRIDE * 2 * sends
    bare_at = load_at + 2 * (slot_count + 1)
    size = round_up(bare_at + piece_blocks, 8 * LANES)
    return Layout(slots, sends, slot_count + 1, sent_at, load_at, bare_at, size)


def plan_kernel(
    n_row,
    piece_blocks,
    lay,
    place,
    *rest,
):
    sources, (own, other), held = rest[:8], rest[8:10], rest[10:18]
    out, asked, seen, in_sems, sems = rest[18:]
    wanted_a, wanted_b, rows_a, cols_a, used_a, rows_b, cols_b, used_b = held
    slot_count = rows_a.shape[0]

    def put(at, *values):
        for i, value in enumerate(values):
            out[at + i] = value

    def scan(tile, rows, cols, used):

        def step(s, carry):
            ends, sent, load = carry
            row = rows[s]
            piece = cols[s] // piece_blocks
            live = s < used[0]
            half = row // piece_blocks
            local = row - half * piece_blocks
            lower = half == 0
            part = jnp.where(lower, tile, 1 - tile)
            at = HEAD + STRIDE * (part * lay.slots + jnp.where(lower, ends[0], ends[1]))
            base = half * lay.size
            put(base + at, s, local, piece)
            sought = jnp.where(live, local, -1)
            hits = [(asked[half * n_row + k] == sought).astype(jnp.int32) for k in range(n_row)]
            found = sum(hits)

            @pl.when(found > 0)
            def _():
                for core in range(2):
                    mine = tile if core == 0 else 1 - tile
                    side = half if core == 0 else 1 - half
                    first = core * lay.size
                    out[first + lay.load_at + mine * lay.loads + load] = s

                    place = sent
                    for k in range(n_row):
                        put(
                            first + lay.sent_at + STRIDE * (mine * lay.sends + place),
                            mine * lay.loads + load,
                            2 * k + side,
                            piece,
                            jnp.where(place == sent, FIRST, 0),
                        )
                        place = place + hits[k]

            one = live.astype(jnp.int32)
            ends = (ends[0] + jnp.where(lower, one, 0), ends[1] + jnp.where(lower, 0, one))
            return ends, sent + found, load + jnp.where(found > 0, 1, 0)

        zero = jnp.int32(0)
        ends, sent, load = lax.fori_loop(0, slot_count, step, ((zero, zero), zero, zero))
        for core in range(2):
            mine = tile if core == 0 else 1 - tile
            base = core * lay.size
            for i, (at, begin, end, unit, spare) in enumerate(
                (
                    (HEAD, mine * lay.slots, ends[core], MANY, piece_blocks),
                    (lay.sent_at, mine * lay.sends, sent, FEW, 2 * n_row),
                )
            ):
                for u in range(unit - 1):
                    put(base + at + STRIDE * (begin + end + u), 0, spare, 0, 0)
                out[base + 2 * i + mine] = begin + (end + unit - 1) // unit * unit
            out[base + 4 + mine] = mine * lay.loads + load

    def mark(core):
        base = core * lay.size
        for b in range(piece_blocks + 1):
            seen[b] = 0
        for part in range(2):

            @pl.loop(part * lay.slots, out[base + part])
            def _(i):
                entry = base + HEAD + STRIDE * i
                row = out[entry + 1]
                out[entry + 3] = jnp.where(seen[row] == 0, FIRST, 0)
                seen[row] = entry

        def close(b, bare):
            entry = seen[b]
            out[base + lay.bare_at + bare] = b

            @pl.when(entry > 0)
            def _():
                out[entry + 3] = out[entry + 3] + LAST

            return bare + jnp.where(entry == 0, 1, 0)

        out[base + 6] = lax.fori_loop(0, piece_blocks, close, jnp.int32(0))
        out[base + 7] = core

    @pl.when(place[1] == 0)
    def _():
        fetches = [
            pltpu.make_async_copy(source, target, in_sems.at[i])
            for i, (source, target) in enumerate(zip(sources, held))
        ]
        for fetch in fetches:
            fetch.start()
        for fetch in fetches:
            fetch.wait()
        for half, wanted in enumerate((wanted_a, wanted_b)):
            for k in range(n_row):
                asked[half * n_row + k] = wanted[k, 0]
        scan(0, rows_a, cols_a, used_a)
        scan(1, rows_b, cols_b, used_b)
        for core in range(2):
            mark(core)
        copies = [
            pltpu.make_async_copy(out.at[pl.ds(core * lay.size, lay.size)], target, sems.at[core])
            for core, target in enumerate((own, other))
        ]
        for copy in copies:
            copy.start()
        for copy in copies:
            copy.wait()


def settle_kernel(place, own, handed, out, sem):
    for half, source in enumerate((own, handed)):

        @pl.when(place[1] == half)
        def _():
            copy = pltpu.make_async_copy(source, out, sem)
            copy.start()
            copy.wait()


def pick_kernel(n_row, block_size, wanted, vectors, out, sems):
    def fetch(k):
        at = pl.multiple_of(wanted[k, 0] * block_size, block_size)
        return pltpu.make_async_copy(vectors.at[pl.ds(at, block_size)], out.at[k], sems.at[k])

    for k in range(n_row):
        fetch(k).start()
    for k in range(n_row):
        fetch(k).wait()


def pack_kernel(place, picked, picked_b, out, held, sems):
    n_row, _, width = picked.shape
    middle = width // 2

    def put(k):
        return pltpu.make_async_copy(held.at[k], out.at[k], sems.at[k])

    for half in range(2):

        @pl.when(place[1] == half)
        def _():
            part = slice(half * middle, (half + 1) * middle)
            for k in range(n_row):
                held[k] = jnp.concatenate([picked[k, :, part], picked_b[k, :, part]], axis=1)
                put(k).start()

    for k in range(n_row):
        put(k).wait()


def fetches(plan, base, stride, ends, part, tiles, blocks, sems):
    def copy(tile, i):
        slot = plan[base + stride * i]
        return pltpu.make_async_copy(tile.at[slot], blocks.at[i], sems.at[i])

    def start():
        for side, tile in enumerate(tiles):

            @pl.loop(side * part, plan[ends + side])
            def _(i):
                copy(tile, i).start()

    def wait(i):
        copy(tiles[0], i).wait()

    return start, wait


def load_kernel(plan, tile_a, array, blocks, held, sems, held_sem):
    whole = pltpu.make_async_copy(array, held, held_sem)
    whole.start()
    start, wait = fetches(plan, HEAD, STRIDE, 0, 0, (tile_a,), blocks, sems)
    start()

    @pl.loop(0, plan[0])
    def _(i):
        wait(i)

    whole.wait()


def each_product(plan, base, ends, part, block_of, pieces, use, then=None, before=None):
    unroll = MANY if base == HEAD else FEW

    for side in range(2):

        @pl.loop(side * part // unroll, plan[ends + side] // unroll)
        def _(j):
            step = [(unroll * j + u, base + STRIDE * (unroll * j + u)) for u in range(unroll)]
            if before is not None:
                for i, entry in step:
                    before(side, i, entry)
            for i, entry in step:
                block = block_of(side, i, entry)
                piece = pieces[side][plan[entry + 2]]
                use(entry, jnp.dot(block, piece, preferred_element_type=jnp.float32))
            if then is not None:
                for i, entry in step:
                    then(entry)


def add_products(plan, base, ends, part, block_of, pieces, total, before=None):
    def use(entry, value):
        total[plan[entry + 1]] += value

    each_product(plan, base, ends, part, block_of, pieces, use, before=before)


def split_sides(pieces, vec):
    middle = vec.shape[-1] // 2
    column = lax.broadcasted_iota(jnp.int32, (1, vec.shape[-1]), 1)
    for side in range(2):
        keep = jnp.where((column // middle) == side, 1.0, 0.0).astype(jnp.bfloat16)
        for p in range(vec.shape[1]):
            vec[side, p] = pieces[p] * keep


def joined(total, k):
    one, two = total[2 * k], total[2 * k + 1]
    low = lax.broadcasted_iota(jnp.int32, one.shape, 1) < one.shape[1] // 2
    return jnp.where(low, one, two) + pltpu.roll(
        jnp.where(low, two, one), one.shape[1] // 2, axis=1
    )


def first_sent_kernel(
    lay, plan, tile_a, tile_b, pieces, start, out, blocks, vec, total, held, held_sem, sems
):
    n_row = out.shape[0]
    begin, wait = fetches(plan, lay.load_at, 1, 4, lay.loads, (tile_a, tile_b), blocks, sems)
    begin()
    copy = pltpu.make_async_copy(start, held, held_sem)
    copy.start()
    split_sides(pieces, vec)
    total[...] = jnp.zeros_like(total)

    def before(side, i, entry):
        @pl.when(plan[entry + 3] == FIRST)
        def _():
            wait(plan[entry])

    add_products(
        plan,
        lay.sent_at,
        2,
        lay.sends,
        lambda side, i, entry: blocks[plan[entry]],
        (vec.at[0], vec.at[1]),
        total,
        before,
    )
    copy.wait()
    for k in range(n_row):
        value = joined(total, k) - center_value * held[k].astype(jnp.float32)
        out[k] = (value / half_width).astype(jnp.bfloat16)


def second_sent_kernel(
    lay, plan, blocks, pieces, current, previous, out, vec, total, held, held_sem, ready, out_sems
):
    n_row = out.shape[0]
    copy = pltpu.make_async_copy(previous, held, held_sem)
    copy.start()
    split_sides(pieces, vec)
    total[...] = jnp.zeros_like(total)
    add_products(
        plan,
        lay.sent_at,
        2,
        lay.sends,
        lambda side, i, entry: blocks[plan[entry]],
        (vec.at[0], vec.at[1]),
        total,
    )
    copy.wait()

    def put(k):
        return pltpu.make_async_copy(ready.at[k], out.at[k], out_sems.at[k])

    for k in range(n_row):
        value = joined(total, k) - center_value * current[k].astype(jnp.float32)
        ready[k] = (value - held[k].astype(jnp.float32)).astype(jnp.bfloat16)
        put(k).start()
    for k in range(n_row):
        put(k).wait()


def whole_columns(half, mine, other, vec, at):
    n_row, _, width = mine.shape
    middle = width // 2

    @pl.when(half == 0)
    def _():
        for p in range(n_row):
            one, two = mine[p], other[p]
            vec[0, p, :, at : at + width] = jnp.concatenate([one[:, :middle], two[:, middle:]], axis=1)
            vec[1, p, :, at : at + width] = jnp.concatenate([one[:, middle:], two[:, :middle]], axis=1)

    @pl.when(half != 0)
    def _():
        for p in range(n_row):
            one, two = mine[p], other[p]
            vec[0, p, :, at : at + width] = jnp.concatenate([two[:, middle:], one[:, :middle]], axis=1)
            vec[1, p, :, at : at + width] = jnp.concatenate([two[:, :middle], one[:, middle:]], axis=1)


def prime_kernel(vectors, total, own, sem):
    _, block_size, double = total.shape
    width = double // 2
    copy = pltpu.make_async_copy(vectors, own, sem)
    copy.start()
    copy.wait()

    @pl.loop(0, vectors.shape[0] // block_size)
    def _(b):
        at = pl.ds(pl.multiple_of(b * block_size, block_size), block_size)
        value = own[at, :].astype(jnp.float32)
        total[b, :, :width] = -center_value * value
        total[b, :, width:] = -value


def early_kernel(
    lay,
    plan,
    tile_a,
    tile_b,
    q1,
    q1_other,
    q2,
    q2_other,
    start,
    base,
    total,
    vec,
    own,
    blocks,
    sems,
    row_sems,
):
    piece_blocks, block_size, width = base.shape
    begin, wait = fetches(plan, HEAD, STRIDE, 0, lay.slots, (tile_a, tile_b), blocks, sems)
    begin()
    whole_columns(plan[7], q1, q1_other, vec, 0)
    whole_columns(plan[7], q2, q2_other, vec, width)

    def rows(b):
        return pl.ds(pl.multiple_of(b * block_size, block_size), block_size)

    def put(b):
        return pltpu.make_async_copy(own.at[rows(b)], base.at[b], row_sems.at[b])

    add_products(
        plan,
        HEAD,
        0,
        lay.slots,
        lambda side, i, entry: blocks[i],
        (vec.at[0], vec.at[1]),
        total,
        lambda side, i, entry: wait(i),
    )

    @pl.loop(0, piece_blocks)
    def _(b):
        first = (total[b, :, :width] / half_width).astype(jnp.bfloat16).astype(jnp.float32)
        second = total[b, :, width:] - center_value * first
        second = second.astype(jnp.bfloat16).astype(jnp.float32)
        own[rows(b), :] = (-center_value * second - first).astype(jnp.bfloat16)
        put(b).start()

    @pl.loop(0, piece_blocks)
    def _(b):
        put(b).wait()


def last_kernel(
    lay, plan, blocks, tile_b, mine, other, base, out, vec, total, own, blocks_b, sems, row_sems
):
    piece_blocks = base.shape[0]
    begin = lay.slots

    def fetch(i):
        slot = plan[HEAD + STRIDE * i]
        return pltpu.make_async_copy(tile_b.at[slot], blocks_b.at[i - begin], sems.at[i - begin])

    @pl.loop(begin, plan[1])
    def _(i):
        fetch(i).start()

    def put(source, b):
        return pltpu.make_async_copy(source.at[b], out.at[b], row_sems.at[b])

    @pl.loop(0, plan[6])
    def _(i):
        b = plan[lay.bare_at + i]
        put(base, b).start()

    whole_columns(plan[7], mine, other, vec, 0)

    def use(entry, value):
        row = plan[entry + 1]
        marks = plan[entry + 3]
        start = base[jnp.minimum(row, piece_blocks - 1)].astype(jnp.float32)
        value = jnp.where(lax.rem(marks, LAST) == FIRST, start, total[row]) + value
        total[row] = value
        own[row] = value.astype(jnp.bfloat16)

    def then(entry):
        @pl.when(plan[entry + 3] >= LAST)
        def _():
            put(own, plan[entry + 1]).start()

    def block_of(side, i, entry):
        return blocks[i] if side == 0 else blocks_b[i - begin]

    def before(side, i, entry):
        if side == 1:
            fetch(i).wait()

    each_product(
        plan, HEAD, 0, lay.slots, block_of, (vec.at[0], vec.at[1]), use, then, before
    )

    @pl.loop(0, piece_blocks)
    def _(b):
        put(own, b).wait()


def after(value, *others):
    return lax.optimization_barrier((value, *others))[0]


def call(kernel, out, args, spaces, scratch, mib, name, estimate=None, aliases=None):
    args = [
        pltpu.with_memory_space_constraint(arg, space) if space in (VMEM, HBM) or tied else arg
        for arg, (space, tied) in zip(args, spaces)
    ]
    return pl.pallas_call(
        kernel,
        out_shape=[space(shape, dtype) for shape, dtype, space in out],
        in_specs=[spec(space) for space, _ in spaces],
        out_specs=[spec(space) for _, _, space in out],
        scratch_shapes=scratch,
        compiler_params=params(mib),
        cost_estimate=estimate,
        input_output_aliases=aliases or {},
        name=name,
    )(*args)


HERE = (VMEM, True)
FAR = (HBM, True)
LIST = (SMEM, True)
SCALARS = (SMEM, False)
ANYWHERE = (pl.ANY, False)


def on_pair(vectors, tile_blocks, block_rows, block_cols, counts):
    n_row = lax.axis_size("row")
    tile = tile_blocks[0, 0]
    slot_rows = block_rows[0, 0]
    slot_cols = block_cols[0, 0]
    used = counts[0]
    slot_count, block_size, _ = tile.shape
    width = vectors.shape[1]
    piece_blocks = vectors.shape[0] // block_size
    place = jnp.stack([lax.axis_index("row"), lax.axis_index("col")]).astype(jnp.int32)

    across = functools.partial(lax.ppermute, axis_name="col", perm=[(0, 1), (1, 0)])

    needed = jnp.max(
        jnp.where(
            slot_cols[None, :] // piece_blocks == jnp.arange(n_row)[:, None],
            slot_cols[None, :] % piece_blocks,
            0,
        ),
        axis=1,
        keepdims=True,
    )
    exchange = functools.partial(
        lax.all_to_all, axis_name="row", split_axis=0, concat_axis=0, tiled=True
    )
    wanted = exchange(jnp.broadcast_to(needed, (n_row, LANES)))
    sent_shape = (n_row, block_size, width)
    (sent,) = call(
        functools.partial(pick_kernel, n_row, block_size),
        [(sent_shape, jnp.bfloat16, VMEM)],
        (wanted, vectors),
        (SCALARS, FAR),
        [DMA((n_row,))],
        2,
        "pick",
    )
    tile_other = across(tile)
    sent_other = across(sent)
    wanted_other = across(after(wanted, sent))
    slots = (slot_rows, slot_cols, used)
    slots_other = [across(after(array, sent)) for array in slots]
    packed = call(
        pack_kernel,
        [(sent_shape, jnp.bfloat16, HBM)],
        (place, sent, sent_other),
        (SCALARS, HERE, HERE),
        [VMEM(sent_shape, jnp.bfloat16), DMA((n_row,))],
        4,
        "pack",
    )[0]

    lay = layout_for(slot_count, n_row, piece_blocks)
    list_shape = ((lay.size,), jnp.int32)
    described = (wanted, after(wanted_other, packed), *slots, *slots_other)
    own_list, other_list = call(
        functools.partial(plan_kernel, n_row, piece_blocks, lay),
        [(*list_shape, HBM)] * 2,
        (place, *described),
        (SCALARS,) + (ANYWHERE,) * len(described),
        [SMEM(array.shape, jnp.int32) for array in described]
        + [
            SMEM((2 * lay.size,), jnp.int32),
            SMEM((2 * n_row,), jnp.int32),
            SMEM((piece_blocks + 1,), jnp.int32),
            DMA((len(described),)),
            DMA((2,)),
        ],
        2,
        "plan",
    )
    q1 = exchange(after(packed, own_list))
    plan = call(
        settle_kernel,
        [(*list_shape, SMEM)],
        (place, own_list, across(after(other_list, packed))),
        (SCALARS, ANYWHERE, ANYWHERE),
        [DMA],
        2,
        "settle",
    )[0]

    def load(cue, array):
        return call(
            load_kernel,
            [
                ((lay.slots, block_size, block_size), jnp.bfloat16, VMEM),
                (array.shape, array.dtype, VMEM),
            ],
            (after(plan, cue), tile, array),
            (LIST, FAR, FAR),
            [DMA((lay.slots,)), DMA],
            2,
            "load",
        )

    def cost(products, rows):
        size = block_size * width
        return pl.CostEstimate(
            flops=2 * products * block_size * size,
            bytes_accessed=2 * (products * block_size * block_size + 3 * rows * size),
            transcendentals=0,
        )

    sums = [
        VMEM((2, n_row, block_size, width), jnp.bfloat16),
        VMEM((2 * n_row + 1, block_size, width), jnp.float32),
    ]

    def first_blocks(*args):
        return call(
            functools.partial(first_sent_kernel, lay),
            [
                (sent_shape, jnp.bfloat16, VMEM),
                ((2 * lay.loads, block_size, block_size), jnp.bfloat16, VMEM),
            ],
            (plan, tile, tile_other, *args),
            (LIST, FAR, ANYWHERE, HERE, FAR),
            sums + [VMEM(sent_shape, jnp.bfloat16), DMA, DMA((2 * lay.loads,))],
            8,
            "sent",
            cost(n_row, n_row),
        )

    def second_blocks(*args):
        return call(
            functools.partial(second_sent_kernel, lay),
            [(sent_shape, jnp.bfloat16, HBM)],
            (plan, *args),
            (LIST, HERE, HERE, HERE, FAR),
            sums
            + [VMEM(sent_shape, jnp.bfloat16), DMA, VMEM(sent_shape, jnp.bfloat16), DMA((n_row,))],
            8,
            "sent",
            cost(n_row, n_row),
        )[0]

    base_shape = (piece_blocks, block_size, width)

    sums_shape = ((piece_blocks + 1, block_size, 2 * width), jnp.float32, VMEM)

    def early(*args):
        return call(
            functools.partial(early_kernel, lay),
            [(base_shape, jnp.bfloat16, HBM), sums_shape],
            (plan, tile, tile_other, *args),
            (LIST, FAR, ANYWHERE, HERE, HERE, HERE, HERE, HERE),
            [
                VMEM((2, n_row, block_size, 2 * width), jnp.bfloat16),
                VMEM(vectors.shape, jnp.bfloat16),
                VMEM((2 * lay.slots, block_size, block_size), jnp.bfloat16),
                DMA((2 * lay.slots,)),
                DMA((piece_blocks,)),
            ],
            18,
            "early",
            cost(2 * slot_count, 2 * piece_blocks),
            {7: 1},
        )[0]

    def last(blocks, *args):
        rows = (piece_blocks + 1, block_size, width)
        (out,) = call(
            functools.partial(last_kernel, lay),
            [(base_shape, jnp.bfloat16, HBM)],
            (plan, blocks, tile_other, *args),
            (LIST, HERE, ANYWHERE, HERE, HERE, HERE),
            [
                VMEM((2, n_row, block_size, width), jnp.bfloat16),
                VMEM(rows, jnp.float32),
                VMEM(rows, jnp.bfloat16),
                VMEM((lay.slots, block_size, block_size), jnp.bfloat16),
                DMA((lay.slots,)),
                DMA((piece_blocks,)),
            ],
            14,
            "last",
            cost(slot_count, piece_blocks),
        )
        return out.reshape(vectors.shape)

    q1 = after(q1, plan)
    first_sent, blocks = first_blocks(q1, packed)
    q2 = exchange(first_sent)
    second_sent = second_blocks(blocks, q2, first_sent, packed)
    q1_other = across(after(q1, second_sent))
    q2_other = across(after(q2, second_sent))
    (start,) = call(
        prime_kernel,
        [sums_shape],
        (after(vectors, second_sent),),
        (FAR,),
        [VMEM(vectors.shape, jnp.bfloat16), DMA],
        4,
        "prime",
        cost(0, 3 * piece_blocks),
    )
    base = early(q1, q1_other, q2, q2_other, start)
    q3 = after(exchange(second_sent), base)
    q3_other = across(q3)
    blocks, base = load(q3, base)
    return last(blocks, q3, q3_other, base)


def on_any(vectors, tile_blocks, block_rows, block_cols, counts):
    n_row = lax.axis_size("row")
    n_col = lax.axis_size("col")
    tile_data = tile_blocks[0, 0]
    slot_rows = block_rows[0, 0]
    slot_cols = block_cols[0, 0]
    used = counts[0, 0]
    block_size = tile_data.shape[-1]
    width = vectors.shape[1]
    piece_blocks = vectors.shape[0] // block_size
    row_blocks = piece_blocks * n_col
    slot_count = tile_data.shape[0]
    live = (jnp.arange(slot_count) < used).astype(jnp.float32)
    onehot = (slot_rows[None, :] == jnp.arange(row_blocks)[:, None]).astype(jnp.float32) * live[
        None, :
    ]
    source_piece = slot_cols // piece_blocks
    offset = slot_cols % piece_blocks
    needed = jnp.max(
        jnp.where(source_piece[None, :] == jnp.arange(n_row)[:, None], offset[None, :], 0), axis=1
    )
    wanted = lax.all_to_all(
        needed.reshape(n_row, 1), "row", split_axis=0, concat_axis=0, tiled=True
    ).reshape(n_row)

    def apply_tiles(current):
        own_blocks = current.reshape(piece_blocks, block_size, width)
        outgoing = jnp.take(own_blocks, wanted, axis=0)
        received = lax.all_to_all(outgoing, "row", split_axis=0, concat_axis=0, tiled=True)
        vec_blocks = jnp.take(received, source_piece, axis=0)
        products = jnp.einsum(
            "sij,sjk->sik", tile_data, vec_blocks, preferred_element_type=jnp.float32
        )
        term = jnp.einsum("ls,sik->lik", onehot, products, precision=lax.Precision.HIGHEST)
        term = term.reshape(row_blocks * block_size, width)
        return lax.psum_scatter(
            term.astype(jnp.bfloat16), "col", scatter_dimension=0, tiled=True
        ).astype(jnp.float32)

    previous = vectors
    applied = apply_tiles(vectors)
    current = ((applied - center_value * previous.astype(jnp.float32)) / half_width).astype(
        jnp.bfloat16
    )
    for repeat in range(DEGREE - 1):
        applied = apply_tiles(current)
        following = (
            2.0 * (applied - center_value * current.astype(jnp.float32)) / half_width
            - previous.astype(jnp.float32)
        ).astype(jnp.bfloat16)
        previous, current = (current, following)
    return current


def solution(mesh):
    n_row, n_col = mesh.shape["row"], mesh.shape["col"]
    paired = n_col == 2 and n_row & (n_row - 1) == 0
    return jax.shard_map(
        on_pair if paired else on_any,
        mesh=mesh,
        in_specs=(
            P(("row", "col"), "vec"),
            P("row", "col", None, None, None),
            P("row", "col", None),
            P("row", "col", None),
            P("row", "col"),
        ),
        out_specs=P(("row", "col"), "vec"),
        check_vma=False,
    )
```

```python
import functools
import typing

import jax
import jax.numpy as jnp
from jax import lax
from jax.experimental import pallas as pl
from jax.experimental.pallas import tpu as pltpu
from jax.sharding import PartitionSpec as P

DEGREE = 3

center_value = 0.5
half_width = 2.0

VMEM = pltpu.VMEM
SMEM = pltpu.SMEM
HBM = pltpu.HBM
DMA = pltpu.SemaphoreType.DMA
LANES = 128
FEW = 4
MANY = 4
HEAD = 8
STRIDE = 4
FIRST = 1
LAST = 2


def spec(space):
    return pl.BlockSpec(memory_space=space)


def params(mib):
    return pltpu.CompilerParams(vmem_limit_bytes=mib * 1024 * 1024)


def round_up(n, step):
    return (n + step - 1) // step * step


class Layout(typing.NamedTuple):
    slots: int
    sends: int
    loads: int
    sent_at: int
    load_at: int
    bare_at: int
    size: int


def layout_for(slot_count, n_row, piece_blocks):
    slots = round_up(slot_count, MANY) + MANY
    sends = round_up(2 * n_row * n_row, FEW) + FEW
    sent_at = HEAD + STRIDE * 2 * slots
    load_at = sent_at + STRIDE * 2 * sends
    bare_at = load_at + 2 * (slot_count + 1)
    size = round_up(bare_at + piece_blocks, 8 * LANES)
    return Layout(slots, sends, slot_count + 1, sent_at, load_at, bare_at, size)


def plan_kernel(
    n_row,
    piece_blocks,
    lay,
    place,
    wanted_a,
    wanted_b,
    meta_a,
    meta_b,
    own,
    other,
    out,
    count,
    asked,
    seen,
    sems,
):
    slot_count = (meta_a.shape[0] - 1) // 2

    def put(at, *values):
        for i, value in enumerate(values):
            out[at + i] = value

    def scan(tile, meta):
        used = meta[2 * slot_count]


        def step(s, carry):
            ends, sent, load = carry
            row = meta[s]
            piece = meta[slot_count + s] // piece_blocks
            live = s < used
            half = row // piece_blocks
            local = row - half * piece_blocks
            lower = half == 0
            part = jnp.where(lower, tile, 1 - tile)
            at = HEAD + STRIDE * (part * lay.slots + jnp.where(lower, ends[0], ends[1]))
            base = half * lay.size
            put(base + at, s, local, piece)
            found = jnp.where(live, count[row], 0)

            @pl.when(found > 0)
            def _():
                for core in range(2):
                    mine = tile if core == 0 else 1 - tile
                    side = half if core == 0 else 1 - half
                    first = core * lay.size
                    out[first + lay.load_at + mine * lay.loads + load] = s

                    @pl.loop(0, found)
                    def _(j):
                        put(
                            first + lay.sent_at + STRIDE * (mine * lay.sends + sent + j),
                            mine * lay.loads + load,
                            2 * asked[row * n_row + j] + side,
                            piece,
                            jnp.where(j == 0, FIRST, 0),
                        )

            one = live.astype(jnp.int32)
            ends = (ends[0] + jnp.where(lower, one, 0), ends[1] + jnp.where(lower, 0, one))
            return ends, sent + found, load + jnp.where(found > 0, 1, 0)

        zero = jnp.int32(0)
        ends, sent, load = lax.fori_loop(0, slot_count, step, ((zero, zero), zero, zero))
        for core in range(2):
            mine = tile if core == 0 else 1 - tile
            base = core * lay.size
            for i, (at, begin, end, unit, spare) in enumerate(
                (
                    (HEAD, mine * lay.slots, ends[core], MANY, piece_blocks),
                    (lay.sent_at, mine * lay.sends, sent, FEW, 2 * n_row),
                )
            ):
                for u in range(unit - 1):
                    put(base + at + STRIDE * (begin + end + u), 0, spare, 0, 0)
                out[base + 2 * i + mine] = begin + (end + unit - 1) // unit * unit
            out[base + 4 + mine] = mine * lay.loads + load

    def mark(core):
        base = core * lay.size
        for b in range(piece_blocks + 1):
            seen[b] = 0
        for part in range(2):

            @pl.loop(part * lay.slots, out[base + part])
            def _(i):
                entry = base + HEAD + STRIDE * i
                row = out[entry + 1]
                out[entry + 3] = jnp.where(seen[row] == 0, FIRST, 0)
                seen[row] = entry

        def close(b, bare):
            entry = seen[b]
            out[base + lay.bare_at + bare] = b

            @pl.when(entry > 0)
            def _():
                out[entry + 3] = out[entry + 3] + LAST

            return bare + jnp.where(entry == 0, 1, 0)

        out[base + 6] = lax.fori_loop(0, piece_blocks, close, jnp.int32(0))
        out[base + 7] = core

    @pl.when(place[1] == 0)
    def _():
        for row in range(2 * piece_blocks):
            count[row] = 0
        for half, wanted in enumerate((wanted_a, wanted_b)):
            for k in range(n_row):
                row = half * piece_blocks + wanted[k, 0]
                number = count[row]
                asked[row * n_row + number] = k
                count[row] = number + 1
        scan(0, meta_a)
        scan(1, meta_b)
        for core in range(2):
            mark(core)
        copies = [
            pltpu.make_async_copy(out.at[pl.ds(core * lay.size, lay.size)], target, sems.at[core])
            for core, target in enumerate((own, other))
        ]
        for copy in copies:
            copy.start()
        for copy in copies:
            copy.wait()


def settle_kernel(place, own, handed, out, sem):
    for half, source in enumerate((own, handed)):

        @pl.when(place[1] == half)
        def _():
            copy = pltpu.make_async_copy(source, out, sem)
            copy.start()
            copy.wait()


def pick_kernel(n_row, block_size, wanted, vectors, out, sems):
    def fetch(k):
        at = pl.multiple_of(wanted[k, 0] * block_size, block_size)
        return pltpu.make_async_copy(vectors.at[pl.ds(at, block_size)], out.at[k], sems.at[k])

    for k in range(n_row):
        fetch(k).start()
    for k in range(n_row):
        fetch(k).wait()


def pack_kernel(place, picked, picked_b, out, held, sems):
    n_row, _, width = picked.shape
    middle = width // 2

    def put(k):
        return pltpu.make_async_copy(held.at[k], out.at[k], sems.at[k])

    for half in range(2):

        @pl.when(place[1] == half)
        def _():
            part = slice(half * middle, (half + 1) * middle)
            for k in range(n_row):
                held[k] = jnp.concatenate([picked[k, :, part], picked_b[k, :, part]], axis=1)
                put(k).start()

    for k in range(n_row):
        put(k).wait()


def fetches(plan, base, stride, ends, part, tiles, blocks, sems):
    def copy(tile, i):
        slot = plan[base + stride * i]
        return pltpu.make_async_copy(tile.at[slot], blocks.at[i], sems.at[i])

    def start():
        for side, tile in enumerate(tiles):

            @pl.loop(side * part, plan[ends + side])
            def _(i):
                copy(tile, i).start()

    def wait(i):
        copy(tiles[0], i).wait()

    return start, wait


def load_kernel(plan, tile_a, array, blocks, held, sems, held_sem):
    whole = pltpu.make_async_copy(array, held, held_sem)
    whole.start()
    start, wait = fetches(plan, HEAD, STRIDE, 0, 0, (tile_a,), blocks, sems)
    start()

    @pl.loop(0, plan[0])
    def _(i):
        wait(i)

    whole.wait()


def each_product(plan, base, ends, part, block_of, pieces, use, then=None, before=None):
    unroll = MANY if base == HEAD else FEW

    for side in range(2):

        @pl.loop(side * part // unroll, plan[ends + side] // unroll)
        def _(j):
            step = [(unroll * j + u, base + STRIDE * (unroll * j + u)) for u in range(unroll)]
            if before is not None:
                for i, entry in step:
                    before(side, i, entry)
            for i, entry in step:
                block = block_of(side, i, entry)
                piece = pieces[side][plan[entry + 2]]
                use(entry, jnp.dot(block, piece, preferred_element_type=jnp.float32))
            if then is not None:
                for i, entry in step:
                    then(entry)


def add_products(plan, base, ends, part, block_of, pieces, total, before=None):
    def use(entry, value):
        total[plan[entry + 1]] += value

    each_product(plan, base, ends, part, block_of, pieces, use, before=before)


def split_sides(pieces, vec):
    middle = vec.shape[-1] // 2
    column = lax.broadcasted_iota(jnp.int32, (1, vec.shape[-1]), 1)
    for side in range(2):
        keep = jnp.where((column // middle) == side, 1.0, 0.0).astype(jnp.bfloat16)
        for p in range(vec.shape[1]):
            vec[side, p] = pieces[p] * keep


def joined(total, k):
    one, two = total[2 * k], total[2 * k + 1]
    low = lax.broadcasted_iota(jnp.int32, one.shape, 1) < one.shape[1] // 2
    return jnp.where(low, one, two) + pltpu.roll(
        jnp.where(low, two, one), one.shape[1] // 2, axis=1
    )


def first_sent_kernel(
    lay, plan, tile_a, tile_b, pieces, start, out, blocks, vec, total, held, held_sem, sems
):
    n_row = out.shape[0]
    begin, wait = fetches(plan, lay.load_at, 1, 4, lay.loads, (tile_a, tile_b), blocks, sems)
    begin()
    copy = pltpu.make_async_copy(start, held, held_sem)
    copy.start()
    split_sides(pieces, vec)
    total[...] = jnp.zeros_like(total)

    def before(side, i, entry):
        @pl.when(plan[entry + 3] == FIRST)
        def _():
            wait(plan[entry])

    add_products(
        plan,
        lay.sent_at,
        2,
        lay.sends,
        lambda side, i, entry: blocks[plan[entry]],
        (vec.at[0], vec.at[1]),
        total,
        before,
    )
    copy.wait()
    for k in range(n_row):
        value = joined(total, k) - center_value * held[k].astype(jnp.float32)
        out[k] = (value / half_width).astype(jnp.bfloat16)


def second_sent_kernel(
    lay, plan, blocks, pieces, current, previous, out, vec, total, held, held_sem, ready, out_sems
):
    n_row = out.shape[0]
    copy = pltpu.make_async_copy(previous, held, held_sem)
    copy.start()
    split_sides(pieces, vec)
    total[...] = jnp.zeros_like(total)
    add_products(
        plan,
        lay.sent_at,
        2,
        lay.sends,
        lambda side, i, entry: blocks[plan[entry]],
        (vec.at[0], vec.at[1]),
        total,
    )
    copy.wait()

    def put(k):
        return pltpu.make_async_copy(ready.at[k], out.at[k], out_sems.at[k])

    for k in range(n_row):
        value = joined(total, k) - center_value * current[k].astype(jnp.float32)
        ready[k] = (value - held[k].astype(jnp.float32)).astype(jnp.bfloat16)
        put(k).start()
    for k in range(n_row):
        put(k).wait()


def whole_columns(half, mine, other, vec, at):
    n_row, _, width = mine.shape
    middle = width // 2

    @pl.when(half == 0)
    def _():
        for p in range(n_row):
            one, two = mine[p], other[p]
            vec[0, p, :, at : at + width] = jnp.concatenate([one[:, :middle], two[:, middle:]], axis=1)
            vec[1, p, :, at : at + width] = jnp.concatenate([one[:, middle:], two[:, :middle]], axis=1)

    @pl.when(half != 0)
    def _():
        for p in range(n_row):
            one, two = mine[p], other[p]
            vec[0, p, :, at : at + width] = jnp.concatenate([two[:, middle:], one[:, :middle]], axis=1)
            vec[1, p, :, at : at + width] = jnp.concatenate([two[:, :middle], one[:, middle:]], axis=1)


def prime_kernel(vectors, total, own, sem):
    _, block_size, double = total.shape
    width = double // 2
    copy = pltpu.make_async_copy(vectors, own, sem)
    copy.start()
    copy.wait()

    @pl.loop(0, vectors.shape[0] // block_size)
    def _(b):
        at = pl.ds(pl.multiple_of(b * block_size, block_size), block_size)
        value = own[at, :].astype(jnp.float32)
        total[b, :, :width] = -center_value * value
        total[b, :, width:] = -value


def early_kernel(
    lay,
    plan,
    tile_a,
    tile_b,
    q1,
    q1_other,
    q2,
    q2_other,
    start,
    base,
    total,
    vec,
    own,
    blocks,
    sems,
    row_sems,
):
    piece_blocks, block_size, width = base.shape
    begin, wait = fetches(plan, HEAD, STRIDE, 0, lay.slots, (tile_a, tile_b), blocks, sems)
    begin()
    whole_columns(plan[7], q1, q1_other, vec, 0)
    whole_columns(plan[7], q2, q2_other, vec, width)

    def rows(b):
        return pl.ds(pl.multiple_of(b * block_size, block_size), block_size)

    def put(b):
        return pltpu.make_async_copy(own.at[rows(b)], base.at[b], row_sems.at[b])

    add_products(
        plan,
        HEAD,
        0,
        lay.slots,
        lambda side, i, entry: blocks[i],
        (vec.at[0], vec.at[1]),
        total,
        lambda side, i, entry: wait(i),
    )

    @pl.loop(0, piece_blocks)
    def _(b):
        first = (total[b, :, :width] / half_width).astype(jnp.bfloat16).astype(jnp.float32)
        second = total[b, :, width:] - center_value * first
        second = second.astype(jnp.bfloat16).astype(jnp.float32)
        own[rows(b), :] = (-center_value * second - first).astype(jnp.bfloat16)
        put(b).start()

    @pl.loop(0, piece_blocks)
    def _(b):
        put(b).wait()


def last_kernel(
    lay, plan, blocks, tile_b, mine, other, base, out, vec, total, own, blocks_b, sems, row_sems
):
    piece_blocks = base.shape[0]
    begin = lay.slots

    def fetch(i):
        slot = plan[HEAD + STRIDE * i]
        return pltpu.make_async_copy(tile_b.at[slot], blocks_b.at[i - begin], sems.at[i - begin])

    @pl.loop(begin, plan[1])
    def _(i):
        fetch(i).start()

    def put(source, b):
        return pltpu.make_async_copy(source.at[b], out.at[b], row_sems.at[b])

    @pl.loop(0, plan[6])
    def _(i):
        b = plan[lay.bare_at + i]
        put(base, b).start()

    whole_columns(plan[7], mine, other, vec, 0)

    def use(entry, value):
        row = plan[entry + 1]
        marks = plan[entry + 3]
        start = base[jnp.minimum(row, piece_blocks - 1)].astype(jnp.float32)
        value = jnp.where(lax.rem(marks, LAST) == FIRST, start, total[row]) + value
        total[row] = value
        own[row] = value.astype(jnp.bfloat16)

    def then(entry):
        @pl.when(plan[entry + 3] >= LAST)
        def _():
            put(own, plan[entry + 1]).start()

    def block_of(side, i, entry):
        return blocks[i] if side == 0 else blocks_b[i - begin]

    def before(side, i, entry):
        if side == 1:
            fetch(i).wait()

    each_product(
        plan, HEAD, 0, lay.slots, block_of, (vec.at[0], vec.at[1]), use, then, before
    )

    @pl.loop(0, piece_blocks)
    def _(b):
        put(own, b).wait()


def after(value, *others):
    return lax.optimization_barrier((value, *others))[0]


def call(kernel, out, args, spaces, scratch, mib, name, estimate=None, aliases=None):
    args = [
        pltpu.with_memory_space_constraint(arg, space) if space in (VMEM, HBM) or tied else arg
        for arg, (space, tied) in zip(args, spaces)
    ]
    return pl.pallas_call(
        kernel,
        out_shape=[space(shape, dtype) for shape, dtype, space in out],
        in_specs=[spec(space) for space, _ in spaces],
        out_specs=[spec(space) for _, _, space in out],
        scratch_shapes=scratch,
        compiler_params=params(mib),
        cost_estimate=estimate,
        input_output_aliases=aliases or {},
        name=name,
    )(*args)


HERE = (VMEM, True)
FAR = (HBM, True)
LIST = (SMEM, True)
SCALARS = (SMEM, False)
ANYWHERE = (pl.ANY, False)


def on_pair(vectors, tile_blocks, block_rows, block_cols, counts):
    n_row = lax.axis_size("row")
    tile = tile_blocks[0, 0]
    slot_rows = block_rows[0, 0]
    slot_cols = block_cols[0, 0]
    used = counts[0]
    slot_count, block_size, _ = tile.shape
    width = vectors.shape[1]
    piece_blocks = vectors.shape[0] // block_size
    place = jnp.stack([lax.axis_index("row"), lax.axis_index("col")]).astype(jnp.int32)

    across = functools.partial(lax.ppermute, axis_name="col", perm=[(0, 1), (1, 0)])

    needed = jnp.max(
        jnp.where(
            slot_cols[None, :] // piece_blocks == jnp.arange(n_row)[:, None],
            slot_cols[None, :] % piece_blocks,
            0,
        ),
        axis=1,
        keepdims=True,
    )
    exchange = functools.partial(
        lax.all_to_all, axis_name="row", split_axis=0, concat_axis=0, tiled=True
    )
    wanted = exchange(jnp.broadcast_to(needed, (n_row, LANES)))
    sent_shape = (n_row, block_size, width)
    (sent,) = call(
        functools.partial(pick_kernel, n_row, block_size),
        [(sent_shape, jnp.bfloat16, VMEM)],
        (wanted, vectors),
        (SCALARS, FAR),
        [DMA((n_row,))],
        2,
        "pick",
    )
    tile_other = across(tile)
    sent_other = across(sent)
    wanted_other = across(after(wanted, sent))
    meta = jnp.concatenate([slot_rows, slot_cols, used])
    meta_other = across(after(meta, sent))
    packed = call(
        pack_kernel,
        [(sent_shape, jnp.bfloat16, HBM)],
        (place, sent, sent_other),
        (SCALARS, HERE, HERE),
        [VMEM(sent_shape, jnp.bfloat16), DMA((n_row,))],
        4,
        "pack",
    )[0]

    lay = layout_for(slot_count, n_row, piece_blocks)
    list_shape = ((lay.size,), jnp.int32)
    own_list, other_list = call(
        functools.partial(plan_kernel, n_row, piece_blocks, lay),
        [(*list_shape, HBM)] * 2,
        (place, wanted, after(wanted_other, packed), meta, meta_other),
        (SCALARS,) * 5,
        [
            SMEM((2 * lay.size,), jnp.int32),
            SMEM((2 * piece_blocks,), jnp.int32),
            SMEM((2 * piece_blocks * n_row,), jnp.int32),
            SMEM((piece_blocks + 1,), jnp.int32),
            DMA((2,)),
        ],
        2,
        "plan",
    )
    q1 = exchange(after(packed, own_list))
    plan = call(
        settle_kernel,
        [(*list_shape, SMEM)],
        (place, own_list, across(after(other_list, packed))),
        (SCALARS, ANYWHERE, ANYWHERE),
        [DMA],
        2,
        "settle",
    )[0]

    def load(cue, array):
        return call(
            load_kernel,
            [
                ((lay.slots, block_size, block_size), jnp.bfloat16, VMEM),
                (array.shape, array.dtype, VMEM),
            ],
            (after(plan, cue), tile, array),
            (LIST, FAR, FAR),
            [DMA((lay.slots,)), DMA],
            2,
            "load",
        )

    def cost(products, rows):
        size = block_size * width
        return pl.CostEstimate(
            flops=2 * products * block_size * size,
            bytes_accessed=2 * (products * block_size * block_size + 3 * rows * size),
            transcendentals=0,
        )

    sums = [
        VMEM((2, n_row, block_size, width), jnp.bfloat16),
        VMEM((2 * n_row + 1, block_size, width), jnp.float32),
    ]

    def first_blocks(*args):
        return call(
            functools.partial(first_sent_kernel, lay),
            [
                (sent_shape, jnp.bfloat16, VMEM),
                ((2 * lay.loads, block_size, block_size), jnp.bfloat16, VMEM),
            ],
            (plan, tile, tile_other, *args),
            (LIST, FAR, ANYWHERE, HERE, FAR),
            sums + [VMEM(sent_shape, jnp.bfloat16), DMA, DMA((2 * lay.loads,))],
            8,
            "sent",
            cost(n_row, n_row),
        )

    def second_blocks(*args):
        return call(
            functools.partial(second_sent_kernel, lay),
            [(sent_shape, jnp.bfloat16, HBM)],
            (plan, *args),
            (LIST, HERE, HERE, HERE, FAR),
            sums
            + [VMEM(sent_shape, jnp.bfloat16), DMA, VMEM(sent_shape, jnp.bfloat16), DMA((n_row,))],
            8,
            "sent",
            cost(n_row, n_row),
        )[0]

    base_shape = (piece_blocks, block_size, width)

    sums_shape = ((piece_blocks + 1, block_size, 2 * width), jnp.float32, VMEM)

    def early(*args):
        return call(
            functools.partial(early_kernel, lay),
            [(base_shape, jnp.bfloat16, HBM), sums_shape],
            (plan, tile, tile_other, *args),
            (LIST, FAR, ANYWHERE, HERE, HERE, HERE, HERE, HERE),
            [
                VMEM((2, n_row, block_size, 2 * width), jnp.bfloat16),
                VMEM(vectors.shape, jnp.bfloat16),
                VMEM((2 * lay.slots, block_size, block_size), jnp.bfloat16),
                DMA((2 * lay.slots,)),
                DMA((piece_blocks,)),
            ],
            18,
            "early",
            cost(2 * slot_count, 2 * piece_blocks),
            {7: 1},
        )[0]

    def last(blocks, *args):
        rows = (piece_blocks + 1, block_size, width)
        (out,) = call(
            functools.partial(last_kernel, lay),
            [(base_shape, jnp.bfloat16, HBM)],
            (plan, blocks, tile_other, *args),
            (LIST, HERE, ANYWHERE, HERE, HERE, HERE),
            [
                VMEM((2, n_row, block_size, width), jnp.bfloat16),
                VMEM(rows, jnp.float32),
                VMEM(rows, jnp.bfloat16),
                VMEM((lay.slots, block_size, block_size), jnp.bfloat16),
                DMA((lay.slots,)),
                DMA((piece_blocks,)),
            ],
            14,
            "last",
            cost(slot_count, piece_blocks),
        )
        return out.reshape(vectors.shape)

    q1 = after(q1, plan)
    first_sent, blocks = first_blocks(q1, packed)
    q2 = exchange(first_sent)
    second_sent = second_blocks(blocks, q2, first_sent, packed)
    q1_other = across(after(q1, second_sent))
    q2_other = across(after(q2, second_sent))
    (start,) = call(
        prime_kernel,
        [sums_shape],
        (after(vectors, second_sent),),
        (FAR,),
        [VMEM(vectors.shape, jnp.bfloat16), DMA],
        4,
        "prime",
        cost(0, 3 * piece_blocks),
    )
    base = early(q1, q1_other, q2, q2_other, start)
    q3 = after(exchange(second_sent), base)
    q3_other = across(q3)
    blocks, base = load(q3, base)
    return last(blocks, q3, q3_other, base)


def on_any(vectors, tile_blocks, block_rows, block_cols, counts):
    n_row = lax.axis_size("row")
    n_col = lax.axis_size("col")
    tile_data = tile_blocks[0, 0]
    slot_rows = block_rows[0, 0]
    slot_cols = block_cols[0, 0]
    used = counts[0, 0]
    block_size = tile_data.shape[-1]
    width = vectors.shape[1]
    piece_blocks = vectors.shape[0] // block_size
    row_blocks = piece_blocks * n_col
    slot_count = tile_data.shape[0]
    live = (jnp.arange(slot_count) < used).astype(jnp.float32)
    onehot = (slot_rows[None, :] == jnp.arange(row_blocks)[:, None]).astype(jnp.float32) * live[
        None, :
    ]
    source_piece = slot_cols // piece_blocks
    offset = slot_cols % piece_blocks
    needed = jnp.max(
        jnp.where(source_piece[None, :] == jnp.arange(n_row)[:, None], offset[None, :], 0), axis=1
    )
    wanted = lax.all_to_all(
        needed.reshape(n_row, 1), "row", split_axis=0, concat_axis=0, tiled=True
    ).reshape(n_row)

    def apply_tiles(current):
        own_blocks = current.reshape(piece_blocks, block_size, width)
        outgoing = jnp.take(own_blocks, wanted, axis=0)
        received = lax.all_to_all(outgoing, "row", split_axis=0, concat_axis=0, tiled=True)
        vec_blocks = jnp.take(received, source_piece, axis=0)
        products = jnp.einsum(
            "sij,sjk->sik", tile_data, vec_blocks, preferred_element_type=jnp.float32
        )
        term = jnp.einsum("ls,sik->lik", onehot, products, precision=lax.Precision.HIGHEST)
        term = term.reshape(row_blocks * block_size, width)
        return lax.psum_scatter(
            term.astype(jnp.bfloat16), "col", scatter_dimension=0, tiled=True
        ).astype(jnp.float32)

    previous = vectors
    applied = apply_tiles(vectors)
    current = ((applied - center_value * previous.astype(jnp.float32)) / half_width).astype(
        jnp.bfloat16
    )
    for repeat in range(DEGREE - 1):
        applied = apply_tiles(current)
        following = (
            2.0 * (applied - center_value * current.astype(jnp.float32)) / half_width
            - previous.astype(jnp.float32)
        ).astype(jnp.bfloat16)
        previous, current = (current, following)
    return current


def solution(mesh):
    n_row, n_col = mesh.shape["row"], mesh.shape["col"]
    paired = n_col == 2 and n_row & (n_row - 1) == 0
    return jax.shard_map(
        on_pair if paired else on_any,
        mesh=mesh,
        in_specs=(
            P(("row", "col"), "vec"),
            P("row", "col", None, None, None),
            P("row", "col", None),
            P("row", "col", None),
            P("row", "col"),
        ),
        out_specs=P(("row", "col"), "vec"),
        check_vma=False,
    )
```

```python
import functools
import typing

import jax
import jax.numpy as jnp
from jax import lax
from jax.experimental import pallas as pl
from jax.experimental.pallas import tpu as pltpu
from jax.sharding import PartitionSpec as P

DEGREE = 3

center_value = 0.5
half_width = 2.0

VMEM = pltpu.VMEM
SMEM = pltpu.SMEM
HBM = pltpu.HBM
DMA = pltpu.SemaphoreType.DMA
LANES = 128
FEW = 4
MANY = 4
HEAD = 8
STRIDE = 4
FIRST = 1
LAST = 2


def spec(space):
    return pl.BlockSpec(memory_space=space)


def params(mib):
    return pltpu.CompilerParams(vmem_limit_bytes=mib * 1024 * 1024)


def round_up(n, step):
    return (n + step - 1) // step * step


class Layout(typing.NamedTuple):
    slots: int
    sends: int
    loads: int
    sent_at: int
    load_at: int
    bare_at: int
    size: int


def layout_for(slot_count, n_row, piece_blocks):
    slots = round_up(slot_count, MANY) + MANY
    sends = round_up(2 * n_row * n_row, FEW) + FEW
    sent_at = HEAD + STRIDE * 2 * slots
    load_at = sent_at + STRIDE * 2 * sends
    bare_at = load_at + 2 * (slot_count + 1)
    size = round_up(bare_at + piece_blocks, 8 * LANES)
    return Layout(slots, sends, slot_count + 1, sent_at, load_at, bare_at, size)


def plan_kernel(
    n_row,
    piece_blocks,
    lay,
    place,
    wanted_a,
    wanted_b,
    meta_a,
    meta_b,
    own,
    other,
    out,
    asked,
    seen,
    sems,
):
    slot_count = (meta_a.shape[0] - 1) // 2

    def put(at, *values):
        for i, value in enumerate(values):
            out[at + i] = value

    def scan(tile, meta):
        used = meta[2 * slot_count]


        def step(s, carry):
            ends, sent, load = carry
            row = meta[s]
            piece = meta[slot_count + s] // piece_blocks
            live = s < used
            half = row // piece_blocks
            local = row - half * piece_blocks
            lower = half == 0
            part = jnp.where(lower, tile, 1 - tile)
            at = HEAD + STRIDE * (part * lay.slots + jnp.where(lower, ends[0], ends[1]))
            base = half * lay.size
            put(base + at, s, local, piece)
            sought = jnp.where(live, local, -1)
            hits = [(asked[half * n_row + k] == sought).astype(jnp.int32) for k in range(n_row)]
            found = sum(hits)

            @pl.when(found > 0)
            def _():
                for core in range(2):
                    mine = tile if core == 0 else 1 - tile
                    side = half if core == 0 else 1 - half
                    first = core * lay.size
                    out[first + lay.load_at + mine * lay.loads + load] = s

                    place = sent
                    for k in range(n_row):
                        put(
                            first + lay.sent_at + STRIDE * (mine * lay.sends + place),
                            mine * lay.loads + load,
                            2 * k + side,
                            piece,
                            jnp.where(place == sent, FIRST, 0),
                        )
                        place = place + hits[k]

            one = live.astype(jnp.int32)
            ends = (ends[0] + jnp.where(lower, one, 0), ends[1] + jnp.where(lower, 0, one))
            return ends, sent + found, load + jnp.where(found > 0, 1, 0)

        zero = jnp.int32(0)
        ends, sent, load = lax.fori_loop(0, slot_count, step, ((zero, zero), zero, zero))
        for core in range(2):
            mine = tile if core == 0 else 1 - tile
            base = core * lay.size
            for i, (at, begin, end, unit, spare) in enumerate(
                (
                    (HEAD, mine * lay.slots, ends[core], MANY, piece_blocks),
                    (lay.sent_at, mine * lay.sends, sent, FEW, 2 * n_row),
                )
            ):
                for u in range(unit - 1):
                    put(base + at + STRIDE * (begin + end + u), 0, spare, 0, 0)
                out[base + 2 * i + mine] = begin + (end + unit - 1) // unit * unit
            out[base + 4 + mine] = mine * lay.loads + load

    def mark(core):
        base = core * lay.size
        for b in range(piece_blocks + 1):
            seen[b] = 0
        for part in range(2):

            @pl.loop(part * lay.slots, out[base + part])
            def _(i):
                entry = base + HEAD + STRIDE * i
                row = out[entry + 1]
                out[entry + 3] = jnp.where(seen[row] == 0, FIRST, 0)
                seen[row] = entry

        def close(b, bare):
            entry = seen[b]
            out[base + lay.bare_at + bare] = b

            @pl.when(entry > 0)
            def _():
                out[entry + 3] = out[entry + 3] + LAST

            return bare + jnp.where(entry == 0, 1, 0)

        out[base + 6] = lax.fori_loop(0, piece_blocks, close, jnp.int32(0))
        out[base + 7] = core

    @pl.when(place[1] == 0)
    def _():
        for half, wanted in enumerate((wanted_a, wanted_b)):
            for k in range(n_row):
                asked[half * n_row + k] = wanted[k, 0]
        scan(0, meta_a)
        scan(1, meta_b)
        for core in range(2):
            mark(core)
        copies = [
            pltpu.make_async_copy(out.at[pl.ds(core * lay.size, lay.size)], target, sems.at[core])
            for core, target in enumerate((own, other))
        ]
        for copy in copies:
            copy.start()
        for copy in copies:
            copy.wait()


def settle_kernel(place, own, handed, out, sem):
    for half, source in enumerate((own, handed)):

        @pl.when(place[1] == half)
        def _():
            copy = pltpu.make_async_copy(source, out, sem)
            copy.start()
            copy.wait()


def pick_kernel(n_row, block_size, wanted, vectors, out, sems):
    def fetch(k):
        at = pl.multiple_of(wanted[k, 0] * block_size, block_size)
        return pltpu.make_async_copy(vectors.at[pl.ds(at, block_size)], out.at[k], sems.at[k])

    for k in range(n_row):
        fetch(k).start()
    for k in range(n_row):
        fetch(k).wait()


def pack_kernel(place, picked, picked_b, out, held, sems):
    n_row, _, width = picked.shape
    middle = width // 2

    def put(k):
        return pltpu.make_async_copy(held.at[k], out.at[k], sems.at[k])

    for half in range(2):

        @pl.when(place[1] == half)
        def _():
            part = slice(half * middle, (half + 1) * middle)
            for k in range(n_row):
                held[k] = jnp.concatenate([picked[k, :, part], picked_b[k, :, part]], axis=1)
                put(k).start()

    for k in range(n_row):
        put(k).wait()


def fetches(plan, base, stride, ends, part, tiles, blocks, sems):
    def copy(tile, i):
        slot = plan[base + stride * i]
        return pltpu.make_async_copy(tile.at[slot], blocks.at[i], sems.at[i])

    def start():
        for side, tile in enumerate(tiles):

            @pl.loop(side * part, plan[ends + side])
            def _(i):
                copy(tile, i).start()

    def wait(i):
        copy(tiles[0], i).wait()

    return start, wait


def load_kernel(plan, tile_a, array, blocks, held, sems, held_sem):
    whole = pltpu.make_async_copy(array, held, held_sem)
    whole.start()
    start, wait = fetches(plan, HEAD, STRIDE, 0, 0, (tile_a,), blocks, sems)
    start()

    @pl.loop(0, plan[0])
    def _(i):
        wait(i)

    whole.wait()


def each_product(plan, base, ends, part, block_of, pieces, use, then=None, before=None):
    unroll = MANY if base == HEAD else FEW

    for side in range(2):

        @pl.loop(side * part // unroll, plan[ends + side] // unroll)
        def _(j):
            step = [(unroll * j + u, base + STRIDE * (unroll * j + u)) for u in range(unroll)]
            if before is not None:
                for i, entry in step:
                    before(side, i, entry)
            for i, entry in step:
                block = block_of(side, i, entry)
                piece = pieces[side][plan[entry + 2]]
                use(entry, jnp.dot(block, piece, preferred_element_type=jnp.float32))
            if then is not None:
                for i, entry in step:
                    then(entry)


def add_products(plan, base, ends, part, block_of, pieces, total, before=None):
    def use(entry, value):
        total[plan[entry + 1]] += value

    each_product(plan, base, ends, part, block_of, pieces, use, before=before)


def split_sides(pieces, vec):
    middle = vec.shape[-1] // 2
    column = lax.broadcasted_iota(jnp.int32, (1, vec.shape[-1]), 1)
    for side in range(2):
        keep = jnp.where((column // middle) == side, 1.0, 0.0).astype(jnp.bfloat16)
        for p in range(vec.shape[1]):
            vec[side, p] = pieces[p] * keep


def joined(total, k):
    one, two = total[2 * k], total[2 * k + 1]
    low = lax.broadcasted_iota(jnp.int32, one.shape, 1) < one.shape[1] // 2
    return jnp.where(low, one, two) + pltpu.roll(
        jnp.where(low, two, one), one.shape[1] // 2, axis=1
    )


def first_sent_kernel(
    lay, plan, tile_a, tile_b, pieces, start, out, blocks, vec, total, held, held_sem, sems
):
    n_row = out.shape[0]
    begin, wait = fetches(plan, lay.load_at, 1, 4, lay.loads, (tile_a, tile_b), blocks, sems)
    begin()
    copy = pltpu.make_async_copy(start, held, held_sem)
    copy.start()
    split_sides(pieces, vec)
    total[...] = jnp.zeros_like(total)

    def before(side, i, entry):
        @pl.when(plan[entry + 3] == FIRST)
        def _():
            wait(plan[entry])

    add_products(
        plan,
        lay.sent_at,
        2,
        lay.sends,
        lambda side, i, entry: blocks[plan[entry]],
        (vec.at[0], vec.at[1]),
        total,
        before,
    )
    copy.wait()
    for k in range(n_row):
        value = joined(total, k) - center_value * held[k].astype(jnp.float32)
        out[k] = (value / half_width).astype(jnp.bfloat16)


def second_sent_kernel(
    lay, plan, blocks, pieces, current, previous, out, vec, total, held, held_sem, ready, out_sems
):
    n_row = out.shape[0]
    copy = pltpu.make_async_copy(previous, held, held_sem)
    copy.start()
    split_sides(pieces, vec)
    total[...] = jnp.zeros_like(total)
    add_products(
        plan,
        lay.sent_at,
        2,
        lay.sends,
        lambda side, i, entry: blocks[plan[entry]],
        (vec.at[0], vec.at[1]),
        total,
    )
    copy.wait()

    def put(k):
        return pltpu.make_async_copy(ready.at[k], out.at[k], out_sems.at[k])

    for k in range(n_row):
        value = joined(total, k) - center_value * current[k].astype(jnp.float32)
        ready[k] = (value - held[k].astype(jnp.float32)).astype(jnp.bfloat16)
        put(k).start()
    for k in range(n_row):
        put(k).wait()


def whole_columns(half, mine, other, vec, at):
    n_row, _, width = mine.shape
    middle = width // 2

    @pl.when(half == 0)
    def _():
        for p in range(n_row):
            one, two = mine[p], other[p]
            vec[0, p, :, at : at + width] = jnp.concatenate([one[:, :middle], two[:, middle:]], axis=1)
            vec[1, p, :, at : at + width] = jnp.concatenate([one[:, middle:], two[:, :middle]], axis=1)

    @pl.when(half != 0)
    def _():
        for p in range(n_row):
            one, two = mine[p], other[p]
            vec[0, p, :, at : at + width] = jnp.concatenate([two[:, middle:], one[:, :middle]], axis=1)
            vec[1, p, :, at : at + width] = jnp.concatenate([two[:, :middle], one[:, middle:]], axis=1)


def prime_kernel(vectors, total, own, sem):
    _, block_size, double = total.shape
    width = double // 2
    copy = pltpu.make_async_copy(vectors, own, sem)
    copy.start()
    copy.wait()

    @pl.loop(0, vectors.shape[0] // block_size)
    def _(b):
        at = pl.ds(pl.multiple_of(b * block_size, block_size), block_size)
        value = own[at, :].astype(jnp.float32)
        total[b, :, :width] = -center_value * value
        total[b, :, width:] = -value


def early_kernel(
    lay,
    plan,
    tile_a,
    tile_b,
    q1,
    q1_other,
    q2,
    q2_other,
    start,
    base,
    total,
    vec,
    own,
    blocks,
    sems,
    row_sems,
):
    piece_blocks, block_size, width = base.shape
    begin, wait = fetches(plan, HEAD, STRIDE, 0, lay.slots, (tile_a, tile_b), blocks, sems)
    begin()
    whole_columns(plan[7], q1, q1_other, vec, 0)
    whole_columns(plan[7], q2, q2_other, vec, width)

    def rows(b):
        return pl.ds(pl.multiple_of(b * block_size, block_size), block_size)

    def put(b):
        return pltpu.make_async_copy(own.at[rows(b)], base.at[b], row_sems.at[b])

    add_products(
        plan,
        HEAD,
        0,
        lay.slots,
        lambda side, i, entry: blocks[i],
        (vec.at[0], vec.at[1]),
        total,
        lambda side, i, entry: wait(i),
    )

    @pl.loop(0, piece_blocks)
    def _(b):
        first = (total[b, :, :width] / half_width).astype(jnp.bfloat16).astype(jnp.float32)
        second = total[b, :, width:] - center_value * first
        second = second.astype(jnp.bfloat16).astype(jnp.float32)
        own[rows(b), :] = (-center_value * second - first).astype(jnp.bfloat16)
        put(b).start()

    @pl.loop(0, piece_blocks)
    def _(b):
        put(b).wait()


def last_kernel(
    lay, plan, blocks, tile_b, mine, other, base, out, vec, total, own, blocks_b, sems, row_sems
):
    piece_blocks = base.shape[0]
    begin = lay.slots

    def fetch(i):
        slot = plan[HEAD + STRIDE * i]
        return pltpu.make_async_copy(tile_b.at[slot], blocks_b.at[i - begin], sems.at[i - begin])

    @pl.loop(begin, plan[1])
    def _(i):
        fetch(i).start()

    def put(source, b):
        return pltpu.make_async_copy(source.at[b], out.at[b], row_sems.at[b])

    @pl.loop(0, plan[6])
    def _(i):
        b = plan[lay.bare_at + i]
        put(base, b).start()

    whole_columns(plan[7], mine, other, vec, 0)

    def use(entry, value):
        row = plan[entry + 1]
        marks = plan[entry + 3]
        start = base[jnp.minimum(row, piece_blocks - 1)].astype(jnp.float32)
        value = jnp.where(lax.rem(marks, LAST) == FIRST, start, total[row]) + value
        total[row] = value
        own[row] = value.astype(jnp.bfloat16)

    def then(entry):
        @pl.when(plan[entry + 3] >= LAST)
        def _():
            put(own, plan[entry + 1]).start()

    def block_of(side, i, entry):
        return blocks[i] if side == 0 else blocks_b[i - begin]

    def before(side, i, entry):
        if side == 1:
            fetch(i).wait()

    each_product(
        plan, HEAD, 0, lay.slots, block_of, (vec.at[0], vec.at[1]), use, then, before
    )

    @pl.loop(0, piece_blocks)
    def _(b):
        put(own, b).wait()


def after(value, *others):
    return lax.optimization_barrier((value, *others))[0]


def call(kernel, out, args, spaces, scratch, mib, name, estimate=None, aliases=None):
    args = [
        pltpu.with_memory_space_constraint(arg, space) if space in (VMEM, HBM) or tied else arg
        for arg, (space, tied) in zip(args, spaces)
    ]
    return pl.pallas_call(
        kernel,
        out_shape=[space(shape, dtype) for shape, dtype, space in out],
        in_specs=[spec(space) for space, _ in spaces],
        out_specs=[spec(space) for _, _, space in out],
        scratch_shapes=scratch,
        compiler_params=params(mib),
        cost_estimate=estimate,
        input_output_aliases=aliases or {},
        name=name,
    )(*args)


HERE = (VMEM, True)
FAR = (HBM, True)
LIST = (SMEM, True)
SCALARS = (SMEM, False)
ANYWHERE = (pl.ANY, False)


def on_pair(vectors, tile_blocks, block_rows, block_cols, counts):
    n_row = lax.axis_size("row")
    tile = tile_blocks[0, 0]
    slot_rows = block_rows[0, 0]
    slot_cols = block_cols[0, 0]
    used = counts[0]
    slot_count, block_size, _ = tile.shape
    width = vectors.shape[1]
    piece_blocks = vectors.shape[0] // block_size
    place = jnp.stack([lax.axis_index("row"), lax.axis_index("col")]).astype(jnp.int32)

    across = functools.partial(lax.ppermute, axis_name="col", perm=[(0, 1), (1, 0)])

    needed = jnp.max(
        jnp.where(
            slot_cols[None, :] // piece_blocks == jnp.arange(n_row)[:, None],
            slot_cols[None, :] % piece_blocks,
            0,
        ),
        axis=1,
        keepdims=True,
    )
    exchange = functools.partial(
        lax.all_to_all, axis_name="row", split_axis=0, concat_axis=0, tiled=True
    )
    wanted = exchange(jnp.broadcast_to(needed, (n_row, LANES)))
    sent_shape = (n_row, block_size, width)
    (sent,) = call(
        functools.partial(pick_kernel, n_row, block_size),
        [(sent_shape, jnp.bfloat16, VMEM)],
        (wanted, vectors),
        (SCALARS, FAR),
        [DMA((n_row,))],
        2,
        "pick",
    )
    tile_other = across(tile)
    sent_other = across(sent)
    wanted_other = across(after(wanted, sent))
    meta = jnp.concatenate([slot_rows, slot_cols, used])
    meta_other = across(after(meta, sent))
    packed = call(
        pack_kernel,
        [(sent_shape, jnp.bfloat16, HBM)],
        (place, sent, sent_other),
        (SCALARS, HERE, HERE),
        [VMEM(sent_shape, jnp.bfloat16), DMA((n_row,))],
        4,
        "pack",
    )[0]

    lay = layout_for(slot_count, n_row, piece_blocks)
    list_shape = ((lay.size,), jnp.int32)
    own_list, other_list = call(
        functools.partial(plan_kernel, n_row, piece_blocks, lay),
        [(*list_shape, HBM)] * 2,
        (place, wanted, after(wanted_other, packed), meta, meta_other),
        (SCALARS,) * 5,
        [
            SMEM((2 * lay.size,), jnp.int32),
            SMEM((2 * n_row,), jnp.int32),
            SMEM((piece_blocks + 1,), jnp.int32),
            DMA((2,)),
        ],
        2,
        "plan",
    )
    q1 = exchange(after(packed, own_list))
    plan = call(
        settle_kernel,
        [(*list_shape, SMEM)],
        (place, own_list, across(after(other_list, packed))),
        (SCALARS, ANYWHERE, ANYWHERE),
        [DMA],
        2,
        "settle",
    )[0]

    def load(cue, array):
        return call(
            load_kernel,
            [
                ((lay.slots, block_size, block_size), jnp.bfloat16, VMEM),
                (array.shape, array.dtype, VMEM),
            ],
            (after(plan, cue), tile, array),
            (LIST, FAR, FAR),
            [DMA((lay.slots,)), DMA],
            2,
            "load",
        )

    def cost(products, rows):
        size = block_size * width
        return pl.CostEstimate(
            flops=2 * products * block_size * size,
            bytes_accessed=2 * (products * block_size * block_size + 3 * rows * size),
            transcendentals=0,
        )

    sums = [
        VMEM((2, n_row, block_size, width), jnp.bfloat16),
        VMEM((2 * n_row + 1, block_size, width), jnp.float32),
    ]

    def first_blocks(*args):
        return call(
            functools.partial(first_sent_kernel, lay),
            [
                (sent_shape, jnp.bfloat16, VMEM),
                ((2 * lay.loads, block_size, block_size), jnp.bfloat16, VMEM),
            ],
            (plan, tile, tile_other, *args),
            (LIST, FAR, ANYWHERE, HERE, FAR),
            sums + [VMEM(sent_shape, jnp.bfloat16), DMA, DMA((2 * lay.loads,))],
            8,
            "sent",
            cost(n_row, n_row),
        )

    def second_blocks(*args):
        return call(
            functools.partial(second_sent_kernel, lay),
            [(sent_shape, jnp.bfloat16, HBM)],
            (plan, *args),
            (LIST, HERE, HERE, HERE, FAR),
            sums
            + [VMEM(sent_shape, jnp.bfloat16), DMA, VMEM(sent_shape, jnp.bfloat16), DMA((n_row,))],
            8,
            "sent",
            cost(n_row, n_row),
        )[0]

    base_shape = (piece_blocks, block_size, width)

    sums_shape = ((piece_blocks + 1, block_size, 2 * width), jnp.float32, VMEM)

    def early(*args):
        return call(
            functools.partial(early_kernel, lay),
            [(base_shape, jnp.bfloat16, HBM), sums_shape],
            (plan, tile, tile_other, *args),
            (LIST, FAR, ANYWHERE, HERE, HERE, HERE, HERE, HERE),
            [
                VMEM((2, n_row, block_size, 2 * width), jnp.bfloat16),
                VMEM(vectors.shape, jnp.bfloat16),
                VMEM((2 * lay.slots, block_size, block_size), jnp.bfloat16),
                DMA((2 * lay.slots,)),
                DMA((piece_blocks,)),
            ],
            18,
            "early",
            cost(2 * slot_count, 2 * piece_blocks),
            {7: 1},
        )[0]

    def last(blocks, *args):
        rows = (piece_blocks + 1, block_size, width)
        (out,) = call(
            functools.partial(last_kernel, lay),
            [(base_shape, jnp.bfloat16, HBM)],
            (plan, blocks, tile_other, *args),
            (LIST, HERE, ANYWHERE, HERE, HERE, HERE),
            [
                VMEM((2, n_row, block_size, width), jnp.bfloat16),
                VMEM(rows, jnp.float32),
                VMEM(rows, jnp.bfloat16),
                VMEM((lay.slots, block_size, block_size), jnp.bfloat16),
                DMA((lay.slots,)),
                DMA((piece_blocks,)),
            ],
            14,
            "last",
            cost(slot_count, piece_blocks),
        )
        return out.reshape(vectors.shape)

    q1 = after(q1, plan)
    first_sent, blocks = first_blocks(q1, packed)
    q2 = exchange(first_sent)
    second_sent = second_blocks(blocks, q2, first_sent, packed)
    q1_other = across(after(q1, second_sent))
    q2_other = across(after(q2, second_sent))
    (start,) = call(
        prime_kernel,
        [sums_shape],
        (after(vectors, second_sent),),
        (FAR,),
        [VMEM(vectors.shape, jnp.bfloat16), DMA],
        4,
        "prime",
        cost(0, 3 * piece_blocks),
    )
    base = early(q1, q1_other, q2, q2_other, start)
    q3 = after(exchange(second_sent), base)
    q3_other = across(q3)
    blocks, base = load(q3, base)
    return last(blocks, q3, q3_other, base)


def on_any(vectors, tile_blocks, block_rows, block_cols, counts):
    n_row = lax.axis_size("row")
    n_col = lax.axis_size("col")
    tile_data = tile_blocks[0, 0]
    slot_rows = block_rows[0, 0]
    slot_cols = block_cols[0, 0]
    used = counts[0, 0]
    block_size = tile_data.shape[-1]
    width = vectors.shape[1]
    piece_blocks = vectors.shape[0] // block_size
    row_blocks = piece_blocks * n_col
    slot_count = tile_data.shape[0]
    live = (jnp.arange(slot_count) < used).astype(jnp.float32)
    onehot = (slot_rows[None, :] == jnp.arange(row_blocks)[:, None]).astype(jnp.float32) * live[
        None, :
    ]
    source_piece = slot_cols // piece_blocks
    offset = slot_cols % piece_blocks
    needed = jnp.max(
        jnp.where(source_piece[None, :] == jnp.arange(n_row)[:, None], offset[None, :], 0), axis=1
    )
    wanted = lax.all_to_all(
        needed.reshape(n_row, 1), "row", split_axis=0, concat_axis=0, tiled=True
    ).reshape(n_row)

    def apply_tiles(current):
        own_blocks = current.reshape(piece_blocks, block_size, width)
        outgoing = jnp.take(own_blocks, wanted, axis=0)
        received = lax.all_to_all(outgoing, "row", split_axis=0, concat_axis=0, tiled=True)
        vec_blocks = jnp.take(received, source_piece, axis=0)
        products = jnp.einsum(
            "sij,sjk->sik", tile_data, vec_blocks, preferred_element_type=jnp.float32
        )
        term = jnp.einsum("ls,sik->lik", onehot, products, precision=lax.Precision.HIGHEST)
        term = term.reshape(row_blocks * block_size, width)
        return lax.psum_scatter(
            term.astype(jnp.bfloat16), "col", scatter_dimension=0, tiled=True
        ).astype(jnp.float32)

    previous = vectors
    applied = apply_tiles(vectors)
    current = ((applied - center_value * previous.astype(jnp.float32)) / half_width).astype(
        jnp.bfloat16
    )
    for repeat in range(DEGREE - 1):
        applied = apply_tiles(current)
        following = (
            2.0 * (applied - center_value * current.astype(jnp.float32)) / half_width
            - previous.astype(jnp.float32)
        ).astype(jnp.bfloat16)
        previous, current = (current, following)
    return current


def solution(mesh):
    n_row, n_col = mesh.shape["row"], mesh.shape["col"]
    paired = n_col == 2 and n_row & (n_row - 1) == 0
    return jax.shard_map(
        on_pair if paired else on_any,
        mesh=mesh,
        in_specs=(
            P(("row", "col"), "vec"),
            P("row", "col", None, None, None),
            P("row", "col", None),
            P("row", "col", None),
            P("row", "col"),
        ),
        out_specs=P(("row", "col"), "vec"),
        check_vma=False,
    )
```

```python
import functools
import typing

import jax
import jax.numpy as jnp
from jax import lax
from jax.experimental import pallas as pl
from jax.experimental.pallas import tpu as pltpu
from jax.sharding import PartitionSpec as P

DEGREE = 3

center_value = 0.5
half_width = 2.0

VMEM = pltpu.VMEM
SMEM = pltpu.SMEM
HBM = pltpu.HBM
DMA = pltpu.SemaphoreType.DMA
LANES = 128
FEW = 4
MANY = 4
HEAD = 8
STRIDE = 4
FIRST = 1
LAST = 2


def spec(space):
    return pl.BlockSpec(memory_space=space)


def params(mib):
    return pltpu.CompilerParams(vmem_limit_bytes=mib * 1024 * 1024)


def round_up(n, step):
    return (n + step - 1) // step * step


class Layout(typing.NamedTuple):
    slots: int
    sends: int
    loads: int
    sent_at: int
    load_at: int
    bare_at: int
    size: int


def layout_for(slot_count, n_row, piece_blocks):
    slots = round_up(slot_count, MANY) + MANY
    sends = round_up(2 * n_row * n_row, FEW) + FEW
    sent_at = HEAD + STRIDE * 2 * slots
    load_at = sent_at + STRIDE * 2 * sends
    bare_at = load_at + 2 * (slot_count + 1)
    size = round_up(bare_at + piece_blocks, 8 * LANES)
    return Layout(slots, sends, slot_count + 1, sent_at, load_at, bare_at, size)


def plan_kernel(
    n_row,
    piece_blocks,
    lay,
    place,
    wanted_a,
    wanted_b,
    meta_a,
    meta_b,
    own,
    other,
    out,
    asked,
    seen,
    sems,
):
    slot_count = (meta_a.shape[0] - 1) // 2

    def put(at, *values):
        for i, value in enumerate(values):
            out[at + i] = value

    def scan(tile, meta):
        used = meta[2 * slot_count]


        def step(s, carry):
            ends, sent, load = carry
            row = meta[s]
            piece = meta[slot_count + s] // piece_blocks
            live = s < used
            half = row // piece_blocks
            local = row - half * piece_blocks
            lower = half == 0
            part = jnp.where(lower, tile, 1 - tile)
            at = HEAD + STRIDE * (part * lay.slots + jnp.where(lower, ends[0], ends[1]))
            base = half * lay.size
            put(base + at, s, local, piece)
            sought = jnp.where(live, local, -1)
            hits = [(asked[half * n_row + k] == sought).astype(jnp.int32) for k in range(n_row)]
            found = sum(hits)

            @pl.when(found > 0)
            def _():
                for core in range(2):
                    mine = tile if core == 0 else 1 - tile
                    side = half if core == 0 else 1 - half
                    first = core * lay.size
                    out[first + lay.load_at + mine * lay.loads + load] = s

                    place = sent
                    for k in range(n_row):
                        put(
                            first + lay.sent_at + STRIDE * (mine * lay.sends + place),
                            mine * lay.loads + load,
                            2 * k + side,
                            piece,
                            jnp.where(place == sent, FIRST, 0),
                        )
                        place = place + hits[k]

            one = live.astype(jnp.int32)
            ends = (ends[0] + jnp.where(lower, one, 0), ends[1] + jnp.where(lower, 0, one))
            return ends, sent + found, load + jnp.where(found > 0, 1, 0)

        zero = jnp.int32(0)
        ends, sent, load = lax.fori_loop(0, slot_count, step, ((zero, zero), zero, zero))
        for core in range(2):
            mine = tile if core == 0 else 1 - tile
            base = core * lay.size
            for i, (at, begin, end, unit, spare) in enumerate(
                (
                    (HEAD, mine * lay.slots, ends[core], MANY, piece_blocks),
                    (lay.sent_at, mine * lay.sends, sent, FEW, 2 * n_row),
                )
            ):
                for u in range(unit - 1):
                    put(base + at + STRIDE * (begin + end + u), 0, spare, 0, 0)
                out[base + 2 * i + mine] = begin + (end + unit - 1) // unit * unit
            out[base + 4 + mine] = mine * lay.loads + load

    def mark(core):
        base = core * lay.size
        for b in range(piece_blocks + 1):
            seen[b] = 0
        for part in range(2):

            @pl.loop(part * lay.slots, out[base + part])
            def _(i):
                entry = base + HEAD + STRIDE * i
                row = out[entry + 1]
                out[entry + 3] = jnp.where(seen[row] == 0, FIRST, 0)
                seen[row] = entry

        def close(b, bare):
            entry = seen[b]
            out[base + lay.bare_at + bare] = b

            @pl.when(entry > 0)
            def _():
                out[entry + 3] = out[entry + 3] + LAST

            return bare + jnp.where(entry == 0, 1, 0)

        out[base + 6] = lax.fori_loop(0, piece_blocks, close, jnp.int32(0))
        out[base + 7] = core

    @pl.when(place[1] == 0)
    def _():
        for half, wanted in enumerate((wanted_a, wanted_b)):
            for k in range(n_row):
                asked[half * n_row + k] = wanted[k, 0]
        scan(0, meta_a)
        scan(1, meta_b)
        for core in range(2):
            mark(core)
        copies = [
            pltpu.make_async_copy(out.at[pl.ds(core * lay.size, lay.size)], target, sems.at[core])
            for core, target in enumerate((own, other))
        ]
        for copy in copies:
            copy.start()
        for copy in copies:
            copy.wait()


def settle_kernel(place, own, handed, out, sem):
    for half, source in enumerate((own, handed)):

        @pl.when(place[1] == half)
        def _():
            copy = pltpu.make_async_copy(source, out, sem)
            copy.start()
            copy.wait()


def pick_kernel(n_row, block_size, wanted, vectors, out, sems):
    def fetch(k):
        at = pl.multiple_of(wanted[k, 0] * block_size, block_size)
        return pltpu.make_async_copy(vectors.at[pl.ds(at, block_size)], out.at[k], sems.at[k])

    for k in range(n_row):
        fetch(k).start()
    for k in range(n_row):
        fetch(k).wait()


def pack_kernel(place, picked, picked_b, out, held, sems):
    n_row, _, width = picked.shape
    middle = width // 2

    def put(k):
        return pltpu.make_async_copy(held.at[k], out.at[k], sems.at[k])

    for half in range(2):

        @pl.when(place[1] == half)
        def _():
            part = slice(half * middle, (half + 1) * middle)
            for k in range(n_row):
                held[k] = jnp.concatenate([picked[k, :, part], picked_b[k, :, part]], axis=1)
                put(k).start()

    for k in range(n_row):
        put(k).wait()


def fetches(plan, base, stride, ends, part, tiles, blocks, sems):
    def copy(tile, i):
        slot = plan[base + stride * i]
        return pltpu.make_async_copy(tile.at[slot], blocks.at[i], sems.at[i])

    def start():
        for side, tile in enumerate(tiles):

            @pl.loop(side * part, plan[ends + side])
            def _(i):
                copy(tile, i).start()

    def wait(i):
        copy(tiles[0], i).wait()

    return start, wait


def load_kernel(plan, tile_a, array, blocks, held, sems, held_sem):
    whole = pltpu.make_async_copy(array, held, held_sem)
    whole.start()
    start, wait = fetches(plan, HEAD, STRIDE, 0, 0, (tile_a,), blocks, sems)
    start()

    @pl.loop(0, plan[0])
    def _(i):
        wait(i)

    whole.wait()


def each_product(plan, base, ends, part, block_of, pieces, use, then=None, before=None):
    unroll = MANY if base == HEAD else FEW

    for side in range(2):

        @pl.loop(side * part // unroll, plan[ends + side] // unroll)
        def _(j):
            step = [(unroll * j + u, base + STRIDE * (unroll * j + u)) for u in range(unroll)]
            if before is not None:
                for i, entry in step:
                    before(side, i, entry)
            for i, entry in step:
                block = block_of(side, i, entry)
                piece = pieces[side][plan[entry + 2]]
                use(entry, jnp.dot(block, piece, preferred_element_type=jnp.float32))
            if then is not None:
                for i, entry in step:
                    then(entry)


def add_products(plan, base, ends, part, block_of, pieces, total, before=None):
    def use(entry, value):
        total[plan[entry + 1]] += value

    each_product(plan, base, ends, part, block_of, pieces, use, before=before)


def split_sides(pieces, vec):
    middle = vec.shape[-1] // 2
    column = lax.broadcasted_iota(jnp.int32, (1, vec.shape[-1]), 1)
    for side in range(2):
        keep = jnp.where((column // middle) == side, 1.0, 0.0).astype(jnp.bfloat16)
        for p in range(vec.shape[1]):
            vec[side, p] = pieces[p] * keep


def joined(total, k):
    one, two = total[2 * k], total[2 * k + 1]
    low = lax.broadcasted_iota(jnp.int32, one.shape, 1) < one.shape[1] // 2
    return jnp.where(low, one, two) + pltpu.roll(
        jnp.where(low, two, one), one.shape[1] // 2, axis=1
    )


def first_sent_kernel(
    lay, plan, tile_a, tile_b, pieces, start, out, blocks, vec, total, held, held_sem, sems
):
    n_row = out.shape[0]
    begin, wait = fetches(plan, lay.load_at, 1, 4, lay.loads, (tile_a, tile_b), blocks, sems)
    begin()
    copy = pltpu.make_async_copy(start, held, held_sem)
    copy.start()
    split_sides(pieces, vec)
    total[...] = jnp.zeros_like(total)

    def before(side, i, entry):
        @pl.when(plan[entry + 3] == FIRST)
        def _():
            wait(plan[entry])

    add_products(
        plan,
        lay.sent_at,
        2,
        lay.sends,
        lambda side, i, entry: blocks[plan[entry]],
        (vec.at[0], vec.at[1]),
        total,
        before,
    )
    copy.wait()
    for k in range(n_row):
        value = joined(total, k) - center_value * held[k].astype(jnp.float32)
        out[k] = (value / half_width).astype(jnp.bfloat16)


def second_sent_kernel(
    lay, plan, blocks, pieces, current, previous, out, vec, total, held, held_sem, ready, out_sems
):
    n_row = out.shape[0]
    copy = pltpu.make_async_copy(previous, held, held_sem)
    copy.start()
    split_sides(pieces, vec)
    total[...] = jnp.zeros_like(total)
    add_products(
        plan,
        lay.sent_at,
        2,
        lay.sends,
        lambda side, i, entry: blocks[plan[entry]],
        (vec.at[0], vec.at[1]),
        total,
    )
    copy.wait()

    def put(k):
        return pltpu.make_async_copy(ready.at[k], out.at[k], out_sems.at[k])

    for k in range(n_row):
        value = joined(total, k) - center_value * current[k].astype(jnp.float32)
        ready[k] = (value - held[k].astype(jnp.float32)).astype(jnp.bfloat16)
        put(k).start()
    for k in range(n_row):
        put(k).wait()


def whole_columns(half, mine, other, vec, at):
    n_row, _, width = mine.shape
    middle = width // 2

    @pl.when(half == 0)
    def _():
        for p in range(n_row):
            one, two = mine[p], other[p]
            vec[0, p, :, at : at + width] = jnp.concatenate([one[:, :middle], two[:, middle:]], axis=1)
            vec[1, p, :, at : at + width] = jnp.concatenate([one[:, middle:], two[:, :middle]], axis=1)

    @pl.when(half != 0)
    def _():
        for p in range(n_row):
            one, two = mine[p], other[p]
            vec[0, p, :, at : at + width] = jnp.concatenate([two[:, middle:], one[:, :middle]], axis=1)
            vec[1, p, :, at : at + width] = jnp.concatenate([two[:, :middle], one[:, middle:]], axis=1)


def prime_kernel(vectors, total, own, sem):
    _, block_size, double = total.shape
    width = double // 2
    copy = pltpu.make_async_copy(vectors, own, sem)
    copy.start()
    copy.wait()

    @pl.loop(0, vectors.shape[0] // block_size)
    def _(b):
        at = pl.ds(pl.multiple_of(b * block_size, block_size), block_size)
        value = own[at, :].astype(jnp.float32)
        total[b, :, :width] = -center_value * value
        total[b, :, width:] = -value


def early_kernel(
    lay,
    plan,
    tile_a,
    tile_b,
    q1,
    q1_other,
    q2,
    q2_other,
    start,
    base,
    total,
    vec,
    own,
    blocks,
    sems,
    row_sems,
):
    piece_blocks, block_size, width = base.shape
    begin, wait = fetches(plan, HEAD, STRIDE, 0, lay.slots, (tile_a, tile_b), blocks, sems)
    begin()
    whole_columns(plan[7], q1, q1_other, vec, 0)
    whole_columns(plan[7], q2, q2_other, vec, width)

    def rows(b):
        return pl.ds(pl.multiple_of(b * block_size, block_size), block_size)

    def put(b):
        return pltpu.make_async_copy(own.at[rows(b)], base.at[b], row_sems.at[b])

    add_products(
        plan,
        HEAD,
        0,
        lay.slots,
        lambda side, i, entry: blocks[i],
        (vec.at[0], vec.at[1]),
        total,
        lambda side, i, entry: wait(i),
    )

    @pl.loop(0, piece_blocks)
    def _(b):
        first = (total[b, :, :width] / half_width).astype(jnp.bfloat16).astype(jnp.float32)
        second = total[b, :, width:] - center_value * first
        second = second.astype(jnp.bfloat16).astype(jnp.float32)
        own[rows(b), :] = (-center_value * second - first).astype(jnp.bfloat16)
        put(b).start()

    @pl.loop(0, piece_blocks)
    def _(b):
        put(b).wait()


def last_kernel(
    lay, plan, blocks, tile_b, mine, other, base, out, vec, total, own, blocks_b, sems, row_sems
):
    piece_blocks = base.shape[0]
    begin = lay.slots

    def fetch(i):
        slot = plan[HEAD + STRIDE * i]
        return pltpu.make_async_copy(tile_b.at[slot], blocks_b.at[i - begin], sems.at[i - begin])

    @pl.loop(begin, plan[1])
    def _(i):
        fetch(i).start()

    def put(source, b):
        return pltpu.make_async_copy(source.at[b], out.at[b], row_sems.at[b])

    @pl.loop(0, plan[6])
    def _(i):
        b = plan[lay.bare_at + i]
        put(base, b).start()

    whole_columns(plan[7], mine, other, vec, 0)

    def use(entry, value):
        row = plan[entry + 1]
        marks = plan[entry + 3]
        start = base[jnp.minimum(row, piece_blocks - 1)].astype(jnp.float32)
        value = jnp.where(lax.rem(marks, LAST) == FIRST, start, total[row]) + value
        total[row] = value
        own[row] = value.astype(jnp.bfloat16)

    def then(entry):
        @pl.when(plan[entry + 3] >= LAST)
        def _():
            put(own, plan[entry + 1]).start()

    def block_of(side, i, entry):
        return blocks[i] if side == 0 else blocks_b[i - begin]

    def before(side, i, entry):
        if side == 1:
            fetch(i).wait()

    each_product(
        plan, HEAD, 0, lay.slots, block_of, (vec.at[0], vec.at[1]), use, then, before
    )

    @pl.loop(0, piece_blocks)
    def _(b):
        put(own, b).wait()


def after(value, *others):
    return lax.optimization_barrier((value, *others))[0]


def call(kernel, out, args, spaces, scratch, mib, name, estimate=None, aliases=None):
    args = [
        pltpu.with_memory_space_constraint(arg, space) if space in (VMEM, HBM) or tied else arg
        for arg, (space, tied) in zip(args, spaces)
    ]
    return pl.pallas_call(
        kernel,
        out_shape=[space(shape, dtype) for shape, dtype, space in out],
        in_specs=[spec(space) for space, _ in spaces],
        out_specs=[spec(space) for _, _, space in out],
        scratch_shapes=scratch,
        compiler_params=params(mib),
        cost_estimate=estimate,
        input_output_aliases=aliases or {},
        name=name,
    )(*args)


HERE = (VMEM, True)
FAR = (HBM, True)
LIST = (SMEM, True)
SCALARS = (SMEM, False)
ANYWHERE = (pl.ANY, False)


def on_pair(vectors, tile_blocks, block_rows, block_cols, counts):
    n_row = lax.axis_size("row")
    tile = tile_blocks[0, 0]
    slot_rows = block_rows[0, 0]
    slot_cols = block_cols[0, 0]
    used = counts[0]
    slot_count, block_size, _ = tile.shape
    width = vectors.shape[1]
    piece_blocks = vectors.shape[0] // block_size
    place = jnp.stack([lax.axis_index("row"), lax.axis_index("col")]).astype(jnp.int32)

    across = functools.partial(lax.ppermute, axis_name="col", perm=[(0, 1), (1, 0)])

    needed = jnp.max(
        jnp.where(
            slot_cols[None, :] // piece_blocks == jnp.arange(n_row)[:, None],
            slot_cols[None, :] % piece_blocks,
            0,
        ),
        axis=1,
        keepdims=True,
    )
    exchange = functools.partial(
        lax.all_to_all, axis_name="row", split_axis=0, concat_axis=0, tiled=True
    )
    wanted = exchange(jnp.broadcast_to(needed, (n_row, LANES)))
    sent_shape = (n_row, block_size, width)
    (sent,) = call(
        functools.partial(pick_kernel, n_row, block_size),
        [(sent_shape, jnp.bfloat16, VMEM)],
        (wanted, vectors),
        (SCALARS, FAR),
        [DMA((n_row,))],
        2,
        "pick",
    )

    sent_other = across(sent)
    wanted_other = across(after(wanted, sent))
    meta = jnp.concatenate([slot_rows, slot_cols, used])
    meta_other = across(after(meta, sent))
    packed = call(
        pack_kernel,
        [(sent_shape, jnp.bfloat16, HBM)],
        (place, sent, sent_other),
        (SCALARS, HERE, HERE),
        [VMEM(sent_shape, jnp.bfloat16), DMA((n_row,))],
        4,
        "pack",
    )[0]

    tile_other = across(after(tile, packed))
    lay = layout_for(slot_count, n_row, piece_blocks)
    list_shape = ((lay.size,), jnp.int32)
    own_list, other_list = call(
        functools.partial(plan_kernel, n_row, piece_blocks, lay),
        [(*list_shape, HBM)] * 2,
        (place, wanted, after(wanted_other, packed), meta, meta_other),
        (SCALARS,) * 5,
        [
            SMEM((2 * lay.size,), jnp.int32),
            SMEM((2 * n_row,), jnp.int32),
            SMEM((piece_blocks + 1,), jnp.int32),
            DMA((2,)),
        ],
        2,
        "plan",
    )
    q1 = exchange(after(packed, own_list))
    plan = call(
        settle_kernel,
        [(*list_shape, SMEM)],
        (place, own_list, across(after(other_list, packed))),
        (SCALARS, ANYWHERE, ANYWHERE),
        [DMA],
        2,
        "settle",
    )[0]

    def load(cue, array):
        return call(
            load_kernel,
            [
                ((lay.slots, block_size, block_size), jnp.bfloat16, VMEM),
                (array.shape, array.dtype, VMEM),
            ],
            (after(plan, cue), tile, array),
            (LIST, FAR, FAR),
            [DMA((lay.slots,)), DMA],
            2,
            "load",
        )

    def cost(products, rows):
        size = block_size * width
        return pl.CostEstimate(
            flops=2 * products * block_size * size,
            bytes_accessed=2 * (products * block_size * block_size + 3 * rows * size),
            transcendentals=0,
        )

    sums = [
        VMEM((2, n_row, block_size, width), jnp.bfloat16),
        VMEM((2 * n_row + 1, block_size, width), jnp.float32),
    ]

    def first_blocks(*args):
        return call(
            functools.partial(first_sent_kernel, lay),
            [
                (sent_shape, jnp.bfloat16, VMEM),
                ((2 * lay.loads, block_size, block_size), jnp.bfloat16, VMEM),
            ],
            (plan, tile, tile_other, *args),
            (LIST, FAR, ANYWHERE, HERE, FAR),
            sums + [VMEM(sent_shape, jnp.bfloat16), DMA, DMA((2 * lay.loads,))],
            8,
            "sent",
            cost(n_row, n_row),
        )

    def second_blocks(*args):
        return call(
            functools.partial(second_sent_kernel, lay),
            [(sent_shape, jnp.bfloat16, HBM)],
            (plan, *args),
            (LIST, HERE, HERE, HERE, FAR),
            sums
            + [VMEM(sent_shape, jnp.bfloat16), DMA, VMEM(sent_shape, jnp.bfloat16), DMA((n_row,))],
            8,
            "sent",
            cost(n_row, n_row),
        )[0]

    base_shape = (piece_blocks, block_size, width)

    sums_shape = ((piece_blocks + 1, block_size, 2 * width), jnp.float32, VMEM)

    def early(*args):
        return call(
            functools.partial(early_kernel, lay),
            [(base_shape, jnp.bfloat16, HBM), sums_shape],
            (plan, tile, tile_other, *args),
            (LIST, FAR, ANYWHERE, HERE, HERE, HERE, HERE, HERE),
            [
                VMEM((2, n_row, block_size, 2 * width), jnp.bfloat16),
                VMEM(vectors.shape, jnp.bfloat16),
                VMEM((2 * lay.slots, block_size, block_size), jnp.bfloat16),
                DMA((2 * lay.slots,)),
                DMA((piece_blocks,)),
            ],
            18,
            "early",
            cost(2 * slot_count, 2 * piece_blocks),
            {7: 1},
        )[0]

    def last(blocks, *args):
        rows = (piece_blocks + 1, block_size, width)
        (out,) = call(
            functools.partial(last_kernel, lay),
            [(base_shape, jnp.bfloat16, HBM)],
            (plan, blocks, tile_other, *args),
            (LIST, HERE, ANYWHERE, HERE, HERE, HERE),
            [
                VMEM((2, n_row, block_size, width), jnp.bfloat16),
                VMEM(rows, jnp.float32),
                VMEM(rows, jnp.bfloat16),
                VMEM((lay.slots, block_size, block_size), jnp.bfloat16),
                DMA((lay.slots,)),
                DMA((piece_blocks,)),
            ],
            14,
            "last",
            cost(slot_count, piece_blocks),
        )
        return out.reshape(vectors.shape)

    q1 = after(q1, plan)
    first_sent, blocks = first_blocks(q1, packed)
    q2 = exchange(first_sent)
    second_sent = second_blocks(blocks, q2, first_sent, packed)
    q1_other = across(after(q1, second_sent))
    q2_other = across(after(q2, second_sent))
    (start,) = call(
        prime_kernel,
        [sums_shape],
        (after(vectors, second_sent),),
        (FAR,),
        [VMEM(vectors.shape, jnp.bfloat16), DMA],
        4,
        "prime",
        cost(0, 3 * piece_blocks),
    )
    base = early(q1, q1_other, q2, q2_other, start)
    q3 = after(exchange(second_sent), base)
    q3_other = across(q3)
    blocks, base = load(q3, base)
    return last(blocks, q3, q3_other, base)


def on_any(vectors, tile_blocks, block_rows, block_cols, counts):
    n_row = lax.axis_size("row")
    n_col = lax.axis_size("col")
    tile_data = tile_blocks[0, 0]
    slot_rows = block_rows[0, 0]
    slot_cols = block_cols[0, 0]
    used = counts[0, 0]
    block_size = tile_data.shape[-1]
    width = vectors.shape[1]
    piece_blocks = vectors.shape[0] // block_size
    row_blocks = piece_blocks * n_col
    slot_count = tile_data.shape[0]
    live = (jnp.arange(slot_count) < used).astype(jnp.float32)
    onehot = (slot_rows[None, :] == jnp.arange(row_blocks)[:, None]).astype(jnp.float32) * live[
        None, :
    ]
    source_piece = slot_cols // piece_blocks
    offset = slot_cols % piece_blocks
    needed = jnp.max(
        jnp.where(source_piece[None, :] == jnp.arange(n_row)[:, None], offset[None, :], 0), axis=1
    )
    wanted = lax.all_to_all(
        needed.reshape(n_row, 1), "row", split_axis=0, concat_axis=0, tiled=True
    ).reshape(n_row)

    def apply_tiles(current):
        own_blocks = current.reshape(piece_blocks, block_size, width)
        outgoing = jnp.take(own_blocks, wanted, axis=0)
        received = lax.all_to_all(outgoing, "row", split_axis=0, concat_axis=0, tiled=True)
        vec_blocks = jnp.take(received, source_piece, axis=0)
        products = jnp.einsum(
            "sij,sjk->sik", tile_data, vec_blocks, preferred_element_type=jnp.float32
        )
        term = jnp.einsum("ls,sik->lik", onehot, products, precision=lax.Precision.HIGHEST)
        term = term.reshape(row_blocks * block_size, width)
        return lax.psum_scatter(
            term.astype(jnp.bfloat16), "col", scatter_dimension=0, tiled=True
        ).astype(jnp.float32)

    previous = vectors
    applied = apply_tiles(vectors)
    current = ((applied - center_value * previous.astype(jnp.float32)) / half_width).astype(
        jnp.bfloat16
    )
    for repeat in range(DEGREE - 1):
        applied = apply_tiles(current)
        following = (
            2.0 * (applied - center_value * current.astype(jnp.float32)) / half_width
            - previous.astype(jnp.float32)
        ).astype(jnp.bfloat16)
        previous, current = (current, following)
    return current


def solution(mesh):
    n_row, n_col = mesh.shape["row"], mesh.shape["col"]
    paired = n_col == 2 and n_row & (n_row - 1) == 0
    return jax.shard_map(
        on_pair if paired else on_any,
        mesh=mesh,
        in_specs=(
            P(("row", "col"), "vec"),
            P("row", "col", None, None, None),
            P("row", "col", None),
            P("row", "col", None),
            P("row", "col"),
        ),
        out_specs=P(("row", "col"), "vec"),
        check_vma=False,
    )
```

```python
import functools
import typing

import jax
import jax.numpy as jnp
from jax import lax
from jax.experimental import pallas as pl
from jax.experimental.pallas import tpu as pltpu
from jax.sharding import PartitionSpec as P

DEGREE = 3

center_value = 0.5
half_width = 2.0

VMEM = pltpu.VMEM
SMEM = pltpu.SMEM
HBM = pltpu.HBM
DMA = pltpu.SemaphoreType.DMA
LANES = 128
FEW = 4
MANY = 4
HEAD = 8
STRIDE = 4
FIRST = 1
LAST = 2


def spec(space):
    return pl.BlockSpec(memory_space=space)


def params(mib):
    return pltpu.CompilerParams(vmem_limit_bytes=mib * 1024 * 1024)


def round_up(n, step):
    return (n + step - 1) // step * step


def core_number():
    return lax.axis_index("col")


class Layout(typing.NamedTuple):
    slots: int
    sends: int
    loads: int
    sent_at: int
    load_at: int
    bare_at: int
    size: int


def layout_for(slot_count, n_row, piece_blocks):
    slots = round_up(slot_count, MANY) + MANY
    sends = round_up(2 * n_row * n_row, FEW) + FEW
    sent_at = HEAD + STRIDE * 2 * slots
    load_at = sent_at + STRIDE * 2 * sends
    bare_at = load_at + 2 * (slot_count + 1)
    size = round_up(bare_at + piece_blocks, 8 * LANES)
    return Layout(slots, sends, slot_count + 1, sent_at, load_at, bare_at, size)


def plan_kernel(
    n_row,
    piece_blocks,
    lay,
    wanted_a,
    wanted_b,
    meta_a,
    meta_b,
    own,
    other,
    out,
    asked,
    seen,
    sems,
):
    slot_count = (meta_a.shape[0] - 1) // 2

    def put(at, *values):
        for i, value in enumerate(values):
            out[at + i] = value

    def scan(tile, meta):
        used = meta[2 * slot_count]


        def step(s, carry):
            ends, sent, load = carry
            row = meta[s]
            piece = meta[slot_count + s] // piece_blocks
            live = s < used
            half = row // piece_blocks
            local = row - half * piece_blocks
            lower = half == 0
            part = jnp.where(lower, tile, 1 - tile)
            at = HEAD + STRIDE * (part * lay.slots + jnp.where(lower, ends[0], ends[1]))
            base = half * lay.size
            put(base + at, s, local, piece)
            sought = jnp.where(live, local, -1)
            hits = [(asked[half * n_row + k] == sought).astype(jnp.int32) for k in range(n_row)]
            found = sum(hits)

            @pl.when(found > 0)
            def _():
                for core in range(2):
                    mine = tile if core == 0 else 1 - tile
                    side = half if core == 0 else 1 - half
                    first = core * lay.size
                    out[first + lay.load_at + mine * lay.loads + load] = s

                    place = sent
                    for k in range(n_row):
                        put(
                            first + lay.sent_at + STRIDE * (mine * lay.sends + place),
                            mine * lay.loads + load,
                            2 * k + side,
                            piece,
                            jnp.where(place == sent, FIRST, 0),
                        )
                        place = place + hits[k]

            one = live.astype(jnp.int32)
            ends = (ends[0] + jnp.where(lower, one, 0), ends[1] + jnp.where(lower, 0, one))
            return ends, sent + found, load + jnp.where(found > 0, 1, 0)

        zero = jnp.int32(0)
        ends, sent, load = lax.fori_loop(0, slot_count, step, ((zero, zero), zero, zero))
        for core in range(2):
            mine = tile if core == 0 else 1 - tile
            base = core * lay.size
            for i, (at, begin, end, unit, spare) in enumerate(
                (
                    (HEAD, mine * lay.slots, ends[core], MANY, piece_blocks),
                    (lay.sent_at, mine * lay.sends, sent, FEW, 2 * n_row),
                )
            ):
                for u in range(unit - 1):
                    put(base + at + STRIDE * (begin + end + u), 0, spare, 0, 0)
                out[base + 2 * i + mine] = begin + (end + unit - 1) // unit * unit
            out[base + 4 + mine] = mine * lay.loads + load

    def mark(core):
        base = core * lay.size
        for b in range(piece_blocks + 1):
            seen[b] = 0
        for part in range(2):

            @pl.loop(part * lay.slots, out[base + part])
            def _(i):
                entry = base + HEAD + STRIDE * i
                row = out[entry + 1]
                out[entry + 3] = jnp.where(seen[row] == 0, FIRST, 0)
                seen[row] = entry

        def close(b, bare):
            entry = seen[b]
            out[base + lay.bare_at + bare] = b

            @pl.when(entry > 0)
            def _():
                out[entry + 3] = out[entry + 3] + LAST

            return bare + jnp.where(entry == 0, 1, 0)

        out[base + 6] = lax.fori_loop(0, piece_blocks, close, jnp.int32(0))
        out[base + 7] = core

    @pl.when(core_number() == 0)
    def _():
        for half, wanted in enumerate((wanted_a, wanted_b)):
            for k in range(n_row):
                asked[half * n_row + k] = wanted[k, 0]
        scan(0, meta_a)
        scan(1, meta_b)
        for core in range(2):
            mark(core)
        copies = [
            pltpu.make_async_copy(out.at[pl.ds(core * lay.size, lay.size)], target, sems.at[core])
            for core, target in enumerate((own, other))
        ]
        for copy in copies:
            copy.start()
        for copy in copies:
            copy.wait()


def settle_kernel(own, handed, out, sem):
    for half, source in enumerate((own, handed)):

        @pl.when(core_number() == half)
        def _():
            copy = pltpu.make_async_copy(source, out, sem)
            copy.start()
            copy.wait()


def pick_kernel(n_row, block_size, wanted, vectors, out, sems):
    def fetch(k):
        at = pl.multiple_of(wanted[k, 0] * block_size, block_size)
        return pltpu.make_async_copy(vectors.at[pl.ds(at, block_size)], out.at[k], sems.at[k])

    for k in range(n_row):
        fetch(k).start()
    for k in range(n_row):
        fetch(k).wait()


def pack_kernel(picked, picked_b, out, held, sems):
    n_row, _, width = picked.shape
    middle = width // 2

    def put(k):
        return pltpu.make_async_copy(held.at[k], out.at[k], sems.at[k])

    for half in range(2):

        @pl.when(core_number() == half)
        def _():
            part = slice(half * middle, (half + 1) * middle)
            for k in range(n_row):
                held[k] = jnp.concatenate([picked[k, :, part], picked_b[k, :, part]], axis=1)
                put(k).start()

    for k in range(n_row):
        put(k).wait()


def fetches(plan, base, stride, ends, part, tiles, blocks, sems):
    def copy(tile, i):
        slot = plan[base + stride * i]
        return pltpu.make_async_copy(tile.at[slot], blocks.at[i], sems.at[i])

    def start():
        for side, tile in enumerate(tiles):

            @pl.loop(side * part, plan[ends + side])
            def _(i):
                copy(tile, i).start()

    def wait(i):
        copy(tiles[0], i).wait()

    return start, wait


def load_kernel(plan, tile_a, array, blocks, held, sems, held_sem):
    whole = pltpu.make_async_copy(array, held, held_sem)
    whole.start()
    start, wait = fetches(plan, HEAD, STRIDE, 0, 0, (tile_a,), blocks, sems)
    start()

    @pl.loop(0, plan[0])
    def _(i):
        wait(i)

    whole.wait()


def each_product(plan, base, ends, part, block_of, pieces, use, then=None, before=None):
    unroll = MANY if base == HEAD else FEW

    for side in range(2):

        @pl.loop(side * part // unroll, plan[ends + side] // unroll)
        def _(j):
            step = [(unroll * j + u, base + STRIDE * (unroll * j + u)) for u in range(unroll)]
            if before is not None:
                for i, entry in step:
                    before(side, i, entry)
            for i, entry in step:
                block = block_of(side, i, entry)
                piece = pieces[side][plan[entry + 2]]
                use(entry, jnp.dot(block, piece, preferred_element_type=jnp.float32))
            if then is not None:
                for i, entry in step:
                    then(entry)


def add_products(plan, base, ends, part, block_of, pieces, total, before=None):
    def use(entry, value):
        total[plan[entry + 1]] += value

    each_product(plan, base, ends, part, block_of, pieces, use, before=before)


def split_sides(pieces, vec):
    middle = vec.shape[-1] // 2
    column = lax.broadcasted_iota(jnp.int32, (1, vec.shape[-1]), 1)
    for side in range(2):
        keep = jnp.where((column // middle) == side, 1.0, 0.0).astype(jnp.bfloat16)
        for p in range(vec.shape[1]):
            vec[side, p] = pieces[p] * keep


def joined(total, k):
    one, two = total[2 * k], total[2 * k + 1]
    low = lax.broadcasted_iota(jnp.int32, one.shape, 1) < one.shape[1] // 2
    return jnp.where(low, one, two) + pltpu.roll(
        jnp.where(low, two, one), one.shape[1] // 2, axis=1
    )


def first_sent_kernel(
    lay, plan, tile_a, tile_b, pieces, start, out, blocks, vec, total, held, held_sem, sems
):
    n_row = out.shape[0]
    begin, wait = fetches(plan, lay.load_at, 1, 4, lay.loads, (tile_a, tile_b), blocks, sems)
    begin()
    copy = pltpu.make_async_copy(start, held, held_sem)
    copy.start()
    split_sides(pieces, vec)
    total[...] = jnp.zeros_like(total)

    def before(side, i, entry):
        @pl.when(plan[entry + 3] == FIRST)
        def _():
            wait(plan[entry])

    add_products(
        plan,
        lay.sent_at,
        2,
        lay.sends,
        lambda side, i, entry: blocks[plan[entry]],
        (vec.at[0], vec.at[1]),
        total,
        before,
    )
    copy.wait()
    for k in range(n_row):
        value = joined(total, k) - center_value * held[k].astype(jnp.float32)
        out[k] = (value / half_width).astype(jnp.bfloat16)


def second_sent_kernel(
    lay, plan, blocks, pieces, current, previous, out, vec, total, held, held_sem, ready, out_sems
):
    n_row = out.shape[0]
    copy = pltpu.make_async_copy(previous, held, held_sem)
    copy.start()
    split_sides(pieces, vec)
    total[...] = jnp.zeros_like(total)
    add_products(
        plan,
        lay.sent_at,
        2,
        lay.sends,
        lambda side, i, entry: blocks[plan[entry]],
        (vec.at[0], vec.at[1]),
        total,
    )
    copy.wait()

    def put(k):
        return pltpu.make_async_copy(ready.at[k], out.at[k], out_sems.at[k])

    for k in range(n_row):
        value = joined(total, k) - center_value * current[k].astype(jnp.float32)
        ready[k] = (value - held[k].astype(jnp.float32)).astype(jnp.bfloat16)
        put(k).start()
    for k in range(n_row):
        put(k).wait()


def whole_columns(half, mine, other, vec, at):
    n_row, _, width = mine.shape
    middle = width // 2

    @pl.when(half == 0)
    def _():
        for p in range(n_row):
            one, two = mine[p], other[p]
            vec[0, p, :, at : at + width] = jnp.concatenate([one[:, :middle], two[:, middle:]], axis=1)
            vec[1, p, :, at : at + width] = jnp.concatenate([one[:, middle:], two[:, :middle]], axis=1)

    @pl.when(half != 0)
    def _():
        for p in range(n_row):
            one, two = mine[p], other[p]
            vec[0, p, :, at : at + width] = jnp.concatenate([two[:, middle:], one[:, :middle]], axis=1)
            vec[1, p, :, at : at + width] = jnp.concatenate([two[:, :middle], one[:, middle:]], axis=1)


def prime_kernel(vectors, total, own, sem):
    _, block_size, double = total.shape
    width = double // 2
    copy = pltpu.make_async_copy(vectors, own, sem)
    copy.start()
    copy.wait()

    @pl.loop(0, vectors.shape[0] // block_size)
    def _(b):
        at = pl.ds(pl.multiple_of(b * block_size, block_size), block_size)
        value = own[at, :].astype(jnp.float32)
        total[b, :, :width] = -center_value * value
        total[b, :, width:] = -value


def early_kernel(
    lay,
    plan,
    tile_a,
    tile_b,
    q1,
    q1_other,
    q2,
    q2_other,
    start,
    base,
    total,
    vec,
    own,
    blocks,
    sems,
    row_sems,
):
    piece_blocks, block_size, width = base.shape
    begin, wait = fetches(plan, HEAD, STRIDE, 0, lay.slots, (tile_a, tile_b), blocks, sems)
    begin()
    whole_columns(plan[7], q1, q1_other, vec, 0)
    whole_columns(plan[7], q2, q2_other, vec, width)

    def rows(b):
        return pl.ds(pl.multiple_of(b * block_size, block_size), block_size)

    def put(b):
        return pltpu.make_async_copy(own.at[rows(b)], base.at[b], row_sems.at[b])

    add_products(
        plan,
        HEAD,
        0,
        lay.slots,
        lambda side, i, entry: blocks[i],
        (vec.at[0], vec.at[1]),
        total,
        lambda side, i, entry: wait(i),
    )

    @pl.loop(0, piece_blocks)
    def _(b):
        first = (total[b, :, :width] / half_width).astype(jnp.bfloat16).astype(jnp.float32)
        second = total[b, :, width:] - center_value * first
        second = second.astype(jnp.bfloat16).astype(jnp.float32)
        own[rows(b), :] = (-center_value * second - first).astype(jnp.bfloat16)
        put(b).start()

    @pl.loop(0, piece_blocks)
    def _(b):
        put(b).wait()


def last_kernel(
    lay, plan, blocks, tile_b, mine, other, base, out, vec, total, own, blocks_b, sems, row_sems
):
    piece_blocks = base.shape[0]
    begin = lay.slots

    def fetch(i):
        slot = plan[HEAD + STRIDE * i]
        return pltpu.make_async_copy(tile_b.at[slot], blocks_b.at[i - begin], sems.at[i - begin])

    @pl.loop(begin, plan[1])
    def _(i):
        fetch(i).start()

    def put(source, b):
        return pltpu.make_async_copy(source.at[b], out.at[b], row_sems.at[b])

    @pl.loop(0, plan[6])
    def _(i):
        b = plan[lay.bare_at + i]
        put(base, b).start()

    whole_columns(plan[7], mine, other, vec, 0)

    def use(entry, value):
        row = plan[entry + 1]
        marks = plan[entry + 3]
        start = base[jnp.minimum(row, piece_blocks - 1)].astype(jnp.float32)
        value = jnp.where(lax.rem(marks, LAST) == FIRST, start, total[row]) + value
        total[row] = value
        own[row] = value.astype(jnp.bfloat16)

    def then(entry):
        @pl.when(plan[entry + 3] >= LAST)
        def _():
            put(own, plan[entry + 1]).start()

    def block_of(side, i, entry):
        return blocks[i] if side == 0 else blocks_b[i - begin]

    def before(side, i, entry):
        if side == 1:
            fetch(i).wait()

    each_product(
        plan, HEAD, 0, lay.slots, block_of, (vec.at[0], vec.at[1]), use, then, before
    )

    @pl.loop(0, piece_blocks)
    def _(b):
        put(own, b).wait()


def after(value, *others):
    return lax.optimization_barrier((value, *others))[0]


def call(kernel, out, args, spaces, scratch, mib, name, estimate=None, aliases=None):
    args = [
        pltpu.with_memory_space_constraint(arg, space) if space in (VMEM, HBM) or tied else arg
        for arg, (space, tied) in zip(args, spaces)
    ]
    return pl.pallas_call(
        kernel,
        out_shape=[space(shape, dtype) for shape, dtype, space in out],
        in_specs=[spec(space) for space, _ in spaces],
        out_specs=[spec(space) for _, _, space in out],
        scratch_shapes=scratch,
        compiler_params=params(mib),
        cost_estimate=estimate,
        input_output_aliases=aliases or {},
        name=name,
    )(*args)


HERE = (VMEM, True)
FAR = (HBM, True)
LIST = (SMEM, True)
SCALARS = (SMEM, False)
ANYWHERE = (pl.ANY, False)


def on_pair(vectors, tile_blocks, block_rows, block_cols, counts):
    n_row = lax.axis_size("row")
    tile = tile_blocks[0, 0]
    slot_rows = block_rows[0, 0]
    slot_cols = block_cols[0, 0]
    used = counts[0]
    slot_count, block_size, _ = tile.shape
    width = vectors.shape[1]
    piece_blocks = vectors.shape[0] // block_size

    across = functools.partial(lax.ppermute, axis_name="col", perm=[(0, 1), (1, 0)])

    needed = jnp.max(
        jnp.where(
            slot_cols[None, :] // piece_blocks == jnp.arange(n_row)[:, None],
            slot_cols[None, :] % piece_blocks,
            0,
        ),
        axis=1,
        keepdims=True,
    )
    exchange = functools.partial(
        lax.all_to_all, axis_name="row", split_axis=0, concat_axis=0, tiled=True
    )
    wanted = exchange(jnp.broadcast_to(needed, (n_row, LANES)))
    sent_shape = (n_row, block_size, width)
    (sent,) = call(
        functools.partial(pick_kernel, n_row, block_size),
        [(sent_shape, jnp.bfloat16, VMEM)],
        (wanted, vectors),
        (SCALARS, FAR),
        [DMA((n_row,))],
        2,
        "pick",
    )
    tile_other = across(tile)
    sent_other = across(sent)
    wanted_other = across(after(wanted, sent))
    meta = jnp.concatenate([slot_rows, slot_cols, used])
    meta_other = across(after(meta, sent))
    packed = call(
        pack_kernel,
        [(sent_shape, jnp.bfloat16, HBM)],
        (sent, sent_other),
        (HERE, HERE),
        [VMEM(sent_shape, jnp.bfloat16), DMA((n_row,))],
        4,
        "pack",
    )[0]

    lay = layout_for(slot_count, n_row, piece_blocks)
    list_shape = ((lay.size,), jnp.int32)
    own_list, other_list = call(
        functools.partial(plan_kernel, n_row, piece_blocks, lay),
        [(*list_shape, HBM)] * 2,
        (wanted, after(wanted_other, packed), meta, meta_other),
        (SCALARS,) * 4,
        [
            SMEM((2 * lay.size,), jnp.int32),
            SMEM((2 * n_row,), jnp.int32),
            SMEM((piece_blocks + 1,), jnp.int32),
            DMA((2,)),
        ],
        2,
        "plan",
    )
    q1 = exchange(after(packed, own_list))
    plan = call(
        settle_kernel,
        [(*list_shape, SMEM)],
        (own_list, across(after(other_list, packed))),
        (ANYWHERE, ANYWHERE),
        [DMA],
        2,
        "settle",
    )[0]

    def load(cue, array):
        return call(
            load_kernel,
            [
                ((lay.slots, block_size, block_size), jnp.bfloat16, VMEM),
                (array.shape, array.dtype, VMEM),
            ],
            (after(plan, cue), tile, array),
            (LIST, FAR, FAR),
            [DMA((lay.slots,)), DMA],
            2,
            "load",
        )

    def cost(products, rows):
        size = block_size * width
        return pl.CostEstimate(
            flops=2 * products * block_size * size,
            bytes_accessed=2 * (products * block_size * block_size + 3 * rows * size),
            transcendentals=0,
        )

    sums = [
        VMEM((2, n_row, block_size, width), jnp.bfloat16),
        VMEM((2 * n_row + 1, block_size, width), jnp.float32),
    ]

    def first_blocks(*args):
        return call(
            functools.partial(first_sent_kernel, lay),
            [
                (sent_shape, jnp.bfloat16, VMEM),
                ((2 * lay.loads, block_size, block_size), jnp.bfloat16, VMEM),
            ],
            (plan, tile, tile_other, *args),
            (LIST, FAR, ANYWHERE, HERE, FAR),
            sums + [VMEM(sent_shape, jnp.bfloat16), DMA, DMA((2 * lay.loads,))],
            8,
            "sent",
            cost(n_row, n_row),
        )

    def second_blocks(*args):
        return call(
            functools.partial(second_sent_kernel, lay),
            [(sent_shape, jnp.bfloat16, HBM)],
            (plan, *args),
            (LIST, HERE, HERE, HERE, FAR),
            sums
            + [VMEM(sent_shape, jnp.bfloat16), DMA, VMEM(sent_shape, jnp.bfloat16), DMA((n_row,))],
            8,
            "sent",
            cost(n_row, n_row),
        )[0]

    base_shape = (piece_blocks, block_size, width)

    sums_shape = ((piece_blocks + 1, block_size, 2 * width), jnp.float32, VMEM)

    def early(*args):
        return call(
            functools.partial(early_kernel, lay),
            [(base_shape, jnp.bfloat16, HBM), sums_shape],
            (plan, tile, tile_other, *args),
            (LIST, FAR, ANYWHERE, HERE, HERE, HERE, HERE, HERE),
            [
                VMEM((2, n_row, block_size, 2 * width), jnp.bfloat16),
                VMEM(vectors.shape, jnp.bfloat16),
                VMEM((2 * lay.slots, block_size, block_size), jnp.bfloat16),
                DMA((2 * lay.slots,)),
                DMA((piece_blocks,)),
            ],
            18,
            "early",
            cost(2 * slot_count, 2 * piece_blocks),
            {7: 1},
        )[0]

    def last(blocks, *args):
        rows = (piece_blocks + 1, block_size, width)
        (out,) = call(
            functools.partial(last_kernel, lay),
            [(base_shape, jnp.bfloat16, HBM)],
            (plan, blocks, tile_other, *args),
            (LIST, HERE, ANYWHERE, HERE, HERE, HERE),
            [
                VMEM((2, n_row, block_size, width), jnp.bfloat16),
                VMEM(rows, jnp.float32),
                VMEM(rows, jnp.bfloat16),
                VMEM((lay.slots, block_size, block_size), jnp.bfloat16),
                DMA((lay.slots,)),
                DMA((piece_blocks,)),
            ],
            14,
            "last",
            cost(slot_count, piece_blocks),
        )
        return out.reshape(vectors.shape)

    q1 = after(q1, plan)
    first_sent, blocks = first_blocks(q1, packed)
    q2 = exchange(first_sent)
    second_sent = second_blocks(blocks, q2, first_sent, packed)
    q1_other = across(after(q1, second_sent))
    q2_other = across(after(q2, second_sent))
    (start,) = call(
        prime_kernel,
        [sums_shape],
        (after(vectors, second_sent),),
        (FAR,),
        [VMEM(vectors.shape, jnp.bfloat16), DMA],
        4,
        "prime",
        cost(0, 3 * piece_blocks),
    )
    base = early(q1, q1_other, q2, q2_other, start)
    q3 = after(exchange(second_sent), base)
    q3_other = across(q3)
    blocks, base = load(q3, base)
    return last(blocks, q3, q3_other, base)


def on_any(vectors, tile_blocks, block_rows, block_cols, counts):
    n_row = lax.axis_size("row")
    n_col = lax.axis_size("col")
    tile_data = tile_blocks[0, 0]
    slot_rows = block_rows[0, 0]
    slot_cols = block_cols[0, 0]
    used = counts[0, 0]
    block_size = tile_data.shape[-1]
    width = vectors.shape[1]
    piece_blocks = vectors.shape[0] // block_size
    row_blocks = piece_blocks * n_col
    slot_count = tile_data.shape[0]
    live = (jnp.arange(slot_count) < used).astype(jnp.float32)
    onehot = (slot_rows[None, :] == jnp.arange(row_blocks)[:, None]).astype(jnp.float32) * live[
        None, :
    ]
    source_piece = slot_cols // piece_blocks
    offset = slot_cols % piece_blocks
    needed = jnp.max(
        jnp.where(source_piece[None, :] == jnp.arange(n_row)[:, None], offset[None, :], 0), axis=1
    )
    wanted = lax.all_to_all(
        needed.reshape(n_row, 1), "row", split_axis=0, concat_axis=0, tiled=True
    ).reshape(n_row)

    def apply_tiles(current):
        own_blocks = current.reshape(piece_blocks, block_size, width)
        outgoing = jnp.take(own_blocks, wanted, axis=0)
        received = lax.all_to_all(outgoing, "row", split_axis=0, concat_axis=0, tiled=True)
        vec_blocks = jnp.take(received, source_piece, axis=0)
        products = jnp.einsum(
            "sij,sjk->sik", tile_data, vec_blocks, preferred_element_type=jnp.float32
        )
        term = jnp.einsum("ls,sik->lik", onehot, products, precision=lax.Precision.HIGHEST)
        term = term.reshape(row_blocks * block_size, width)
        return lax.psum_scatter(
            term.astype(jnp.bfloat16), "col", scatter_dimension=0, tiled=True
        ).astype(jnp.float32)

    previous = vectors
    applied = apply_tiles(vectors)
    current = ((applied - center_value * previous.astype(jnp.float32)) / half_width).astype(
        jnp.bfloat16
    )
    for repeat in range(DEGREE - 1):
        applied = apply_tiles(current)
        following = (
            2.0 * (applied - center_value * current.astype(jnp.float32)) / half_width
            - previous.astype(jnp.float32)
        ).astype(jnp.bfloat16)
        previous, current = (current, following)
    return current


def solution(mesh):
    n_row, n_col = mesh.shape["row"], mesh.shape["col"]
    paired = n_col == 2 and n_row & (n_row - 1) == 0
    return jax.shard_map(
        on_pair if paired else on_any,
        mesh=mesh,
        in_specs=(
            P(("row", "col"), "vec"),
            P("row", "col", None, None, None),
            P("row", "col", None),
            P("row", "col", None),
            P("row", "col"),
        ),
        out_specs=P(("row", "col"), "vec"),
        check_vma=False,
    )
```

```python
import functools
import typing

import jax
import jax.numpy as jnp
from jax import lax
from jax.experimental import pallas as pl
from jax.experimental.pallas import tpu as pltpu
from jax.sharding import PartitionSpec as P

DEGREE = 3

center_value = 0.5
half_width = 2.0

VMEM = pltpu.VMEM
SMEM = pltpu.SMEM
HBM = pltpu.HBM
DMA = pltpu.SemaphoreType.DMA
LANES = 128
FEW = 4
MANY = 4
HEAD = 8
STRIDE = 4
FIRST = 1
LAST = 2


def spec(space):
    return pl.BlockSpec(memory_space=space)


def params(mib):
    return pltpu.CompilerParams(vmem_limit_bytes=mib * 1024 * 1024)


def round_up(n, step):
    return (n + step - 1) // step * step


def core_number():
    return lax.axis_index("col")


class Layout(typing.NamedTuple):
    slots: int
    sends: int
    loads: int
    sent_at: int
    load_at: int
    bare_at: int
    size: int


def layout_for(slot_count, n_row, piece_blocks):
    slots = round_up(slot_count, MANY) + MANY
    sends = round_up(2 * n_row * n_row, FEW) + FEW
    sent_at = HEAD + STRIDE * 2 * slots
    load_at = sent_at + STRIDE * 2 * sends
    bare_at = load_at + 2 * (slot_count + 1)
    size = round_up(bare_at + piece_blocks, 8 * LANES)
    return Layout(slots, sends, slot_count + 1, sent_at, load_at, bare_at, size)


def plan_kernel(
    n_row,
    piece_blocks,
    lay,
    wanted_a,
    wanted_b,
    meta_a,
    meta_b,
    own,
    other,
    out,
    asked,
    seen,
    sems,
):
    slot_count = (meta_a.shape[0] - 1) // 2

    def put(at, *values):
        for i, value in enumerate(values):
            out[at + i] = value

    def scan(tile, meta):
        used = meta[2 * slot_count]


        def step(s, carry):
            ends, sent, load = carry
            row = meta[s]
            piece = meta[slot_count + s] // piece_blocks
            live = s < used
            half = row // piece_blocks
            local = row - half * piece_blocks
            lower = half == 0
            part = jnp.where(lower, tile, 1 - tile)
            at = HEAD + STRIDE * (part * lay.slots + jnp.where(lower, ends[0], ends[1]))
            base = half * lay.size
            put(base + at, s, local, piece)
            sought = jnp.where(live, local, -1)
            hits = [(asked[half * n_row + k] == sought).astype(jnp.int32) for k in range(n_row)]
            found = sum(hits)

            @pl.when(found > 0)
            def _():
                for core in range(2):
                    mine = tile if core == 0 else 1 - tile
                    side = half if core == 0 else 1 - half
                    first = core * lay.size
                    out[first + lay.load_at + mine * lay.loads + load] = s

                    place = sent
                    for k in range(n_row):
                        put(
                            first + lay.sent_at + STRIDE * (mine * lay.sends + place),
                            mine * lay.loads + load,
                            2 * k + side,
                            piece,
                            jnp.where(place == sent, FIRST, 0),
                        )
                        place = place + hits[k]

            one = live.astype(jnp.int32)
            ends = (ends[0] + jnp.where(lower, one, 0), ends[1] + jnp.where(lower, 0, one))
            return ends, sent + found, load + jnp.where(found > 0, 1, 0)

        zero = jnp.int32(0)
        ends, sent, load = lax.fori_loop(0, slot_count, step, ((zero, zero), zero, zero))
        for core in range(2):
            mine = tile if core == 0 else 1 - tile
            base = core * lay.size
            for i, (at, begin, end, unit, spare) in enumerate(
                (
                    (HEAD, mine * lay.slots, ends[core], MANY, piece_blocks),
                    (lay.sent_at, mine * lay.sends, sent, FEW, 2 * n_row),
                )
            ):
                for u in range(unit - 1):
                    put(base + at + STRIDE * (begin + end + u), 0, spare, 0, 0)
                out[base + 2 * i + mine] = begin + (end + unit - 1) // unit * unit
            out[base + 4 + mine] = mine * lay.loads + load

    def mark(core):
        base = core * lay.size
        for b in range(piece_blocks + 1):
            seen[b] = 0
        for part in range(2):

            @pl.loop(part * lay.slots, out[base + part])
            def _(i):
                entry = base + HEAD + STRIDE * i
                row = out[entry + 1]
                out[entry + 3] = jnp.where(seen[row] == 0, FIRST, 0)
                seen[row] = entry

        def close(b, bare):
            entry = seen[b]
            out[base + lay.bare_at + bare] = b

            @pl.when(entry > 0)
            def _():
                out[entry + 3] = out[entry + 3] + LAST

            return bare + jnp.where(entry == 0, 1, 0)

        out[base + 6] = lax.fori_loop(0, piece_blocks, close, jnp.int32(0))
        out[base + 7] = core

    @pl.when(core_number() == 0)
    def _():
        for half, wanted in enumerate((wanted_a, wanted_b)):
            for k in range(n_row):
                asked[half * n_row + k] = wanted[k, 0]
        scan(0, meta_a)
        scan(1, meta_b)
        for core in range(2):
            mark(core)
        copies = [
            pltpu.make_async_copy(out.at[pl.ds(core * lay.size, lay.size)], target, sems.at[core])
            for core, target in enumerate((own, other))
        ]
        for copy in copies:
            copy.start()
        for copy in copies:
            copy.wait()


def settle_kernel(own, handed, out, sem):
    for half, source in enumerate((own, handed)):

        @pl.when(core_number() == half)
        def _():
            copy = pltpu.make_async_copy(source, out, sem)
            copy.start()
            copy.wait()


def pick_kernel(n_row, block_size, wanted, vectors, out, sems):
    def fetch(k):
        at = pl.multiple_of(wanted[k, 0] * block_size, block_size)
        return pltpu.make_async_copy(vectors.at[pl.ds(at, block_size)], out.at[k], sems.at[k])

    for k in range(n_row):
        fetch(k).start()
    for k in range(n_row):
        fetch(k).wait()


def pack_kernel(picked, picked_b, out, held, sems):
    n_row, _, width = picked.shape
    middle = width // 2

    def put(k):
        return pltpu.make_async_copy(held.at[k], out.at[k], sems.at[k])

    for half in range(2):

        @pl.when(core_number() == half)
        def _():
            part = slice(half * middle, (half + 1) * middle)
            for k in range(n_row):
                held[k] = jnp.concatenate([picked[k, :, part], picked_b[k, :, part]], axis=1)
                put(k).start()

    for k in range(n_row):
        put(k).wait()


def fetches(plan, base, stride, ends, part, tiles, blocks, sems):
    def copy(tile, i):
        slot = plan[base + stride * i]
        return pltpu.make_async_copy(tile.at[slot], blocks.at[i], sems.at[i])

    def start():
        for side, tile in enumerate(tiles):

            @pl.loop(side * part, plan[ends + side])
            def _(i):
                copy(tile, i).start()

    def wait(i):
        copy(tiles[0], i).wait()

    return start, wait


def hold_kernel(array, held, sem):
    copy = pltpu.make_async_copy(array, held, sem)
    copy.start()
    copy.wait()


def load_kernel(plan, tile_a, blocks, sems):
    start, wait = fetches(plan, HEAD, STRIDE, 0, 0, (tile_a,), blocks, sems)
    start()

    @pl.loop(0, plan[0])
    def _(i):
        wait(i)


def each_product(plan, base, ends, part, block_of, pieces, use, then=None, before=None):
    unroll = MANY if base == HEAD else FEW

    for side in range(2):

        @pl.loop(side * part // unroll, plan[ends + side] // unroll)
        def _(j):
            step = [(unroll * j + u, base + STRIDE * (unroll * j + u)) for u in range(unroll)]
            if before is not None:
                for i, entry in step:
                    before(side, i, entry)
            for i, entry in step:
                block = block_of(side, i, entry)
                piece = pieces[side][plan[entry + 2]]
                use(entry, jnp.dot(block, piece, preferred_element_type=jnp.float32))
            if then is not None:
                for i, entry in step:
                    then(entry)


def add_products(plan, base, ends, part, block_of, pieces, total, before=None):
    def use(entry, value):
        total[plan[entry + 1]] += value

    each_product(plan, base, ends, part, block_of, pieces, use, before=before)


def split_sides(pieces, vec):
    middle = vec.shape[-1] // 2
    column = lax.broadcasted_iota(jnp.int32, (1, vec.shape[-1]), 1)
    for side in range(2):
        keep = jnp.where((column // middle) == side, 1.0, 0.0).astype(jnp.bfloat16)
        for p in range(vec.shape[1]):
            vec[side, p] = pieces[p] * keep


def joined(total, k):
    one, two = total[2 * k], total[2 * k + 1]
    low = lax.broadcasted_iota(jnp.int32, one.shape, 1) < one.shape[1] // 2
    return jnp.where(low, one, two) + pltpu.roll(
        jnp.where(low, two, one), one.shape[1] // 2, axis=1
    )


def first_sent_kernel(
    lay, plan, tile_a, tile_b, pieces, start, out, blocks, vec, total, held, held_sem, sems
):
    n_row = out.shape[0]
    begin, wait = fetches(plan, lay.load_at, 1, 4, lay.loads, (tile_a, tile_b), blocks, sems)
    begin()
    copy = pltpu.make_async_copy(start, held, held_sem)
    copy.start()
    split_sides(pieces, vec)
    total[...] = jnp.zeros_like(total)

    def before(side, i, entry):
        @pl.when(plan[entry + 3] == FIRST)
        def _():
            wait(plan[entry])

    add_products(
        plan,
        lay.sent_at,
        2,
        lay.sends,
        lambda side, i, entry: blocks[plan[entry]],
        (vec.at[0], vec.at[1]),
        total,
        before,
    )
    copy.wait()
    for k in range(n_row):
        value = joined(total, k) - center_value * held[k].astype(jnp.float32)
        out[k] = (value / half_width).astype(jnp.bfloat16)


def second_sent_kernel(
    lay, plan, blocks, pieces, current, previous, out, vec, total, held, held_sem, ready, out_sems
):
    n_row = out.shape[0]
    copy = pltpu.make_async_copy(previous, held, held_sem)
    copy.start()
    split_sides(pieces, vec)
    total[...] = jnp.zeros_like(total)
    add_products(
        plan,
        lay.sent_at,
        2,
        lay.sends,
        lambda side, i, entry: blocks[plan[entry]],
        (vec.at[0], vec.at[1]),
        total,
    )
    copy.wait()

    def put(k):
        return pltpu.make_async_copy(ready.at[k], out.at[k], out_sems.at[k])

    for k in range(n_row):
        value = joined(total, k) - center_value * current[k].astype(jnp.float32)
        ready[k] = (value - held[k].astype(jnp.float32)).astype(jnp.bfloat16)
        put(k).start()
    for k in range(n_row):
        put(k).wait()


def whole_columns(half, mine, other, vec, at):
    n_row, _, width = mine.shape
    middle = width // 2

    @pl.when(half == 0)
    def _():
        for p in range(n_row):
            one, two = mine[p], other[p]
            vec[0, p, :, at : at + width] = jnp.concatenate([one[:, :middle], two[:, middle:]], axis=1)
            vec[1, p, :, at : at + width] = jnp.concatenate([one[:, middle:], two[:, :middle]], axis=1)

    @pl.when(half != 0)
    def _():
        for p in range(n_row):
            one, two = mine[p], other[p]
            vec[0, p, :, at : at + width] = jnp.concatenate([two[:, middle:], one[:, :middle]], axis=1)
            vec[1, p, :, at : at + width] = jnp.concatenate([two[:, :middle], one[:, middle:]], axis=1)


def prime_kernel(vectors, total, own, sem):
    _, block_size, double = total.shape
    width = double // 2
    copy = pltpu.make_async_copy(vectors, own, sem)
    copy.start()
    copy.wait()

    @pl.loop(0, vectors.shape[0] // block_size)
    def _(b):
        at = pl.ds(pl.multiple_of(b * block_size, block_size), block_size)
        value = own[at, :].astype(jnp.float32)
        total[b, :, :width] = -center_value * value
        total[b, :, width:] = -value


def early_kernel(
    lay,
    plan,
    tile_a,
    tile_b,
    q1,
    q1_other,
    q2,
    q2_other,
    start,
    base,
    total,
    vec,
    own,
    blocks,
    sems,
    row_sems,
):
    piece_blocks, block_size, width = base.shape
    begin, wait = fetches(plan, HEAD, STRIDE, 0, lay.slots, (tile_a, tile_b), blocks, sems)
    begin()
    whole_columns(plan[7], q1, q1_other, vec, 0)
    whole_columns(plan[7], q2, q2_other, vec, width)

    def rows(b):
        return pl.ds(pl.multiple_of(b * block_size, block_size), block_size)

    def put(b):
        return pltpu.make_async_copy(own.at[rows(b)], base.at[b], row_sems.at[b])

    add_products(
        plan,
        HEAD,
        0,
        lay.slots,
        lambda side, i, entry: blocks[i],
        (vec.at[0], vec.at[1]),
        total,
        lambda side, i, entry: wait(i),
    )

    @pl.loop(0, piece_blocks)
    def _(b):
        first = (total[b, :, :width] / half_width).astype(jnp.bfloat16).astype(jnp.float32)
        second = total[b, :, width:] - center_value * first
        second = second.astype(jnp.bfloat16).astype(jnp.float32)
        own[rows(b), :] = (-center_value * second - first).astype(jnp.bfloat16)
        put(b).start()

    @pl.loop(0, piece_blocks)
    def _(b):
        put(b).wait()


def last_kernel(
    lay, plan, blocks, tile_b, mine, other, base, out, vec, total, own, blocks_b, sems, row_sems
):
    piece_blocks = base.shape[0]
    begin = lay.slots

    def fetch(i):
        slot = plan[HEAD + STRIDE * i]
        return pltpu.make_async_copy(tile_b.at[slot], blocks_b.at[i - begin], sems.at[i - begin])

    @pl.loop(begin, plan[1])
    def _(i):
        fetch(i).start()

    def put(source, b):
        return pltpu.make_async_copy(source.at[b], out.at[b], row_sems.at[b])

    @pl.loop(0, plan[6])
    def _(i):
        b = plan[lay.bare_at + i]
        put(base, b).start()

    whole_columns(plan[7], mine, other, vec, 0)

    def use(entry, value):
        row = plan[entry + 1]
        marks = plan[entry + 3]
        start = base[jnp.minimum(row, piece_blocks - 1)].astype(jnp.float32)
        value = jnp.where(lax.rem(marks, LAST) == FIRST, start, total[row]) + value
        total[row] = value
        own[row] = value.astype(jnp.bfloat16)

    def then(entry):
        @pl.when(plan[entry + 3] >= LAST)
        def _():
            put(own, plan[entry + 1]).start()

    def block_of(side, i, entry):
        return blocks[i] if side == 0 else blocks_b[i - begin]

    def before(side, i, entry):
        if side == 1:
            fetch(i).wait()

    each_product(
        plan, HEAD, 0, lay.slots, block_of, (vec.at[0], vec.at[1]), use, then, before
    )

    @pl.loop(0, piece_blocks)
    def _(b):
        put(own, b).wait()


def after(value, *others):
    return lax.optimization_barrier((value, *others))[0]


def call(kernel, out, args, spaces, scratch, mib, name, estimate=None, aliases=None):
    args = [
        pltpu.with_memory_space_constraint(arg, space) if space in (VMEM, HBM) or tied else arg
        for arg, (space, tied) in zip(args, spaces)
    ]
    return pl.pallas_call(
        kernel,
        out_shape=[space(shape, dtype) for shape, dtype, space in out],
        in_specs=[spec(space) for space, _ in spaces],
        out_specs=[spec(space) for _, _, space in out],
        scratch_shapes=scratch,
        compiler_params=params(mib),
        cost_estimate=estimate,
        input_output_aliases=aliases or {},
        name=name,
    )(*args)


HERE = (VMEM, True)
FAR = (HBM, True)
LIST = (SMEM, True)
SCALARS = (SMEM, False)
ANYWHERE = (pl.ANY, False)


def on_pair(vectors, tile_blocks, block_rows, block_cols, counts):
    n_row = lax.axis_size("row")
    tile = tile_blocks[0, 0]
    slot_rows = block_rows[0, 0]
    slot_cols = block_cols[0, 0]
    used = counts[0]
    slot_count, block_size, _ = tile.shape
    width = vectors.shape[1]
    piece_blocks = vectors.shape[0] // block_size

    across = functools.partial(lax.ppermute, axis_name="col", perm=[(0, 1), (1, 0)])

    needed = jnp.max(
        jnp.where(
            slot_cols[None, :] // piece_blocks == jnp.arange(n_row)[:, None],
            slot_cols[None, :] % piece_blocks,
            0,
        ),
        axis=1,
        keepdims=True,
    )
    exchange = functools.partial(
        lax.all_to_all, axis_name="row", split_axis=0, concat_axis=0, tiled=True
    )
    wanted = exchange(jnp.broadcast_to(needed, (n_row, LANES)))
    sent_shape = (n_row, block_size, width)
    (sent,) = call(
        functools.partial(pick_kernel, n_row, block_size),
        [(sent_shape, jnp.bfloat16, VMEM)],
        (wanted, vectors),
        (SCALARS, FAR),
        [DMA((n_row,))],
        2,
        "pick",
    )
    tile_other = across(tile)
    sent_other = across(sent)
    wanted_other = across(after(wanted, sent))
    meta = jnp.concatenate([slot_rows, slot_cols, used])
    meta_other = across(after(meta, sent))
    packed = call(
        pack_kernel,
        [(sent_shape, jnp.bfloat16, HBM)],
        (sent, sent_other),
        (HERE, HERE),
        [VMEM(sent_shape, jnp.bfloat16), DMA((n_row,))],
        4,
        "pack",
    )[0]

    lay = layout_for(slot_count, n_row, piece_blocks)
    list_shape = ((lay.size,), jnp.int32)
    own_list, other_list = call(
        functools.partial(plan_kernel, n_row, piece_blocks, lay),
        [(*list_shape, HBM)] * 2,
        (wanted, after(wanted_other, packed), meta, meta_other),
        (SCALARS,) * 4,
        [
            SMEM((2 * lay.size,), jnp.int32),
            SMEM((2 * n_row,), jnp.int32),
            SMEM((piece_blocks + 1,), jnp.int32),
            DMA((2,)),
        ],
        2,
        "plan",
    )
    q1 = exchange(after(packed, own_list))
    plan = call(
        settle_kernel,
        [(*list_shape, SMEM)],
        (own_list, across(after(other_list, packed))),
        (ANYWHERE, ANYWHERE),
        [DMA],
        2,
        "settle",
    )[0]

    def load(cue):
        return call(
            load_kernel,
            [((lay.slots, block_size, block_size), jnp.bfloat16, VMEM)],
            (after(plan, cue), tile),
            (LIST, FAR),
            [DMA((lay.slots,))],
            2,
            "load",
        )[0]

    def cost(products, rows):
        size = block_size * width
        return pl.CostEstimate(
            flops=2 * products * block_size * size,
            bytes_accessed=2 * (products * block_size * block_size + 3 * rows * size),
            transcendentals=0,
        )

    sums = [
        VMEM((2, n_row, block_size, width), jnp.bfloat16),
        VMEM((2 * n_row + 1, block_size, width), jnp.float32),
    ]

    def first_blocks(*args):
        return call(
            functools.partial(first_sent_kernel, lay),
            [
                (sent_shape, jnp.bfloat16, VMEM),
                ((2 * lay.loads, block_size, block_size), jnp.bfloat16, VMEM),
            ],
            (plan, tile, tile_other, *args),
            (LIST, FAR, ANYWHERE, HERE, FAR),
            sums + [VMEM(sent_shape, jnp.bfloat16), DMA, DMA((2 * lay.loads,))],
            8,
            "sent",
            cost(n_row, n_row),
        )

    def second_blocks(*args):
        return call(
            functools.partial(second_sent_kernel, lay),
            [(sent_shape, jnp.bfloat16, HBM)],
            (plan, *args),
            (LIST, HERE, HERE, HERE, FAR),
            sums
            + [VMEM(sent_shape, jnp.bfloat16), DMA, VMEM(sent_shape, jnp.bfloat16), DMA((n_row,))],
            8,
            "sent",
            cost(n_row, n_row),
        )[0]

    base_shape = (piece_blocks, block_size, width)

    sums_shape = ((piece_blocks + 1, block_size, 2 * width), jnp.float32, VMEM)

    def early(*args):
        return call(
            functools.partial(early_kernel, lay),
            [(base_shape, jnp.bfloat16, HBM), sums_shape],
            (plan, tile, tile_other, *args),
            (LIST, FAR, ANYWHERE, HERE, HERE, HERE, HERE, HERE),
            [
                VMEM((2, n_row, block_size, 2 * width), jnp.bfloat16),
                VMEM(vectors.shape, jnp.bfloat16),
                VMEM((2 * lay.slots, block_size, block_size), jnp.bfloat16),
                DMA((2 * lay.slots,)),
                DMA((piece_blocks,)),
            ],
            18,
            "early",
            cost(2 * slot_count, 2 * piece_blocks),
            {7: 1},
        )[0]

    def last(blocks, *args):
        rows = (piece_blocks + 1, block_size, width)
        (out,) = call(
            functools.partial(last_kernel, lay),
            [(base_shape, jnp.bfloat16, HBM)],
            (plan, blocks, tile_other, *args),
            (LIST, HERE, ANYWHERE, HERE, HERE, HERE),
            [
                VMEM((2, n_row, block_size, width), jnp.bfloat16),
                VMEM(rows, jnp.float32),
                VMEM(rows, jnp.bfloat16),
                VMEM((lay.slots, block_size, block_size), jnp.bfloat16),
                DMA((lay.slots,)),
                DMA((piece_blocks,)),
            ],
            14,
            "last",
            cost(slot_count, piece_blocks),
        )
        return out.reshape(vectors.shape)

    q1 = after(q1, plan)
    first_sent, blocks = first_blocks(q1, packed)
    q2 = exchange(first_sent)
    second_sent = second_blocks(blocks, q2, first_sent, packed)
    q1_other = across(after(q1, second_sent))
    q2_other = across(after(q2, second_sent))
    (start,) = call(
        prime_kernel,
        [sums_shape],
        (after(vectors, second_sent),),
        (FAR,),
        [VMEM(vectors.shape, jnp.bfloat16), DMA],
        4,
        "prime",
        cost(0, 3 * piece_blocks),
    )
    base = early(q1, q1_other, q2, q2_other, start)
    base = call(hold_kernel, [(base.shape, base.dtype, VMEM)], (base,), (FAR,), [DMA], 2, "hold")[0]
    q3 = after(exchange(second_sent), base)
    q3_other = across(q3)
    return last(load(q3), q3, q3_other, base)


def on_any(vectors, tile_blocks, block_rows, block_cols, counts):
    n_row = lax.axis_size("row")
    n_col = lax.axis_size("col")
    tile_data = tile_blocks[0, 0]
    slot_rows = block_rows[0, 0]
    slot_cols = block_cols[0, 0]
    used = counts[0, 0]
    block_size = tile_data.shape[-1]
    width = vectors.shape[1]
    piece_blocks = vectors.shape[0] // block_size
    row_blocks = piece_blocks * n_col
    slot_count = tile_data.shape[0]
    live = (jnp.arange(slot_count) < used).astype(jnp.float32)
    onehot = (slot_rows[None, :] == jnp.arange(row_blocks)[:, None]).astype(jnp.float32) * live[
        None, :
    ]
    source_piece = slot_cols // piece_blocks
    offset = slot_cols % piece_blocks
    needed = jnp.max(
        jnp.where(source_piece[None, :] == jnp.arange(n_row)[:, None], offset[None, :], 0), axis=1
    )
    wanted = lax.all_to_all(
        needed.reshape(n_row, 1), "row", split_axis=0, concat_axis=0, tiled=True
    ).reshape(n_row)

    def apply_tiles(current):
        own_blocks = current.reshape(piece_blocks, block_size, width)
        outgoing = jnp.take(own_blocks, wanted, axis=0)
        received = lax.all_to_all(outgoing, "row", split_axis=0, concat_axis=0, tiled=True)
        vec_blocks = jnp.take(received, source_piece, axis=0)
        products = jnp.einsum(
            "sij,sjk->sik", tile_data, vec_blocks, preferred_element_type=jnp.float32
        )
        term = jnp.einsum("ls,sik->lik", onehot, products, precision=lax.Precision.HIGHEST)
        term = term.reshape(row_blocks * block_size, width)
        return lax.psum_scatter(
            term.astype(jnp.bfloat16), "col", scatter_dimension=0, tiled=True
        ).astype(jnp.float32)

    previous = vectors
    applied = apply_tiles(vectors)
    current = ((applied - center_value * previous.astype(jnp.float32)) / half_width).astype(
        jnp.bfloat16
    )
    for repeat in range(DEGREE - 1):
        applied = apply_tiles(current)
        following = (
            2.0 * (applied - center_value * current.astype(jnp.float32)) / half_width
            - previous.astype(jnp.float32)
        ).astype(jnp.bfloat16)
        previous, current = (current, following)
    return current


def solution(mesh):
    n_row, n_col = mesh.shape["row"], mesh.shape["col"]
    paired = n_col == 2 and n_row & (n_row - 1) == 0
    return jax.shard_map(
        on_pair if paired else on_any,
        mesh=mesh,
        in_specs=(
            P(("row", "col"), "vec"),
            P("row", "col", None, None, None),
            P("row", "col", None),
            P("row", "col", None),
            P("row", "col"),
        ),
        out_specs=P(("row", "col"), "vec"),
        check_vma=False,
    )
```

```python
import functools
import typing

import jax
import jax.numpy as jnp
from jax import lax
from jax.experimental import pallas as pl
from jax.experimental.pallas import tpu as pltpu
from jax.sharding import PartitionSpec as P

DEGREE = 3

center_value = 0.5
half_width = 2.0

VMEM = pltpu.VMEM
SMEM = pltpu.SMEM
HBM = pltpu.HBM
DMA = pltpu.SemaphoreType.DMA
LANES = 128
FEW = 4
MANY = 4
AHEAD = 8
HEAD = 8
STRIDE = 4
FIRST = 1
LAST = 2


def spec(space):
    return pl.BlockSpec(memory_space=space)


def params(mib):
    return pltpu.CompilerParams(vmem_limit_bytes=mib * 1024 * 1024)


def round_up(n, step):
    return (n + step - 1) // step * step


def core_number():
    return lax.axis_index("col")


class Layout(typing.NamedTuple):
    slots: int
    sends: int
    loads: int
    sent_at: int
    load_at: int
    bare_at: int
    size: int


def layout_for(slot_count, n_row, piece_blocks):
    slots = round_up(slot_count, MANY) + MANY
    sends = round_up(2 * n_row * n_row, FEW) + FEW
    sent_at = HEAD + STRIDE * 2 * slots
    load_at = sent_at + STRIDE * 2 * sends
    bare_at = load_at + 2 * (slot_count + 1)
    size = round_up(bare_at + piece_blocks, 8 * LANES)
    return Layout(slots, sends, slot_count + 1, sent_at, load_at, bare_at, size)


def plan_kernel(
    n_row,
    piece_blocks,
    lay,
    wanted_a,
    wanted_b,
    meta_a,
    meta_b,
    own,
    other,
    out,
    asked,
    seen,
    sems,
):
    slot_count = (meta_a.shape[0] - 1) // 2

    def put(at, *values):
        for i, value in enumerate(values):
            out[at + i] = value

    def scan(tile, meta):
        used = meta[2 * slot_count]


        def step(s, carry):
            ends, sent, load = carry
            row = meta[s]
            piece = meta[slot_count + s] // piece_blocks
            live = s < used
            half = row // piece_blocks
            local = row - half * piece_blocks
            lower = half == 0
            part = jnp.where(lower, tile, 1 - tile)
            at = HEAD + STRIDE * (part * lay.slots + jnp.where(lower, ends[0], ends[1]))
            base = half * lay.size
            put(base + at, s, local, piece)
            sought = jnp.where(live, local, -1)
            hits = [(asked[half * n_row + k] == sought).astype(jnp.int32) for k in range(n_row)]
            found = sum(hits)

            @pl.when(found > 0)
            def _():
                for core in range(2):
                    mine = tile if core == 0 else 1 - tile
                    side = half if core == 0 else 1 - half
                    first = core * lay.size
                    out[first + lay.load_at + mine * lay.loads + load] = s

                    place = sent
                    for k in range(n_row):
                        put(
                            first + lay.sent_at + STRIDE * (mine * lay.sends + place),
                            mine * lay.loads + load,
                            2 * k + side,
                            piece,
                            jnp.where(place == sent, FIRST, 0),
                        )
                        place = place + hits[k]

            one = live.astype(jnp.int32)
            ends = (ends[0] + jnp.where(lower, one, 0), ends[1] + jnp.where(lower, 0, one))
            return ends, sent + found, load + jnp.where(found > 0, 1, 0)

        zero = jnp.int32(0)
        ends, sent, load = lax.fori_loop(0, slot_count, step, ((zero, zero), zero, zero))
        for core in range(2):
            mine = tile if core == 0 else 1 - tile
            base = core * lay.size
            for i, (at, begin, end, unit, spare) in enumerate(
                (
                    (HEAD, mine * lay.slots, ends[core], MANY, piece_blocks),
                    (lay.sent_at, mine * lay.sends, sent, FEW, 2 * n_row),
                )
            ):
                for u in range(unit - 1):
                    put(base + at + STRIDE * (begin + end + u), 0, spare, 0, 0)
                out[base + 2 * i + mine] = begin + (end + unit - 1) // unit * unit
            out[base + 4 + mine] = mine * lay.loads + load

    def mark(core):
        base = core * lay.size
        for b in range(piece_blocks + 1):
            seen[b] = 0
        for part in range(2):

            @pl.loop(part * lay.slots, out[base + part])
            def _(i):
                entry = base + HEAD + STRIDE * i
                row = out[entry + 1]
                out[entry + 3] = jnp.where(seen[row] == 0, FIRST, 0)
                seen[row] = entry

        def close(b, bare):
            entry = seen[b]
            out[base + lay.bare_at + bare] = b

            @pl.when(entry > 0)
            def _():
                out[entry + 3] = out[entry + 3] + LAST

            return bare + jnp.where(entry == 0, 1, 0)

        out[base + 6] = lax.fori_loop(0, piece_blocks, close, jnp.int32(0))
        out[base + 7] = core

    @pl.when(core_number() == 0)
    def _():
        for half, wanted in enumerate((wanted_a, wanted_b)):
            for k in range(n_row):
                asked[half * n_row + k] = wanted[k, 0]
        scan(0, meta_a)
        scan(1, meta_b)
        for core in range(2):
            mark(core)
        copies = [
            pltpu.make_async_copy(out.at[pl.ds(core * lay.size, lay.size)], target, sems.at[core])
            for core, target in enumerate((own, other))
        ]
        for copy in copies:
            copy.start()
        for copy in copies:
            copy.wait()


def settle_kernel(own, handed, out, sem):
    for half, source in enumerate((own, handed)):

        @pl.when(core_number() == half)
        def _():
            copy = pltpu.make_async_copy(source, out, sem)
            copy.start()
            copy.wait()


def pick_kernel(n_row, block_size, wanted, vectors, out, sems):
    def fetch(k):
        at = pl.multiple_of(wanted[k, 0] * block_size, block_size)
        return pltpu.make_async_copy(vectors.at[pl.ds(at, block_size)], out.at[k], sems.at[k])

    for k in range(n_row):
        fetch(k).start()
    for k in range(n_row):
        fetch(k).wait()


def pack_kernel(picked, picked_b, out, held, sems):
    n_row, _, width = picked.shape
    middle = width // 2

    def put(k):
        return pltpu.make_async_copy(held.at[k], out.at[k], sems.at[k])

    for half in range(2):

        @pl.when(core_number() == half)
        def _():
            part = slice(half * middle, (half + 1) * middle)
            for k in range(n_row):
                held[k] = jnp.concatenate([picked[k, :, part], picked_b[k, :, part]], axis=1)
                put(k).start()

    for k in range(n_row):
        put(k).wait()


def fetches(plan, base, stride, ends, part, tiles, blocks, sems):
    def copy(tile, i):
        slot = plan[base + stride * i]
        return pltpu.make_async_copy(tile.at[slot], blocks.at[i], sems.at[i])

    def start():
        for side, tile in enumerate(tiles):

            @pl.loop(side * part, plan[ends + side])
            def _(i):
                copy(tile, i).start()

    def wait(i):
        copy(tiles[0], i).wait()

    return start, wait


def load_kernel(plan, tile_a, array, blocks, held, sems, held_sem):
    whole = pltpu.make_async_copy(array, held, held_sem)
    whole.start()
    start, wait = fetches(plan, HEAD, STRIDE, 0, 0, (tile_a,), blocks, sems)
    start()

    @pl.loop(0, plan[0])
    def _(i):
        wait(i)

    whole.wait()


def each_product(plan, base, ends, part, block_of, pieces, use, then=None, before=None):
    unroll = MANY if base == HEAD else FEW

    for side in range(2):

        @pl.loop(side * part // unroll, plan[ends + side] // unroll)
        def _(j):
            step = [(unroll * j + u, base + STRIDE * (unroll * j + u)) for u in range(unroll)]
            if before is not None:
                for i, entry in step:
                    before(side, i, entry)
            for i, entry in step:
                block = block_of(side, i, entry)
                piece = pieces[side][plan[entry + 2]]
                use(entry, jnp.dot(block, piece, preferred_element_type=jnp.float32))
            if then is not None:
                for i, entry in step:
                    then(entry)


def add_products(plan, base, ends, part, block_of, pieces, total, before=None):
    def use(entry, value):
        total[plan[entry + 1]] += value

    each_product(plan, base, ends, part, block_of, pieces, use, before=before)


def ahead_kernel(lay, plan, tile_a, tile_b, held, sems):
    for side, tile in enumerate((tile_a, tile_b)):
        number = jnp.minimum(plan[4 + side] - side * lay.loads, AHEAD)

        @pl.loop(0, number)
        def _(i):
            slot = plan[lay.load_at + side * lay.loads + i]
            at = side * AHEAD + i
            pltpu.make_async_copy(tile.at[slot], held.at[at], sems.at[at]).start()

    for side in range(2):
        number = jnp.minimum(plan[4 + side] - side * lay.loads, AHEAD)

        @pl.loop(0, number)
        def _(i):
            at = side * AHEAD + i
            pltpu.make_async_copy(tile_a.at[0], held.at[at], sems.at[at]).wait()


def split_sides(pieces, vec):
    middle = vec.shape[-1] // 2
    column = lax.broadcasted_iota(jnp.int32, (1, vec.shape[-1]), 1)
    for side in range(2):
        keep = jnp.where((column // middle) == side, 1.0, 0.0).astype(jnp.bfloat16)
        for p in range(vec.shape[1]):
            vec[side, p] = pieces[p] * keep


def joined(total, k):
    one, two = total[2 * k], total[2 * k + 1]
    low = lax.broadcasted_iota(jnp.int32, one.shape, 1) < one.shape[1] // 2
    return jnp.where(low, one, two) + pltpu.roll(
        jnp.where(low, two, one), one.shape[1] // 2, axis=1
    )


def first_sent_kernel(
    lay, plan, tile_a, tile_b, early_blocks, pieces, start, out, blocks, vec, total, held, held_sem, sems
):
    n_row = out.shape[0]
    for side, tile in enumerate((tile_a, tile_b)):
        begin, end = side * lay.loads, plan[4 + side]

        @pl.loop(begin, jnp.minimum(end, begin + AHEAD))
        def _(i):
            source = early_blocks.at[side * AHEAD + i - begin]
            pltpu.make_async_copy(source, blocks.at[i], sems.at[i]).start()

        @pl.loop(begin + AHEAD, end)
        def _(i):
            source = tile.at[plan[lay.load_at + i]]
            pltpu.make_async_copy(source, blocks.at[i], sems.at[i]).start()

    def wait(i):
        pltpu.make_async_copy(tile_a.at[0], blocks.at[i], sems.at[i]).wait()

    copy = pltpu.make_async_copy(start, held, held_sem)
    copy.start()
    split_sides(pieces, vec)
    total[...] = jnp.zeros_like(total)

    def before(side, i, entry):
        @pl.when(plan[entry + 3] == FIRST)
        def _():
            wait(plan[entry])

    add_products(
        plan,
        lay.sent_at,
        2,
        lay.sends,
        lambda side, i, entry: blocks[plan[entry]],
        (vec.at[0], vec.at[1]),
        total,
        before,
    )
    copy.wait()
    for k in range(n_row):
        value = joined(total, k) - center_value * held[k].astype(jnp.float32)
        out[k] = (value / half_width).astype(jnp.bfloat16)


def second_sent_kernel(
    lay, plan, blocks, pieces, current, previous, out, vec, total, held, held_sem, ready, out_sems
):
    n_row = out.shape[0]
    copy = pltpu.make_async_copy(previous, held, held_sem)
    copy.start()
    split_sides(pieces, vec)
    total[...] = jnp.zeros_like(total)
    add_products(
        plan,
        lay.sent_at,
        2,
        lay.sends,
        lambda side, i, entry: blocks[plan[entry]],
        (vec.at[0], vec.at[1]),
        total,
    )
    copy.wait()

    def put(k):
        return pltpu.make_async_copy(ready.at[k], out.at[k], out_sems.at[k])

    for k in range(n_row):
        value = joined(total, k) - center_value * current[k].astype(jnp.float32)
        ready[k] = (value - held[k].astype(jnp.float32)).astype(jnp.bfloat16)
        put(k).start()
    for k in range(n_row):
        put(k).wait()


def whole_columns(half, mine, other, vec, at):
    n_row, _, width = mine.shape
    middle = width // 2

    @pl.when(half == 0)
    def _():
        for p in range(n_row):
            one, two = mine[p], other[p]
            vec[0, p, :, at : at + width] = jnp.concatenate([one[:, :middle], two[:, middle:]], axis=1)
            vec[1, p, :, at : at + width] = jnp.concatenate([one[:, middle:], two[:, :middle]], axis=1)

    @pl.when(half != 0)
    def _():
        for p in range(n_row):
            one, two = mine[p], other[p]
            vec[0, p, :, at : at + width] = jnp.concatenate([two[:, middle:], one[:, :middle]], axis=1)
            vec[1, p, :, at : at + width] = jnp.concatenate([two[:, :middle], one[:, middle:]], axis=1)


def prime_kernel(vectors, total, own, sem):
    _, block_size, double = total.shape
    width = double // 2
    copy = pltpu.make_async_copy(vectors, own, sem)
    copy.start()
    copy.wait()

    @pl.loop(0, vectors.shape[0] // block_size)
    def _(b):
        at = pl.ds(pl.multiple_of(b * block_size, block_size), block_size)
        value = own[at, :].astype(jnp.float32)
        total[b, :, :width] = -center_value * value
        total[b, :, width:] = -value


def early_kernel(
    lay,
    plan,
    tile_a,
    tile_b,
    q1,
    q1_other,
    q2,
    q2_other,
    start,
    base,
    total,
    vec,
    own,
    blocks,
    sems,
    row_sems,
):
    piece_blocks, block_size, width = base.shape
    begin, wait = fetches(plan, HEAD, STRIDE, 0, lay.slots, (tile_a, tile_b), blocks, sems)
    begin()
    whole_columns(plan[7], q1, q1_other, vec, 0)
    whole_columns(plan[7], q2, q2_other, vec, width)

    def rows(b):
        return pl.ds(pl.multiple_of(b * block_size, block_size), block_size)

    def put(b):
        return pltpu.make_async_copy(own.at[rows(b)], base.at[b], row_sems.at[b])

    add_products(
        plan,
        HEAD,
        0,
        lay.slots,
        lambda side, i, entry: blocks[i],
        (vec.at[0], vec.at[1]),
        total,
        lambda side, i, entry: wait(i),
    )

    @pl.loop(0, piece_blocks)
    def _(b):
        first = (total[b, :, :width] / half_width).astype(jnp.bfloat16).astype(jnp.float32)
        second = total[b, :, width:] - center_value * first
        second = second.astype(jnp.bfloat16).astype(jnp.float32)
        own[rows(b), :] = (-center_value * second - first).astype(jnp.bfloat16)
        put(b).start()

    @pl.loop(0, piece_blocks)
    def _(b):
        put(b).wait()


def last_kernel(
    lay, plan, blocks, tile_b, mine, other, base, out, vec, total, own, blocks_b, sems, row_sems
):
    piece_blocks = base.shape[0]
    begin = lay.slots

    def fetch(i):
        slot = plan[HEAD + STRIDE * i]
        return pltpu.make_async_copy(tile_b.at[slot], blocks_b.at[i - begin], sems.at[i - begin])

    @pl.loop(begin, plan[1])
    def _(i):
        fetch(i).start()

    def put(source, b):
        return pltpu.make_async_copy(source.at[b], out.at[b], row_sems.at[b])

    @pl.loop(0, plan[6])
    def _(i):
        b = plan[lay.bare_at + i]
        put(base, b).start()

    whole_columns(plan[7], mine, other, vec, 0)

    def use(entry, value):
        row = plan[entry + 1]
        marks = plan[entry + 3]
        start = base[jnp.minimum(row, piece_blocks - 1)].astype(jnp.float32)
        value = jnp.where(lax.rem(marks, LAST) == FIRST, start, total[row]) + value
        total[row] = value
        own[row] = value.astype(jnp.bfloat16)

    def then(entry):
        @pl.when(plan[entry + 3] >= LAST)
        def _():
            put(own, plan[entry + 1]).start()

    def block_of(side, i, entry):
        return blocks[i] if side == 0 else blocks_b[i - begin]

    def before(side, i, entry):
        if side == 1:
            fetch(i).wait()

    each_product(
        plan, HEAD, 0, lay.slots, block_of, (vec.at[0], vec.at[1]), use, then, before
    )

    @pl.loop(0, piece_blocks)
    def _(b):
        put(own, b).wait()


def after(value, *others):
    return lax.optimization_barrier((value, *others))[0]


def call(kernel, out, args, spaces, scratch, mib, name, estimate=None, aliases=None):
    args = [
        pltpu.with_memory_space_constraint(arg, space) if space in (VMEM, HBM) or tied else arg
        for arg, (space, tied) in zip(args, spaces)
    ]
    return pl.pallas_call(
        kernel,
        out_shape=[space(shape, dtype) for shape, dtype, space in out],
        in_specs=[spec(space) for space, _ in spaces],
        out_specs=[spec(space) for _, _, space in out],
        scratch_shapes=scratch,
        compiler_params=params(mib),
        cost_estimate=estimate,
        input_output_aliases=aliases or {},
        name=name,
    )(*args)


HERE = (VMEM, True)
FAR = (HBM, True)
LIST = (SMEM, True)
SCALARS = (SMEM, False)
ANYWHERE = (pl.ANY, False)


def on_pair(vectors, tile_blocks, block_rows, block_cols, counts):
    n_row = lax.axis_size("row")
    tile = tile_blocks[0, 0]
    slot_rows = block_rows[0, 0]
    slot_cols = block_cols[0, 0]
    used = counts[0]
    slot_count, block_size, _ = tile.shape
    width = vectors.shape[1]
    piece_blocks = vectors.shape[0] // block_size

    across = functools.partial(lax.ppermute, axis_name="col", perm=[(0, 1), (1, 0)])

    needed = jnp.max(
        jnp.where(
            slot_cols[None, :] // piece_blocks == jnp.arange(n_row)[:, None],
            slot_cols[None, :] % piece_blocks,
            0,
        ),
        axis=1,
        keepdims=True,
    )
    exchange = functools.partial(
        lax.all_to_all, axis_name="row", split_axis=0, concat_axis=0, tiled=True
    )
    wanted = exchange(jnp.broadcast_to(needed, (n_row, LANES)))
    sent_shape = (n_row, block_size, width)
    (sent,) = call(
        functools.partial(pick_kernel, n_row, block_size),
        [(sent_shape, jnp.bfloat16, VMEM)],
        (wanted, vectors),
        (SCALARS, FAR),
        [DMA((n_row,))],
        2,
        "pick",
    )
    tile_other = across(tile)
    sent_other = across(sent)
    wanted_other = across(after(wanted, sent))
    meta = jnp.concatenate([slot_rows, slot_cols, used])
    meta_other = across(after(meta, sent))
    packed = call(
        pack_kernel,
        [(sent_shape, jnp.bfloat16, HBM)],
        (sent, sent_other),
        (HERE, HERE),
        [VMEM(sent_shape, jnp.bfloat16), DMA((n_row,))],
        4,
        "pack",
    )[0]

    lay = layout_for(slot_count, n_row, piece_blocks)
    list_shape = ((lay.size,), jnp.int32)
    own_list, other_list = call(
        functools.partial(plan_kernel, n_row, piece_blocks, lay),
        [(*list_shape, HBM)] * 2,
        (wanted, after(wanted_other, packed), meta, meta_other),
        (SCALARS,) * 4,
        [
            SMEM((2 * lay.size,), jnp.int32),
            SMEM((2 * n_row,), jnp.int32),
            SMEM((piece_blocks + 1,), jnp.int32),
            DMA((2,)),
        ],
        2,
        "plan",
    )
    q1 = exchange(after(packed, own_list))
    plan = call(
        settle_kernel,
        [(*list_shape, SMEM)],
        (own_list, across(after(other_list, packed))),
        (ANYWHERE, ANYWHERE),
        [DMA],
        2,
        "settle",
    )[0]

    def load(cue, array):
        return call(
            load_kernel,
            [
                ((lay.slots, block_size, block_size), jnp.bfloat16, VMEM),
                (array.shape, array.dtype, VMEM),
            ],
            (after(plan, cue), tile, array),
            (LIST, FAR, FAR),
            [DMA((lay.slots,)), DMA],
            2,
            "load",
        )

    def cost(products, rows):
        size = block_size * width
        return pl.CostEstimate(
            flops=2 * products * block_size * size,
            bytes_accessed=2 * (products * block_size * block_size + 3 * rows * size),
            transcendentals=0,
        )

    sums = [
        VMEM((2, n_row, block_size, width), jnp.bfloat16),
        VMEM((2 * n_row + 1, block_size, width), jnp.float32),
    ]

    def first_blocks(*args):
        return call(
            functools.partial(first_sent_kernel, lay),
            [
                (sent_shape, jnp.bfloat16, VMEM),
                ((2 * lay.loads, block_size, block_size), jnp.bfloat16, VMEM),
            ],
            (plan, tile, tile_other, *args),
            (LIST, FAR, ANYWHERE, HERE, HERE, FAR),
            sums + [VMEM(sent_shape, jnp.bfloat16), DMA, DMA((2 * lay.loads,))],
            8,
            "sent",
            cost(n_row, n_row),
        )

    def second_blocks(*args):
        return call(
            functools.partial(second_sent_kernel, lay),
            [(sent_shape, jnp.bfloat16, HBM)],
            (plan, *args),
            (LIST, HERE, HERE, HERE, FAR),
            sums
            + [VMEM(sent_shape, jnp.bfloat16), DMA, VMEM(sent_shape, jnp.bfloat16), DMA((n_row,))],
            8,
            "sent",
            cost(n_row, n_row),
        )[0]

    base_shape = (piece_blocks, block_size, width)

    sums_shape = ((piece_blocks + 1, block_size, 2 * width), jnp.float32, VMEM)

    def early(*args):
        return call(
            functools.partial(early_kernel, lay),
            [(base_shape, jnp.bfloat16, HBM), sums_shape],
            (plan, tile, tile_other, *args),
            (LIST, FAR, ANYWHERE, HERE, HERE, HERE, HERE, HERE),
            [
                VMEM((2, n_row, block_size, 2 * width), jnp.bfloat16),
                VMEM(vectors.shape, jnp.bfloat16),
                VMEM((2 * lay.slots, block_size, block_size), jnp.bfloat16),
                DMA((2 * lay.slots,)),
                DMA((piece_blocks,)),
            ],
            18,
            "early",
            cost(2 * slot_count, 2 * piece_blocks),
            {7: 1},
        )[0]

    def last(blocks, *args):
        rows = (piece_blocks + 1, block_size, width)
        (out,) = call(
            functools.partial(last_kernel, lay),
            [(base_shape, jnp.bfloat16, HBM)],
            (plan, blocks, tile_other, *args),
            (LIST, HERE, ANYWHERE, HERE, HERE, HERE),
            [
                VMEM((2, n_row, block_size, width), jnp.bfloat16),
                VMEM(rows, jnp.float32),
                VMEM(rows, jnp.bfloat16),
                VMEM((lay.slots, block_size, block_size), jnp.bfloat16),
                DMA((lay.slots,)),
                DMA((piece_blocks,)),
            ],
            14,
            "last",
            cost(slot_count, piece_blocks),
        )
        return out.reshape(vectors.shape)

    early_blocks = call(
        functools.partial(ahead_kernel, lay),
        [((2 * AHEAD, block_size, block_size), jnp.bfloat16, VMEM)],
        (plan, tile, tile_other),
        (LIST, FAR, ANYWHERE),
        [DMA((2 * AHEAD,))],
        2,
        "ahead",
    )[0]
    q1 = after(q1, early_blocks)
    first_sent, blocks = first_blocks(early_blocks, q1, packed)
    q2 = exchange(first_sent)
    second_sent = second_blocks(blocks, q2, first_sent, packed)
    q1_other = across(after(q1, second_sent))
    q2_other = across(after(q2, second_sent))
    (start,) = call(
        prime_kernel,
        [sums_shape],
        (after(vectors, second_sent),),
        (FAR,),
        [VMEM(vectors.shape, jnp.bfloat16), DMA],
        4,
        "prime",
        cost(0, 3 * piece_blocks),
    )
    base = early(q1, q1_other, q2, q2_other, start)
    q3 = after(exchange(second_sent), base)
    q3_other = across(q3)
    blocks, base = load(q3, base)
    return last(blocks, q3, q3_other, base)


def on_any(vectors, tile_blocks, block_rows, block_cols, counts):
    n_row = lax.axis_size("row")
    n_col = lax.axis_size("col")
    tile_data = tile_blocks[0, 0]
    slot_rows = block_rows[0, 0]
    slot_cols = block_cols[0, 0]
    used = counts[0, 0]
    block_size = tile_data.shape[-1]
    width = vectors.shape[1]
    piece_blocks = vectors.shape[0] // block_size
    row_blocks = piece_blocks * n_col
    slot_count = tile_data.shape[0]
    live = (jnp.arange(slot_count) < used).astype(jnp.float32)
    onehot = (slot_rows[None, :] == jnp.arange(row_blocks)[:, None]).astype(jnp.float32) * live[
        None, :
    ]
    source_piece = slot_cols // piece_blocks
    offset = slot_cols % piece_blocks
    needed = jnp.max(
        jnp.where(source_piece[None, :] == jnp.arange(n_row)[:, None], offset[None, :], 0), axis=1
    )
    wanted = lax.all_to_all(
        needed.reshape(n_row, 1), "row", split_axis=0, concat_axis=0, tiled=True
    ).reshape(n_row)

    def apply_tiles(current):
        own_blocks = current.reshape(piece_blocks, block_size, width)
        outgoing = jnp.take(own_blocks, wanted, axis=0)
        received = lax.all_to_all(outgoing, "row", split_axis=0, concat_axis=0, tiled=True)
        vec_blocks = jnp.take(received, source_piece, axis=0)
        products = jnp.einsum(
            "sij,sjk->sik", tile_data, vec_blocks, preferred_element_type=jnp.float32
        )
        term = jnp.einsum("ls,sik->lik", onehot, products, precision=lax.Precision.HIGHEST)
        term = term.reshape(row_blocks * block_size, width)
        return lax.psum_scatter(
            term.astype(jnp.bfloat16), "col", scatter_dimension=0, tiled=True
        ).astype(jnp.float32)

    previous = vectors
    applied = apply_tiles(vectors)
    current = ((applied - center_value * previous.astype(jnp.float32)) / half_width).astype(
        jnp.bfloat16
    )
    for repeat in range(DEGREE - 1):
        applied = apply_tiles(current)
        following = (
            2.0 * (applied - center_value * current.astype(jnp.float32)) / half_width
            - previous.astype(jnp.float32)
        ).astype(jnp.bfloat16)
        previous, current = (current, following)
    return current


def solution(mesh):
    n_row, n_col = mesh.shape["row"], mesh.shape["col"]
    paired = n_col == 2 and n_row & (n_row - 1) == 0
    return jax.shard_map(
        on_pair if paired else on_any,
        mesh=mesh,
        in_specs=(
            P(("row", "col"), "vec"),
            P("row", "col", None, None, None),
            P("row", "col", None),
            P("row", "col", None),
            P("row", "col"),
        ),
        out_specs=P(("row", "col"), "vec"),
        check_vma=False,
    )
```

```python
import functools
import typing

import jax
import jax.numpy as jnp
from jax import lax
from jax.experimental import pallas as pl
from jax.experimental.pallas import tpu as pltpu
from jax.sharding import PartitionSpec as P

DEGREE = 3

center_value = 0.5
half_width = 2.0

VMEM = pltpu.VMEM
SMEM = pltpu.SMEM
HBM = pltpu.HBM
DMA = pltpu.SemaphoreType.DMA
LANES = 128
FEW = 4
MANY = 4
HEAD = 8
STRIDE = 4
FIRST = 1
LAST = 2


def spec(space):
    return pl.BlockSpec(memory_space=space)


def params(mib):
    return pltpu.CompilerParams(vmem_limit_bytes=mib * 1024 * 1024)


def round_up(n, step):
    return (n + step - 1) // step * step


def core_number():
    return lax.axis_index("col")


class Layout(typing.NamedTuple):
    slots: int
    sends: int
    loads: int
    sent_at: int
    load_at: int
    bare_at: int
    size: int


def layout_for(slot_count, n_row, piece_blocks):
    slots = round_up(slot_count, MANY) + MANY
    sends = round_up(2 * n_row * n_row, FEW) + FEW
    sent_at = HEAD + STRIDE * 2 * slots
    load_at = sent_at + STRIDE * 2 * sends
    bare_at = load_at + 2 * (slot_count + 1)
    size = round_up(bare_at + piece_blocks, 8 * LANES)
    return Layout(slots, sends, slot_count + 1, sent_at, load_at, bare_at, size)


def plan_kernel(
    n_row,
    piece_blocks,
    lay,
    wanted_a,
    wanted_b,
    meta_a,
    meta_b,
    used_a,
    used_b,
    own,
    other,
    out,
    asked,
    seen,
    sems,
):
    slot_count = meta_a.shape[1] // 2

    def put(at, *values):
        for i, value in enumerate(values):
            out[at + i] = value

    def scan(tile, meta, used):


        def step(s, carry):
            ends, sent, load = carry
            row = meta[0, s]
            piece = meta[0, slot_count + s] // piece_blocks
            live = s < used[0, 0]
            half = row // piece_blocks
            local = row - half * piece_blocks
            lower = half == 0
            part = jnp.where(lower, tile, 1 - tile)
            at = HEAD + STRIDE * (part * lay.slots + jnp.where(lower, ends[0], ends[1]))
            base = half * lay.size
            put(base + at, s, local, piece)
            sought = jnp.where(live, local, -1)
            hits = [(asked[half * n_row + k] == sought).astype(jnp.int32) for k in range(n_row)]
            found = sum(hits)

            @pl.when(found > 0)
            def _():
                for core in range(2):
                    mine = tile if core == 0 else 1 - tile
                    side = half if core == 0 else 1 - half
                    first = core * lay.size
                    out[first + lay.load_at + mine * lay.loads + load] = s

                    place = sent
                    for k in range(n_row):
                        put(
                            first + lay.sent_at + STRIDE * (mine * lay.sends + place),
                            mine * lay.loads + load,
                            2 * k + side,
                            piece,
                            jnp.where(place == sent, FIRST, 0),
                        )
                        place = place + hits[k]

            one = live.astype(jnp.int32)
            ends = (ends[0] + jnp.where(lower, one, 0), ends[1] + jnp.where(lower, 0, one))
            return ends, sent + found, load + jnp.where(found > 0, 1, 0)

        zero = jnp.int32(0)
        ends, sent, load = lax.fori_loop(0, slot_count, step, ((zero, zero), zero, zero))
        for core in range(2):
            mine = tile if core == 0 else 1 - tile
            base = core * lay.size
            for i, (at, begin, end, unit, spare) in enumerate(
                (
                    (HEAD, mine * lay.slots, ends[core], MANY, piece_blocks),
                    (lay.sent_at, mine * lay.sends, sent, FEW, 2 * n_row),
                )
            ):
                for u in range(unit - 1):
                    put(base + at + STRIDE * (begin + end + u), 0, spare, 0, 0)
                out[base + 2 * i + mine] = begin + (end + unit - 1) // unit * unit
            out[base + 4 + mine] = mine * lay.loads + load

    def mark(core):
        base = core * lay.size
        for b in range(piece_blocks + 1):
            seen[b] = 0
        for part in range(2):

            @pl.loop(part * lay.slots, out[base + part])
            def _(i):
                entry = base + HEAD + STRIDE * i
                row = out[entry + 1]
                out[entry + 3] = jnp.where(seen[row] == 0, FIRST, 0)
                seen[row] = entry

        def close(b, bare):
            entry = seen[b]
            out[base + lay.bare_at + bare] = b

            @pl.when(entry > 0)
            def _():
                out[entry + 3] = out[entry + 3] + LAST

            return bare + jnp.where(entry == 0, 1, 0)

        out[base + 6] = lax.fori_loop(0, piece_blocks, close, jnp.int32(0))
        out[base + 7] = core

    @pl.when(core_number() == 0)
    def _():
        for half, wanted in enumerate((wanted_a, wanted_b)):
            for k in range(n_row):
                asked[half * n_row + k] = wanted[k, 0]
        scan(0, meta_a, used_a)
        scan(1, meta_b, used_b)
        for core in range(2):
            mark(core)
        copies = [
            pltpu.make_async_copy(out.at[pl.ds(core * lay.size, lay.size)], target, sems.at[core])
            for core, target in enumerate((own, other))
        ]
        for copy in copies:
            copy.start()
        for copy in copies:
            copy.wait()


def settle_kernel(own, handed, out, sem):
    for half, source in enumerate((own, handed)):

        @pl.when(core_number() == half)
        def _():
            copy = pltpu.make_async_copy(source, out, sem)
            copy.start()
            copy.wait()


def pick_kernel(n_row, block_size, wanted, vectors, out, sems):
    def fetch(k):
        at = pl.multiple_of(wanted[k, 0] * block_size, block_size)
        return pltpu.make_async_copy(vectors.at[pl.ds(at, block_size)], out.at[k], sems.at[k])

    for k in range(n_row):
        fetch(k).start()
    for k in range(n_row):
        fetch(k).wait()


def pack_kernel(picked, picked_b, out, held, sems):
    n_row, _, width = picked.shape
    middle = width // 2

    def put(k):
        return pltpu.make_async_copy(held.at[k], out.at[k], sems.at[k])

    for half in range(2):

        @pl.when(core_number() == half)
        def _():
            part = slice(half * middle, (half + 1) * middle)
            for k in range(n_row):
                held[k] = jnp.concatenate([picked[k, :, part], picked_b[k, :, part]], axis=1)
                put(k).start()

    for k in range(n_row):
        put(k).wait()


def fetches(plan, base, stride, ends, part, tiles, blocks, sems):
    def copy(tile, i):
        slot = plan[base + stride * i]
        return pltpu.make_async_copy(tile.at[slot], blocks.at[i], sems.at[i])

    def start():
        for side, tile in enumerate(tiles):

            @pl.loop(side * part, plan[ends + side])
            def _(i):
                copy(tile, i).start()

    def wait(i):
        copy(tiles[0], i).wait()

    return start, wait


def load_kernel(plan, tile_a, array, blocks, held, sems, held_sem):
    whole = pltpu.make_async_copy(array, held, held_sem)
    whole.start()
    start, wait = fetches(plan, HEAD, STRIDE, 0, 0, (tile_a,), blocks, sems)
    start()

    @pl.loop(0, plan[0])
    def _(i):
        wait(i)

    whole.wait()


def each_product(plan, base, ends, part, block_of, pieces, use, then=None, before=None):
    unroll = MANY if base == HEAD else FEW

    for side in range(2):

        @pl.loop(side * part // unroll, plan[ends + side] // unroll)
        def _(j):
            step = [(unroll * j + u, base + STRIDE * (unroll * j + u)) for u in range(unroll)]
            if before is not None:
                for i, entry in step:
                    before(side, i, entry)
            for i, entry in step:
                block = block_of(side, i, entry)
                piece = pieces[side][plan[entry + 2]]
                use(entry, jnp.dot(block, piece, preferred_element_type=jnp.float32))
            if then is not None:
                for i, entry in step:
                    then(entry)


def add_products(plan, base, ends, part, block_of, pieces, total, before=None):
    def use(entry, value):
        total[plan[entry + 1]] += value

    each_product(plan, base, ends, part, block_of, pieces, use, before=before)


def split_sides(pieces, vec):
    middle = vec.shape[-1] // 2
    column = lax.broadcasted_iota(jnp.int32, (1, vec.shape[-1]), 1)
    for side in range(2):
        keep = jnp.where((column // middle) == side, 1.0, 0.0).astype(jnp.bfloat16)
        for p in range(vec.shape[1]):
            vec[side, p] = pieces[p] * keep


def joined(total, k):
    one, two = total[2 * k], total[2 * k + 1]
    low = lax.broadcasted_iota(jnp.int32, one.shape, 1) < one.shape[1] // 2
    return jnp.where(low, one, two) + pltpu.roll(
        jnp.where(low, two, one), one.shape[1] // 2, axis=1
    )


def first_sent_kernel(
    lay, plan, tile_a, tile_b, pieces, start, out, blocks, vec, total, held, held_sem, sems
):
    n_row = out.shape[0]
    begin, wait = fetches(plan, lay.load_at, 1, 4, lay.loads, (tile_a, tile_b), blocks, sems)
    begin()
    copy = pltpu.make_async_copy(start, held, held_sem)
    copy.start()
    split_sides(pieces, vec)
    total[...] = jnp.zeros_like(total)

    def before(side, i, entry):
        @pl.when(plan[entry + 3] == FIRST)
        def _():
            wait(plan[entry])

    add_products(
        plan,
        lay.sent_at,
        2,
        lay.sends,
        lambda side, i, entry: blocks[plan[entry]],
        (vec.at[0], vec.at[1]),
        total,
        before,
    )
    copy.wait()
    for k in range(n_row):
        value = joined(total, k) - center_value * held[k].astype(jnp.float32)
        out[k] = (value / half_width).astype(jnp.bfloat16)


def second_sent_kernel(
    lay, plan, blocks, pieces, current, previous, out, vec, total, held, held_sem, ready, out_sems
):
    n_row = out.shape[0]
    copy = pltpu.make_async_copy(previous, held, held_sem)
    copy.start()
    split_sides(pieces, vec)
    total[...] = jnp.zeros_like(total)
    add_products(
        plan,
        lay.sent_at,
        2,
        lay.sends,
        lambda side, i, entry: blocks[plan[entry]],
        (vec.at[0], vec.at[1]),
        total,
    )
    copy.wait()

    def put(k):
        return pltpu.make_async_copy(ready.at[k], out.at[k], out_sems.at[k])

    for k in range(n_row):
        value = joined(total, k) - center_value * current[k].astype(jnp.float32)
        ready[k] = (value - held[k].astype(jnp.float32)).astype(jnp.bfloat16)
        put(k).start()
    for k in range(n_row):
        put(k).wait()


def whole_columns(half, mine, other, vec, at):
    n_row, _, width = mine.shape
    middle = width // 2

    @pl.when(half == 0)
    def _():
        for p in range(n_row):
            one, two = mine[p], other[p]
            vec[0, p, :, at : at + width] = jnp.concatenate([one[:, :middle], two[:, middle:]], axis=1)
            vec[1, p, :, at : at + width] = jnp.concatenate([one[:, middle:], two[:, :middle]], axis=1)

    @pl.when(half != 0)
    def _():
        for p in range(n_row):
            one, two = mine[p], other[p]
            vec[0, p, :, at : at + width] = jnp.concatenate([two[:, middle:], one[:, :middle]], axis=1)
            vec[1, p, :, at : at + width] = jnp.concatenate([two[:, :middle], one[:, middle:]], axis=1)


def prime_kernel(vectors, total, own, sem):
    _, block_size, double = total.shape
    width = double // 2
    copy = pltpu.make_async_copy(vectors, own, sem)
    copy.start()
    copy.wait()

    @pl.loop(0, vectors.shape[0] // block_size)
    def _(b):
        at = pl.ds(pl.multiple_of(b * block_size, block_size), block_size)
        value = own[at, :].astype(jnp.float32)
        total[b, :, :width] = -center_value * value
        total[b, :, width:] = -value


def early_kernel(
    lay,
    plan,
    tile_a,
    tile_b,
    q1,
    q1_other,
    q2,
    q2_other,
    start,
    base,
    total,
    vec,
    own,
    blocks,
    sems,
    row_sems,
):
    piece_blocks, block_size, width = base.shape
    begin, wait = fetches(plan, HEAD, STRIDE, 0, lay.slots, (tile_a, tile_b), blocks, sems)
    begin()
    whole_columns(plan[7], q1, q1_other, vec, 0)
    whole_columns(plan[7], q2, q2_other, vec, width)

    def rows(b):
        return pl.ds(pl.multiple_of(b * block_size, block_size), block_size)

    def put(b):
        return pltpu.make_async_copy(own.at[rows(b)], base.at[b], row_sems.at[b])

    add_products(
        plan,
        HEAD,
        0,
        lay.slots,
        lambda side, i, entry: blocks[i],
        (vec.at[0], vec.at[1]),
        total,
        lambda side, i, entry: wait(i),
    )

    @pl.loop(0, piece_blocks)
    def _(b):
        first = (total[b, :, :width] / half_width).astype(jnp.bfloat16).astype(jnp.float32)
        second = total[b, :, width:] - center_value * first
        second = second.astype(jnp.bfloat16).astype(jnp.float32)
        own[rows(b), :] = (-center_value * second - first).astype(jnp.bfloat16)
        put(b).start()

    @pl.loop(0, piece_blocks)
    def _(b):
        put(b).wait()


def last_kernel(
    lay, plan, blocks, tile_b, mine, other, base, out, vec, total, own, blocks_b, sems, row_sems
):
    piece_blocks = base.shape[0]
    begin = lay.slots

    def fetch(i):
        slot = plan[HEAD + STRIDE * i]
        return pltpu.make_async_copy(tile_b.at[slot], blocks_b.at[i - begin], sems.at[i - begin])

    @pl.loop(begin, plan[1])
    def _(i):
        fetch(i).start()

    def put(source, b):
        return pltpu.make_async_copy(source.at[b], out.at[b], row_sems.at[b])

    @pl.loop(0, plan[6])
    def _(i):
        b = plan[lay.bare_at + i]
        put(base, b).start()

    whole_columns(plan[7], mine, other, vec, 0)

    def use(entry, value):
        row = plan[entry + 1]
        marks = plan[entry + 3]
        start = base[jnp.minimum(row, piece_blocks - 1)].astype(jnp.float32)
        value = jnp.where(lax.rem(marks, LAST) == FIRST, start, total[row]) + value
        total[row] = value
        own[row] = value.astype(jnp.bfloat16)

    def then(entry):
        @pl.when(plan[entry + 3] >= LAST)
        def _():
            put(own, plan[entry + 1]).start()

    def block_of(side, i, entry):
        return blocks[i] if side == 0 else blocks_b[i - begin]

    def before(side, i, entry):
        if side == 1:
            fetch(i).wait()

    each_product(
        plan, HEAD, 0, lay.slots, block_of, (vec.at[0], vec.at[1]), use, then, before
    )

    @pl.loop(0, piece_blocks)
    def _(b):
        put(own, b).wait()


def after(value, *others):
    return lax.optimization_barrier((value, *others))[0]


def call(kernel, out, args, spaces, scratch, mib, name, estimate=None, aliases=None):
    args = [
        pltpu.with_memory_space_constraint(arg, space) if space in (VMEM, HBM) or tied else arg
        for arg, (space, tied) in zip(args, spaces)
    ]
    return pl.pallas_call(
        kernel,
        out_shape=[space(shape, dtype) for shape, dtype, space in out],
        in_specs=[spec(space) for space, _ in spaces],
        out_specs=[spec(space) for _, _, space in out],
        scratch_shapes=scratch,
        compiler_params=params(mib),
        cost_estimate=estimate,
        input_output_aliases=aliases or {},
        name=name,
    )(*args)


HERE = (VMEM, True)
FAR = (HBM, True)
LIST = (SMEM, True)
SCALARS = (SMEM, False)
ANYWHERE = (pl.ANY, False)


def on_pair(vectors, tile_blocks, block_rows, block_cols, counts):
    n_row = lax.axis_size("row")
    tile = tile_blocks[0, 0]
    slot_cols = block_cols[0, 0]
    slot_count, block_size, _ = tile.shape
    width = vectors.shape[1]
    piece_blocks = vectors.shape[0] // block_size

    across = functools.partial(lax.ppermute, axis_name="col", perm=[(0, 1), (1, 0)])

    needed = jnp.max(
        jnp.where(
            slot_cols[None, :] // piece_blocks == jnp.arange(n_row)[:, None],
            slot_cols[None, :] % piece_blocks,
            0,
        ),
        axis=1,
        keepdims=True,
    )
    exchange = functools.partial(
        lax.all_to_all, axis_name="row", split_axis=0, concat_axis=0, tiled=True
    )
    wanted = exchange(jnp.broadcast_to(needed, (n_row, LANES)))
    sent_shape = (n_row, block_size, width)
    (sent,) = call(
        functools.partial(pick_kernel, n_row, block_size),
        [(sent_shape, jnp.bfloat16, VMEM)],
        (wanted, vectors),
        (SCALARS, FAR),
        [DMA((n_row,))],
        2,
        "pick",
    )
    tile_other = across(tile)
    sent_other = across(sent)
    wanted_other = across(after(wanted, sent))
    meta = jnp.concatenate([block_rows[0], block_cols[0]], axis=1)
    meta_other = across(after(meta, sent))
    counts_other = across(after(counts, sent))
    packed = call(
        pack_kernel,
        [(sent_shape, jnp.bfloat16, HBM)],
        (sent, sent_other),
        (HERE, HERE),
        [VMEM(sent_shape, jnp.bfloat16), DMA((n_row,))],
        4,
        "pack",
    )[0]

    lay = layout_for(slot_count, n_row, piece_blocks)
    list_shape = ((lay.size,), jnp.int32)
    own_list, other_list = call(
        functools.partial(plan_kernel, n_row, piece_blocks, lay),
        [(*list_shape, HBM)] * 2,
        (wanted, after(wanted_other, packed), meta, meta_other, counts, counts_other),
        (SCALARS,) * 6,
        [
            SMEM((2 * lay.size,), jnp.int32),
            SMEM((2 * n_row,), jnp.int32),
            SMEM((piece_blocks + 1,), jnp.int32),
            DMA((2,)),
        ],
        2,
        "plan",
    )
    q1 = exchange(after(packed, own_list))
    plan = call(
        settle_kernel,
        [(*list_shape, SMEM)],
        (own_list, across(after(other_list, packed))),
        (ANYWHERE, ANYWHERE),
        [DMA],
        2,
        "settle",
    )[0]

    def load(cue, array):
        return call(
            load_kernel,
            [
                ((lay.slots, block_size, block_size), jnp.bfloat16, VMEM),
                (array.shape, array.dtype, VMEM),
            ],
            (after(plan, cue), tile, array),
            (LIST, FAR, FAR),
            [DMA((lay.slots,)), DMA],
            2,
            "load",
        )

    def cost(products, rows):
        size = block_size * width
        return pl.CostEstimate(
            flops=2 * products * block_size * size,
            bytes_accessed=2 * (products * block_size * block_size + 3 * rows * size),
            transcendentals=0,
        )

    sums = [
        VMEM((2, n_row, block_size, width), jnp.bfloat16),
        VMEM((2 * n_row + 1, block_size, width), jnp.float32),
    ]

    def first_blocks(*args):
        return call(
            functools.partial(first_sent_kernel, lay),
            [
                (sent_shape, jnp.bfloat16, VMEM),
                ((2 * lay.loads, block_size, block_size), jnp.bfloat16, VMEM),
            ],
            (plan, tile, tile_other, *args),
            (LIST, FAR, ANYWHERE, HERE, FAR),
            sums + [VMEM(sent_shape, jnp.bfloat16), DMA, DMA((2 * lay.loads,))],
            8,
            "sent",
            cost(n_row, n_row),
        )

    def second_blocks(*args):
        return call(
            functools.partial(second_sent_kernel, lay),
            [(sent_shape, jnp.bfloat16, HBM)],
            (plan, *args),
            (LIST, HERE, HERE, HERE, FAR),
            sums
            + [VMEM(sent_shape, jnp.bfloat16), DMA, VMEM(sent_shape, jnp.bfloat16), DMA((n_row,))],
            8,
            "sent",
            cost(n_row, n_row),
        )[0]

    base_shape = (piece_blocks, block_size, width)

    sums_shape = ((piece_blocks + 1, block_size, 2 * width), jnp.float32, VMEM)

    def early(*args):
        return call(
            functools.partial(early_kernel, lay),
            [(base_shape, jnp.bfloat16, HBM), sums_shape],
            (plan, tile, tile_other, *args),
            (LIST, FAR, ANYWHERE, HERE, HERE, HERE, HERE, HERE),
            [
                VMEM((2, n_row, block_size, 2 * width), jnp.bfloat16),
                VMEM(vectors.shape, jnp.bfloat16),
                VMEM((2 * lay.slots, block_size, block_size), jnp.bfloat16),
                DMA((2 * lay.slots,)),
                DMA((piece_blocks,)),
            ],
            18,
            "early",
            cost(2 * slot_count, 2 * piece_blocks),
            {7: 1},
        )[0]

    def last(blocks, *args):
        rows = (piece_blocks + 1, block_size, width)
        (out,) = call(
            functools.partial(last_kernel, lay),
            [(base_shape, jnp.bfloat16, HBM)],
            (plan, blocks, tile_other, *args),
            (LIST, HERE, ANYWHERE, HERE, HERE, HERE),
            [
                VMEM((2, n_row, block_size, width), jnp.bfloat16),
                VMEM(rows, jnp.float32),
                VMEM(rows, jnp.bfloat16),
                VMEM((lay.slots, block_size, block_size), jnp.bfloat16),
                DMA((lay.slots,)),
                DMA((piece_blocks,)),
            ],
            14,
            "last",
            cost(slot_count, piece_blocks),
        )
        return out.reshape(vectors.shape)

    q1 = after(q1, plan)
    first_sent, blocks = first_blocks(q1, packed)
    q2 = exchange(first_sent)
    second_sent = second_blocks(blocks, q2, first_sent, packed)
    q1_other = across(after(q1, second_sent))
    q2_other = across(after(q2, second_sent))
    (start,) = call(
        prime_kernel,
        [sums_shape],
        (after(vectors, second_sent),),
        (FAR,),
        [VMEM(vectors.shape, jnp.bfloat16), DMA],
        4,
        "prime",
        cost(0, 3 * piece_blocks),
    )
    base = early(q1, q1_other, q2, q2_other, start)
    q3 = after(exchange(second_sent), base)
    q3_other = across(q3)
    blocks, base = load(q3, base)
    return last(blocks, q3, q3_other, base)


def on_any(vectors, tile_blocks, block_rows, block_cols, counts):
    n_row = lax.axis_size("row")
    n_col = lax.axis_size("col")
    tile_data = tile_blocks[0, 0]
    slot_rows = block_rows[0, 0]
    slot_cols = block_cols[0, 0]
    used = counts[0, 0]
    block_size = tile_data.shape[-1]
    width = vectors.shape[1]
    piece_blocks = vectors.shape[0] // block_size
    row_blocks = piece_blocks * n_col
    slot_count = tile_data.shape[0]
    live = (jnp.arange(slot_count) < used).astype(jnp.float32)
    onehot = (slot_rows[None, :] == jnp.arange(row_blocks)[:, None]).astype(jnp.float32) * live[
        None, :
    ]
    source_piece = slot_cols // piece_blocks
    offset = slot_cols % piece_blocks
    needed = jnp.max(
        jnp.where(source_piece[None, :] == jnp.arange(n_row)[:, None], offset[None, :], 0), axis=1
    )
    wanted = lax.all_to_all(
        needed.reshape(n_row, 1), "row", split_axis=0, concat_axis=0, tiled=True
    ).reshape(n_row)

    def apply_tiles(current):
        own_blocks = current.reshape(piece_blocks, block_size, width)
        outgoing = jnp.take(own_blocks, wanted, axis=0)
        received = lax.all_to_all(outgoing, "row", split_axis=0, concat_axis=0, tiled=True)
        vec_blocks = jnp.take(received, source_piece, axis=0)
        products = jnp.einsum(
            "sij,sjk->sik", tile_data, vec_blocks, preferred_element_type=jnp.float32
        )
        term = jnp.einsum("ls,sik->lik", onehot, products, precision=lax.Precision.HIGHEST)
        term = term.reshape(row_blocks * block_size, width)
        return lax.psum_scatter(
            term.astype(jnp.bfloat16), "col", scatter_dimension=0, tiled=True
        ).astype(jnp.float32)

    previous = vectors
    applied = apply_tiles(vectors)
    current = ((applied - center_value * previous.astype(jnp.float32)) / half_width).astype(
        jnp.bfloat16
    )
    for repeat in range(DEGREE - 1):
        applied = apply_tiles(current)
        following = (
            2.0 * (applied - center_value * current.astype(jnp.float32)) / half_width
            - previous.astype(jnp.float32)
        ).astype(jnp.bfloat16)
        previous, current = (current, following)
    return current


def solution(mesh):
    n_row, n_col = mesh.shape["row"], mesh.shape["col"]
    paired = n_col == 2 and n_row & (n_row - 1) == 0
    return jax.shard_map(
        on_pair if paired else on_any,
        mesh=mesh,
        in_specs=(
            P(("row", "col"), "vec"),
            P("row", "col", None, None, None),
            P("row", "col", None),
            P("row", "col", None),
            P("row", "col"),
        ),
        out_specs=P(("row", "col"), "vec"),
        check_vma=False,
    )
```

```python
import functools
import typing

import jax
import jax.numpy as jnp
from jax import lax
from jax.experimental import pallas as pl
from jax.experimental.pallas import tpu as pltpu
from jax.sharding import PartitionSpec as P

DEGREE = 3

center_value = 0.5
half_width = 2.0

VMEM = pltpu.VMEM
SMEM = pltpu.SMEM
HBM = pltpu.HBM
DMA = pltpu.SemaphoreType.DMA
LANES = 128
FEW = 4
MANY = 4
LEAD = 3 * MANY
HEAD = 8
STRIDE = 4
FIRST = 1
LAST = 2


def spec(space):
    return pl.BlockSpec(memory_space=space)


def params(mib):
    return pltpu.CompilerParams(vmem_limit_bytes=mib * 1024 * 1024)


def round_up(n, step):
    return (n + step - 1) // step * step


def core_number():
    return lax.axis_index("col")


class Layout(typing.NamedTuple):
    slots: int
    sends: int
    loads: int
    sent_at: int
    load_at: int
    bare_at: int
    size: int


def layout_for(slot_count, n_row, piece_blocks):
    slots = round_up(slot_count, MANY) + MANY
    sends = round_up(2 * n_row * n_row, FEW) + FEW
    sent_at = HEAD + STRIDE * 2 * slots
    load_at = sent_at + STRIDE * 2 * sends
    bare_at = load_at + 2 * (slot_count + 1)
    size = round_up(bare_at + piece_blocks, 8 * LANES)
    return Layout(slots, sends, slot_count + 1, sent_at, load_at, bare_at, size)


def plan_kernel(
    n_row,
    piece_blocks,
    lay,
    wanted_a,
    wanted_b,
    meta_a,
    meta_b,
    own,
    other,
    out,
    asked,
    seen,
    sems,
):
    slot_count = (meta_a.shape[0] - 1) // 2

    def put(at, *values):
        for i, value in enumerate(values):
            out[at + i] = value

    def scan(tile, meta):
        used = meta[2 * slot_count]


        def step(s, carry):
            ends, sent, load = carry
            row = meta[s]
            piece = meta[slot_count + s] // piece_blocks
            live = s < used
            half = row // piece_blocks
            local = row - half * piece_blocks
            lower = half == 0
            part = jnp.where(lower, tile, 1 - tile)
            at = HEAD + STRIDE * (part * lay.slots + jnp.where(lower, ends[0], ends[1]))
            base = half * lay.size
            put(base + at, s, local, piece)
            sought = jnp.where(live, local, -1)
            hits = [(asked[half * n_row + k] == sought).astype(jnp.int32) for k in range(n_row)]
            found = sum(hits)

            @pl.when(found > 0)
            def _():
                for core in range(2):
                    mine = tile if core == 0 else 1 - tile
                    side = half if core == 0 else 1 - half
                    first = core * lay.size
                    out[first + lay.load_at + mine * lay.loads + load] = s

                    place = sent
                    for k in range(n_row):
                        put(
                            first + lay.sent_at + STRIDE * (mine * lay.sends + place),
                            mine * lay.loads + load,
                            2 * k + side,
                            piece,
                            jnp.where(place == sent, FIRST, 0),
                        )
                        place = place + hits[k]

            one = live.astype(jnp.int32)
            ends = (ends[0] + jnp.where(lower, one, 0), ends[1] + jnp.where(lower, 0, one))
            return ends, sent + found, load + jnp.where(found > 0, 1, 0)

        zero = jnp.int32(0)
        ends, sent, load = lax.fori_loop(0, slot_count, step, ((zero, zero), zero, zero))
        for core in range(2):
            mine = tile if core == 0 else 1 - tile
            base = core * lay.size
            for i, (at, begin, end, unit, spare) in enumerate(
                (
                    (HEAD, mine * lay.slots, ends[core], MANY, piece_blocks),
                    (lay.sent_at, mine * lay.sends, sent, FEW, 2 * n_row),
                )
            ):
                for u in range(unit - 1):
                    put(base + at + STRIDE * (begin + end + u), 0, spare, 0, 0)
                out[base + 2 * i + mine] = begin + (end + unit - 1) // unit * unit
            out[base + 4 + mine] = mine * lay.loads + load

    def mark(core):
        base = core * lay.size
        for b in range(piece_blocks + 1):
            seen[b] = 0
        for part in range(2):

            @pl.loop(part * lay.slots, out[base + part])
            def _(i):
                entry = base + HEAD + STRIDE * i
                row = out[entry + 1]
                out[entry + 3] = jnp.where(seen[row] == 0, FIRST, 0)
                seen[row] = entry

        def close(b, bare):
            entry = seen[b]
            out[base + lay.bare_at + bare] = b

            @pl.when(entry > 0)
            def _():
                out[entry + 3] = out[entry + 3] + LAST

            return bare + jnp.where(entry == 0, 1, 0)

        out[base + 6] = lax.fori_loop(0, piece_blocks, close, jnp.int32(0))
        out[base + 7] = core

    @pl.when(core_number() == 0)
    def _():
        for half, wanted in enumerate((wanted_a, wanted_b)):
            for k in range(n_row):
                asked[half * n_row + k] = wanted[k, 0]
        scan(0, meta_a)
        scan(1, meta_b)
        for core in range(2):
            mark(core)
        copies = [
            pltpu.make_async_copy(out.at[pl.ds(core * lay.size, lay.size)], target, sems.at[core])
            for core, target in enumerate((own, other))
        ]
        for copy in copies:
            copy.start()
        for copy in copies:
            copy.wait()


def settle_kernel(own, handed, out, sem):
    for half, source in enumerate((own, handed)):

        @pl.when(core_number() == half)
        def _():
            copy = pltpu.make_async_copy(source, out, sem)
            copy.start()
            copy.wait()


def pick_kernel(n_row, block_size, wanted, vectors, out, sems):
    def fetch(k):
        at = pl.multiple_of(wanted[k, 0] * block_size, block_size)
        return pltpu.make_async_copy(vectors.at[pl.ds(at, block_size)], out.at[k], sems.at[k])

    for k in range(n_row):
        fetch(k).start()
    for k in range(n_row):
        fetch(k).wait()


def pack_kernel(picked, picked_b, out, held, sems):
    n_row, _, width = picked.shape
    middle = width // 2

    def put(k):
        return pltpu.make_async_copy(held.at[k], out.at[k], sems.at[k])

    for half in range(2):

        @pl.when(core_number() == half)
        def _():
            part = slice(half * middle, (half + 1) * middle)
            for k in range(n_row):
                held[k] = jnp.concatenate([picked[k, :, part], picked_b[k, :, part]], axis=1)
                put(k).start()

    for k in range(n_row):
        put(k).wait()


def fetches(plan, base, stride, ends, part, tiles, blocks, sems):
    def copy(tile, i):
        slot = plan[base + stride * i]
        return pltpu.make_async_copy(tile.at[slot], blocks.at[i], sems.at[i])

    def start():
        for side, tile in enumerate(tiles):

            @pl.loop(side * part, plan[ends + side])
            def _(i):
                copy(tile, i).start()

    def wait(i):
        copy(tiles[0], i).wait()

    return start, wait


def load_kernel(plan, tile_a, array, blocks, held, sems, held_sem):
    whole = pltpu.make_async_copy(array, held, held_sem)
    whole.start()
    number = jnp.minimum(plan[0], LEAD)

    def copy(i):
        return pltpu.make_async_copy(
            tile_a.at[plan[HEAD + STRIDE * i]], blocks.at[i], sems.at[i]
        )

    @pl.loop(0, number)
    def _(i):
        copy(i).start()

    @pl.loop(0, number)
    def _(i):
        copy(i).wait()

    whole.wait()


def each_product(
    plan, base, ends, part, block_of, pieces, use, then=None, before=None, segments=None
):
    unroll = MANY if base == HEAD else FEW

    if segments is None:
        segments = [(side, side * part, plan[ends + side]) for side in range(2)]
    for number, (side, begin, end) in enumerate(segments):

        @pl.loop(begin // unroll, end // unroll)
        def _(j):
            step = [(unroll * j + u, base + STRIDE * (unroll * j + u)) for u in range(unroll)]
            if before is not None:
                for i, entry in step:
                    before(number, i, entry)
            for i, entry in step:
                block = block_of(number, i, entry)
                piece = pieces[side][plan[entry + 2]]
                use(entry, jnp.dot(block, piece, preferred_element_type=jnp.float32))
            if then is not None:
                for i, entry in step:
                    then(entry)


def add_products(plan, base, ends, part, block_of, pieces, total, before=None):
    def use(entry, value):
        total[plan[entry + 1]] += value

    each_product(plan, base, ends, part, block_of, pieces, use, before=before)


def split_sides(pieces, vec):
    middle = vec.shape[-1] // 2
    column = lax.broadcasted_iota(jnp.int32, (1, vec.shape[-1]), 1)
    for side in range(2):
        keep = jnp.where((column // middle) == side, 1.0, 0.0).astype(jnp.bfloat16)
        for p in range(vec.shape[1]):
            vec[side, p] = pieces[p] * keep


def joined(total, k):
    one, two = total[2 * k], total[2 * k + 1]
    low = lax.broadcasted_iota(jnp.int32, one.shape, 1) < one.shape[1] // 2
    return jnp.where(low, one, two) + pltpu.roll(
        jnp.where(low, two, one), one.shape[1] // 2, axis=1
    )


def first_sent_kernel(
    lay, plan, tile_a, tile_b, pieces, start, out, blocks, vec, total, held, held_sem, sems
):
    n_row = out.shape[0]
    begin, wait = fetches(plan, lay.load_at, 1, 4, lay.loads, (tile_a, tile_b), blocks, sems)
    begin()
    copy = pltpu.make_async_copy(start, held, held_sem)
    copy.start()
    split_sides(pieces, vec)
    total[...] = jnp.zeros_like(total)

    def before(side, i, entry):
        @pl.when(plan[entry + 3] == FIRST)
        def _():
            wait(plan[entry])

    add_products(
        plan,
        lay.sent_at,
        2,
        lay.sends,
        lambda side, i, entry: blocks[plan[entry]],
        (vec.at[0], vec.at[1]),
        total,
        before,
    )
    copy.wait()
    for k in range(n_row):
        value = joined(total, k) - center_value * held[k].astype(jnp.float32)
        out[k] = (value / half_width).astype(jnp.bfloat16)


def second_sent_kernel(
    lay, plan, blocks, pieces, current, previous, out, vec, total, held, held_sem, ready, out_sems
):
    n_row = out.shape[0]
    copy = pltpu.make_async_copy(previous, held, held_sem)
    copy.start()
    split_sides(pieces, vec)
    total[...] = jnp.zeros_like(total)
    add_products(
        plan,
        lay.sent_at,
        2,
        lay.sends,
        lambda side, i, entry: blocks[plan[entry]],
        (vec.at[0], vec.at[1]),
        total,
    )
    copy.wait()

    def put(k):
        return pltpu.make_async_copy(ready.at[k], out.at[k], out_sems.at[k])

    for k in range(n_row):
        value = joined(total, k) - center_value * current[k].astype(jnp.float32)
        ready[k] = (value - held[k].astype(jnp.float32)).astype(jnp.bfloat16)
        put(k).start()
    for k in range(n_row):
        put(k).wait()


def whole_columns(half, mine, other, vec, at):
    n_row, _, width = mine.shape
    middle = width // 2

    @pl.when(half == 0)
    def _():
        for p in range(n_row):
            one, two = mine[p], other[p]
            vec[0, p, :, at : at + width] = jnp.concatenate([one[:, :middle], two[:, middle:]], axis=1)
            vec[1, p, :, at : at + width] = jnp.concatenate([one[:, middle:], two[:, :middle]], axis=1)

    @pl.when(half != 0)
    def _():
        for p in range(n_row):
            one, two = mine[p], other[p]
            vec[0, p, :, at : at + width] = jnp.concatenate([two[:, middle:], one[:, :middle]], axis=1)
            vec[1, p, :, at : at + width] = jnp.concatenate([two[:, :middle], one[:, middle:]], axis=1)


def prime_kernel(vectors, total, own, sem):
    _, block_size, double = total.shape
    width = double // 2
    copy = pltpu.make_async_copy(vectors, own, sem)
    copy.start()
    copy.wait()

    @pl.loop(0, vectors.shape[0] // block_size)
    def _(b):
        at = pl.ds(pl.multiple_of(b * block_size, block_size), block_size)
        value = own[at, :].astype(jnp.float32)
        total[b, :, :width] = -center_value * value
        total[b, :, width:] = -value


def early_kernel(
    lay,
    plan,
    tile_a,
    tile_b,
    q1,
    q1_other,
    q2,
    q2_other,
    start,
    base,
    total,
    vec,
    own,
    blocks,
    sems,
    row_sems,
):
    piece_blocks, block_size, width = base.shape
    begin, wait = fetches(plan, HEAD, STRIDE, 0, lay.slots, (tile_a, tile_b), blocks, sems)
    begin()
    whole_columns(plan[7], q1, q1_other, vec, 0)
    whole_columns(plan[7], q2, q2_other, vec, width)

    def rows(b):
        return pl.ds(pl.multiple_of(b * block_size, block_size), block_size)

    def put(b):
        return pltpu.make_async_copy(own.at[rows(b)], base.at[b], row_sems.at[b])

    add_products(
        plan,
        HEAD,
        0,
        lay.slots,
        lambda side, i, entry: blocks[i],
        (vec.at[0], vec.at[1]),
        total,
        lambda side, i, entry: wait(i),
    )

    @pl.loop(0, piece_blocks)
    def _(b):
        first = (total[b, :, :width] / half_width).astype(jnp.bfloat16).astype(jnp.float32)
        second = total[b, :, width:] - center_value * first
        second = second.astype(jnp.bfloat16).astype(jnp.float32)
        own[rows(b), :] = (-center_value * second - first).astype(jnp.bfloat16)
        put(b).start()

    @pl.loop(0, piece_blocks)
    def _(b):
        put(b).wait()


def last_kernel(
    lay, plan, blocks, tile_a, tile_b, mine, other, base, out, vec, total, own, blocks_b, sems, row_sems
):
    piece_blocks = base.shape[0]
    begin, own_end = lay.slots, plan[0]

    def fetch(tile, i):
        slot = plan[HEAD + STRIDE * i]
        return pltpu.make_async_copy(
            tile.at[slot], blocks_b.at[i - LEAD], sems.at[i - LEAD]
        )

    @pl.loop(LEAD, own_end)
    def _(i):
        fetch(tile_a, i).start()

    @pl.loop(begin, plan[1])
    def _(i):
        fetch(tile_b, i).start()

    def put(source, b):
        return pltpu.make_async_copy(source.at[b], out.at[b], row_sems.at[b])

    @pl.loop(0, plan[6])
    def _(i):
        b = plan[lay.bare_at + i]
        put(base, b).start()

    whole_columns(plan[7], mine, other, vec, 0)

    def use(entry, value):
        row = plan[entry + 1]
        marks = plan[entry + 3]
        start = base[jnp.minimum(row, piece_blocks - 1)].astype(jnp.float32)
        value = jnp.where(lax.rem(marks, LAST) == FIRST, start, total[row]) + value
        total[row] = value
        own[row] = value.astype(jnp.bfloat16)

    def then(entry):
        @pl.when(plan[entry + 3] >= LAST)
        def _():
            put(own, plan[entry + 1]).start()

    def block_of(number, i, entry):
        return blocks[i] if number == 0 else blocks_b[i - LEAD]

    def before(number, i, entry):
        if number > 0:
            fetch(tile_a, i).wait()

    segments = [
        (0, 0, jnp.minimum(own_end, LEAD)),
        (0, LEAD, own_end),
        (1, begin, plan[1]),
    ]
    each_product(
        plan,
        HEAD,
        0,
        lay.slots,
        block_of,
        (vec.at[0], vec.at[1]),
        use,
        then,
        before,
        segments,
    )

    @pl.loop(0, piece_blocks)
    def _(b):
        put(own, b).wait()


def after(value, *others):
    return lax.optimization_barrier((value, *others))[0]


def call(kernel, out, args, spaces, scratch, mib, name, estimate=None, aliases=None):
    args = [
        pltpu.with_memory_space_constraint(arg, space) if space in (VMEM, HBM) or tied else arg
        for arg, (space, tied) in zip(args, spaces)
    ]
    return pl.pallas_call(
        kernel,
        out_shape=[space(shape, dtype) for shape, dtype, space in out],
        in_specs=[spec(space) for space, _ in spaces],
        out_specs=[spec(space) for _, _, space in out],
        scratch_shapes=scratch,
        compiler_params=params(mib),
        cost_estimate=estimate,
        input_output_aliases=aliases or {},
        name=name,
    )(*args)


HERE = (VMEM, True)
FAR = (HBM, True)
LIST = (SMEM, True)
SCALARS = (SMEM, False)
ANYWHERE = (pl.ANY, False)


def on_pair(vectors, tile_blocks, block_rows, block_cols, counts):
    n_row = lax.axis_size("row")
    tile = tile_blocks[0, 0]
    slot_rows = block_rows[0, 0]
    slot_cols = block_cols[0, 0]
    used = counts[0]
    slot_count, block_size, _ = tile.shape
    width = vectors.shape[1]
    piece_blocks = vectors.shape[0] // block_size

    across = functools.partial(lax.ppermute, axis_name="col", perm=[(0, 1), (1, 0)])

    needed = jnp.max(
        jnp.where(
            slot_cols[None, :] // piece_blocks == jnp.arange(n_row)[:, None],
            slot_cols[None, :] % piece_blocks,
            0,
        ),
        axis=1,
        keepdims=True,
    )
    exchange = functools.partial(
        lax.all_to_all, axis_name="row", split_axis=0, concat_axis=0, tiled=True
    )
    wanted = exchange(jnp.broadcast_to(needed, (n_row, LANES)))
    sent_shape = (n_row, block_size, width)
    (sent,) = call(
        functools.partial(pick_kernel, n_row, block_size),
        [(sent_shape, jnp.bfloat16, VMEM)],
        (wanted, vectors),
        (SCALARS, FAR),
        [DMA((n_row,))],
        2,
        "pick",
    )
    tile_other = across(tile)
    sent_other = across(sent)
    wanted_other = across(after(wanted, sent))
    meta = jnp.concatenate([slot_rows, slot_cols, used])
    meta_other = across(after(meta, sent))
    packed = call(
        pack_kernel,
        [(sent_shape, jnp.bfloat16, HBM)],
        (sent, sent_other),
        (HERE, HERE),
        [VMEM(sent_shape, jnp.bfloat16), DMA((n_row,))],
        4,
        "pack",
    )[0]

    lay = layout_for(slot_count, n_row, piece_blocks)
    list_shape = ((lay.size,), jnp.int32)
    own_list, other_list = call(
        functools.partial(plan_kernel, n_row, piece_blocks, lay),
        [(*list_shape, HBM)] * 2,
        (wanted, after(wanted_other, packed), meta, meta_other),
        (SCALARS,) * 4,
        [
            SMEM((2 * lay.size,), jnp.int32),
            SMEM((2 * n_row,), jnp.int32),
            SMEM((piece_blocks + 1,), jnp.int32),
            DMA((2,)),
        ],
        2,
        "plan",
    )
    q1 = exchange(after(packed, own_list))
    plan = call(
        settle_kernel,
        [(*list_shape, SMEM)],
        (own_list, across(after(other_list, packed))),
        (ANYWHERE, ANYWHERE),
        [DMA],
        2,
        "settle",
    )[0]

    def load(cue, array):
        return call(
            load_kernel,
            [
                ((LEAD, block_size, block_size), jnp.bfloat16, VMEM),
                (array.shape, array.dtype, VMEM),
            ],
            (after(plan, cue), tile, array),
            (LIST, FAR, FAR),
            [DMA((LEAD,)), DMA],
            2,
            "load",
        )

    def cost(products, rows):
        size = block_size * width
        return pl.CostEstimate(
            flops=2 * products * block_size * size,
            bytes_accessed=2 * (products * block_size * block_size + 3 * rows * size),
            transcendentals=0,
        )

    sums = [
        VMEM((2, n_row, block_size, width), jnp.bfloat16),
        VMEM((2 * n_row + 1, block_size, width), jnp.float32),
    ]

    def first_blocks(*args):
        return call(
            functools.partial(first_sent_kernel, lay),
            [
                (sent_shape, jnp.bfloat16, VMEM),
                ((2 * lay.loads, block_size, block_size), jnp.bfloat16, VMEM),
            ],
            (plan, tile, tile_other, *args),
            (LIST, FAR, ANYWHERE, HERE, FAR),
            sums + [VMEM(sent_shape, jnp.bfloat16), DMA, DMA((2 * lay.loads,))],
            8,
            "sent",
            cost(n_row, n_row),
        )

    def second_blocks(*args):
        return call(
            functools.partial(second_sent_kernel, lay),
            [(sent_shape, jnp.bfloat16, HBM)],
            (plan, *args),
            (LIST, HERE, HERE, HERE, FAR),
            sums
            + [VMEM(sent_shape, jnp.bfloat16), DMA, VMEM(sent_shape, jnp.bfloat16), DMA((n_row,))],
            8,
            "sent",
            cost(n_row, n_row),
        )[0]

    base_shape = (piece_blocks, block_size, width)

    sums_shape = ((piece_blocks + 1, block_size, 2 * width), jnp.float32, VMEM)

    def early(*args):
        return call(
            functools.partial(early_kernel, lay),
            [(base_shape, jnp.bfloat16, HBM), sums_shape],
            (plan, tile, tile_other, *args),
            (LIST, FAR, ANYWHERE, HERE, HERE, HERE, HERE, HERE),
            [
                VMEM((2, n_row, block_size, 2 * width), jnp.bfloat16),
                VMEM(vectors.shape, jnp.bfloat16),
                VMEM((2 * lay.slots, block_size, block_size), jnp.bfloat16),
                DMA((2 * lay.slots,)),
                DMA((piece_blocks,)),
            ],
            18,
            "early",
            cost(2 * slot_count, 2 * piece_blocks),
            {7: 1},
        )[0]

    def last(blocks, *args):
        rows = (piece_blocks + 1, block_size, width)
        (out,) = call(
            functools.partial(last_kernel, lay),
            [(base_shape, jnp.bfloat16, HBM)],
            (plan, blocks, tile, tile_other, *args),
            (LIST, HERE, FAR, ANYWHERE, HERE, HERE, HERE),
            [
                VMEM((2, n_row, block_size, width), jnp.bfloat16),
                VMEM(rows, jnp.float32),
                VMEM(rows, jnp.bfloat16),
                VMEM((2 * lay.slots - LEAD, block_size, block_size), jnp.bfloat16),
                DMA((2 * lay.slots - LEAD,)),
                DMA((piece_blocks,)),
            ],
            18,
            "last",
            cost(slot_count, piece_blocks),
        )
        return out.reshape(vectors.shape)

    q1 = after(q1, plan)
    first_sent, blocks = first_blocks(q1, packed)
    q2 = exchange(first_sent)
    second_sent = second_blocks(blocks, q2, first_sent, packed)
    q1_other = across(after(q1, second_sent))
    q2_other = across(after(q2, second_sent))
    (start,) = call(
        prime_kernel,
        [sums_shape],
        (after(vectors, second_sent),),
        (FAR,),
        [VMEM(vectors.shape, jnp.bfloat16), DMA],
        4,
        "prime",
        cost(0, 3 * piece_blocks),
    )
    base = early(q1, q1_other, q2, q2_other, start)
    q3 = after(exchange(second_sent), base)
    q3_other = across(q3)
    blocks, base = load(q3, base)
    return last(blocks, q3, q3_other, base)


def on_any(vectors, tile_blocks, block_rows, block_cols, counts):
    n_row = lax.axis_size("row")
    n_col = lax.axis_size("col")
    tile_data = tile_blocks[0, 0]
    slot_rows = block_rows[0, 0]
    slot_cols = block_cols[0, 0]
    used = counts[0, 0]
    block_size = tile_data.shape[-1]
    width = vectors.shape[1]
    piece_blocks = vectors.shape[0] // block_size
    row_blocks = piece_blocks * n_col
    slot_count = tile_data.shape[0]
    live = (jnp.arange(slot_count) < used).astype(jnp.float32)
    onehot = (slot_rows[None, :] == jnp.arange(row_blocks)[:, None]).astype(jnp.float32) * live[
        None, :
    ]
    source_piece = slot_cols // piece_blocks
    offset = slot_cols % piece_blocks
    needed = jnp.max(
        jnp.where(source_piece[None, :] == jnp.arange(n_row)[:, None], offset[None, :], 0), axis=1
    )
    wanted = lax.all_to_all(
        needed.reshape(n_row, 1), "row", split_axis=0, concat_axis=0, tiled=True
    ).reshape(n_row)

    def apply_tiles(current):
        own_blocks = current.reshape(piece_blocks, block_size, width)
        outgoing = jnp.take(own_blocks, wanted, axis=0)
        received = lax.all_to_all(outgoing, "row", split_axis=0, concat_axis=0, tiled=True)
        vec_blocks = jnp.take(received, source_piece, axis=0)
        products = jnp.einsum(
            "sij,sjk->sik", tile_data, vec_blocks, preferred_element_type=jnp.float32
        )
        term = jnp.einsum("ls,sik->lik", onehot, products, precision=lax.Precision.HIGHEST)
        term = term.reshape(row_blocks * block_size, width)
        return lax.psum_scatter(
            term.astype(jnp.bfloat16), "col", scatter_dimension=0, tiled=True
        ).astype(jnp.float32)

    previous = vectors
    applied = apply_tiles(vectors)
    current = ((applied - center_value * previous.astype(jnp.float32)) / half_width).astype(
        jnp.bfloat16
    )
    for repeat in range(DEGREE - 1):
        applied = apply_tiles(current)
        following = (
            2.0 * (applied - center_value * current.astype(jnp.float32)) / half_width
            - previous.astype(jnp.float32)
        ).astype(jnp.bfloat16)
        previous, current = (current, following)
    return current


def solution(mesh):
    n_row, n_col = mesh.shape["row"], mesh.shape["col"]
    paired = n_col == 2 and n_row & (n_row - 1) == 0
    return jax.shard_map(
        on_pair if paired else on_any,
        mesh=mesh,
        in_specs=(
            P(("row", "col"), "vec"),
            P("row", "col", None, None, None),
            P("row", "col", None),
            P("row", "col", None),
            P("row", "col"),
        ),
        out_specs=P(("row", "col"), "vec"),
        check_vma=False,
    )
```

```python
import functools
import typing

import jax
import jax.numpy as jnp
from jax import lax
from jax.experimental import pallas as pl
from jax.experimental.pallas import tpu as pltpu
from jax.sharding import PartitionSpec as P

DEGREE = 3

center_value = 0.5
half_width = 2.0

VMEM = pltpu.VMEM
SMEM = pltpu.SMEM
HBM = pltpu.HBM
DMA = pltpu.SemaphoreType.DMA
LANES = 128
FEW = 4
MANY = 4
LEAD = 3 * MANY
HEAD = 8
STRIDE = 4
FIRST = 1
LAST = 2


def spec(space):
    return pl.BlockSpec(memory_space=space)


def params(mib):
    return pltpu.CompilerParams(vmem_limit_bytes=mib * 1024 * 1024)


def round_up(n, step):
    return (n + step - 1) // step * step


def core_number():
    return lax.axis_index("col")


class Layout(typing.NamedTuple):
    slots: int
    sends: int
    loads: int
    sent_at: int
    load_at: int
    bare_at: int
    size: int


def layout_for(slot_count, n_row, piece_blocks):
    slots = round_up(slot_count, MANY) + MANY
    sends = round_up(2 * n_row * n_row, FEW) + FEW
    sent_at = HEAD + STRIDE * 2 * slots
    load_at = sent_at + STRIDE * 2 * sends
    bare_at = load_at + 2 * (slot_count + 1)
    size = round_up(bare_at + piece_blocks, 8 * LANES)
    return Layout(slots, sends, slot_count + 1, sent_at, load_at, bare_at, size)


def plan_kernel(
    n_row,
    piece_blocks,
    lay,
    wanted_a,
    wanted_b,
    meta_a,
    meta_b,
    own,
    other,
    out,
    asked,
    seen,
    sems,
):
    slot_count = (meta_a.shape[0] - 1) // 2

    def put(at, *values):
        for i, value in enumerate(values):
            out[at + i] = value

    def scan(tile, meta):
        used = meta[2 * slot_count]


        def step(s, carry):
            ends, sent, load = carry
            row = meta[s]
            piece = meta[slot_count + s] // piece_blocks
            live = s < used
            half = row // piece_blocks
            local = row - half * piece_blocks
            lower = half == 0
            part = jnp.where(lower, tile, 1 - tile)
            at = HEAD + STRIDE * (part * lay.slots + jnp.where(lower, ends[0], ends[1]))
            base = half * lay.size
            put(base + at, s, local, piece)
            sought = jnp.where(live, local, -1)
            hits = [(asked[half * n_row + k] == sought).astype(jnp.int32) for k in range(n_row)]
            found = sum(hits)

            @pl.when(found > 0)
            def _():
                for core in range(2):
                    mine = tile if core == 0 else 1 - tile
                    side = half if core == 0 else 1 - half
                    first = core * lay.size
                    out[first + lay.load_at + mine * lay.loads + load] = s

                    place = sent
                    for k in range(n_row):
                        put(
                            first + lay.sent_at + STRIDE * (mine * lay.sends + place),
                            mine * lay.loads + load,
                            2 * k + side,
                            piece,
                            jnp.where(place == sent, FIRST, 0),
                        )
                        place = place + hits[k]

            one = live.astype(jnp.int32)
            ends = (ends[0] + jnp.where(lower, one, 0), ends[1] + jnp.where(lower, 0, one))
            return ends, sent + found, load + jnp.where(found > 0, 1, 0)

        zero = jnp.int32(0)
        ends, sent, load = lax.fori_loop(0, slot_count, step, ((zero, zero), zero, zero))
        for core in range(2):
            mine = tile if core == 0 else 1 - tile
            base = core * lay.size
            for i, (at, begin, end, unit, spare) in enumerate(
                (
                    (HEAD, mine * lay.slots, ends[core], MANY, piece_blocks),
                    (lay.sent_at, mine * lay.sends, sent, FEW, 2 * n_row),
                )
            ):
                for u in range(unit - 1):
                    put(base + at + STRIDE * (begin + end + u), 0, spare, 0, 0)
                out[base + 2 * i + mine] = begin + (end + unit - 1) // unit * unit
            out[base + 4 + mine] = mine * lay.loads + load

    def mark(core):
        base = core * lay.size
        for b in range(piece_blocks + 1):
            seen[b] = 0
        for part in range(2):

            @pl.loop(part * lay.slots, out[base + part])
            def _(i):
                entry = base + HEAD + STRIDE * i
                row = out[entry + 1]
                out[entry + 3] = jnp.where(seen[row] == 0, FIRST, 0)
                seen[row] = entry

        def close(b, bare):
            entry = seen[b]
            out[base + lay.bare_at + bare] = b

            @pl.when(entry > 0)
            def _():
                out[entry + 3] = out[entry + 3] + LAST

            return bare + jnp.where(entry == 0, 1, 0)

        out[base + 6] = lax.fori_loop(0, piece_blocks, close, jnp.int32(0))
        out[base + 7] = core

    @pl.when(core_number() == 0)
    def _():
        for half, wanted in enumerate((wanted_a, wanted_b)):
            for k in range(n_row):
                asked[half * n_row + k] = wanted[k, 0]
        scan(0, meta_a)
        scan(1, meta_b)
        for core in range(2):
            mark(core)
        copies = [
            pltpu.make_async_copy(out.at[pl.ds(core * lay.size, lay.size)], target, sems.at[core])
            for core, target in enumerate((own, other))
        ]
        for copy in copies:
            copy.start()
        for copy in copies:
            copy.wait()


def settle_kernel(own, handed, out, sem):
    for half, source in enumerate((own, handed)):

        @pl.when(core_number() == half)
        def _():
            copy = pltpu.make_async_copy(source, out, sem)
            copy.start()
            copy.wait()


def pick_kernel(n_row, block_size, wanted, vectors, out, sems):
    def fetch(k):
        at = pl.multiple_of(wanted[k, 0] * block_size, block_size)
        return pltpu.make_async_copy(vectors.at[pl.ds(at, block_size)], out.at[k], sems.at[k])

    for k in range(n_row):
        fetch(k).start()
    for k in range(n_row):
        fetch(k).wait()


def pack_kernel(picked, picked_b, out, held, sem):
    n_row, _, width = picked.shape
    middle = width // 2

    def put(k):
        return pltpu.make_async_copy(held.at[k], out.at[k], sem)

    for half in range(2):

        @pl.when(core_number() == half)
        def _():
            part = slice(half * middle, (half + 1) * middle)
            for k in range(n_row):
                held[k] = jnp.concatenate([picked[k, :, part], picked_b[k, :, part]], axis=1)
                put(k).start()

    pltpu.make_async_copy(held, out, sem).wait()


def fetches(plan, base, stride, ends, part, tiles, blocks, sems):
    def copy(tile, i):
        slot = plan[base + stride * i]
        return pltpu.make_async_copy(tile.at[slot], blocks.at[i], sems.at[i])

    def start():
        for side, tile in enumerate(tiles):

            @pl.loop(side * part, plan[ends + side])
            def _(i):
                copy(tile, i).start()

    def wait(i):
        copy(tiles[0], i).wait()

    return start, wait


def load_kernel(plan, tile_a, array, blocks, held, sems, held_sem):
    whole = pltpu.make_async_copy(array, held, held_sem)
    whole.start()
    number = jnp.minimum(plan[0], LEAD)

    def copy(i):
        return pltpu.make_async_copy(
            tile_a.at[plan[HEAD + STRIDE * i]], blocks.at[i], sems.at[i]
        )

    @pl.loop(0, number)
    def _(i):
        copy(i).start()

    @pl.loop(0, number)
    def _(i):
        copy(i).wait()

    whole.wait()


def each_product(
    plan, base, ends, part, block_of, pieces, use, then=None, before=None, segments=None
):
    unroll = MANY if base == HEAD else FEW

    if segments is None:
        segments = [(side, side * part, plan[ends + side]) for side in range(2)]
    for number, (side, begin, end) in enumerate(segments):

        @pl.loop(begin // unroll, end // unroll)
        def _(j):
            step = [(unroll * j + u, base + STRIDE * (unroll * j + u)) for u in range(unroll)]
            if before is not None:
                for i, entry in step:
                    before(number, i, entry)
            for i, entry in step:
                block = block_of(number, i, entry)
                piece = pieces[side][plan[entry + 2]]
                use(entry, jnp.dot(block, piece, preferred_element_type=jnp.float32))
            if then is not None:
                for i, entry in step:
                    then(entry)


def add_products(plan, base, ends, part, block_of, pieces, total, before=None):
    def use(entry, value):
        total[plan[entry + 1]] += value

    each_product(plan, base, ends, part, block_of, pieces, use, before=before)


def split_sides(pieces, vec):
    middle = vec.shape[-1] // 2
    column = lax.broadcasted_iota(jnp.int32, (1, vec.shape[-1]), 1)
    for side in range(2):
        keep = jnp.where((column // middle) == side, 1.0, 0.0).astype(jnp.bfloat16)
        for p in range(vec.shape[1]):
            vec[side, p] = pieces[p] * keep


def joined(total, k):
    one, two = total[2 * k], total[2 * k + 1]
    low = lax.broadcasted_iota(jnp.int32, one.shape, 1) < one.shape[1] // 2
    return jnp.where(low, one, two) + pltpu.roll(
        jnp.where(low, two, one), one.shape[1] // 2, axis=1
    )


def first_sent_kernel(
    lay, plan, tile_a, tile_b, pieces, start, out, blocks, vec, total, held, held_sem, sems
):
    n_row = out.shape[0]
    begin, wait = fetches(plan, lay.load_at, 1, 4, lay.loads, (tile_a, tile_b), blocks, sems)
    begin()
    copy = pltpu.make_async_copy(start, held, held_sem)
    copy.start()
    split_sides(pieces, vec)
    total[...] = jnp.zeros_like(total)

    def before(side, i, entry):
        @pl.when(plan[entry + 3] == FIRST)
        def _():
            wait(plan[entry])

    add_products(
        plan,
        lay.sent_at,
        2,
        lay.sends,
        lambda side, i, entry: blocks[plan[entry]],
        (vec.at[0], vec.at[1]),
        total,
        before,
    )
    copy.wait()
    for k in range(n_row):
        value = joined(total, k) - center_value * held[k].astype(jnp.float32)
        out[k] = (value / half_width).astype(jnp.bfloat16)


def second_sent_kernel(
    lay, plan, blocks, pieces, current, previous, out, vec, total, held, held_sem, ready, out_sem
):
    n_row = out.shape[0]
    copy = pltpu.make_async_copy(previous, held, held_sem)
    copy.start()
    split_sides(pieces, vec)
    total[...] = jnp.zeros_like(total)
    add_products(
        plan,
        lay.sent_at,
        2,
        lay.sends,
        lambda side, i, entry: blocks[plan[entry]],
        (vec.at[0], vec.at[1]),
        total,
    )
    copy.wait()

    def put(k):
        return pltpu.make_async_copy(ready.at[k], out.at[k], out_sem)

    for k in range(n_row):
        value = joined(total, k) - center_value * current[k].astype(jnp.float32)
        ready[k] = (value - held[k].astype(jnp.float32)).astype(jnp.bfloat16)
        put(k).start()
    pltpu.make_async_copy(ready, out, out_sem).wait()


def whole_columns(half, mine, other, vec, at):
    n_row, _, width = mine.shape
    middle = width // 2

    @pl.when(half == 0)
    def _():
        for p in range(n_row):
            one, two = mine[p], other[p]
            vec[0, p, :, at : at + width] = jnp.concatenate([one[:, :middle], two[:, middle:]], axis=1)
            vec[1, p, :, at : at + width] = jnp.concatenate([one[:, middle:], two[:, :middle]], axis=1)

    @pl.when(half != 0)
    def _():
        for p in range(n_row):
            one, two = mine[p], other[p]
            vec[0, p, :, at : at + width] = jnp.concatenate([two[:, middle:], one[:, :middle]], axis=1)
            vec[1, p, :, at : at + width] = jnp.concatenate([two[:, :middle], one[:, middle:]], axis=1)


def prime_kernel(vectors, total, own, sem):
    _, block_size, double = total.shape
    width = double // 2
    copy = pltpu.make_async_copy(vectors, own, sem)
    copy.start()
    copy.wait()

    @pl.loop(0, vectors.shape[0] // block_size)
    def _(b):
        at = pl.ds(pl.multiple_of(b * block_size, block_size), block_size)
        value = own[at, :].astype(jnp.float32)
        total[b, :, :width] = -center_value * value
        total[b, :, width:] = -value


def early_kernel(
    lay,
    plan,
    tile_a,
    tile_b,
    q1,
    q1_other,
    q2,
    q2_other,
    start,
    base,
    total,
    vec,
    own,
    blocks,
    sems,
    row_sems,
):
    piece_blocks, block_size, width = base.shape
    begin, wait = fetches(plan, HEAD, STRIDE, 0, lay.slots, (tile_a, tile_b), blocks, sems)
    begin()
    whole_columns(plan[7], q1, q1_other, vec, 0)
    whole_columns(plan[7], q2, q2_other, vec, width)

    def rows(b):
        return pl.ds(pl.multiple_of(b * block_size, block_size), block_size)

    def put(b):
        return pltpu.make_async_copy(own.at[rows(b)], base.at[b], row_sems.at[b])

    add_products(
        plan,
        HEAD,
        0,
        lay.slots,
        lambda side, i, entry: blocks[i],
        (vec.at[0], vec.at[1]),
        total,
        lambda side, i, entry: wait(i),
    )

    @pl.loop(0, piece_blocks)
    def _(b):
        first = (total[b, :, :width] / half_width).astype(jnp.bfloat16).astype(jnp.float32)
        second = total[b, :, width:] - center_value * first
        second = second.astype(jnp.bfloat16).astype(jnp.float32)
        own[rows(b), :] = (-center_value * second - first).astype(jnp.bfloat16)
        put(b).start()

    @pl.loop(0, piece_blocks)
    def _(b):
        put(b).wait()


def last_kernel(
    lay, plan, blocks, tile_a, tile_b, mine, other, base, out, vec, total, own, blocks_b, sems, out_sem
):
    piece_blocks = base.shape[0]
    begin, own_end = lay.slots, plan[0]

    def fetch(tile, i):
        slot = plan[HEAD + STRIDE * i]
        return pltpu.make_async_copy(
            tile.at[slot], blocks_b.at[i - LEAD], sems.at[i - LEAD]
        )

    @pl.loop(LEAD, own_end)
    def _(i):
        fetch(tile_a, i).start()

    @pl.loop(begin, plan[1])
    def _(i):
        fetch(tile_b, i).start()

    def put(source, b):
        return pltpu.make_async_copy(source.at[b], out.at[b], out_sem)

    @pl.loop(0, plan[6])
    def _(i):
        b = plan[lay.bare_at + i]
        put(base, b).start()

    whole_columns(plan[7], mine, other, vec, 0)

    def use(entry, value):
        row = plan[entry + 1]
        marks = plan[entry + 3]
        start = base[jnp.minimum(row, piece_blocks - 1)].astype(jnp.float32)
        value = jnp.where(lax.rem(marks, LAST) == FIRST, start, total[row]) + value
        total[row] = value
        own[row] = value.astype(jnp.bfloat16)

    def then(entry):
        @pl.when(plan[entry + 3] >= LAST)
        def _():
            put(own, plan[entry + 1]).start()

    def block_of(number, i, entry):
        return blocks[i] if number == 0 else blocks_b[i - LEAD]

    def before(number, i, entry):
        if number > 0:
            fetch(tile_a, i).wait()

    segments = [
        (0, 0, jnp.minimum(own_end, LEAD)),
        (0, LEAD, own_end),
        (1, begin, plan[1]),
    ]
    each_product(
        plan,
        HEAD,
        0,
        lay.slots,
        block_of,
        (vec.at[0], vec.at[1]),
        use,
        then,
        before,
        segments,
    )

    pltpu.make_async_copy(base, out, out_sem).wait()


def after(value, *others):
    return lax.optimization_barrier((value, *others))[0]


def call(kernel, out, args, spaces, scratch, mib, name, estimate=None, aliases=None):
    args = [
        pltpu.with_memory_space_constraint(arg, space) if space in (VMEM, HBM) or tied else arg
        for arg, (space, tied) in zip(args, spaces)
    ]
    return pl.pallas_call(
        kernel,
        out_shape=[space(shape, dtype) for shape, dtype, space in out],
        in_specs=[spec(space) for space, _ in spaces],
        out_specs=[spec(space) for _, _, space in out],
        scratch_shapes=scratch,
        compiler_params=params(mib),
        cost_estimate=estimate,
        input_output_aliases=aliases or {},
        name=name,
    )(*args)


HERE = (VMEM, True)
FAR = (HBM, True)
LIST = (SMEM, True)
SCALARS = (SMEM, False)
ANYWHERE = (pl.ANY, False)


def on_pair(vectors, tile_blocks, block_rows, block_cols, counts):
    n_row = lax.axis_size("row")
    tile = tile_blocks[0, 0]
    slot_rows = block_rows[0, 0]
    slot_cols = block_cols[0, 0]
    used = counts[0]
    slot_count, block_size, _ = tile.shape
    width = vectors.shape[1]
    piece_blocks = vectors.shape[0] // block_size

    across = functools.partial(lax.ppermute, axis_name="col", perm=[(0, 1), (1, 0)])

    needed = jnp.max(
        jnp.where(
            slot_cols[None, :] // piece_blocks == jnp.arange(n_row)[:, None],
            slot_cols[None, :] % piece_blocks,
            0,
        ),
        axis=1,
        keepdims=True,
    )
    exchange = functools.partial(
        lax.all_to_all, axis_name="row", split_axis=0, concat_axis=0, tiled=True
    )
    wanted = exchange(jnp.broadcast_to(needed, (n_row, LANES)))
    sent_shape = (n_row, block_size, width)
    (sent,) = call(
        functools.partial(pick_kernel, n_row, block_size),
        [(sent_shape, jnp.bfloat16, VMEM)],
        (wanted, vectors),
        (SCALARS, FAR),
        [DMA((n_row,))],
        2,
        "pick",
    )
    tile_other = across(tile)
    sent_other = across(sent)
    wanted_other = across(after(wanted, sent))
    meta = jnp.concatenate([slot_rows, slot_cols, used])
    meta_other = across(after(meta, sent))
    packed = call(
        pack_kernel,
        [(sent_shape, jnp.bfloat16, HBM)],
        (sent, sent_other),
        (HERE, HERE),
        [VMEM(sent_shape, jnp.bfloat16), DMA],
        4,
        "pack",
    )[0]

    lay = layout_for(slot_count, n_row, piece_blocks)
    list_shape = ((lay.size,), jnp.int32)
    own_list, other_list = call(
        functools.partial(plan_kernel, n_row, piece_blocks, lay),
        [(*list_shape, HBM)] * 2,
        (wanted, after(wanted_other, packed), meta, meta_other),
        (SCALARS,) * 4,
        [
            SMEM((2 * lay.size,), jnp.int32),
            SMEM((2 * n_row,), jnp.int32),
            SMEM((piece_blocks + 1,), jnp.int32),
            DMA((2,)),
        ],
        2,
        "plan",
    )
    q1 = exchange(after(packed, own_list))
    plan = call(
        settle_kernel,
        [(*list_shape, SMEM)],
        (own_list, across(after(other_list, packed))),
        (ANYWHERE, ANYWHERE),
        [DMA],
        2,
        "settle",
    )[0]

    def load(cue, array):
        return call(
            load_kernel,
            [
                ((LEAD, block_size, block_size), jnp.bfloat16, VMEM),
                (array.shape, array.dtype, VMEM),
            ],
            (after(plan, cue), tile, array),
            (LIST, FAR, FAR),
            [DMA((LEAD,)), DMA],
            2,
            "load",
        )

    def cost(products, rows):
        size = block_size * width
        return pl.CostEstimate(
            flops=2 * products * block_size * size,
            bytes_accessed=2 * (products * block_size * block_size + 3 * rows * size),
            transcendentals=0,
        )

    sums = [
        VMEM((2, n_row, block_size, width), jnp.bfloat16),
        VMEM((2 * n_row + 1, block_size, width), jnp.float32),
    ]

    def first_blocks(*args):
        return call(
            functools.partial(first_sent_kernel, lay),
            [
                (sent_shape, jnp.bfloat16, VMEM),
                ((2 * lay.loads, block_size, block_size), jnp.bfloat16, VMEM),
            ],
            (plan, tile, tile_other, *args),
            (LIST, FAR, ANYWHERE, HERE, FAR),
            sums + [VMEM(sent_shape, jnp.bfloat16), DMA, DMA((2 * lay.loads,))],
            8,
            "sent",
            cost(n_row, n_row),
        )

    def second_blocks(*args):
        return call(
            functools.partial(second_sent_kernel, lay),
            [(sent_shape, jnp.bfloat16, HBM)],
            (plan, *args),
            (LIST, HERE, HERE, HERE, FAR),
            sums
            + [VMEM(sent_shape, jnp.bfloat16), DMA, VMEM(sent_shape, jnp.bfloat16), DMA],
            8,
            "sent",
            cost(n_row, n_row),
        )[0]

    base_shape = (piece_blocks, block_size, width)

    sums_shape = ((piece_blocks + 1, block_size, 2 * width), jnp.float32, VMEM)

    def early(*args):
        return call(
            functools.partial(early_kernel, lay),
            [(base_shape, jnp.bfloat16, HBM), sums_shape],
            (plan, tile, tile_other, *args),
            (LIST, FAR, ANYWHERE, HERE, HERE, HERE, HERE, HERE),
            [
                VMEM((2, n_row, block_size, 2 * width), jnp.bfloat16),
                VMEM(vectors.shape, jnp.bfloat16),
                VMEM((2 * lay.slots, block_size, block_size), jnp.bfloat16),
                DMA((2 * lay.slots,)),
                DMA((piece_blocks,)),
            ],
            18,
            "early",
            cost(2 * slot_count, 2 * piece_blocks),
            {7: 1},
        )[0]

    def last(blocks, *args):
        rows = (piece_blocks + 1, block_size, width)
        (out,) = call(
            functools.partial(last_kernel, lay),
            [(base_shape, jnp.bfloat16, HBM)],
            (plan, blocks, tile, tile_other, *args),
            (LIST, HERE, FAR, ANYWHERE, HERE, HERE, HERE),
            [
                VMEM((2, n_row, block_size, width), jnp.bfloat16),
                VMEM(rows, jnp.float32),
                VMEM(rows, jnp.bfloat16),
                VMEM((2 * lay.slots - LEAD, block_size, block_size), jnp.bfloat16),
                DMA((2 * lay.slots - LEAD,)),
                DMA,
            ],
            18,
            "last",
            cost(slot_count, piece_blocks),
        )
        return out.reshape(vectors.shape)

    q1 = after(q1, plan)
    first_sent, blocks = first_blocks(q1, packed)
    q2 = exchange(first_sent)
    second_sent = second_blocks(blocks, q2, first_sent, packed)
    q1_other = across(after(q1, second_sent))
    q2_other = across(after(q2, second_sent))
    (start,) = call(
        prime_kernel,
        [sums_shape],
        (after(vectors, second_sent),),
        (FAR,),
        [VMEM(vectors.shape, jnp.bfloat16), DMA],
        4,
        "prime",
        cost(0, 3 * piece_blocks),
    )
    base = early(q1, q1_other, q2, q2_other, start)
    q3 = after(exchange(second_sent), base)
    q3_other = across(q3)
    blocks, base = load(q3, base)
    return last(blocks, q3, q3_other, base)


def on_any(vectors, tile_blocks, block_rows, block_cols, counts):
    n_row = lax.axis_size("row")
    n_col = lax.axis_size("col")
    tile_data = tile_blocks[0, 0]
    slot_rows = block_rows[0, 0]
    slot_cols = block_cols[0, 0]
    used = counts[0, 0]
    block_size = tile_data.shape[-1]
    width = vectors.shape[1]
    piece_blocks = vectors.shape[0] // block_size
    row_blocks = piece_blocks * n_col
    slot_count = tile_data.shape[0]
    live = (jnp.arange(slot_count) < used).astype(jnp.float32)
    onehot = (slot_rows[None, :] == jnp.arange(row_blocks)[:, None]).astype(jnp.float32) * live[
        None, :
    ]
    source_piece = slot_cols // piece_blocks
    offset = slot_cols % piece_blocks
    needed = jnp.max(
        jnp.where(source_piece[None, :] == jnp.arange(n_row)[:, None], offset[None, :], 0), axis=1
    )
    wanted = lax.all_to_all(
        needed.reshape(n_row, 1), "row", split_axis=0, concat_axis=0, tiled=True
    ).reshape(n_row)

    def apply_tiles(current):
        own_blocks = current.reshape(piece_blocks, block_size, width)
        outgoing = jnp.take(own_blocks, wanted, axis=0)
        received = lax.all_to_all(outgoing, "row", split_axis=0, concat_axis=0, tiled=True)
        vec_blocks = jnp.take(received, source_piece, axis=0)
        products = jnp.einsum(
            "sij,sjk->sik", tile_data, vec_blocks, preferred_element_type=jnp.float32
        )
        term = jnp.einsum("ls,sik->lik", onehot, products, precision=lax.Precision.HIGHEST)
        term = term.reshape(row_blocks * block_size, width)
        return lax.psum_scatter(
            term.astype(jnp.bfloat16), "col", scatter_dimension=0, tiled=True
        ).astype(jnp.float32)

    previous = vectors
    applied = apply_tiles(vectors)
    current = ((applied - center_value * previous.astype(jnp.float32)) / half_width).astype(
        jnp.bfloat16
    )
    for repeat in range(DEGREE - 1):
        applied = apply_tiles(current)
        following = (
            2.0 * (applied - center_value * current.astype(jnp.float32)) / half_width
            - previous.astype(jnp.float32)
        ).astype(jnp.bfloat16)
        previous, current = (current, following)
    return current


def solution(mesh):
    n_row, n_col = mesh.shape["row"], mesh.shape["col"]
    paired = n_col == 2 and n_row & (n_row - 1) == 0
    return jax.shard_map(
        on_pair if paired else on_any,
        mesh=mesh,
        in_specs=(
            P(("row", "col"), "vec"),
            P("row", "col", None, None, None),
            P("row", "col", None),
            P("row", "col", None),
            P("row", "col"),
        ),
        out_specs=P(("row", "col"), "vec"),
        check_vma=False,
    )
```

```python
import functools
import typing

import jax
import jax.numpy as jnp
from jax import lax
from jax.experimental import pallas as pl
from jax.experimental.pallas import tpu as pltpu
from jax.sharding import PartitionSpec as P

DEGREE = 3

center_value = 0.5
half_width = 2.0

VMEM = pltpu.VMEM
SMEM = pltpu.SMEM
HBM = pltpu.HBM
DMA = pltpu.SemaphoreType.DMA
LANES = 128
FEW = 4
MANY = 4
LEAD = 3 * MANY
HEAD = 8
STRIDE = 4
FIRST = 1
LAST = 2


def spec(space):
    return pl.BlockSpec(memory_space=space)


def params(mib):
    return pltpu.CompilerParams(vmem_limit_bytes=mib * 1024 * 1024)


def round_up(n, step):
    return (n + step - 1) // step * step


def core_number():
    return lax.axis_index("col")


class Layout(typing.NamedTuple):
    slots: int
    sends: int
    loads: int
    sent_at: int
    load_at: int
    bare_at: int
    size: int


def layout_for(slot_count, n_row, piece_blocks):
    slots = round_up(slot_count, MANY) + MANY
    sends = round_up(2 * n_row * n_row, FEW) + FEW
    sent_at = HEAD + STRIDE * 2 * slots
    load_at = sent_at + STRIDE * 2 * sends
    bare_at = load_at + 2 * (slot_count + 1)
    size = round_up(bare_at + piece_blocks, 8 * LANES)
    return Layout(slots, sends, slot_count + 1, sent_at, load_at, bare_at, size)


def plan_kernel(
    n_row,
    piece_blocks,
    lay,
    wanted_a,
    wanted_b,
    meta_a,
    meta_b,
    own,
    other,
    out,
    asked,
    seen,
    sems,
):
    slot_count = (meta_a.shape[0] - 1) // 2

    def put(at, *values):
        for i, value in enumerate(values):
            out[at + i] = value

    def scan(tile, meta):
        used = meta[2 * slot_count]


        def step(s, carry):
            ends, sent, load = carry
            row = meta[s]
            piece = meta[slot_count + s] // piece_blocks
            live = s < used
            half = row // piece_blocks
            local = row - half * piece_blocks
            lower = half == 0
            part = jnp.where(lower, tile, 1 - tile)
            at = HEAD + STRIDE * (part * lay.slots + jnp.where(lower, ends[0], ends[1]))
            base = half * lay.size
            put(base + at, s, local, piece)
            sought = jnp.where(live, local, -1)
            hits = [(asked[half * n_row + k] == sought).astype(jnp.int32) for k in range(n_row)]
            found = sum(hits)

            @pl.when(found > 0)
            def _():
                for core in range(2):
                    mine = tile if core == 0 else 1 - tile
                    side = half if core == 0 else 1 - half
                    first = core * lay.size
                    out[first + lay.load_at + mine * lay.loads + load] = s

                    place = sent
                    for k in range(n_row):
                        put(
                            first + lay.sent_at + STRIDE * (mine * lay.sends + place),
                            mine * lay.loads + load,
                            2 * k + side,
                            piece,
                            jnp.where(place == sent, FIRST, 0),
                        )
                        place = place + hits[k]

            one = live.astype(jnp.int32)
            ends = (ends[0] + jnp.where(lower, one, 0), ends[1] + jnp.where(lower, 0, one))
            return ends, sent + found, load + jnp.where(found > 0, 1, 0)

        zero = jnp.int32(0)
        ends, sent, load = lax.fori_loop(0, slot_count, step, ((zero, zero), zero, zero))
        for core in range(2):
            mine = tile if core == 0 else 1 - tile
            base = core * lay.size
            for i, (at, begin, end, unit, spare) in enumerate(
                (
                    (HEAD, mine * lay.slots, ends[core], MANY, piece_blocks),
                    (lay.sent_at, mine * lay.sends, sent, FEW, 2 * n_row),
                )
            ):
                for u in range(unit - 1):
                    put(base + at + STRIDE * (begin + end + u), 0, spare, 0, 0)
                out[base + 2 * i + mine] = begin + (end + unit - 1) // unit * unit
            out[base + 4 + mine] = mine * lay.loads + load

    def mark(core):
        base = core * lay.size
        for b in range(piece_blocks + 1):
            seen[b] = 0
        for part in range(2):

            @pl.loop(part * lay.slots, out[base + part])
            def _(i):
                entry = base + HEAD + STRIDE * i
                row = out[entry + 1]
                out[entry + 3] = jnp.where(seen[row] == 0, FIRST, 0)
                seen[row] = entry

        def close(b, bare):
            entry = seen[b]
            out[base + lay.bare_at + bare] = b

            @pl.when(entry > 0)
            def _():
                out[entry + 3] = out[entry + 3] + LAST

            return bare + jnp.where(entry == 0, 1, 0)

        out[base + 6] = lax.fori_loop(0, piece_blocks, close, jnp.int32(0))
        out[base + 7] = core

    @pl.when(core_number() == 0)
    def _():
        for half, wanted in enumerate((wanted_a, wanted_b)):
            for k in range(n_row):
                asked[half * n_row + k] = wanted[k, 0]
        scan(0, meta_a)
        scan(1, meta_b)
        for core in range(2):
            mark(core)
        copies = [
            pltpu.make_async_copy(out.at[pl.ds(core * lay.size, lay.size)], target, sems.at[core])
            for core, target in enumerate((own, other))
        ]
        for copy in copies:
            copy.start()
        for copy in copies:
            copy.wait()


def settle_kernel(own, handed, out, sem):
    for half, source in enumerate((own, handed)):

        @pl.when(core_number() == half)
        def _():
            copy = pltpu.make_async_copy(source, out, sem)
            copy.start()
            copy.wait()


def pick_kernel(n_row, block_size, wanted, vectors, out, sems):
    def fetch(k):
        at = pl.multiple_of(wanted[k, 0] * block_size, block_size)
        return pltpu.make_async_copy(vectors.at[pl.ds(at, block_size)], out.at[k], sems.at[k])

    for k in range(n_row):
        fetch(k).start()
    for k in range(n_row):
        fetch(k).wait()


def pack_kernel(picked, picked_b, out, held, sem):
    n_row, _, width = picked.shape
    middle = width // 2

    def put(k):
        return pltpu.make_async_copy(held.at[k], out.at[k], sem)

    for half in range(2):

        @pl.when(core_number() == half)
        def _():
            part = slice(half * middle, (half + 1) * middle)
            for k in range(n_row):
                held[k] = jnp.concatenate([picked[k, :, part], picked_b[k, :, part]], axis=1)
                put(k).start()

    pltpu.make_async_copy(held, out, sem).wait()


def fetches(plan, base, stride, ends, part, tiles, blocks, sems):
    def copy(tile, i):
        slot = plan[base + stride * i]
        return pltpu.make_async_copy(tile.at[slot], blocks.at[i], sems.at[i])

    def start():
        for side, tile in enumerate(tiles):

            @pl.loop(side * part, plan[ends + side])
            def _(i):
                copy(tile, i).start()

    def wait(i):
        copy(tiles[0], i).wait()

    return start, wait


def load_kernel(plan, tile_a, array, blocks, held, sems, held_sem):
    whole = pltpu.make_async_copy(array, held, held_sem)
    whole.start()
    number = jnp.minimum(plan[0], LEAD)

    def copy(i):
        return pltpu.make_async_copy(
            tile_a.at[plan[HEAD + STRIDE * i]], blocks.at[i], sems.at[i]
        )

    @pl.loop(0, number)
    def _(i):
        copy(i).start()

    @pl.loop(0, number)
    def _(i):
        copy(i).wait()

    whole.wait()


def each_product(
    plan, base, ends, part, block_of, pieces, use, then=None, before=None, segments=None
):
    unroll = MANY if base == HEAD else FEW

    if segments is None:
        segments = [(side, side * part, plan[ends + side]) for side in range(2)]
    for number, (side, begin, end) in enumerate(segments):

        @pl.loop(begin // unroll, end // unroll)
        def _(j):
            step = [(unroll * j + u, base + STRIDE * (unroll * j + u)) for u in range(unroll)]
            if before is not None:
                for i, entry in step:
                    before(number, i, entry)
            for i, entry in step:
                block = block_of(number, i, entry)
                piece = pieces[side][plan[entry + 2]]
                use(entry, jnp.dot(block, piece, preferred_element_type=jnp.float32))
            if then is not None:
                for i, entry in step:
                    then(entry)


def add_products(plan, base, ends, part, block_of, pieces, total, before=None):
    def use(entry, value):
        total[plan[entry + 1]] += value

    each_product(plan, base, ends, part, block_of, pieces, use, before=before)


def split_sides(pieces, vec):
    middle = vec.shape[-1] // 2
    column = lax.broadcasted_iota(jnp.int32, (1, vec.shape[-1]), 1)
    for side in range(2):
        keep = jnp.where((column // middle) == side, 1.0, 0.0).astype(jnp.bfloat16)
        for p in range(vec.shape[1]):
            vec[side, p] = pieces[p] * keep


def joined(total, k):
    one, two = total[2 * k], total[2 * k + 1]
    low = lax.broadcasted_iota(jnp.int32, one.shape, 1) < one.shape[1] // 2
    return jnp.where(low, one, two) + pltpu.roll(
        jnp.where(low, two, one), one.shape[1] // 2, axis=1
    )


def first_sent_kernel(
    lay, plan, tile_a, tile_b, pieces, start, out, blocks, vec, total, held, held_sem, sems
):
    n_row = out.shape[0]
    begin, wait = fetches(plan, lay.load_at, 1, 4, lay.loads, (tile_a, tile_b), blocks, sems)
    begin()
    copy = pltpu.make_async_copy(start, held, held_sem)
    copy.start()
    split_sides(pieces, vec)
    total[...] = jnp.zeros_like(total)

    def before(side, i, entry):
        @pl.when(plan[entry + 3] == FIRST)
        def _():
            wait(plan[entry])

    add_products(
        plan,
        lay.sent_at,
        2,
        lay.sends,
        lambda side, i, entry: blocks[plan[entry]],
        (vec.at[0], vec.at[1]),
        total,
        before,
    )
    copy.wait()
    for k in range(n_row):
        value = joined(total, k) - center_value * held[k].astype(jnp.float32)
        out[k] = (value / half_width).astype(jnp.bfloat16)


def second_sent_kernel(
    lay, plan, blocks, pieces, current, previous, out, vec, total, held, held_sem, ready, out_sem
):
    n_row = out.shape[0]
    copy = pltpu.make_async_copy(previous, held, held_sem)
    copy.start()
    split_sides(pieces, vec)
    total[...] = jnp.zeros_like(total)
    add_products(
        plan,
        lay.sent_at,
        2,
        lay.sends,
        lambda side, i, entry: blocks[plan[entry]],
        (vec.at[0], vec.at[1]),
        total,
    )
    copy.wait()

    def put(k):
        return pltpu.make_async_copy(ready.at[k], out.at[k], out_sem)

    for k in range(n_row):
        value = joined(total, k) - center_value * current[k].astype(jnp.float32)
        ready[k] = (value - held[k].astype(jnp.float32)).astype(jnp.bfloat16)
        put(k).start()
    pltpu.make_async_copy(ready, out, out_sem).wait()


def whole_columns(half, mine, other, vec, at):
    n_row, _, width = mine.shape
    middle = width // 2

    @pl.when(half == 0)
    def _():
        for p in range(n_row):
            one, two = mine[p], other[p]
            vec[0, p, :, at : at + width] = jnp.concatenate([one[:, :middle], two[:, middle:]], axis=1)
            vec[1, p, :, at : at + width] = jnp.concatenate([one[:, middle:], two[:, :middle]], axis=1)

    @pl.when(half != 0)
    def _():
        for p in range(n_row):
            one, two = mine[p], other[p]
            vec[0, p, :, at : at + width] = jnp.concatenate([two[:, middle:], one[:, :middle]], axis=1)
            vec[1, p, :, at : at + width] = jnp.concatenate([two[:, :middle], one[:, middle:]], axis=1)


def prime_kernel(vectors, total, own, sem):
    _, block_size, double = total.shape
    width = double // 2
    copy = pltpu.make_async_copy(vectors, own, sem)
    copy.start()
    copy.wait()

    @pl.loop(0, vectors.shape[0] // block_size)
    def _(b):
        at = pl.ds(pl.multiple_of(b * block_size, block_size), block_size)
        value = own[at, :].astype(jnp.float32)
        total[b, :, :width] = -center_value * value
        total[b, :, width:] = -value


def early_kernel(
    lay,
    plan,
    tile_a,
    tile_b,
    q1,
    q1_other,
    q2,
    q2_other,
    start,
    base,
    total,
    vec,
    own,
    blocks,
    sems,
    row_sem,
):
    piece_blocks, block_size, width = base.shape
    begin, wait = fetches(plan, HEAD, STRIDE, 0, lay.slots, (tile_a, tile_b), blocks, sems)
    begin()
    whole_columns(plan[7], q1, q1_other, vec, 0)
    whole_columns(plan[7], q2, q2_other, vec, width)

    def rows(b):
        return pl.ds(pl.multiple_of(b * block_size, block_size), block_size)

    def put(b):
        return pltpu.make_async_copy(own.at[rows(b)], base.at[b], row_sem)

    add_products(
        plan,
        HEAD,
        0,
        lay.slots,
        lambda side, i, entry: blocks[i],
        (vec.at[0], vec.at[1]),
        total,
        lambda side, i, entry: wait(i),
    )

    @pl.loop(0, piece_blocks)
    def _(b):
        first = (total[b, :, :width] / half_width).astype(jnp.bfloat16).astype(jnp.float32)
        second = total[b, :, width:] - center_value * first
        second = second.astype(jnp.bfloat16).astype(jnp.float32)
        own[rows(b), :] = (-center_value * second - first).astype(jnp.bfloat16)
        put(b).start()

    pltpu.make_async_copy(base, base, row_sem).wait()


def last_kernel(
    lay, plan, blocks, tile_a, tile_b, mine, other, base, out, vec, total, own, blocks_b, sems, out_sem
):
    piece_blocks = base.shape[0]
    begin, own_end = lay.slots, plan[0]

    def fetch(tile, i):
        slot = plan[HEAD + STRIDE * i]
        return pltpu.make_async_copy(
            tile.at[slot], blocks_b.at[i - LEAD], sems.at[i - LEAD]
        )

    @pl.loop(LEAD, own_end)
    def _(i):
        fetch(tile_a, i).start()

    @pl.loop(begin, plan[1])
    def _(i):
        fetch(tile_b, i).start()

    def put(source, b):
        return pltpu.make_async_copy(source.at[b], out.at[b], out_sem)

    @pl.loop(0, plan[6])
    def _(i):
        b = plan[lay.bare_at + i]
        put(base, b).start()

    whole_columns(plan[7], mine, other, vec, 0)

    def use(entry, value):
        row = plan[entry + 1]
        marks = plan[entry + 3]
        start = base[jnp.minimum(row, piece_blocks - 1)].astype(jnp.float32)
        value = jnp.where(lax.rem(marks, LAST) == FIRST, start, total[row]) + value
        total[row] = value
        own[row] = value.astype(jnp.bfloat16)

    def then(entry):
        @pl.when(plan[entry + 3] >= LAST)
        def _():
            put(own, plan[entry + 1]).start()

    def block_of(number, i, entry):
        return blocks[i] if number == 0 else blocks_b[i - LEAD]

    def before(number, i, entry):
        if number > 0:
            fetch(tile_a, i).wait()

    segments = [
        (0, 0, jnp.minimum(own_end, LEAD)),
        (0, LEAD, own_end),
        (1, begin, plan[1]),
    ]
    each_product(
        plan,
        HEAD,
        0,
        lay.slots,
        block_of,
        (vec.at[0], vec.at[1]),
        use,
        then,
        before,
        segments,
    )

    pltpu.make_async_copy(base, out, out_sem).wait()


def after(value, *others):
    return lax.optimization_barrier((value, *others))[0]


def call(kernel, out, args, spaces, scratch, mib, name, estimate=None, aliases=None):
    args = [
        pltpu.with_memory_space_constraint(arg, space) if space in (VMEM, HBM) or tied else arg
        for arg, (space, tied) in zip(args, spaces)
    ]
    return pl.pallas_call(
        kernel,
        out_shape=[space(shape, dtype) for shape, dtype, space in out],
        in_specs=[spec(space) for space, _ in spaces],
        out_specs=[spec(space) for _, _, space in out],
        scratch_shapes=scratch,
        compiler_params=params(mib),
        cost_estimate=estimate,
        input_output_aliases=aliases or {},
        name=name,
    )(*args)


HERE = (VMEM, True)
FAR = (HBM, True)
LIST = (SMEM, True)
SCALARS = (SMEM, False)
ANYWHERE = (pl.ANY, False)


def on_pair(vectors, tile_blocks, block_rows, block_cols, counts):
    n_row = lax.axis_size("row")
    tile = tile_blocks[0, 0]
    slot_rows = block_rows[0, 0]
    slot_cols = block_cols[0, 0]
    used = counts[0]
    slot_count, block_size, _ = tile.shape
    width = vectors.shape[1]
    piece_blocks = vectors.shape[0] // block_size

    across = functools.partial(lax.ppermute, axis_name="col", perm=[(0, 1), (1, 0)])

    needed = jnp.max(
        jnp.where(
            slot_cols[None, :] // piece_blocks == jnp.arange(n_row)[:, None],
            slot_cols[None, :] % piece_blocks,
            0,
        ),
        axis=1,
        keepdims=True,
    )
    exchange = functools.partial(
        lax.all_to_all, axis_name="row", split_axis=0, concat_axis=0, tiled=True
    )
    wanted = exchange(jnp.broadcast_to(needed, (n_row, LANES)))
    sent_shape = (n_row, block_size, width)
    (sent,) = call(
        functools.partial(pick_kernel, n_row, block_size),
        [(sent_shape, jnp.bfloat16, VMEM)],
        (wanted, vectors),
        (SCALARS, FAR),
        [DMA((n_row,))],
        2,
        "pick",
    )
    tile_other = across(tile)
    sent_other = across(sent)
    wanted_other = across(after(wanted, sent))
    meta = jnp.concatenate([slot_rows, slot_cols, used])
    meta_other = across(after(meta, sent))
    packed = call(
        pack_kernel,
        [(sent_shape, jnp.bfloat16, HBM)],
        (sent, sent_other),
        (HERE, HERE),
        [VMEM(sent_shape, jnp.bfloat16), DMA],
        4,
        "pack",
    )[0]

    lay = layout_for(slot_count, n_row, piece_blocks)
    list_shape = ((lay.size,), jnp.int32)
    own_list, other_list = call(
        functools.partial(plan_kernel, n_row, piece_blocks, lay),
        [(*list_shape, HBM)] * 2,
        (wanted, after(wanted_other, packed), meta, meta_other),
        (SCALARS,) * 4,
        [
            SMEM((2 * lay.size,), jnp.int32),
            SMEM((2 * n_row,), jnp.int32),
            SMEM((piece_blocks + 1,), jnp.int32),
            DMA((2,)),
        ],
        2,
        "plan",
    )
    q1 = exchange(after(packed, own_list))
    plan = call(
        settle_kernel,
        [(*list_shape, SMEM)],
        (own_list, across(after(other_list, packed))),
        (ANYWHERE, ANYWHERE),
        [DMA],
        2,
        "settle",
    )[0]

    def load(cue, array):
        return call(
            load_kernel,
            [
                ((LEAD, block_size, block_size), jnp.bfloat16, VMEM),
                (array.shape, array.dtype, VMEM),
            ],
            (after(plan, cue), tile, array),
            (LIST, FAR, FAR),
            [DMA((LEAD,)), DMA],
            2,
            "load",
        )

    def cost(products, rows):
        size = block_size * width
        return pl.CostEstimate(
            flops=2 * products * block_size * size,
            bytes_accessed=2 * (products * block_size * block_size + 3 * rows * size),
            transcendentals=0,
        )

    sums = [
        VMEM((2, n_row, block_size, width), jnp.bfloat16),
        VMEM((2 * n_row + 1, block_size, width), jnp.float32),
    ]

    def first_blocks(*args):
        return call(
            functools.partial(first_sent_kernel, lay),
            [
                (sent_shape, jnp.bfloat16, VMEM),
                ((2 * lay.loads, block_size, block_size), jnp.bfloat16, VMEM),
            ],
            (plan, tile, tile_other, *args),
            (LIST, FAR, ANYWHERE, HERE, FAR),
            sums + [VMEM(sent_shape, jnp.bfloat16), DMA, DMA((2 * lay.loads,))],
            8,
            "sent",
            cost(n_row, n_row),
        )

    def second_blocks(*args):
        return call(
            functools.partial(second_sent_kernel, lay),
            [(sent_shape, jnp.bfloat16, HBM)],
            (plan, *args),
            (LIST, HERE, HERE, HERE, FAR),
            sums
            + [VMEM(sent_shape, jnp.bfloat16), DMA, VMEM(sent_shape, jnp.bfloat16), DMA],
            8,
            "sent",
            cost(n_row, n_row),
        )[0]

    base_shape = (piece_blocks, block_size, width)

    sums_shape = ((piece_blocks + 1, block_size, 2 * width), jnp.float32, VMEM)

    def early(*args):
        return call(
            functools.partial(early_kernel, lay),
            [(base_shape, jnp.bfloat16, HBM), sums_shape],
            (plan, tile, tile_other, *args),
            (LIST, FAR, ANYWHERE, HERE, HERE, HERE, HERE, HERE),
            [
                VMEM((2, n_row, block_size, 2 * width), jnp.bfloat16),
                VMEM(vectors.shape, jnp.bfloat16),
                VMEM((2 * lay.slots, block_size, block_size), jnp.bfloat16),
                DMA((2 * lay.slots,)),
                DMA,
            ],
            18,
            "early",
            cost(2 * slot_count, 2 * piece_blocks),
            {7: 1},
        )[0]

    def last(blocks, *args):
        rows = (piece_blocks + 1, block_size, width)
        (out,) = call(
            functools.partial(last_kernel, lay),
            [(base_shape, jnp.bfloat16, HBM)],
            (plan, blocks, tile, tile_other, *args),
            (LIST, HERE, FAR, ANYWHERE, HERE, HERE, HERE),
            [
                VMEM((2, n_row, block_size, width), jnp.bfloat16),
                VMEM(rows, jnp.float32),
                VMEM(rows, jnp.bfloat16),
                VMEM((2 * lay.slots - LEAD, block_size, block_size), jnp.bfloat16),
                DMA((2 * lay.slots - LEAD,)),
                DMA,
            ],
            18,
            "last",
            cost(slot_count, piece_blocks),
        )
        return out.reshape(vectors.shape)

    q1 = after(q1, plan)
    first_sent, blocks = first_blocks(q1, packed)
    q2 = exchange(first_sent)
    second_sent = second_blocks(blocks, q2, first_sent, packed)
    q1_other = across(after(q1, second_sent))
    q2_other = across(after(q2, second_sent))
    (start,) = call(
        prime_kernel,
        [sums_shape],
        (after(vectors, second_sent),),
        (FAR,),
        [VMEM(vectors.shape, jnp.bfloat16), DMA],
        4,
        "prime",
        cost(0, 3 * piece_blocks),
    )
    base = early(q1, q1_other, q2, q2_other, start)
    q3 = after(exchange(second_sent), base)
    q3_other = across(q3)
    blocks, base = load(q3, base)
    return last(blocks, q3, q3_other, base)


def on_any(vectors, tile_blocks, block_rows, block_cols, counts):
    n_row = lax.axis_size("row")
    n_col = lax.axis_size("col")
    tile_data = tile_blocks[0, 0]
    slot_rows = block_rows[0, 0]
    slot_cols = block_cols[0, 0]
    used = counts[0, 0]
    block_size = tile_data.shape[-1]
    width = vectors.shape[1]
    piece_blocks = vectors.shape[0] // block_size
    row_blocks = piece_blocks * n_col
    slot_count = tile_data.shape[0]
    live = (jnp.arange(slot_count) < used).astype(jnp.float32)
    onehot = (slot_rows[None, :] == jnp.arange(row_blocks)[:, None]).astype(jnp.float32) * live[
        None, :
    ]
    source_piece = slot_cols // piece_blocks
    offset = slot_cols % piece_blocks
    needed = jnp.max(
        jnp.where(source_piece[None, :] == jnp.arange(n_row)[:, None], offset[None, :], 0), axis=1
    )
    wanted = lax.all_to_all(
        needed.reshape(n_row, 1), "row", split_axis=0, concat_axis=0, tiled=True
    ).reshape(n_row)

    def apply_tiles(current):
        own_blocks = current.reshape(piece_blocks, block_size, width)
        outgoing = jnp.take(own_blocks, wanted, axis=0)
        received = lax.all_to_all(outgoing, "row", split_axis=0, concat_axis=0, tiled=True)
        vec_blocks = jnp.take(received, source_piece, axis=0)
        products = jnp.einsum(
            "sij,sjk->sik", tile_data, vec_blocks, preferred_element_type=jnp.float32
        )
        term = jnp.einsum("ls,sik->lik", onehot, products, precision=lax.Precision.HIGHEST)
        term = term.reshape(row_blocks * block_size, width)
        return lax.psum_scatter(
            term.astype(jnp.bfloat16), "col", scatter_dimension=0, tiled=True
        ).astype(jnp.float32)

    previous = vectors
    applied = apply_tiles(vectors)
    current = ((applied - center_value * previous.astype(jnp.float32)) / half_width).astype(
        jnp.bfloat16
    )
    for repeat in range(DEGREE - 1):
        applied = apply_tiles(current)
        following = (
            2.0 * (applied - center_value * current.astype(jnp.float32)) / half_width
            - previous.astype(jnp.float32)
        ).astype(jnp.bfloat16)
        previous, current = (current, following)
    return current


def solution(mesh):
    n_row, n_col = mesh.shape["row"], mesh.shape["col"]
    paired = n_col == 2 and n_row & (n_row - 1) == 0
    return jax.shard_map(
        on_pair if paired else on_any,
        mesh=mesh,
        in_specs=(
            P(("row", "col"), "vec"),
            P("row", "col", None, None, None),
            P("row", "col", None),
            P("row", "col", None),
            P("row", "col"),
        ),
        out_specs=P(("row", "col"), "vec"),
        check_vma=False,
    )
```

```python
import functools
import typing

import jax
import jax.numpy as jnp
from jax import lax
from jax.experimental import pallas as pl
from jax.experimental.pallas import tpu as pltpu
from jax.sharding import PartitionSpec as P

DEGREE = 3

center_value = 0.5
half_width = 2.0

VMEM = pltpu.VMEM
SMEM = pltpu.SMEM
HBM = pltpu.HBM
DMA = pltpu.SemaphoreType.DMA
LANES = 128
FEW = 4
MANY = 4
LEAD = 3 * MANY
HEAD = 8
STRIDE = 4
FIRST = 1
LAST = 2


def spec(space):
    return pl.BlockSpec(memory_space=space)


def params(mib):
    return pltpu.CompilerParams(vmem_limit_bytes=mib * 1024 * 1024)


def round_up(n, step):
    return (n + step - 1) // step * step


def core_number():
    return lax.axis_index("col")


class Layout(typing.NamedTuple):
    slots: int
    sends: int
    loads: int
    sent_at: int
    load_at: int
    bare_at: int
    size: int


def layout_for(slot_count, n_row, piece_blocks):
    slots = round_up(slot_count, MANY) + MANY
    sends = round_up(2 * n_row * n_row, FEW) + FEW
    sent_at = HEAD + STRIDE * 2 * slots
    load_at = sent_at + STRIDE * 2 * sends
    bare_at = load_at + 2 * (slot_count + 1)
    size = round_up(bare_at + piece_blocks, 8 * LANES)
    return Layout(slots, sends, slot_count + 1, sent_at, load_at, bare_at, size)


def plan_kernel(
    n_row,
    piece_blocks,
    lay,
    wanted_a,
    wanted_b,
    meta_a,
    meta_b,
    own,
    other,
    out,
    asked,
    seen,
    sems,
):
    slot_count = (meta_a.shape[0] - 1) // 2

    def put(at, *values):
        for i, value in enumerate(values):
            out[at + i] = value

    def scan(tile, meta):
        used = meta[2 * slot_count]


        def step(s, carry):
            ends, sent, load = carry
            row = meta[s]
            piece = meta[slot_count + s] // piece_blocks
            live = s < used
            half = row // piece_blocks
            local = row - half * piece_blocks
            lower = half == 0
            part = jnp.where(lower, tile, 1 - tile)
            at = HEAD + STRIDE * (part * lay.slots + jnp.where(lower, ends[0], ends[1]))
            base = half * lay.size
            put(base + at, s, local, piece)
            sought = jnp.where(live, local, -1)
            hits = [(asked[half * n_row + k] == sought).astype(jnp.int32) for k in range(n_row)]
            found = sum(hits)

            @pl.when(found > 0)
            def _():
                for core in range(2):
                    mine = tile if core == 0 else 1 - tile
                    side = half if core == 0 else 1 - half
                    first = core * lay.size
                    out[first + lay.load_at + mine * lay.loads + load] = s

                    place = sent
                    for k in range(n_row):
                        put(
                            first + lay.sent_at + STRIDE * (mine * lay.sends + place),
                            mine * lay.loads + load,
                            2 * k + side,
                            piece,
                            jnp.where(place == sent, FIRST, 0),
                        )
                        place = place + hits[k]

            one = live.astype(jnp.int32)
            ends = (ends[0] + jnp.where(lower, one, 0), ends[1] + jnp.where(lower, 0, one))
            return ends, sent + found, load + jnp.where(found > 0, 1, 0)

        zero = jnp.int32(0)
        ends, sent, load = lax.fori_loop(0, slot_count, step, ((zero, zero), zero, zero))
        for core in range(2):
            mine = tile if core == 0 else 1 - tile
            base = core * lay.size
            for i, (at, begin, end, unit, spare) in enumerate(
                (
                    (HEAD, mine * lay.slots, ends[core], MANY, piece_blocks),
                    (lay.sent_at, mine * lay.sends, sent, FEW, 2 * n_row),
                )
            ):
                for u in range(unit - 1):
                    put(base + at + STRIDE * (begin + end + u), 0, spare, 0, 0)
                out[base + 2 * i + mine] = begin + (end + unit - 1) // unit * unit
            out[base + 4 + mine] = mine * lay.loads + load

    def mark(core):
        base = core * lay.size
        for b in range(piece_blocks + 1):
            seen[b] = 0
        for part in range(2):

            @pl.loop(part * lay.slots, out[base + part])
            def _(i):
                entry = base + HEAD + STRIDE * i
                row = out[entry + 1]
                out[entry + 3] = jnp.where(seen[row] == 0, FIRST, 0)
                seen[row] = entry

        def close(b, bare):
            entry = seen[b]
            out[base + lay.bare_at + bare] = b

            @pl.when(entry > 0)
            def _():
                out[entry + 3] = out[entry + 3] + LAST

            return bare + jnp.where(entry == 0, 1, 0)

        out[base + 6] = lax.fori_loop(0, piece_blocks, close, jnp.int32(0))
        out[base + 7] = core

    @pl.when(core_number() == 0)
    def _():
        for half, wanted in enumerate((wanted_a, wanted_b)):
            for k in range(n_row):
                asked[half * n_row + k] = wanted[k, 0]
        scan(0, meta_a)
        scan(1, meta_b)
        for core in range(2):
            mark(core)
        copies = [
            pltpu.make_async_copy(out.at[pl.ds(core * lay.size, lay.size)], target, sems.at[core])
            for core, target in enumerate((own, other))
        ]
        for copy in copies:
            copy.start()
        for copy in copies:
            copy.wait()


def settle_kernel(own, handed, out, sem):
    for half, source in enumerate((own, handed)):

        @pl.when(core_number() == half)
        def _():
            copy = pltpu.make_async_copy(source, out, sem)
            copy.start()
            copy.wait()


def pick_kernel(n_row, block_size, wanted, vectors, out, sem):
    def fetch(k):
        at = pl.multiple_of(wanted[k, 0] * block_size, block_size)
        return pltpu.make_async_copy(vectors.at[pl.ds(at, block_size)], out.at[k], sem)

    for k in range(n_row):
        fetch(k).start()
    pltpu.make_async_copy(out, out, sem).wait()


def pack_kernel(picked, picked_b, out, held, sem):
    n_row, _, width = picked.shape
    middle = width // 2

    def put(k):
        return pltpu.make_async_copy(held.at[k], out.at[k], sem)

    for half in range(2):

        @pl.when(core_number() == half)
        def _():
            part = slice(half * middle, (half + 1) * middle)
            for k in range(n_row):
                held[k] = jnp.concatenate([picked[k, :, part], picked_b[k, :, part]], axis=1)
                put(k).start()

    pltpu.make_async_copy(held, out, sem).wait()


def fetches(plan, base, stride, ends, part, tiles, blocks, sems):
    def copy(tile, i):
        slot = plan[base + stride * i]
        return pltpu.make_async_copy(tile.at[slot], blocks.at[i], sems.at[i])

    def start():
        for side, tile in enumerate(tiles):

            @pl.loop(side * part, plan[ends + side])
            def _(i):
                copy(tile, i).start()

    def wait(i):
        copy(tiles[0], i).wait()

    return start, wait


def load_kernel(plan, tile_a, array, blocks, held, sems, held_sem):
    whole = pltpu.make_async_copy(array, held, held_sem)
    whole.start()
    number = jnp.minimum(plan[0], LEAD)

    def copy(i):
        return pltpu.make_async_copy(
            tile_a.at[plan[HEAD + STRIDE * i]], blocks.at[i], sems.at[i]
        )

    @pl.loop(0, number)
    def _(i):
        copy(i).start()

    @pl.loop(0, number)
    def _(i):
        copy(i).wait()

    whole.wait()


def each_product(
    plan, base, ends, part, block_of, pieces, use, then=None, before=None, segments=None
):
    unroll = MANY if base == HEAD else FEW

    if segments is None:
        segments = [(side, side * part, plan[ends + side]) for side in range(2)]
    for number, (side, begin, end) in enumerate(segments):

        @pl.loop(begin // unroll, end // unroll)
        def _(j):
            step = [(unroll * j + u, base + STRIDE * (unroll * j + u)) for u in range(unroll)]
            if before is not None:
                for i, entry in step:
                    before(number, i, entry)
            for i, entry in step:
                block = block_of(number, i, entry)
                piece = pieces[side][plan[entry + 2]]
                use(entry, jnp.dot(block, piece, preferred_element_type=jnp.float32))
            if then is not None:
                for i, entry in step:
                    then(entry)


def add_products(plan, base, ends, part, block_of, pieces, total, before=None):
    def use(entry, value):
        total[plan[entry + 1]] += value

    each_product(plan, base, ends, part, block_of, pieces, use, before=before)


def split_sides(pieces, vec):
    middle = vec.shape[-1] // 2
    column = lax.broadcasted_iota(jnp.int32, (1, vec.shape[-1]), 1)
    for side in range(2):
        keep = jnp.where((column // middle) == side, 1.0, 0.0).astype(jnp.bfloat16)
        for p in range(vec.shape[1]):
            vec[side, p] = pieces[p] * keep


def joined(total, k):
    one, two = total[2 * k], total[2 * k + 1]
    low = lax.broadcasted_iota(jnp.int32, one.shape, 1) < one.shape[1] // 2
    return jnp.where(low, one, two) + pltpu.roll(
        jnp.where(low, two, one), one.shape[1] // 2, axis=1
    )


def first_sent_kernel(
    lay, plan, tile_a, tile_b, pieces, start, out, blocks, vec, total, held, held_sem, sems
):
    n_row = out.shape[0]
    begin, wait = fetches(plan, lay.load_at, 1, 4, lay.loads, (tile_a, tile_b), blocks, sems)
    begin()
    copy = pltpu.make_async_copy(start, held, held_sem)
    copy.start()
    split_sides(pieces, vec)
    total[...] = jnp.zeros_like(total)

    def before(side, i, entry):
        @pl.when(plan[entry + 3] == FIRST)
        def _():
            wait(plan[entry])

    add_products(
        plan,
        lay.sent_at,
        2,
        lay.sends,
        lambda side, i, entry: blocks[plan[entry]],
        (vec.at[0], vec.at[1]),
        total,
        before,
    )
    copy.wait()
    for k in range(n_row):
        value = joined(total, k) - center_value * held[k].astype(jnp.float32)
        out[k] = (value / half_width).astype(jnp.bfloat16)


def second_sent_kernel(
    lay, plan, blocks, pieces, current, previous, out, vec, total, held, held_sem, ready, out_sem
):
    n_row = out.shape[0]
    copy = pltpu.make_async_copy(previous, held, held_sem)
    copy.start()
    split_sides(pieces, vec)
    total[...] = jnp.zeros_like(total)
    add_products(
        plan,
        lay.sent_at,
        2,
        lay.sends,
        lambda side, i, entry: blocks[plan[entry]],
        (vec.at[0], vec.at[1]),
        total,
    )
    copy.wait()

    def put(k):
        return pltpu.make_async_copy(ready.at[k], out.at[k], out_sem)

    for k in range(n_row):
        value = joined(total, k) - center_value * current[k].astype(jnp.float32)
        ready[k] = (value - held[k].astype(jnp.float32)).astype(jnp.bfloat16)
        put(k).start()
    pltpu.make_async_copy(ready, out, out_sem).wait()


def whole_columns(half, mine, other, vec, at):
    n_row, _, width = mine.shape
    middle = width // 2

    @pl.when(half == 0)
    def _():
        for p in range(n_row):
            one, two = mine[p], other[p]
            vec[0, p, :, at : at + width] = jnp.concatenate([one[:, :middle], two[:, middle:]], axis=1)
            vec[1, p, :, at : at + width] = jnp.concatenate([one[:, middle:], two[:, :middle]], axis=1)

    @pl.when(half != 0)
    def _():
        for p in range(n_row):
            one, two = mine[p], other[p]
            vec[0, p, :, at : at + width] = jnp.concatenate([two[:, middle:], one[:, :middle]], axis=1)
            vec[1, p, :, at : at + width] = jnp.concatenate([two[:, :middle], one[:, middle:]], axis=1)


def prime_kernel(vectors, total, own, sem):
    _, block_size, double = total.shape
    width = double // 2
    copy = pltpu.make_async_copy(vectors, own, sem)
    copy.start()
    copy.wait()

    @pl.loop(0, vectors.shape[0] // block_size)
    def _(b):
        at = pl.ds(pl.multiple_of(b * block_size, block_size), block_size)
        value = own[at, :].astype(jnp.float32)
        total[b, :, :width] = -center_value * value
        total[b, :, width:] = -value


def early_kernel(
    lay,
    plan,
    tile_a,
    tile_b,
    q1,
    q1_other,
    q2,
    q2_other,
    start,
    base,
    total,
    vec,
    own,
    blocks,
    sems,
    row_sem,
):
    piece_blocks, block_size, width = base.shape
    begin, wait = fetches(plan, HEAD, STRIDE, 0, lay.slots, (tile_a, tile_b), blocks, sems)
    begin()
    whole_columns(plan[7], q1, q1_other, vec, 0)
    whole_columns(plan[7], q2, q2_other, vec, width)

    def rows(b):
        return pl.ds(pl.multiple_of(b * block_size, block_size), block_size)

    def put(b):
        return pltpu.make_async_copy(own.at[rows(b)], base.at[b], row_sem)

    add_products(
        plan,
        HEAD,
        0,
        lay.slots,
        lambda side, i, entry: blocks[i],
        (vec.at[0], vec.at[1]),
        total,
        lambda side, i, entry: wait(i),
    )

    @pl.loop(0, piece_blocks)
    def _(b):
        first = (total[b, :, :width] / half_width).astype(jnp.bfloat16).astype(jnp.float32)
        second = total[b, :, width:] - center_value * first
        second = second.astype(jnp.bfloat16).astype(jnp.float32)
        own[rows(b), :] = (-center_value * second - first).astype(jnp.bfloat16)
        put(b).start()

    pltpu.make_async_copy(base, base, row_sem).wait()


def last_kernel(
    lay, plan, blocks, tile_a, tile_b, mine, other, base, out, vec, total, own, blocks_b, sems, out_sem
):
    piece_blocks = base.shape[0]
    begin, own_end = lay.slots, plan[0]

    def fetch(tile, i):
        slot = plan[HEAD + STRIDE * i]
        return pltpu.make_async_copy(
            tile.at[slot], blocks_b.at[i - LEAD], sems.at[i - LEAD]
        )

    @pl.loop(LEAD, own_end)
    def _(i):
        fetch(tile_a, i).start()

    @pl.loop(begin, plan[1])
    def _(i):
        fetch(tile_b, i).start()

    def put(source, b):
        return pltpu.make_async_copy(source.at[b], out.at[b], out_sem)

    @pl.loop(0, plan[6])
    def _(i):
        b = plan[lay.bare_at + i]
        put(base, b).start()

    whole_columns(plan[7], mine, other, vec, 0)

    def use(entry, value):
        row = plan[entry + 1]
        marks = plan[entry + 3]
        start = base[jnp.minimum(row, piece_blocks - 1)].astype(jnp.float32)
        value = jnp.where(lax.rem(marks, LAST) == FIRST, start, total[row]) + value
        total[row] = value
        own[row] = value.astype(jnp.bfloat16)

    def then(entry):
        @pl.when(plan[entry + 3] >= LAST)
        def _():
            put(own, plan[entry + 1]).start()

    def block_of(number, i, entry):
        return blocks[i] if number == 0 else blocks_b[i - LEAD]

    def before(number, i, entry):
        if number > 0:
            fetch(tile_a, i).wait()

    segments = [
        (0, 0, jnp.minimum(own_end, LEAD)),
        (0, LEAD, own_end),
        (1, begin, plan[1]),
    ]
    each_product(
        plan,
        HEAD,
        0,
        lay.slots,
        block_of,
        (vec.at[0], vec.at[1]),
        use,
        then,
        before,
        segments,
    )

    pltpu.make_async_copy(base, out, out_sem).wait()


def after(value, *others):
    return lax.optimization_barrier((value, *others))[0]


def call(kernel, out, args, spaces, scratch, mib, name, estimate=None, aliases=None):
    args = [
        pltpu.with_memory_space_constraint(arg, space) if space in (VMEM, HBM) or tied else arg
        for arg, (space, tied) in zip(args, spaces)
    ]
    return pl.pallas_call(
        kernel,
        out_shape=[space(shape, dtype) for shape, dtype, space in out],
        in_specs=[spec(space) for space, _ in spaces],
        out_specs=[spec(space) for _, _, space in out],
        scratch_shapes=scratch,
        compiler_params=params(mib),
        cost_estimate=estimate,
        input_output_aliases=aliases or {},
        name=name,
    )(*args)


HERE = (VMEM, True)
FAR = (HBM, True)
LIST = (SMEM, True)
SCALARS = (SMEM, False)
ANYWHERE = (pl.ANY, False)


def on_pair(vectors, tile_blocks, block_rows, block_cols, counts):
    n_row = lax.axis_size("row")
    tile = tile_blocks[0, 0]
    slot_rows = block_rows[0, 0]
    slot_cols = block_cols[0, 0]
    used = counts[0]
    slot_count, block_size, _ = tile.shape
    width = vectors.shape[1]
    piece_blocks = vectors.shape[0] // block_size

    across = functools.partial(lax.ppermute, axis_name="col", perm=[(0, 1), (1, 0)])

    needed = jnp.max(
        jnp.where(
            slot_cols[None, :] // piece_blocks == jnp.arange(n_row)[:, None],
            slot_cols[None, :] % piece_blocks,
            0,
        ),
        axis=1,
        keepdims=True,
    )
    exchange = functools.partial(
        lax.all_to_all, axis_name="row", split_axis=0, concat_axis=0, tiled=True
    )
    wanted = exchange(jnp.broadcast_to(needed, (n_row, LANES)))
    sent_shape = (n_row, block_size, width)
    (sent,) = call(
        functools.partial(pick_kernel, n_row, block_size),
        [(sent_shape, jnp.bfloat16, VMEM)],
        (wanted, vectors),
        (SCALARS, FAR),
        [DMA],
        2,
        "pick",
    )
    tile_other = across(tile)
    sent_other = across(sent)
    wanted_other = across(after(wanted, sent))
    meta = jnp.concatenate([slot_rows, slot_cols, used])
    meta_other = across(after(meta, sent))
    packed = call(
        pack_kernel,
        [(sent_shape, jnp.bfloat16, HBM)],
        (sent, sent_other),
        (HERE, HERE),
        [VMEM(sent_shape, jnp.bfloat16), DMA],
        4,
        "pack",
    )[0]

    lay = layout_for(slot_count, n_row, piece_blocks)
    list_shape = ((lay.size,), jnp.int32)
    own_list, other_list = call(
        functools.partial(plan_kernel, n_row, piece_blocks, lay),
        [(*list_shape, HBM)] * 2,
        (wanted, after(wanted_other, packed), meta, meta_other),
        (SCALARS,) * 4,
        [
            SMEM((2 * lay.size,), jnp.int32),
            SMEM((2 * n_row,), jnp.int32),
            SMEM((piece_blocks + 1,), jnp.int32),
            DMA((2,)),
        ],
        2,
        "plan",
    )
    q1 = exchange(after(packed, own_list))
    plan = call(
        settle_kernel,
        [(*list_shape, SMEM)],
        (own_list, across(after(other_list, packed))),
        (ANYWHERE, ANYWHERE),
        [DMA],
        2,
        "settle",
    )[0]

    def load(cue, array):
        return call(
            load_kernel,
            [
                ((LEAD, block_size, block_size), jnp.bfloat16, VMEM),
                (array.shape, array.dtype, VMEM),
            ],
            (after(plan, cue), tile, array),
            (LIST, FAR, FAR),
            [DMA((LEAD,)), DMA],
            2,
            "load",
        )

    def cost(products, rows):
        size = block_size * width
        return pl.CostEstimate(
            flops=2 * products * block_size * size,
            bytes_accessed=2 * (products * block_size * block_size + 3 * rows * size),
            transcendentals=0,
        )

    sums = [
        VMEM((2, n_row, block_size, width), jnp.bfloat16),
        VMEM((2 * n_row + 1, block_size, width), jnp.float32),
    ]

    def first_blocks(*args):
        return call(
            functools.partial(first_sent_kernel, lay),
            [
                (sent_shape, jnp.bfloat16, VMEM),
                ((2 * lay.loads, block_size, block_size), jnp.bfloat16, VMEM),
            ],
            (plan, tile, tile_other, *args),
            (LIST, FAR, ANYWHERE, HERE, FAR),
            sums + [VMEM(sent_shape, jnp.bfloat16), DMA, DMA((2 * lay.loads,))],
            8,
            "sent",
            cost(n_row, n_row),
        )

    def second_blocks(*args):
        return call(
            functools.partial(second_sent_kernel, lay),
            [(sent_shape, jnp.bfloat16, HBM)],
            (plan, *args),
            (LIST, HERE, HERE, HERE, FAR),
            sums
            + [VMEM(sent_shape, jnp.bfloat16), DMA, VMEM(sent_shape, jnp.bfloat16), DMA],
            8,
            "sent",
            cost(n_row, n_row),
        )[0]

    base_shape = (piece_blocks, block_size, width)

    sums_shape = ((piece_blocks + 1, block_size, 2 * width), jnp.float32, VMEM)

    def early(*args):
        return call(
            functools.partial(early_kernel, lay),
            [(base_shape, jnp.bfloat16, HBM), sums_shape],
            (plan, tile, tile_other, *args),
            (LIST, FAR, ANYWHERE, HERE, HERE, HERE, HERE, HERE),
            [
                VMEM((2, n_row, block_size, 2 * width), jnp.bfloat16),
                VMEM(vectors.shape, jnp.bfloat16),
                VMEM((2 * lay.slots, block_size, block_size), jnp.bfloat16),
                DMA((2 * lay.slots,)),
                DMA,
            ],
            18,
            "early",
            cost(2 * slot_count, 2 * piece_blocks),
            {7: 1},
        )[0]

    def last(blocks, *args):
        rows = (piece_blocks + 1, block_size, width)
        (out,) = call(
            functools.partial(last_kernel, lay),
            [(base_shape, jnp.bfloat16, HBM)],
            (plan, blocks, tile, tile_other, *args),
            (LIST, HERE, FAR, ANYWHERE, HERE, HERE, HERE),
            [
                VMEM((2, n_row, block_size, width), jnp.bfloat16),
                VMEM(rows, jnp.float32),
                VMEM(rows, jnp.bfloat16),
                VMEM((2 * lay.slots - LEAD, block_size, block_size), jnp.bfloat16),
                DMA((2 * lay.slots - LEAD,)),
                DMA,
            ],
            18,
            "last",
            cost(slot_count, piece_blocks),
        )
        return out.reshape(vectors.shape)

    q1 = after(q1, plan)
    first_sent, blocks = first_blocks(q1, packed)
    q2 = exchange(first_sent)
    second_sent = second_blocks(blocks, q2, first_sent, packed)
    q1_other = across(after(q1, second_sent))
    q2_other = across(after(q2, second_sent))
    (start,) = call(
        prime_kernel,
        [sums_shape],
        (after(vectors, second_sent),),
        (FAR,),
        [VMEM(vectors.shape, jnp.bfloat16), DMA],
        4,
        "prime",
        cost(0, 3 * piece_blocks),
    )
    base = early(q1, q1_other, q2, q2_other, start)
    q3 = after(exchange(second_sent), base)
    q3_other = across(q3)
    blocks, base = load(q3, base)
    return last(blocks, q3, q3_other, base)


def on_any(vectors, tile_blocks, block_rows, block_cols, counts):
    n_row = lax.axis_size("row")
    n_col = lax.axis_size("col")
    tile_data = tile_blocks[0, 0]
    slot_rows = block_rows[0, 0]
    slot_cols = block_cols[0, 0]
    used = counts[0, 0]
    block_size = tile_data.shape[-1]
    width = vectors.shape[1]
    piece_blocks = vectors.shape[0] // block_size
    row_blocks = piece_blocks * n_col
    slot_count = tile_data.shape[0]
    live = (jnp.arange(slot_count) < used).astype(jnp.float32)
    onehot = (slot_rows[None, :] == jnp.arange(row_blocks)[:, None]).astype(jnp.float32) * live[
        None, :
    ]
    source_piece = slot_cols // piece_blocks
    offset = slot_cols % piece_blocks
    needed = jnp.max(
        jnp.where(source_piece[None, :] == jnp.arange(n_row)[:, None], offset[None, :], 0), axis=1
    )
    wanted = lax.all_to_all(
        needed.reshape(n_row, 1), "row", split_axis=0, concat_axis=0, tiled=True
    ).reshape(n_row)

    def apply_tiles(current):
        own_blocks = current.reshape(piece_blocks, block_size, width)
        outgoing = jnp.take(own_blocks, wanted, axis=0)
        received = lax.all_to_all(outgoing, "row", split_axis=0, concat_axis=0, tiled=True)
        vec_blocks = jnp.take(received, source_piece, axis=0)
        products = jnp.einsum(
            "sij,sjk->sik", tile_data, vec_blocks, preferred_element_type=jnp.float32
        )
        term = jnp.einsum("ls,sik->lik", onehot, products, precision=lax.Precision.HIGHEST)
        term = term.reshape(row_blocks * block_size, width)
        return lax.psum_scatter(
            term.astype(jnp.bfloat16), "col", scatter_dimension=0, tiled=True
        ).astype(jnp.float32)

    previous = vectors
    applied = apply_tiles(vectors)
    current = ((applied - center_value * previous.astype(jnp.float32)) / half_width).astype(
        jnp.bfloat16
    )
    for repeat in range(DEGREE - 1):
        applied = apply_tiles(current)
        following = (
            2.0 * (applied - center_value * current.astype(jnp.float32)) / half_width
            - previous.astype(jnp.float32)
        ).astype(jnp.bfloat16)
        previous, current = (current, following)
    return current


def solution(mesh):
    n_row, n_col = mesh.shape["row"], mesh.shape["col"]
    paired = n_col == 2 and n_row & (n_row - 1) == 0
    return jax.shard_map(
        on_pair if paired else on_any,
        mesh=mesh,
        in_specs=(
            P(("row", "col"), "vec"),
            P("row", "col", None, None, None),
            P("row", "col", None),
            P("row", "col", None),
            P("row", "col"),
        ),
        out_specs=P(("row", "col"), "vec"),
        check_vma=False,
    )
```
